32 devices in a mesh: section: 2 (over y), dp: 16 (over z, x, core).
Axes of the slice: x: 2, y: 2, z: 4, core: 2. Of those that a mesh axis runs over, the one named last changes fastest.
Arguments:
- layer_input: bfloat16 [2, 2, 16, 1024, 512], P('section', None, 'dp'), may hold values from -6 to 6
- cotangent: bfloat16 [2, 16, 1024, 512], P(None, 'dp'), may hold values from -6 to 6
- src_segments: int32 [2, 16, 1024], P(None, 'dp'), may hold values from 0 to 3, as said below
- tgt_segments: int32 [2, 16, 1024], P(None, 'dp'), may hold values from 0 to 3, as said below
- attn_qkv: bfloat16 [2, 512, 1536], P('section'), may hold values from -0.25 to 0.25
- attn_out: bfloat16 [2, 512, 512], P('section'), may hold values from -1 to 1
- cross_proj: bfloat16 [2, 512, 1024], P('section'), may hold values from -0.5 to 0.5
- ffn_in: bfloat16 [2, 512, 2048], P('section'), may hold values from -0.25 to 0.25
- ffn_in_bias: float32 [2, 2048], P('section'), may hold values from -3 to 3
- ffn_out: bfloat16 [2, 2048, 512], P('section'), may hold values from -0.125 to 0.125
- ffn_out_bias: float32 [2, 512], P('section'), may hold values from -3 to 3
- norm_gain: float32 [2, 3, 512], P('section'), may hold values from 0.1 to 1.9
- norm_bias: float32 [2, 3, 512], P('section'), may hold values from -3 to 3
Outputs:
- layer_output: bfloat16 [2, 2, 16, 1024, 512], P('section', None, 'dp')
- input_grad: float32 [2, 2, 16, 1024, 512], P('section', None, 'dp')
- attn_qkv_grad: float32 [2, 512, 1536], P('section')
- attn_out_grad: float32 [2, 512, 512], P('section')
- cross_proj_grad: float32 [2, 512, 1024], P('section')
- ffn_in_grad: float32 [2, 512, 2048], P('section')
- ffn_in_bias_grad: float32 [2, 2048], P('section')
- ffn_out_grad: float32 [2, 2048, 512], P('section')
- ffn_out_bias_grad: float32 [2, 512], P('section')
- norm_gain_grad: float32 [2, 3, 512], P('section')
- norm_bias_grad: float32 [2, 3, 512], P('section')
The draws below stay inside these ranges and needn't reach their ends.
Inputs may be any that keep to these rules, and one draw needn't show every extreme that they name: `src_segments`: in every packed row the document numbers never fall and take every value of 0 to 3, each on 128 tokens or more. `tgt_segments`: in every packed row the document numbers never fall and take every value of 0 to 3, each on 128 tokens or more.
All inputs are finite; a program needn't handle non-finite values.
Results may differ from the reference program's by a relative error of at most 0.04.
Values may be sent and summed in bfloat16 or wider, within the bound.
A program may use at most 320 MiB of HBM per device.

```python
import math
import jax
import jax.numpy as jnp
from jax import lax

D = 512
HEADS = 8
FF = 2048
LEN = 1024
DOCS = 4
MICRO = 2
BATCH = 16


def cut_points(key):
    reach = LEN // (4 * DOCS)
    jitter = jax.random.randint(key, (MICRO, BATCH, DOCS - 1), -reach, reach + 1)
    cuts = jnp.arange(1, DOCS, dtype=jnp.int32) * (LEN // DOCS) + jitter
    positions = jnp.arange(LEN, dtype=jnp.int32)
    above = (positions[None, None, :, None] >= cuts[:, :, None, :]).astype(jnp.int32)
    return jnp.sum(above, axis=-1).astype(jnp.int32)


def draw_src_segments(key, part):
    key = jax.random.fold_in(key, 11)
    return cut_points(key)


def draw_tgt_segments(key, part):
    key = jax.random.fold_in(key, 23)
    return cut_points(key)


def shard_levels(key, dims, cuts, smallest, high):
    loudness, own = 1.0, jax.random.fold_in(key, 6)
    for position, blocks in cuts:
        heights = jnp.exp(jax.random.uniform(jax.random.fold_in(own, position), (blocks,), jnp.float32, smallest / len(cuts), high / len(cuts)))
        loudness = loudness * jnp.repeat(heights, dims[position] // blocks).reshape([-1 if axis == position else 1 for axis in range(len(dims))])
    return loudness


def gaussian(own_key, dims, scale, most, cuts=(), held_as=jnp.bfloat16):
    entries = jax.random.normal(own_key, dims, jnp.float32) * scale
    if len(cuts) > 0:
        entries = shard_levels(own_key, dims, cuts, -0.22, 0.18) * entries
    return jnp.clip(entries, min=-most, max=most).astype(held_as)


def setup_inputs(seed: int = 0) -> dict:
    streams_of = jax.random.split(jax.random.key(seed), 14)
    layer_input = gaussian(streams_of[0], (2, MICRO, BATCH, LEN, D), 1.0, 6.0, ((0, 2), (2, 16)))
    cotangent = gaussian(streams_of[1], (MICRO, BATCH, LEN, D), 1.0, 6.0, ((1, 16),))
    src_segments = draw_src_segments(jax.random.fold_in(streams_of[13], 71), 0)
    tgt_segments = draw_tgt_segments(jax.random.fold_in(streams_of[13], 71), 0)
    attn_qkv = gaussian(streams_of[4], (2, D, 3 * D), D ** -0.5, 0.25, ((0, 2),))
    attn_out = gaussian(streams_of[5], (2, D, D), (D // 16) ** -0.5, 1.0, ((0, 2),))
    cross_proj = gaussian(streams_of[6], (2, D, 2 * D), (D // 4) ** -0.5, 0.5, ((0, 2),))
    ffn_in = gaussian(streams_of[7], (2, D, FF), D ** -0.5, 0.25, ((0, 2),))
    ffn_in_bias = gaussian(streams_of[8], (2, FF), 0.5, 3.0, ((0, 2),), jnp.float32)
    ffn_out = gaussian(streams_of[9], (2, FF, D), FF ** -0.5, 0.125, ((0, 2),))
    ffn_out_bias = gaussian(streams_of[10], (2, D), 0.5, 3.0, ((0, 2),), jnp.float32)
    norm_gain = jnp.clip(1.0 + 0.18 * jax.random.normal(streams_of[11], (2, 3, D), jnp.float32), 0.1, 1.9)
    norm_bias = gaussian(streams_of[12], (2, 3, D), 0.5, 3.0, ((0, 2),), jnp.float32)
    return {"layer_input": layer_input, "cotangent": cotangent, "src_segments": src_segments, "tgt_segments": tgt_segments, "attn_qkv": attn_qkv, "attn_out": attn_out, "cross_proj": cross_proj, "ffn_in": ffn_in, "ffn_in_bias": ffn_in_bias, "ffn_out": ffn_out, "ffn_out_bias": ffn_out_bias, "norm_gain": norm_gain, "norm_bias": norm_bias}


EPSILON = 1e-05
NEGATIVE = -1000000000.0
HIGHEST = lax.Precision.HIGHEST

@jax.custom_vjp
def low(v):
    return lax.optimization_barrier(v.astype(jnp.bfloat16)).astype(jnp.float32)

@jax.custom_vjp
def low_back(v):
    return v

def low_keep(v):
    return (low(v), None)

def low_pass(kept, grad):
    return (grad,)

def back_keep(v):
    return (v, None)

def back_low(kept, grad):
    return (low(grad),)
low.defvjp(low_keep, low_pass)
low_back.defvjp(back_keep, back_low)

def matmul(left, right):
    return jnp.dot(left, right, precision=HIGHEST)

def norm_rows(value, gain, shift):
    centered = value - lax.optimization_barrier(jnp.mean(value, axis=-1, keepdims=True))
    spread = lax.optimization_barrier(jnp.mean(centered * centered, axis=-1, keepdims=True))
    return centered * lax.rsqrt(spread + EPSILON) * gain + shift

def attention(query, keys, values, allowed):
    length, width = query.shape
    span = keys.shape[0]
    head_dim = width // HEADS
    query_heads = query.reshape(length, HEADS, head_dim)
    key_heads = keys.reshape(span, HEADS, head_dim)
    value_heads = values.reshape(span, HEADS, head_dim)
    scores = jnp.einsum('qhd,khd->hqk', query_heads, key_heads, precision=HIGHEST) * (1.0 / math.sqrt(head_dim))
    scores = low_back(scores)
    scores = jnp.where(allowed[None], scores, NEGATIVE)
    weights = low(jax.nn.softmax(scores, axis=-1))
    mixed = jnp.einsum('hqk,khd->qhd', weights, value_heads, precision=HIGHEST).reshape(length, width)
    return low(low_back(mixed))

def feed_forward(hidden, w_in, b_in, w_back, b_back):
    pre_act = low_back(matmul(low(hidden), w_in) + b_in)
    activation = low(jax.nn.gelu(pre_act, approximate=False))
    return low_back(matmul(activation, w_back) + b_back)

def self_block(tokens, allowed, w_joint, w_out, gain, shift):
    width = tokens.shape[1]
    joint = low(low_back(matmul(tokens, w_joint)))
    attended = attention(joint[:, :width], joint[:, width:2 * width], joint[:, 2 * width:], allowed)
    return norm_rows(tokens + low_back(matmul(attended, w_out)), gain, shift)

def encoder_row(tokens, source_ids, params):
    w_joint, w_out, w_cross, w_in, b_in, w_back, b_back, gains, shifts = params
    allowed = source_ids[:, None] == source_ids[None, :]
    hidden = self_block(tokens, allowed, w_joint, w_out, gains[0], shifts[0])
    hidden = norm_rows(hidden + feed_forward(hidden, w_in, b_in, w_back, b_back), gains[1], shifts[1])
    memory = norm_rows(hidden, gains[2], shifts[2])
    cross_keys = low(low_back(matmul(low(memory), w_cross)))
    return (memory, cross_keys)

def decoder_row(tokens, cross_keys, target_ids, source_ids, params):
    w_joint, w_out, w_cross, w_in, b_in, w_back, b_back, gains, shifts = params
    length, width = tokens.shape
    positions = jnp.arange(length, dtype=jnp.int32)
    allowed = (target_ids[:, None] == target_ids[None, :]) & (positions[:, None] >= positions[None, :])
    hidden = self_block(tokens, allowed, w_joint, w_out, gains[0], shifts[0])
    query = low(low_back(matmul(low(hidden), w_cross[:, :width])))
    crossed = attention(query, cross_keys[:, :width], cross_keys[:, width:], target_ids[:, None] == source_ids[None, :])
    hidden = norm_rows(hidden + low_back(matmul(crossed, w_cross[:, width:])), gains[1], shifts[1])
    return norm_rows(hidden + feed_forward(hidden, w_in, b_in, w_back, b_back), gains[2], shifts[2])

def one_row(stack, row):
    source, target, source_ids, target_ids = row
    first = tuple((weight[0] for weight in stack))
    second = tuple((weight[1] for weight in stack))
    memory, cross_keys = encoder_row(source, source_ids, first)
    return (memory, decoder_row(target, cross_keys, target_ids, source_ids, second))

def reference(layer_input, cotangent, src_segments, tgt_segments, attn_qkv, attn_out, cross_proj, ffn_in, ffn_in_bias, ffn_out, ffn_out_bias, norm_gain, norm_bias):
    stack = tuple((weight.astype(jnp.float32) for weight in (attn_qkv, attn_out, cross_proj, ffn_in, ffn_in_bias, ffn_out, ffn_out_bias, norm_gain, norm_bias)))
    inputs = layer_input.astype(jnp.float32)
    count = MICRO * BATCH
    source_flat = src_segments.reshape(count, LEN)
    target_flat = tgt_segments.reshape(count, LEN)
    checked = jax.checkpoint(one_row)

    def forward(weights, both):
        rows = (both[0].reshape(count, LEN, D), both[1].reshape(count, LEN, D), source_flat, target_flat)
        return lax.map(lambda row: checked(weights, row), rows)
    (memories, outputs), pull = jax.vjp(forward, stack, inputs)
    weight_grads, input_grad = pull((jnp.zeros_like(memories), cotangent.astype(jnp.float32).reshape(count, LEN, D)))
    layer_output = jnp.stack([memories, outputs]).reshape(2, MICRO, BATCH, LEN, D).astype(jnp.bfloat16)
    return (layer_output, input_grad, weight_grads[0], weight_grads[1], weight_grads[2], weight_grads[3], weight_grads[4], weight_grads[5], weight_grads[6], weight_grads[7], weight_grads[8])
```

```python
import functools
import math

import jax
import jax.numpy as jnp
from jax import lax
from jax.experimental import pallas as pl
from jax.experimental.pallas import tpu as pltpu
from jax.sharding import PartitionSpec as P

HEADS = 8
EPSILON = 1e-05
NEGATIVE = -1000000000.0
BF = jnp.bfloat16
F32 = jnp.float32
LOG2E = 1.4426950408889634
QB = 256
CK = 128
TB = 256
VMEM_LIMIT = 60 * 1024 * 1024


def dot(left, right, lc=1, rc=0):
    return lax.dot_general(
        left, right, (((lc,), (rc,)), ((), ())), preferred_element_type=F32
    )


def norm_stats(value):
    centered = value - jnp.mean(value, axis=-1, keepdims=True)
    spread = jnp.mean(centered * centered, axis=-1, keepdims=True)
    scale = lax.rsqrt(spread + EPSILON)
    return centered * scale, scale


def norm_back(out_grad, unit, scale, gain):
    gain_grad = jnp.sum(out_grad * unit, axis=0, keepdims=True)
    shift_grad = jnp.sum(out_grad, axis=0, keepdims=True)
    inner = out_grad * gain
    mean_one = jnp.mean(inner, axis=-1, keepdims=True)
    mean_two = jnp.mean(inner * unit, axis=-1, keepdims=True)
    return scale * (inner - mean_one - unit * mean_two), gain_grad, shift_grad


def gelu_pair(u):
    phi = 0.5 + 0.5 * lax.erf(u * (1.0 / math.sqrt(2.0)))
    bell = jnp.exp(-0.5 * u * u) * (1.0 / math.sqrt(2.0 * math.pi))
    return u * phi, phi + u * bell


def key_codes(ids_row, length):
    column = jnp.broadcast_to(ids_row.astype(F32), (128, length)).T
    lane = lax.broadcasted_iota(jnp.int32, (length, 128), 1)
    spot = jnp.where(lane < 64, lane, lane - 64)
    codes = jnp.where(
        spot < 4,
        jnp.where(column == spot.astype(F32), 0.0, NEGATIVE),
        jnp.where(spot < 7, -1.0, 0.0),
    )
    return codes, lane < 64


def fill_keys(dst, keys_ref, codes, low_half):
    for pair in range(HEADS // 2):
        slab = keys_ref[:, pair * 128 : pair * 128 + 128].astype(F32)
        dst[2 * pair] = jnp.where(low_half, slab, codes).astype(BF)
        dst[2 * pair + 1] = jnp.where(low_half, codes, slab).astype(BF)


def query_rows(head):
    return (0, 64) if head % 2 == 0 else (64, 0)


def attend_loop(tab_ref, qaug, kaug, vt, attT_ref, lse_ref, oacc, mrow, lrow, length):
    for qb in range(length // QB):
        q = slice(qb * QB, qb * QB + QB)
        oacc[...] = jnp.zeros_like(oacc)
        mrow[...] = jnp.full_like(mrow, -3e38)
        lrow[...] = jnp.zeros_like(lrow)

        def step(kc, masked):
            k0 = pl.multiple_of(kc * CK, CK)
            ks = pl.ds(k0, CK)
            if masked:
                key_pos = k0 + lax.broadcasted_iota(jnp.int32, (CK, QB), 0)
                query_pos = qb * QB + lax.broadcasted_iota(jnp.int32, (CK, QB), 1)
                allowed = key_pos <= query_pos
            for h in range(HEADS):
                s = dot(kaug[h, ks, :], qaug[h, :, q])
                if masked:
                    s = jnp.where(allowed, s, NEGATIVE)
                m_old = mrow[h : h + 1, :]
                m_new = jnp.maximum(m_old, jnp.max(s, axis=0, keepdims=True))
                alpha = jnp.exp2(m_old - m_new)
                p = jnp.exp2(s - m_new)
                lrow[h : h + 1, :] = lrow[h : h + 1, :] * alpha + jnp.sum(
                    p, axis=0, keepdims=True
                )
                mrow[h : h + 1, :] = m_new
                hs = slice(h * 64, h * 64 + 64)
                oacc[hs, :] = oacc[hs, :] * alpha + dot(vt[hs, ks], p.astype(BF))

        @pl.loop(tab_ref[qb, 0], tab_ref[qb, 1])
        def _(kc):
            step(kc, False)

        @pl.loop(tab_ref[qb, 1], tab_ref[qb, 2])
        def _(kc):
            step(kc, True)

        for h in range(HEADS):
            hs = slice(h * 64, h * 64 + 64)
            attT_ref[hs, q] = (oacc[hs, :] * (1.0 / lrow[h : h + 1, :])).astype(BF)
        lse_ref[:, q] = mrow[...] + jnp.log2(lrow[...])


def query_codes(ids_row, length):
    row = lax.broadcasted_iota(jnp.int32, (16, length), 0)
    return jnp.where(row == jnp.broadcast_to(ids_row, (16, length)), 1.0, 0.0), row


def fill_queries(qaug, qT_ref, codes, row, lse_ref, length):
    for h in range(HEADS):
        a, b = query_rows(h)
        qaug[h, a : a + 64, :] = qT_ref[h * 64 : h * 64 + 64, :]
        extra = codes
        if lse_ref is not None:
            lse = lse_ref[h : h + 1, :]
            hi = lse.astype(BF).astype(F32)
            mid = (lse - hi).astype(BF).astype(F32)
            low = lse - hi - mid
            extra = jnp.where(row == 4, hi, jnp.where(row == 5, mid, jnp.where(row == 6, low, codes)))
        qaug[h, b : b + 16, :] = extra.astype(BF)
        qaug[h, b + 16 : b + 64, :] = jnp.zeros((48, length), BF)


def project_queries(src_ref, w_ref, qT_ref, length, width):
    @pl.loop(0, length // TB)
    def _(t):
        rows = pl.ds(pl.multiple_of(t * TB, TB), TB)
        q = dot(src_ref[rows, :], w_ref[:, :width]) * (0.125 * LOG2E)
        qT_ref[:, rows] = q.T.astype(BF)


def out_and_norm(attT_ref, w_ref, resid_ref, ln_ref, res_ref, hid_ref, length):
    @pl.loop(0, length // TB)
    def _(t):
        rows = pl.ds(pl.multiple_of(t * TB, TB), TB)
        a = dot(attT_ref[:, rows], w_ref[...], 0, 0)
        r = resid_ref[rows, :].astype(F32) + a
        res_ref[rows, :] = r.astype(BF)
        unit, _ = norm_stats(r)
        hid_ref[rows, :] = (unit * ln_ref[0:1, :] + ln_ref[1:2, :]).astype(BF)


def self_fwd_kernel(tab_ref, x_ref, ids_ref, w_ref, wout_ref, ln_ref,
                    qT_ref, k_ref, v_ref, attT_ref, lse_ref, res_ref, hid_ref,
                    kaug, qaug, vt, oacc, mrow, lrow):
    length, width = x_ref.shape
    project_queries(x_ref, w_ref, qT_ref, length, width)

    @pl.loop(0, length // TB)
    def _(t):
        rows = pl.ds(pl.multiple_of(t * TB, TB), TB)
        k_ref[rows, :] = dot(x_ref[rows, :], w_ref[:, width : 2 * width]).astype(BF)
        v = dot(x_ref[rows, :], w_ref[:, 2 * width :])
        v_ref[rows, :] = v.astype(BF)
        vt[:, rows] = v.T.astype(BF)

    codes, low_half = key_codes(ids_ref[...], length)
    fill_keys(kaug, k_ref, codes, low_half)
    qcodes, row = query_codes(ids_ref[...], length)
    fill_queries(qaug, qT_ref, qcodes, row, None, length)
    attend_loop(tab_ref, qaug, kaug, vt, attT_ref, lse_ref, oacc, mrow, lrow, length)
    out_and_norm(attT_ref, wout_ref, x_ref, ln_ref, res_ref, hid_ref, length)


def cross_fwd_kernel(tab_ref, h_ref, kv_ref, qids_ref, kids_ref, w_ref, ln_ref,
                     qT_ref, attT_ref, lse_ref, res_ref, hid_ref,
                     kaug, qaug, vt, oacc, mrow, lrow):
    length, width = h_ref.shape
    project_queries(h_ref, w_ref, qT_ref, length, width)

    @pl.loop(0, length // TB)
    def _(t):
        rows = pl.ds(pl.multiple_of(t * TB, TB), TB)
        vt[:, rows] = kv_ref[rows, width:].astype(F32).T.astype(BF)

    codes, low_half = key_codes(kids_ref[...], length)
    fill_keys(kaug, kv_ref, codes, low_half)
    qcodes, row = query_codes(qids_ref[...], length)
    fill_queries(qaug, qT_ref, qcodes, row, None, length)
    attend_loop(tab_ref, qaug, kaug, vt, attT_ref, lse_ref, oacc, mrow, lrow, length)
    out_and_norm(attT_ref, w_ref.at[:, width:], h_ref, ln_ref, res_ref, hid_ref, length)


def attend_back_loop(tab_ref, qaug, kaug, kt, vaug, doaug, jgT, qoff, koff, voff, dqacc, length):
    for qb in range(length // QB):
        q = slice(qb * QB, qb * QB + QB)
        dqacc[...] = jnp.zeros_like(dqacc)

        def step(kc, masked):
            k0 = pl.multiple_of(kc * CK, CK)
            ks = pl.ds(k0, CK)
            if masked:
                key_pos = k0 + lax.broadcasted_iota(jnp.int32, (CK, QB), 0)
                query_pos = qb * QB + lax.broadcasted_iota(jnp.int32, (CK, QB), 1)
                allowed = key_pos <= query_pos
            for h in range(HEADS):
                a, _ = query_rows(h)
                hs = slice(h * 64, h * 64 + 64)
                s = dot(kaug[h, ks, :], qaug[h, :, q])
                if masked:
                    s = jnp.where(allowed, s, NEGATIVE)
                p = jnp.exp2(s)
                dp = dot(vaug[h, ks, :], doaug[h, :, q])
                ds = (p * dp).astype(BF)
                pb = p.astype(BF)
                dqacc[hs, :] += dot(kt[hs, ks], ds)
                jgT[voff + h * 64 : voff + h * 64 + 64, ks] += dot(doaug[h, a : a + 64, q], pb, 1, 1)
                jgT[koff + h * 64 : koff + h * 64 + 64, ks] += dot(qaug[h, a : a + 64, q], ds, 1, 1)

        @pl.loop(tab_ref[qb, 0], tab_ref[qb, 1])
        def _(kc):
            step(kc, False)

        @pl.loop(tab_ref[qb, 1], tab_ref[qb, 2])
        def _(kc):
            step(kc, True)

        jgT[qoff : qoff + 512, q] = dqacc[...] * 0.125


def prepare_back(dr_ref, w_out, attT_ref, doT, doaug, length):
    @pl.loop(0, length // TB)
    def _(t):
        rows = pl.ds(pl.multiple_of(t * TB, TB), TB)
        doT[:, rows] = dot(w_out, dr_ref[rows, :], 1, 1).astype(BF)

    row = lax.broadcasted_iota(jnp.int32, (16, length), 0)
    for h in range(HEADS):
        a, b = query_rows(h)
        hs = slice(h * 64, h * 64 + 64)
        doh = doT[hs, :]
        doaug[h, a : a + 64, :] = doh
        delta = jnp.sum(doh.astype(F32) * attT_ref[hs, :].astype(F32), axis=0, keepdims=True)
        hi = delta.astype(BF).astype(F32)
        mid = (delta - hi).astype(BF).astype(F32)
        low = delta - hi - mid
        extra = jnp.where(row == 4, hi, jnp.where(row == 5, mid, jnp.where(row == 6, low, 0.0)))
        doaug[h, b : b + 16, :] = extra.astype(BF)
        doaug[h, b + 16 : b + 64, :] = jnp.zeros((48, length), BF)


def prepare_keys(keys_ref, values_ref, codes, low_half, kaug, kt, vaug, length):
    fill_keys(kaug, keys_ref, codes, low_half)
    fill_keys(vaug, values_ref, jnp.where(codes == NEGATIVE, 0.0, codes), low_half)

    @pl.loop(0, length // TB)
    def _(t):
        rows = pl.ds(pl.multiple_of(t * TB, TB), TB)
        kt[:, rows] = keys_ref[rows, :].astype(F32).T.astype(BF)


def finish_grads(jgT, jg, koff, length):
    rows_total = jgT.shape[0]
    for r in range(0, rows_total, 512):
        f = math.log(2.0) if r == koff else 1.0
        jg[r : r + 512, :] = (jgT[r : r + 512, :] * f).astype(BF)


def self_bwd_kernel(tab_ref, dh_ref, res_ref, x_ref, ids_ref, qT_ref, k_ref, v_ref, attT_ref,
                    lse_ref, w_ref, wout_ref, ln_ref,
                    dx_ref, dwT_ref, dwout_ref, dln_ref,
                    kaug, kt, vaug, qaug, doaug, doT, dqacc, jgT, jg, dr):
    length, width = x_ref.shape
    dln_ref[...] = jnp.zeros_like(dln_ref)

    @pl.loop(0, length // TB)
    def _(t):
        rows = pl.ds(pl.multiple_of(t * TB, TB), TB)
        unit, scale = norm_stats(res_ref[rows, :].astype(F32))
        d, gg, sg = norm_back(dh_ref[rows, :].astype(F32), unit, scale, ln_ref[0:1, :])
        dln_ref[0:1, :] += gg
        dln_ref[1:2, :] += sg
        dr[rows, :] = d.astype(BF)

    dwout_ref[...] = dot(attT_ref[...], dr[...]).astype(BF)
    prepare_back(dr, wout_ref[...], attT_ref, doT, doaug, length)
    codes, low_half = key_codes(ids_ref[...], length)
    prepare_keys(k_ref, v_ref, codes, low_half, kaug, kt, vaug, length)
    qcodes, row = query_codes(ids_ref[...], length)
    fill_queries(qaug, qT_ref, qcodes, row, lse_ref, length)
    jgT[width:, :] = jnp.zeros((2 * width, length), F32)
    attend_back_loop(tab_ref, qaug, kaug, kt, vaug, doaug, jgT, 0, width, 2 * width, dqacc, length)
    finish_grads(jgT, jg, width, length)
    @pl.loop(0, 3 * width // TB)
    def _(t):
        rows = pl.ds(pl.multiple_of(t * TB, TB), TB)
        dwT_ref[rows, :] = dot(jg[rows, :], x_ref[...]).astype(BF)

    @pl.loop(0, length // TB)
    def _(t):
        rows = pl.ds(pl.multiple_of(t * TB, TB), TB)
        d = dot(jg[:, rows], w_ref[...], 0, 1)
        dx_ref[rows, :] = (dr[rows, :].astype(F32) + d).astype(dx_ref.dtype)


def cross_bwd_kernel(tab_ref, dr_ref, h_ref, mem_ref, qids_ref, kids_ref, qT_ref, kv_ref, attT_ref,
                     lse_ref, w_ref, wkv_ref,
                     dh_ref, dmem_ref, dwqT_ref, dwo_ref, dwkvT_ref,
                     kaug, kt, vaug, qaug, doaug, doT, dqacc, jgT, jg):
    length, width = h_ref.shape
    dwo_ref[...] = dot(attT_ref[...], dr_ref[...]).astype(BF)
    prepare_back(dr_ref, w_ref[:, width:], attT_ref, doT, doaug, length)
    codes, low_half = key_codes(kids_ref[...], length)
    prepare_keys(kv_ref.at[:, :width], kv_ref.at[:, width:], codes, low_half, kaug, kt, vaug, length)
    qcodes, row = query_codes(qids_ref[...], length)
    fill_queries(qaug, qT_ref, qcodes, row, lse_ref, length)
    jgT[width:, :] = jnp.zeros((2 * width, length), F32)
    attend_back_loop(tab_ref, qaug, kaug, kt, vaug, doaug, jgT, 0, width, 2 * width, dqacc, length)
    finish_grads(jgT, jg, width, length)
    dwqT_ref[...] = dot(jg[:width, :], h_ref[...]).astype(BF)
    @pl.loop(0, 2 * width // TB)
    def _(t):
        at = pl.multiple_of(t * TB, TB)
        dwkvT_ref[pl.ds(at, TB), :] = dot(jg[pl.ds(at + width, TB), :], mem_ref[...]).astype(BF)

    @pl.loop(0, length // TB)
    def _(t):
        rows = pl.ds(pl.multiple_of(t * TB, TB), TB)
        d = dot(jg[:width, rows], w_ref[:, :width], 0, 1)
        dh_ref[rows, :] = (dr_ref[rows, :].astype(F32) + d).astype(BF)
        dmem_ref[rows, :] = dot(jg[width:, rows], wkv_ref[...], 0, 1).astype(BF)


def enc_ffn_fwd_kernel(e1_ref, win_ref, bin_ref, wout_ref, bout_ref, ln_ref, wkv_ref,
                       g_ref, gp_ref, r_ref, mem_ref, kv_ref):
    length, width = e1_ref.shape
    ff = win_ref.shape[1]

    @pl.loop(0, length // TB)
    def _(t):
        rows = pl.ds(pl.multiple_of(t * TB, TB), TB)
        e1 = e1_ref[rows, :]
        total = e1.astype(F32) + bout_ref[...]
        for j in range(0, ff, 512):
            u = dot(e1, win_ref[:, j : j + 512]) + bin_ref[:, j : j + 512]
            g, gp = gelu_pair(u)
            gb = g.astype(BF)
            g_ref[rows, j : j + 512] = gb
            gp_ref[rows, j : j + 512] = gp.astype(BF)
            total += dot(gb, wout_ref[j : j + 512, :])
        r_ref[rows, :] = total.astype(BF)
        unit, _ = norm_stats(total)
        e2 = unit * ln_ref[0:1, :] + ln_ref[1:2, :]
        unit, _ = norm_stats(e2)
        mem = (unit * ln_ref[2:3, :] + ln_ref[3:4, :]).astype(BF)
        mem_ref[rows, :] = mem
        kv_ref[rows, :] = dot(mem, wkv_ref[...]).astype(BF)


def weight_grads(act_ref, du_ref, df_ref, g_ref, dwin_ref, dwoutT_ref):
    ff = du_ref.shape[1]

    @pl.loop(0, ff // TB)
    def _(t):
        cols = pl.ds(pl.multiple_of(t * TB, TB), TB)
        dwin_ref[:, cols] = dot(act_ref[...], du_ref[:, cols], 0, 0).astype(BF)
        dwoutT_ref[:, cols] = dot(df_ref[...], g_ref[:, cols], 0, 0).astype(BF)


def enc_ffn_bwd_kernel(dmem_ref, r_ref, g_ref, gp_ref, e1_ref, win_ref, wout_ref, ln_ref,
                       de1_ref, dwin_ref, dwoutT_ref, dln_ref, dbin_ref, dbout_ref,
                       du_ref, df_ref):
    length, width = e1_ref.shape
    ff = win_ref.shape[1]
    dln_ref[...] = jnp.zeros_like(dln_ref)
    dbin_ref[...] = jnp.zeros_like(dbin_ref)
    dbout_ref[...] = jnp.zeros_like(dbout_ref)

    @pl.loop(0, length // TB)
    def _(t):
        rows = pl.ds(pl.multiple_of(t * TB, TB), TB)
        unit2, scale2 = norm_stats(r_ref[rows, :].astype(F32))
        e2 = unit2 * ln_ref[0:1, :] + ln_ref[1:2, :]
        unit3, scale3 = norm_stats(e2)
        de2, gg, sg = norm_back(dmem_ref[rows, :].astype(F32), unit3, scale3, ln_ref[2:3, :])
        dln_ref[2:3, :] += gg
        dln_ref[3:4, :] += sg
        dr, gg, sg = norm_back(de2, unit2, scale2, ln_ref[0:1, :])
        dln_ref[0:1, :] += gg
        dln_ref[1:2, :] += sg
        df = dr.astype(BF)
        df_ref[rows, :] = df
        dbout_ref[...] += jnp.sum(df.astype(F32), axis=0, keepdims=True)
        total = dr
        for j in range(0, ff, 512):
            dg = dot(df, wout_ref[j : j + 512, :], 1, 1)
            du = dg * gp_ref[rows, j : j + 512].astype(F32)
            dub = du.astype(BF)
            du_ref[rows, j : j + 512] = dub
            dbin_ref[:, j : j + 512] += jnp.sum(du, axis=0, keepdims=True)
            total += dot(dub, win_ref[:, j : j + 512], 1, 1)
        de1_ref[rows, :] = total.astype(BF)

    weight_grads(e1_ref, du_ref, df_ref, g_ref, dwin_ref, dwoutT_ref)


def dec_ffn_kernel(h_ref, res_ref, cot_ref, win_ref, bin_ref, wout_ref, bout_ref, ln_ref,
                   out_ref, dres_ref, dwin_ref, dwoutT_ref, dln_ref, dbin_ref, dbout_ref,
                   g_ref, gp_ref, du_ref, df_ref):
    length, width = h_ref.shape
    ff = win_ref.shape[1]
    dln_ref[...] = jnp.zeros_like(dln_ref)
    dbin_ref[...] = jnp.zeros_like(dbin_ref)
    dbout_ref[...] = jnp.zeros_like(dbout_ref)

    @pl.loop(0, length // TB)
    def _(t):
        rows = pl.ds(pl.multiple_of(t * TB, TB), TB)
        h = h_ref[rows, :]
        total = h.astype(F32) + bout_ref[...]
        for j in range(0, ff, 512):
            u = dot(h, win_ref[:, j : j + 512]) + bin_ref[:, j : j + 512]
            g, gp = gelu_pair(u)
            gb = g.astype(BF)
            g_ref[rows, j : j + 512] = gb
            gp_ref[:, j : j + 512] = gp.astype(BF)
            total += dot(gb, wout_ref[j : j + 512, :])
        unit3, scale3 = norm_stats(total)
        out_ref[rows, :] = (unit3 * ln_ref[2:3, :] + ln_ref[3:4, :]).astype(BF)
        dr, gg, sg = norm_back(cot_ref[rows, :].astype(F32), unit3, scale3, ln_ref[2:3, :])
        dln_ref[2:3, :] += gg
        dln_ref[3:4, :] += sg
        df = dr.astype(BF)
        df_ref[rows, :] = df
        dbout_ref[...] += jnp.sum(df.astype(F32), axis=0, keepdims=True)
        total = dr
        for j in range(0, ff, 512):
            dg = dot(df, wout_ref[j : j + 512, :], 1, 1)
            du = dg * gp_ref[:, j : j + 512].astype(F32)
            dub = du.astype(BF)
            du_ref[rows, j : j + 512] = dub
            dbin_ref[:, j : j + 512] += jnp.sum(du, axis=0, keepdims=True)
            total += dot(dub, win_ref[:, j : j + 512], 1, 1)
        unit2, scale2 = norm_stats(res_ref[rows, :].astype(F32))
        d, gg, sg = norm_back(total, unit2, scale2, ln_ref[0:1, :])
        dln_ref[0:1, :] += gg
        dln_ref[1:2, :] += sg
        dres_ref[rows, :] = d.astype(BF)

    weight_grads(h_ref, du_ref, df_ref, g_ref, dwin_ref, dwoutT_ref)


def call(kernel, outs, scratch, flops, n_smem, *args):
    vm = pl.BlockSpec(memory_space=pltpu.VMEM)
    return pl.pallas_call(
        kernel,
        out_shape=[jax.ShapeDtypeStruct(s, d) for s, d in outs],
        in_specs=[pl.BlockSpec(memory_space=pltpu.SMEM)] * n_smem + [vm] * (len(args) - n_smem),
        out_specs=[vm] * len(outs),
        scratch_shapes=scratch,
        compiler_params=pltpu.CompilerParams(vmem_limit_bytes=VMEM_LIMIT),
        cost_estimate=pl.CostEstimate(flops=flops, bytes_accessed=8 << 20, transcendentals=0),
        name=kernel.__name__,
    )(*args)


def fwd_scratch(n, w):
    return [
        pltpu.VMEM((HEADS, n, 128), BF),
        pltpu.VMEM((HEADS, 128, n), BF),
        pltpu.VMEM((w, n), BF),
        pltpu.VMEM((w, QB), F32),
        pltpu.VMEM((HEADS, QB), F32),
        pltpu.VMEM((HEADS, QB), F32),
    ]


def self_fwd(tab, x, ids, w, wout, ln):
    n, w_ = x.shape
    return call(self_fwd_kernel,
                [((w_, n), BF), ((n, w_), BF), ((n, w_), BF), ((w_, n), BF), ((HEADS, n), F32), ((n, w_), BF), ((n, w_), BF)],
                fwd_scratch(n, w_), 10 << 30, 1, tab, x, ids, w, wout, ln)


def cross_fwd(tab, h, kv, qids, kids, w, ln):
    n, w_ = h.shape
    return call(cross_fwd_kernel,
                [((w_, n), BF), ((w_, n), BF), ((HEADS, n), F32), ((n, w_), BF), ((n, w_), BF)],
                fwd_scratch(n, w_), 10 << 30, 1, tab, h, kv, qids, kids, w, ln)


def bwd_scratch(n, w):
    return [
        pltpu.VMEM((HEADS, n, 128), BF),
        pltpu.VMEM((w, n), BF),
        pltpu.VMEM((HEADS, n, 128), BF),
        pltpu.VMEM((HEADS, 128, n), BF),
        pltpu.VMEM((HEADS, 128, n), BF),
        pltpu.VMEM((w, n), BF),
        pltpu.VMEM((w, QB), F32),
        pltpu.VMEM((3 * w, n), F32),
        pltpu.VMEM((3 * w, n), BF),
    ]


def self_bwd(tab, dh, res, x, ids, qT, k, v, attT, lse, w, wout, ln, dx_type):
    n, w_ = x.shape
    return call(self_bwd_kernel,
                [((n, w_), dx_type), ((3 * w_, w_), BF), ((w_, w_), BF), ((2, w_), F32)],
                bwd_scratch(n, w_) + [pltpu.VMEM((n, w_), BF)], 25 << 30, 1,
                tab, dh, res, x, ids, qT, k, v, attT, lse, w, wout, ln)


def cross_bwd(tab, dr, h, mem, qids, kids, qT, kv, attT, lse, w, wkv):
    n, w_ = h.shape
    return call(cross_bwd_kernel,
                [((n, w_), BF), ((n, w_), BF), ((w_, w_), BF), ((w_, w_), BF), ((2 * w_, w_), BF)],
                bwd_scratch(n, w_), 25 << 30, 1,
                tab, dr, h, mem, qids, kids, qT, kv, attT, lse, w, wkv)


def enc_ffn_fwd(e1, win, b_in, wout, bout, ln, wkv):
    n, w_ = e1.shape
    ff = win.shape[1]
    return call(enc_ffn_fwd_kernel,
                [((n, ff), BF), ((n, ff), BF), ((n, w_), BF), ((n, w_), BF), ((n, 2 * w_), BF)],
                [], 6 << 30, 0, e1, win, b_in, wout, bout, ln, wkv)


def enc_ffn_bwd(dmem, r, g, gp, e1, win, wout, ln):
    n, w_ = e1.shape
    ff = win.shape[1]
    return call(enc_ffn_bwd_kernel,
                [((n, w_), BF), ((w_, ff), BF), ((w_, ff), BF), ((4, w_), F32), ((1, ff), F32), ((1, w_), F32)],
                [pltpu.VMEM((n, ff), BF), pltpu.VMEM((n, w_), BF)], 9 << 30, 0,
                dmem, r, g, gp, e1, win, wout, ln)


def dec_ffn(h, res, cot, win, b_in, wout, bout, ln):
    n, w_ = h.shape
    ff = win.shape[1]
    return call(dec_ffn_kernel,
                [((n, w_), BF), ((n, w_), BF), ((w_, ff), BF), ((w_, ff), BF), ((4, w_), F32), ((1, ff), F32), ((1, w_), F32)],
                [pltpu.VMEM((n, ff), BF), pltpu.VMEM((TB, ff), BF), pltpu.VMEM((n, ff), BF), pltpu.VMEM((n, w_), BF)], 13 << 30, 0,
                h, res, cot, win, b_in, wout, bout, ln)


def block_table(query_ids, key_ids, causal):
    n = query_ids.shape[0]
    starts = jnp.sum((key_ids[None, :] < jnp.arange(5, dtype=jnp.int32)[:, None]).astype(jnp.int32), axis=1)
    first = query_ids[::QB]
    last = query_ids[QB - 1 :: QB]
    lo = starts[first] // CK
    hi = (starts[last + 1] + CK - 1) // CK
    qb = jnp.arange(n // QB, dtype=jnp.int32)
    diag = qb * (QB // CK)
    kd = jnp.where(causal, diag, hi)
    hi = jnp.where(causal, jnp.minimum(hi, diag + QB // CK), hi)
    lo = jnp.minimum(lo, kd)
    return jnp.stack([lo, kd, hi], axis=1)


def row_step(x, y, cot, src, tgt, enc, dec):
    def ln(p, *idx):
        return jnp.stack([p[7 + s][i] for i in idx for s in (0, 1)])
    src_row, tgt_row = src[None, :], tgt[None, :]
    tab_e = block_table(src, src, False)
    tab_d = block_table(tgt, tgt, True)
    tab_c = block_table(tgt, src, False)
    eq, ek, ev, eatt, else_, er, e1 = self_fwd(tab_e, x, src_row, enc[0], enc[1], ln(enc, 0))
    dq, dk, dv, datt, dlse, dr, d1 = self_fwd(tab_d, y, tgt_row, dec[0], dec[1], ln(dec, 0))
    g, gp, r2, mem, kv = enc_ffn_fwd(e1, enc[3], enc[4], enc[5], enc[6], ln(enc, 1, 2), enc[2])
    cq, catt, clse, cr, d2 = cross_fwd(tab_c, d1, kv, tgt_row, src_row, dec[2], ln(dec, 1))
    out, dres, ddwin, ddwoutT, ddln, ddbin, ddbout = dec_ffn(d2, cr, cot, dec[3], dec[4], dec[5], dec[6], ln(dec, 1, 2))
    dh1, dmem, dwqT, dwo, dwkvT = cross_bwd(tab_c, dres, d1, mem, tgt_row, src_row, cq, kv, catt, clse, dec[2], enc[2])
    de1, edwin, edwoutT, edln, edbin, edbout = enc_ffn_bwd(dmem, r2, g, gp, e1, enc[3], enc[5], ln(enc, 1, 2))
    dy, ddqkvT, ddout, ddln1 = self_bwd(tab_d, dh1, dr, y, tgt_row, dq, dk, dv, datt, dlse, dec[0], dec[1], ln(dec, 0), F32)
    dx, edqkvT, edout, edln1 = self_bwd(tab_e, de1, er, x, src_row, eq, ek, ev, eatt, else_, enc[0], enc[1], ln(enc, 0), F32)
    enc_g = (edqkvT, edout, dwkvT, edwin, edwoutT, edln1, edln, edbin, edbout)
    dec_g = (ddqkvT, ddout, jnp.concatenate([dwqT, dwo.T], 0), ddwin, ddwoutT, ddln1, ddln, ddbin, ddbout)
    return mem, out, dx, dy, enc_g, dec_g


def swap(value):
    return lax.ppermute(value, "section", [(0, 1), (1, 0)])


def far_weight(weight):
    n = lax.axis_size("dp")
    index = lax.axis_index("dp")
    rows = weight.shape[0] // n
    part = lax.dynamic_slice_in_dim(weight, index * rows, rows, 0)
    return lax.all_gather(swap(part), "dp", axis=0, tiled=True)


def sum_grads(first, second, sec):
    n = lax.axis_size("dp")
    def flat(parts):
        return jnp.concatenate([p.reshape(n, -1).astype(BF) for p in parts], axis=1)
    both = jnp.stack([flat(first), flat(second)], axis=1)
    mine = lax.psum_scatter(both, "dp", scatter_dimension=0, tiled=True)[0]
    keep = lax.dynamic_index_in_dim(mine, sec, 0, keepdims=False)
    give = lax.dynamic_index_in_dim(mine, 1 - sec, 0, keepdims=False)
    total = keep.astype(F32) + swap(give).astype(F32)
    every = lax.all_gather(total.astype(BF), "dp", axis=0, tiled=False)
    out, at = [], 0
    for p in first:
        size = p.size // n
        out.append(every[:, at : at + size].reshape(p.shape).astype(F32))
        at += size
    return out


def shards(layer_input, cotangent, src_segments, tgt_segments, attn_qkv, attn_out, cross_proj,
           ffn_in, ffn_in_bias, ffn_out, ffn_out_bias, norm_gain, norm_bias):
    sec = lax.axis_index("section")
    first = sec == 0
    own = layer_input[0, :, 0]
    pick = lambda a, i: lax.dynamic_index_in_dim(a, i, 0, keepdims=False)
    keep, away = pick(own, sec), swap(pick(own, 1 - sec))
    x = jnp.where(first, keep, away)
    y = jnp.where(first, away, keep)
    near = [attn_qkv[0], attn_out[0], cross_proj[0], ffn_in[0], ffn_in_bias, ffn_out[0], ffn_out_bias, norm_gain[0], norm_bias[0]]
    far = [far_weight(w) if w.ndim == 2 and w.dtype == BF else swap(w) for w in near]
    enc = [jnp.where(first, a, b) for a, b in zip(near, far)]
    dec = [jnp.where(first, b, a) for a, b in zip(near, far)]
    mem, out, dx, dy, eg, dg = row_step(
        x, y, pick(cotangent[:, 0], sec), pick(src_segments[:, 0], sec), pick(tgt_segments[:, 0], sec), enc, dec)
    there = swap(jnp.where(first, out, mem))
    here = jnp.where(first, mem, out)
    layer_output = jnp.where(first, jnp.stack([here, there]), jnp.stack([there, here]))
    there = swap(jnp.where(first, dy, dx).astype(BF)).astype(F32)
    here = jnp.where(first, dx, dy)
    input_grad = jnp.where(first, jnp.stack([here, there]), jnp.stack([there, here]))
    tot = sum_grads(eg[:5], dg[:5], sec)
    def small(g):
        return jnp.concatenate([g[5], g[6], g[7].reshape(-1, 512), g[8]], axis=0)
    both = lax.psum(jnp.stack([small(eg), small(dg)]), "dp")
    s = pick(both, sec) + swap(pick(both, 1 - sec))
    gain = jnp.stack([s[0], s[2], s[4]])
    shift = jnp.stack([s[1], s[3], s[5]])
    cross = tot[2].T
    return (layer_output[None, :, None], input_grad[None, :, None], tot[0].T[None], tot[1][None], cross[None], tot[3][None],
            s[6:10].reshape(1, -1), tot[4].T[None], s[10:11], gain[None], shift[None])


def solution(mesh):
    return jax.shard_map(
        shards,
        mesh=mesh,
        in_specs=(
            P("section", None, "dp", None, None),
            P(None, "dp", None, None),
            P(None, "dp", None),
            P(None, "dp", None),
            P("section", None, None),
            P("section", None, None),
            P("section", None, None),
            P("section", None, None),
            P("section", None),
            P("section", None, None),
            P("section", None),
            P("section", None, None),
            P("section", None, None),
        ),
        out_specs=(
            P("section", None, "dp", None, None),
            P("section", None, "dp", None, None),
            P("section", None, None),
            P("section", None, None),
            P("section", None, None),
            P("section", None, None),
            P("section", None),
            P("section", None, None),
            P("section", None),
            P("section", None, None),
            P("section", None, None),
        ),
        check_vma=False,
    )
```

```python
import functools
import math

import jax
import jax.numpy as jnp
from jax import lax
from jax.experimental import pallas as pl
from jax.experimental.pallas import tpu as pltpu
from jax.sharding import PartitionSpec as P

HEADS = 8
EPSILON = 1e-05
NEGATIVE = -1000000000.0
BF = jnp.bfloat16
F32 = jnp.float32
LOG2E = 1.4426950408889634
QB = 256
UNIT = 128
WIDE = 256
TB = 256
VMEM_LIMIT = 60 * 1024 * 1024


def dot(left, right, lc=1, rc=0):
    return lax.dot_general(
        left, right, (((lc,), (rc,)), ((), ())), preferred_element_type=F32
    )


def norm_stats(value):
    centered = value - jnp.mean(value, axis=-1, keepdims=True)
    spread = jnp.mean(centered * centered, axis=-1, keepdims=True)
    scale = lax.rsqrt(spread + EPSILON)
    return centered * scale, scale


def norm_back(out_grad, unit, scale, gain):
    gain_grad = jnp.sum(out_grad * unit, axis=0, keepdims=True)
    shift_grad = jnp.sum(out_grad, axis=0, keepdims=True)
    inner = out_grad * gain
    mean_one = jnp.mean(inner, axis=-1, keepdims=True)
    mean_two = jnp.mean(inner * unit, axis=-1, keepdims=True)
    return scale * (inner - mean_one - unit * mean_two), gain_grad, shift_grad


def gelu_pair(u):
    phi = 0.5 + 0.5 * lax.erf(u * (1.0 / math.sqrt(2.0)))
    bell = jnp.exp(-0.5 * u * u) * (1.0 / math.sqrt(2.0 * math.pi))
    return u * phi, phi + u * bell


def gain_of(small, norm):
    return small[5 + norm : 6 + norm, :]


def shift_of(small, norm):
    return small[8 + norm : 9 + norm, :]


def key_codes(ids_row, length):
    column = jnp.broadcast_to(ids_row.astype(F32), (128, length)).T
    lane = lax.broadcasted_iota(jnp.int32, (length, 128), 1)
    spot = jnp.where(lane < 64, lane, lane - 64)
    codes = jnp.where(
        spot < 4,
        jnp.where(column == spot.astype(F32), 0.0, NEGATIVE),
        jnp.where(spot < 7, -1.0, 0.0),
    )
    return codes, lane < 64


def fill_keys(dst, keys_ref, codes, low_half):
    for pair in range(HEADS // 2):
        slab = keys_ref[:, pair * 128 : pair * 128 + 128].astype(F32)
        dst[2 * pair] = jnp.where(low_half, slab, codes).astype(BF)
        dst[2 * pair + 1] = jnp.where(low_half, codes, slab).astype(BF)


def query_rows(head):
    return (0, 64) if head % 2 == 0 else (64, 0)


def key_range(query_ids, key_ids, qb):
    ids = query_ids[:, pl.ds(pl.multiple_of(qb * QB, QB), QB)].astype(F32)
    keys = key_ids[...].astype(F32)
    start = jnp.sum((keys < jnp.min(ids)).astype(F32)).astype(jnp.int32)
    stop = jnp.sum((keys <= jnp.max(ids)).astype(F32)).astype(jnp.int32)
    return start // UNIT, (stop + UNIT - 1) // UNIT


def visit_keys(query_ids, key_ids, qb, causal, step):
    lo, hi = key_range(query_ids, key_ids, qb)
    if causal:
        hi = qb * (QB // UNIT)
    count = hi - lo

    @pl.loop(0, count // 2)
    def _(i):
        step(lo + 2 * i, WIDE, False)

    @pl.when(count % 2 == 1)
    def _():
        step(hi - 1, UNIT, False)

    if causal:
        step(hi, WIDE, True)


def below_diagonal():
    return lax.broadcasted_iota(jnp.int32, (WIDE, QB), 0) <= lax.broadcasted_iota(jnp.int32, (WIDE, QB), 1)


def staged(first, lag_one, second, lag_two, third):
    for i in range(HEADS + lag_one + lag_two):
        if i < HEADS:
            first(i)
        if 0 <= i - lag_one < HEADS:
            second(i - lag_one)
        if 0 <= i - lag_one - lag_two < HEADS:
            third(i - lag_one - lag_two)


def attend_loop(query_ids, key_ids, causal, qaug, kaug, vt, attT_ref, lse_ref, oacc, mrow, lrow, sbuf, pbuf, length):
    @pl.loop(0, length // QB)
    def _(qb):
        q = pl.ds(pl.multiple_of(qb * QB, QB), QB)
        oacc[...] = jnp.zeros_like(oacc)
        mrow[...] = jnp.full_like(mrow, -3e38)
        lrow[...] = jnp.zeros_like(lrow)

        def step(unit, size, masked):
            ks = pl.ds(pl.multiple_of(unit * UNIT, UNIT), size)
            scale = {}

            def scores(h):
                s = dot(kaug[h, ks, :], qaug[h, :, q])
                sbuf[h, :size] = jnp.where(below_diagonal(), s, NEGATIVE) if masked else s

            def softmax(h):
                s = sbuf[h, :size]
                m_old = mrow[h : h + 1, :]
                m_new = jnp.maximum(m_old, jnp.max(s, axis=0, keepdims=True))
                scale[h] = jnp.exp2(m_old - m_new)
                p = jnp.exp2(s - m_new)
                lrow[h : h + 1, :] = lrow[h : h + 1, :] * scale[h] + jnp.sum(p, axis=0, keepdims=True)
                mrow[h : h + 1, :] = m_new
                pbuf[h, :size] = p.astype(BF)

            def mix(h):
                hs = slice(h * 64, h * 64 + 64)
                oacc[hs, :] = oacc[hs, :] * scale[h] + dot(vt[hs, ks], pbuf[h, :size])

            staged(scores, 7, softmax, 1, mix)

        visit_keys(query_ids, key_ids, qb, causal, step)
        for h in range(HEADS):
            hs = slice(h * 64, h * 64 + 64)
            attT_ref[hs, q] = (oacc[hs, :] * (1.0 / lrow[h : h + 1, :])).astype(BF)
        lse_ref[:, q] = mrow[...] + jnp.log2(lrow[...])


def query_codes(ids_row, length):
    row = lax.broadcasted_iota(jnp.int32, (16, length), 0)
    return jnp.where(row == jnp.broadcast_to(ids_row, (16, length)), 1.0, 0.0), row


def fill_queries(qaug, qT_ref, codes, row, lse_ref, length):
    for h in range(HEADS):
        a, b = query_rows(h)
        qaug[h, a : a + 64, :] = qT_ref[h * 64 : h * 64 + 64, :]
        extra = codes
        if lse_ref is not None:
            lse = lse_ref[h : h + 1, :]
            hi = lse.astype(BF).astype(F32)
            mid = (lse - hi).astype(BF).astype(F32)
            low = lse - hi - mid
            extra = jnp.where(row == 4, hi, jnp.where(row == 5, mid, jnp.where(row == 6, low, codes)))
        qaug[h, b : b + 16, :] = extra.astype(BF)
        qaug[h, b + 16 : b + 64, :] = jnp.zeros((48, length), BF)


def project_queries(src_ref, w_ref, qT_ref, length, width):
    @pl.loop(0, length // TB)
    def _(t):
        rows = pl.ds(pl.multiple_of(t * TB, TB), TB)
        q = dot(src_ref[rows, :], w_ref[:, :width]) * (0.125 * LOG2E)
        qT_ref[:, rows] = q.T.astype(BF)


def out_and_norm(attT_ref, w_ref, resid_ref, sm_ref, norm, res_ref, hid_ref, length):
    @pl.loop(0, length // TB)
    def _(t):
        rows = pl.ds(pl.multiple_of(t * TB, TB), TB)
        a = dot(attT_ref[:, rows], w_ref[...], 0, 0)
        r = resid_ref[rows, :].astype(F32) + a
        res_ref[rows, :] = r.astype(BF)
        unit, _ = norm_stats(r)
        hid_ref[rows, :] = (unit * gain_of(sm_ref, norm) + shift_of(sm_ref, norm)).astype(BF)


def self_fwd_kernel(causal, x_ref, ids_ref, w_ref, wout_ref, ln_ref,
                    qT_ref, k_ref, v_ref, attT_ref, lse_ref, res_ref, hid_ref,
                    kaug, qaug, vt, oacc, mrow, lrow, sbuf, pbuf):
    x_ref, w_ref = ready(x_ref, w_ref)
    length, width = x_ref.shape
    project_queries(x_ref, w_ref, qT_ref, length, width)

    @pl.loop(0, length // TB)
    def _(t):
        rows = pl.ds(pl.multiple_of(t * TB, TB), TB)
        k_ref[rows, :] = dot(x_ref[rows, :], w_ref[:, width : 2 * width]).astype(BF)
        v = dot(x_ref[rows, :], w_ref[:, 2 * width :])
        v_ref[rows, :] = v.astype(BF)
        vt[:, rows] = v.T.astype(BF)

    for result in (qT_ref, k_ref, v_ref):
        result.flush()
    (ids_ref,) = ready(ids_ref)
    codes, low_half = key_codes(ids_ref[...], length)
    fill_keys(kaug, k_ref, codes, low_half)
    qcodes, row = query_codes(ids_ref[...], length)
    fill_queries(qaug, qT_ref, qcodes, row, None, length)
    attend_loop(ids_ref, ids_ref, causal, qaug, kaug, vt, attT_ref, lse_ref, oacc, mrow, lrow, sbuf, pbuf, length)
    attT_ref.flush()
    lse_ref.flush()
    wout_ref, ln_ref = ready(wout_ref, ln_ref)
    out_and_norm(attT_ref, wout_ref, x_ref, ln_ref, 0, res_ref, hid_ref, length)


def cross_fwd_kernel(h_ref, kv_ref, qids_ref, kids_ref, w_ref, ln_ref,
                     qT_ref, attT_ref, lse_ref, res_ref, hid_ref,
                     kaug, qaug, vt, oacc, mrow, lrow, sbuf, pbuf):
    h_ref, w_ref = ready(h_ref, w_ref)
    length, width = h_ref.shape
    project_queries(h_ref, w_ref, qT_ref, length, width)
    qT_ref.flush()
    kv_ref, qids_ref, kids_ref = ready(kv_ref, qids_ref, kids_ref)

    @pl.loop(0, length // TB)
    def _(t):
        rows = pl.ds(pl.multiple_of(t * TB, TB), TB)
        vt[:, rows] = kv_ref[rows, width:].astype(F32).T.astype(BF)

    codes, low_half = key_codes(kids_ref[...], length)
    fill_keys(kaug, kv_ref, codes, low_half)
    qcodes, row = query_codes(qids_ref[...], length)
    fill_queries(qaug, qT_ref, qcodes, row, None, length)
    attend_loop(qids_ref, kids_ref, False, qaug, kaug, vt, attT_ref, lse_ref, oacc, mrow, lrow, sbuf, pbuf, length)
    attT_ref.flush()
    lse_ref.flush()
    (ln_ref,) = ready(ln_ref)
    out_and_norm(attT_ref, w_ref.at[:, width:], h_ref, ln_ref, 1, res_ref, hid_ref, length)


def attend_back_loop(query_ids, key_ids, causal, qaug, kaug, kt, vaug, doaug, jgT, dqacc, sbuf, dbuf, pbuf, gbuf, length):
    width = HEADS * 64

    @pl.loop(0, length // QB)
    def _(qb):
        q = pl.ds(pl.multiple_of(qb * QB, QB), QB)
        dqacc[...] = jnp.zeros_like(dqacc)

        def step(unit, size, masked):
            ks = pl.ds(pl.multiple_of(unit * UNIT, UNIT), size)

            def products(h):
                s = dot(kaug[h, ks, :], qaug[h, :, q])
                sbuf[h, :size] = jnp.where(below_diagonal(), s, NEGATIVE) if masked else s
                dbuf[h, :size] = dot(vaug[h, ks, :], doaug[h, :, q])

            def grads(h):
                p = jnp.exp2(sbuf[h, :size])
                pbuf[h, :size] = p.astype(BF)
                gbuf[h, :size] = (p * dbuf[h, :size]).astype(BF)

            def add(h):
                a, _ = query_rows(h)
                at = h * 64
                hs = slice(at, at + 64)
                dqacc[hs, :] += dot(kt[hs, ks], gbuf[h, :size])
                jgT[2 * width + at : 2 * width + at + 64, ks] += dot(doaug[h, a : a + 64, q], pbuf[h, :size], 1, 1)
                jgT[width + at : width + at + 64, ks] += dot(qaug[h, a : a + 64, q], gbuf[h, :size], 1, 1)

            lag = 1 if size == WIDE else 2
            staged(products, lag, grads, lag, add)

        visit_keys(query_ids, key_ids, qb, causal, step)
        jgT[:width, q] = dqacc[...] * 0.125


def prepare_back(dr_ref, w_out, attT_ref, doT, doaug, length):
    @pl.loop(0, length // TB)
    def _(t):
        rows = pl.ds(pl.multiple_of(t * TB, TB), TB)
        doT[:, rows] = dot(w_out, dr_ref[rows, :], 1, 1).astype(BF)

    row = lax.broadcasted_iota(jnp.int32, (16, length), 0)
    for h in range(HEADS):
        a, b = query_rows(h)
        hs = slice(h * 64, h * 64 + 64)
        doh = doT[hs, :]
        doaug[h, a : a + 64, :] = doh
        delta = jnp.sum(doh.astype(F32) * attT_ref[hs, :].astype(F32), axis=0, keepdims=True)
        hi = delta.astype(BF).astype(F32)
        mid = (delta - hi).astype(BF).astype(F32)
        low = delta - hi - mid
        extra = jnp.where(row == 4, hi, jnp.where(row == 5, mid, jnp.where(row == 6, low, 0.0)))
        doaug[h, b : b + 16, :] = extra.astype(BF)
        doaug[h, b + 16 : b + 64, :] = jnp.zeros((48, length), BF)


def prepare_keys(keys_ref, values_ref, codes, low_half, kaug, kt, vaug, length):
    fill_keys(kaug, keys_ref, codes, low_half)
    fill_keys(vaug, values_ref, jnp.where(codes == NEGATIVE, 0.0, codes), low_half)

    @pl.loop(0, length // TB)
    def _(t):
        rows = pl.ds(pl.multiple_of(t * TB, TB), TB)
        kt[:, rows] = keys_ref[rows, :].astype(F32).T.astype(BF)


def finish_grads(jgT, jg, koff, length):
    rows_total = jgT.shape[0]
    for r in range(0, rows_total, 512):
        f = math.log(2.0) if r == koff else 1.0
        jg[r : r + 512, :] = (jgT[r : r + 512, :] * f).astype(BF)


def self_bwd_kernel(causal, dh_ref, res_ref, x_ref, ids_ref, qT_ref, k_ref, v_ref, attT_ref,
                    lse_ref, w_ref, wout_ref, ln_ref,
                    dx_ref, dw_ref, dln_ref,
                    kaug, kt, vaug, qaug, doaug, doT, dqacc, jgT, jg, sbuf, dbuf, pbuf, gbuf, dr):
    dh_ref, res_ref, ln_ref = ready(dh_ref, res_ref, ln_ref)
    length, width = res_ref.shape
    dln_ref[...] = jnp.zeros(dln_ref.shape, F32)

    @pl.loop(0, length // TB)
    def _(t):
        rows = pl.ds(pl.multiple_of(t * TB, TB), TB)
        unit, scale = norm_stats(res_ref[rows, :].astype(F32))
        d, gg, sg = norm_back(dh_ref[rows, :].astype(F32), unit, scale, gain_of(ln_ref, 0))
        dln_ref[5:6, :] += gg
        dln_ref[8:9, :] += sg
        dr[rows, :] = d.astype(BF)

    attT_ref, wout_ref, ids_ref = ready(attT_ref, wout_ref, ids_ref)
    dw_ref[3] = dot(attT_ref[...], dr[...]).astype(BF)
    prepare_back(dr, wout_ref[...], attT_ref, doT, doaug, length)
    codes, low_half = key_codes(ids_ref[...], length)
    k_ref, v_ref, qT_ref, lse_ref = ready(k_ref, v_ref, qT_ref, lse_ref)
    prepare_keys(k_ref, v_ref, codes, low_half, kaug, kt, vaug, length)
    qcodes, row = query_codes(ids_ref[...], length)
    fill_queries(qaug, qT_ref, qcodes, row, lse_ref, length)
    jgT[width:, :] = jnp.zeros((2 * width, length), F32)
    attend_back_loop(ids_ref, ids_ref, causal, qaug, kaug, kt, vaug, doaug, jgT, dqacc, sbuf, dbuf, pbuf, gbuf, length)
    finish_grads(jgT, jg, width, length)
    x_ref, w_ref = ready(x_ref, w_ref)

    @pl.loop(0, 3)
    def _(t):
        rows = pl.ds(pl.multiple_of(t * 512, 512), 512)
        dw_ref[t] = dot(jg[rows, :], x_ref[...]).astype(BF)

    dw_ref.flush()

    @pl.loop(0, length // TB)
    def _(t):
        rows = pl.ds(pl.multiple_of(t * TB, TB), TB)
        d = dot(jg[:, rows], w_ref[...], 0, 1)
        dx_ref[rows, :] = (dr[rows, :].astype(F32) + d).astype(dx_ref.dtype)


def cross_bwd_kernel(dr_ref, h_ref, mem_ref, qids_ref, kids_ref, qT_ref, kv_ref, attT_ref,
                     lse_ref, w_ref, wkv_ref,
                     dh_ref, dmem_ref, dwd_ref, dwe_ref,
                     kaug, kt, vaug, qaug, doaug, doT, dqacc, jgT, jg, sbuf, dbuf, pbuf, gbuf):
    dr_ref, attT_ref, w_ref, qids_ref, kids_ref = ready(dr_ref, attT_ref, w_ref, qids_ref, kids_ref)
    length, width = dr_ref.shape
    dwd_ref[1] = dot(dr_ref[...], attT_ref[...], 0, 1).astype(BF)
    prepare_back(dr_ref, w_ref[:, width:], attT_ref, doT, doaug, length)
    codes, low_half = key_codes(kids_ref[...], length)
    kv_ref, qT_ref, lse_ref = ready(kv_ref, qT_ref, lse_ref)
    prepare_keys(kv_ref.at[:, :width], kv_ref.at[:, width:], codes, low_half, kaug, kt, vaug, length)
    qcodes, row = query_codes(qids_ref[...], length)
    fill_queries(qaug, qT_ref, qcodes, row, lse_ref, length)
    jgT[width:, :] = jnp.zeros((2 * width, length), F32)
    attend_back_loop(qids_ref, kids_ref, False, qaug, kaug, kt, vaug, doaug, jgT, dqacc, sbuf, dbuf, pbuf, gbuf, length)
    finish_grads(jgT, jg, width, length)
    h_ref, mem_ref, wkv_ref = ready(h_ref, mem_ref, wkv_ref)
    dwd_ref[0] = dot(jg[:width, :], h_ref[...]).astype(BF)
    for half in range(2):
        dwe_ref[half] = dot(jg[(half + 1) * width : (half + 2) * width, :], mem_ref[...]).astype(BF)
    dwd_ref.flush()
    dwe_ref.flush()

    @pl.loop(0, length // TB)
    def _(t):
        rows = pl.ds(pl.multiple_of(t * TB, TB), TB)
        d = dot(jg[:width, rows], w_ref[:, :width], 0, 1)
        dh_ref[rows, :] = (dr_ref[rows, :].astype(F32) + d).astype(BF)
        dmem_ref[rows, :] = dot(jg[width:, rows], wkv_ref[...], 0, 1).astype(BF)


def enc_ffn_fwd_kernel(e1_ref, win_ref, wout_ref, ln_ref, wkv_ref,
                       g_ref, gp_ref, r_ref, mem_ref, kv_ref):
    e1_ref, win_ref, wout_ref, ln_ref, wkv_ref = ready(e1_ref, win_ref, wout_ref, ln_ref, wkv_ref)
    length, width = e1_ref.shape
    ff = win_ref.shape[1]

    @pl.loop(0, length // TB)
    def _(t):
        rows = pl.ds(pl.multiple_of(t * TB, TB), TB)
        e1 = e1_ref[rows, :]
        total = e1.astype(F32) + ln_ref[4:5, :]
        for j in range(0, ff, 512):
            u = dot(e1, win_ref[:, j : j + 512]) + ln_ref[j // 512 : j // 512 + 1, :]
            g, gp = gelu_pair(u)
            gb = g.astype(BF)
            g_ref[rows, j : j + 512] = gb
            gp_ref[rows, j : j + 512] = gp.astype(BF)
            total += dot(gb, wout_ref[j : j + 512, :])
        r_ref[rows, :] = total.astype(BF)
        unit, _ = norm_stats(total)
        e2 = unit * gain_of(ln_ref, 1) + shift_of(ln_ref, 1)
        unit, _ = norm_stats(e2)
        mem = (unit * gain_of(ln_ref, 2) + shift_of(ln_ref, 2)).astype(BF)
        mem_ref[rows, :] = mem
        kv_ref[rows, :] = dot(mem, wkv_ref[...]).astype(BF)


def weight_grads(act_ref, du_ref, df_ref, g_ref, dw_ref):
    slabs = du_ref.shape[1] // 512

    @pl.loop(0, slabs)
    def _(t):
        cols = pl.ds(pl.multiple_of(t * 512, 512), 512)
        dw_ref[t] = dot(act_ref[...], du_ref[:, cols], 0, 0).astype(BF)
        dw_ref[slabs + t] = dot(df_ref[...], g_ref[:, cols], 0, 0).astype(BF)


def enc_ffn_bwd_kernel(dmem_ref, r_ref, g_ref, gp_ref, e1_ref, win_ref, wout_ref, ln_ref,
                       de1_ref, dw_ref, dln_ref,
                       du_ref, df_ref):
    dmem_ref, r_ref, ln_ref, wout_ref, gp_ref, win_ref = ready(dmem_ref, r_ref, ln_ref, wout_ref, gp_ref, win_ref)
    length, width = r_ref.shape
    ff = win_ref.shape[1]
    dln_ref[...] = jnp.zeros(dln_ref.shape, F32)

    @pl.loop(0, length // TB)
    def _(t):
        rows = pl.ds(pl.multiple_of(t * TB, TB), TB)
        unit2, scale2 = norm_stats(r_ref[rows, :].astype(F32))
        e2 = unit2 * gain_of(ln_ref, 1) + shift_of(ln_ref, 1)
        unit3, scale3 = norm_stats(e2)
        de2, gg, sg = norm_back(dmem_ref[rows, :].astype(F32), unit3, scale3, gain_of(ln_ref, 2))
        dln_ref[7:8, :] += gg
        dln_ref[10:11, :] += sg
        dr, gg, sg = norm_back(de2, unit2, scale2, gain_of(ln_ref, 1))
        dln_ref[6:7, :] += gg
        dln_ref[9:10, :] += sg
        df = dr.astype(BF)
        df_ref[rows, :] = df
        dln_ref[4:5, :] += jnp.sum(df.astype(F32), axis=0, keepdims=True)
        total = dr
        for j in range(0, ff, 512):
            dg = dot(df, wout_ref[j : j + 512, :], 1, 1)
            du = dg * gp_ref[rows, j : j + 512].astype(F32)
            dub = du.astype(BF)
            du_ref[rows, j : j + 512] = dub
            dln_ref[j // 512 : j // 512 + 1, :] += jnp.sum(du, axis=0, keepdims=True)
            total += dot(dub, win_ref[:, j : j + 512], 1, 1)
        de1_ref[rows, :] = total.astype(BF)

    de1_ref.flush()
    e1_ref, g_ref = ready(e1_ref, g_ref)
    weight_grads(e1_ref, du_ref, df_ref, g_ref, dw_ref)


def dec_ffn_kernel(h_ref, res_ref, cot_ref, win_ref, wout_ref, ln_ref,
                   out_ref, dres_ref, dw_ref, dln_ref,
                   g_ref, gp_ref, du_ref, df_ref):
    h_ref, win_ref, ln_ref, wout_ref, cot_ref, res_ref = ready(h_ref, win_ref, ln_ref, wout_ref, cot_ref, res_ref)
    length, width = h_ref.shape
    ff = win_ref.shape[1]
    dln_ref[...] = jnp.zeros(dln_ref.shape, F32)

    @pl.loop(0, length // TB)
    def _(t):
        rows = pl.ds(pl.multiple_of(t * TB, TB), TB)
        h = h_ref[rows, :]
        total = h.astype(F32) + ln_ref[4:5, :]
        for j in range(0, ff, 512):
            u = dot(h, win_ref[:, j : j + 512]) + ln_ref[j // 512 : j // 512 + 1, :]
            g, gp = gelu_pair(u)
            gb = g.astype(BF)
            g_ref[rows, j : j + 512] = gb
            gp_ref[:, j : j + 512] = gp.astype(BF)
            total += dot(gb, wout_ref[j : j + 512, :])
        unit3, scale3 = norm_stats(total)
        out_ref[rows, :] = (unit3 * gain_of(ln_ref, 2) + shift_of(ln_ref, 2)).astype(BF)
        dr, gg, sg = norm_back(cot_ref[rows, :].astype(F32), unit3, scale3, gain_of(ln_ref, 2))
        dln_ref[7:8, :] += gg
        dln_ref[10:11, :] += sg
        df = dr.astype(BF)
        df_ref[rows, :] = df
        dln_ref[4:5, :] += jnp.sum(df.astype(F32), axis=0, keepdims=True)
        total = dr
        for j in range(0, ff, 512):
            dg = dot(df, wout_ref[j : j + 512, :], 1, 1)
            du = dg * gp_ref[:, j : j + 512].astype(F32)
            dub = du.astype(BF)
            du_ref[rows, j : j + 512] = dub
            dln_ref[j // 512 : j // 512 + 1, :] += jnp.sum(du, axis=0, keepdims=True)
            total += dot(dub, win_ref[:, j : j + 512], 1, 1)
        unit2, scale2 = norm_stats(res_ref[rows, :].astype(F32))
        d, gg, sg = norm_back(total, unit2, scale2, gain_of(ln_ref, 1))
        dln_ref[6:7, :] += gg
        dln_ref[9:10, :] += sg
        dres_ref[rows, :] = d.astype(BF)

    out_ref.flush()
    dres_ref.flush()
    weight_grads(h_ref, du_ref, df_ref, g_ref, dw_ref)


class Operand:
    def __init__(self, copy, ref):
        self.copy, self.ref = copy, ref


def ready(*operands):
    refs = []
    for operand in operands:
        if operand.copy is not None:
            operand.copy.wait()
            operand.copy = None
        refs.append(operand.ref)
    return refs


class Result:
    def __init__(self, copy, ref):
        self.copy, self.ref, self.started = copy, ref, False

    def __getitem__(self, at):
        return self.ref[at]

    def __setitem__(self, at, value):
        self.ref[at] = value

    def __getattr__(self, name):
        return getattr(self.ref, name)

    def flush(self):
        if not self.started:
            self.copy.start()
            self.started = True


class Near:
    def __init__(self, array):
        self.arrays, self.shape, self.dtype = [array], array.shape[1:], array.dtype

    def copy(self, refs, dst, sem, section):
        copy = pltpu.make_async_copy(refs[0].at[section], dst, sem)
        copy.start()
        return copy


class Whole:
    def __init__(self, array):
        self.arrays, self.shape, self.dtype = [array], array.shape, array.dtype

    def copy(self, refs, dst, sem, section):
        copy = pltpu.make_async_copy(refs[0], dst, sem)
        copy.start()
        return copy


class Layer:
    def __init__(self, near, far, layer, rows=False):
        self.arrays, self.shape, self.dtype = [near, far], far.shape, far.dtype
        self.layer, self.rows = layer, rows

    def copy(self, refs, dst, sem, section):
        near = refs[0].at[section] if self.rows else refs[0]

        @pl.when(section == self.layer)
        def _():
            pltpu.make_async_copy(near, dst, sem).start()

        @pl.when(section != self.layer)
        def _():
            pltpu.make_async_copy(refs[1], dst, sem).start()

        return pltpu.make_async_copy(refs[1], dst, sem)


def run_kernel(kernel, plan, n_out, *refs):
    n_in = sum(len(p.arrays) for p in plan)
    ins, outs = list(refs[:n_in]), refs[n_in : n_in + n_out]
    rest = refs[n_in + n_out :]
    in_bufs, out_bufs = rest[: len(plan)], rest[len(plan) : len(plan) + n_out]
    in_sem, out_sem = rest[len(plan) + n_out : len(plan) + n_out + 2]
    scratch = rest[len(plan) + n_out + 2 :]
    section = lax.axis_index("section")
    operands = []
    for k, entry in enumerate(plan):
        given = [ins.pop(0) for _ in entry.arrays]
        operands.append(Operand(entry.copy(given, in_bufs[k], in_sem.at[k], section), in_bufs[k]))
    results = [
        Result(pltpu.make_async_copy(out_bufs[k], outs[k], out_sem.at[k]), out_bufs[k]) for k in range(n_out)
    ]
    kernel(*operands, *results, *scratch)
    ready(*operands)
    for result in results:
        result.flush()
    for result in results:
        result.copy.wait()


def call(kernel, name, outs, scratch, flops, *args):
    any_space = pl.BlockSpec(memory_space=pl.ANY)
    plan = [a if hasattr(a, "arrays") else Whole(a) for a in args]
    given = [array for entry in plan for array in entry.arrays]
    return pl.pallas_call(
        functools.partial(run_kernel, kernel, plan, len(outs)),
        out_shape=[jax.ShapeDtypeStruct(s, d) for s, d in outs],
        in_specs=[any_space] * len(given),
        out_specs=[any_space] * len(outs),
        scratch_shapes=[pltpu.VMEM(entry.shape, entry.dtype) for entry in plan]
        + [pltpu.VMEM(s, d) for s, d in outs]
        + [pltpu.SemaphoreType.DMA((len(plan),)), pltpu.SemaphoreType.DMA((len(outs),))]
        + scratch,
        compiler_params=pltpu.CompilerParams(vmem_limit_bytes=VMEM_LIMIT),
        cost_estimate=pl.CostEstimate(flops=flops, bytes_accessed=8 << 20, transcendentals=0),
        name=name,
    )(*given)


def fwd_scratch(n, w):
    return [
        pltpu.VMEM((HEADS, n, 128), BF),
        pltpu.VMEM((HEADS, 128, n), BF),
        pltpu.VMEM((w, n), BF),
        pltpu.VMEM((w, QB), F32),
        pltpu.VMEM((HEADS, QB), F32),
        pltpu.VMEM((HEADS, QB), F32),
        pltpu.VMEM((HEADS, WIDE, QB), F32),
        pltpu.VMEM((HEADS, WIDE, QB), BF),
    ]


def self_fwd(causal, x, ids, w, wout, small):
    n, w_ = x.shape
    return call(functools.partial(self_fwd_kernel, causal), "self_forward",
                [((w_, n), BF), ((n, w_), BF), ((n, w_), BF), ((w_, n), BF), ((HEADS, n), F32), ((n, w_), BF), ((n, w_), BF)],
                fwd_scratch(n, w_), 10 << 30, x, ids, w, wout, small)


def cross_fwd(h, kv, qids, kids, w, small):
    n, w_ = h.shape
    return call(cross_fwd_kernel, "cross_forward",
                [((w_, n), BF), ((w_, n), BF), ((HEADS, n), F32), ((n, w_), BF), ((n, w_), BF)],
                fwd_scratch(n, w_), 10 << 30, h, kv, qids, kids, w, small)


def bwd_scratch(n, w):
    return [
        pltpu.VMEM((HEADS, n, 128), BF),
        pltpu.VMEM((w, n), BF),
        pltpu.VMEM((HEADS, n, 128), BF),
        pltpu.VMEM((HEADS, 128, n), BF),
        pltpu.VMEM((HEADS, 128, n), BF),
        pltpu.VMEM((w, n), BF),
        pltpu.VMEM((w, QB), F32),
        pltpu.VMEM((3 * w, n), F32),
        pltpu.VMEM((3 * w, n), BF),
        pltpu.VMEM((HEADS, WIDE, QB), F32),
        pltpu.VMEM((HEADS, WIDE, QB), F32),
        pltpu.VMEM((HEADS, WIDE, QB), BF),
        pltpu.VMEM((HEADS, WIDE, QB), BF),
    ]


def self_bwd(causal, dh, res, x, ids, qT, k, v, attT, lse, w, wout, small):
    n, w_ = res.shape
    return call(functools.partial(self_bwd_kernel, causal), "self_backward",
                [((n, w_), F32), ((4, w_, w_), BF), ((16, w_), F32)],
                bwd_scratch(n, w_) + [pltpu.VMEM((n, w_), BF)], 25 << 30,
                dh, res, x, ids, qT, k, v, attT, lse, w, wout, small)


def cross_bwd(dr, h, mem, qids, kids, qT, kv, attT, lse, w, wkv):
    n, w_ = h.shape
    return call(cross_bwd_kernel, "cross_backward",
                [((n, w_), BF), ((n, w_), BF), ((2, w_, w_), BF), ((2, w_, w_), BF)],
                bwd_scratch(n, w_), 25 << 30,
                dr, h, mem, qids, kids, qT, kv, attT, lse, w, wkv)


def enc_ffn_fwd(e1, win, wout, small, wkv):
    n, w_ = e1.shape
    ff = win.shape[-1]
    return call(enc_ffn_fwd_kernel, "encoder_ffn_forward",
                [((n, ff), BF), ((n, ff), BF), ((n, w_), BF), ((n, w_), BF), ((n, 2 * w_), BF)],
                [], 6 << 30, e1, win, wout, small, wkv)


def enc_ffn_bwd(dmem, r, g, gp, e1, win, wout, small):
    n, w_ = e1.shape
    ff = win.shape[-1]
    return call(enc_ffn_bwd_kernel, "encoder_ffn_backward",
                [((n, w_), BF), ((2 * ff // w_, w_, w_), BF), ((16, w_), F32)],
                [pltpu.VMEM((n, ff), BF), pltpu.VMEM((n, w_), BF)], 9 << 30,
                dmem, r, g, gp, e1, win, wout, small)


def dec_ffn(h, res, cot, win, wout, small):
    n, w_ = h.shape
    ff = win.shape[-1]
    return call(dec_ffn_kernel, "decoder_ffn",
                [((n, w_), BF), ((n, w_), BF), ((2 * ff // w_, w_, w_), BF), ((16, w_), F32)],
                [pltpu.VMEM((n, ff), BF), pltpu.VMEM((TB, ff), BF), pltpu.VMEM((n, ff), BF), pltpu.VMEM((n, w_), BF)], 13 << 30,
                h, res, cot, win, wout, small)


def row_step(tokens, far_tokens, cot, src, tgt, near, far, small, far_small):
    x, y = (Layer(tokens, far_tokens, k, True) for k in range(2))
    (qkv, wo, cross, win, wout), (qkv2, wo2, cross2, win2, wout2) = (
        [Layer(a, b, k) for a, b in zip(near, far)] for k in range(2))
    sm, sm2 = (Layer(small, far_small, k) for k in range(2))
    cot, src, tgt = Near(cot), Near(src), Near(tgt)
    eq, ek, ev, eatt, else_, er, e1 = self_fwd(False, x, src, qkv, wo, sm)
    dq, dk, dv, datt, dlse, dr, d1 = self_fwd(True, y, tgt, qkv2, wo2, sm2)
    g, gp, r2, mem, kv = enc_ffn_fwd(e1, win, wout, sm, cross)
    cq, catt, clse, cr, d2 = cross_fwd(d1, kv, tgt, src, cross2, sm2)
    out, dres, dw_dffn, s_dffn = dec_ffn(d2, cr, cot, win2, wout2, sm2)
    dh1, dmem, dw_dcross, dw_ecross = cross_bwd(dres, d1, mem, tgt, src, cq, kv, catt, clse, cross2, cross)
    de1, dw_effn, s_effn = enc_ffn_bwd(dmem, r2, g, gp, e1, win, wout, sm)
    dy, dw_dself, s_dself = self_bwd(True, dh1, dr, y, tgt, dq, dk, dv, datt, dlse, qkv2, wo2, sm2)
    dx, dw_eself, s_eself = self_bwd(False, de1, er, x, src, eq, ek, ev, eatt, else_, qkv, wo, sm)
    groups = [(dw_effn, dw_dffn), (dw_ecross, dw_dcross), (dw_eself, dw_dself)]
    return mem, out, dx, dy, groups, jnp.stack([s_effn + s_eself, s_dffn + s_dself])


CHUNK = 512
MESH = pl.DeviceIdType.MESH
ANY = pl.BlockSpec(memory_space=pl.ANY)


def bit_of(index, bit):
    return (index // 2**bit) % 2


def partner_of(index, bit):
    return index + 2**bit - 2 * 2**bit * bit_of(index, bit)


def greet(partners):
    barrier = pltpu.get_barrier_semaphore()
    for device in partners:
        pl.semaphore_signal(barrier, inc=1, device_id=device, device_id_type=MESH)
    pl.semaphore_wait(barrier, len(partners))


def halvings(devices, rows):
    bits = devices.bit_length() - 1
    halved = 0
    while halved < bits and (rows >> (halved + 1)) >= 16 and (rows >> (halved + 1)) % 16 == 0:
        halved += 1
    return list(range(halved)), list(range(halved, bits))


def place(index, count, rows):
    at, size = 0, rows
    for bit in range(count):
        size //= 2
        at = at + bit_of(index, bit) * size
    return at, size


def sum_kernel(devices, kinds, *refs):
    n_in = len(kinds)
    ins, small_ref = refs[:n_in], refs[n_in]
    out_ref, small_out = refs[n_in + 1 : n_in + 3]
    scratch = refs[n_in + 3 :]
    held, gathered, load_sem, out_sem, send_sem, recv_sem = scratch[:6]
    small, small_in, ssend, srecv = scratch[6:10]
    landing = scratch[10:]
    chunks = held.shape[0]
    index = lax.axis_index("dp")
    section = lax.axis_index("section")
    halved, rest = halvings(devices, CHUNK)
    all_bits = halved + rest
    across = (1 - section, index)
    mates = [(section, partner_of(index, bit)) for bit in all_bits]
    greet([across] + mates)

    def loads(c, go):
        at = 0
        for pair, count in zip(range(0, n_in, 2), [k for k in kinds[::2]]):
            @pl.when((c >= at) & (c < at + count))
            def _(pair=pair, at=at):
                for layer in range(2):
                    copy = pltpu.make_async_copy(ins[pair + layer].at[c - at], held.at[c, layer], load_sem.at[c, layer])
                    copy.start() if go else copy.wait()
            at += count

    def remote(src, dst, slot, c, device):
        return pltpu.make_async_remote_copy(
            src_ref=src, dst_ref=dst, send_sem=send_sem.at[slot, c], recv_sem=recv_sem.at[slot, c],
            device_id=device, device_id_type=MESH)

    def copy_core(c):
        _, size = place(index, 1, CHUNK)
        other = (1 - bit_of(index, 0)) * size
        return remote(held.at[c, :, pl.ds(pl.multiple_of(other, 16), size)], landing[0].at[c], 0, c, mates[0])

    def copy_section(c):
        at, size = place(index, 1, CHUNK)
        return remote(held.at[c, 1 - section, pl.ds(pl.multiple_of(at, 16), size)], landing[1].at[c], 1, c, across)

    def copy_bit(bit):
        def make(c):
            if bit in halved:
                at, size = place(index, bit, CHUNK)
                size //= 2
                at = at + (1 - bit_of(index, bit)) * size
            else:
                at, size = place(index, len(halved), CHUNK)
            return remote(held.at[c, section, pl.ds(pl.multiple_of(at, 16), size)], landing[bit + 1].at[c], bit + 1, c, mates[bit])
        return make

    def copy_gather(bit, slot):
        def make(c):
            at, size = place(index, bit + 1, CHUNK)
            rows = pl.ds(pl.multiple_of(at, 16), size)
            return remote(gathered.at[c, rows], gathered.at[c, rows], slot, c, mates[bit])
        return make

    def add_core(c):
        at, size = place(index, 1, CHUNK)
        rows = pl.ds(pl.multiple_of(at, 16), size)
        for layer in range(2):
            held[c, layer, rows, :] = (held[c, layer, rows, :].astype(F32) + landing[0][c, layer].astype(F32)).astype(BF)

    def add_to(step, count, last):
        def add(c):
            at, size = place(index, count, CHUNK)
            rows = pl.ds(pl.multiple_of(at, 16), size)
            total = (held[c, section, rows, :].astype(F32) + landing[step][c].astype(F32)).astype(BF)
            if last:
                gathered[c, rows, :] = total
            else:
                held[c, section, rows, :] = total
        return add

    copies = [copy_core, copy_section] + [copy_bit(bit) for bit in all_bits[1:]]
    n_reduce = len(copies)
    adds = [add_core, add_to(1, 1, n_reduce == 2)]
    for bit in all_bits[1:]:
        adds.append(add_to(bit + 1, min(bit + 1, len(halved)), bit == all_bits[-1]))
    for bit in reversed(halved):
        copies.append(copy_gather(bit, len(copies)))
        adds.append(None)
    steps = len(copies)

    def out_copy(c):
        return pltpu.make_async_copy(gathered.at[c], out_ref.at[c], out_sem.at[c])

    small[...] = small_ref[...]
    small_steps = [across] + mates

    def small_copy(k):
        src = small.at[1 - section] if k == 0 else small.at[section]
        return pltpu.make_async_remote_copy(
            src_ref=src, dst_ref=small_in.at[k], send_sem=ssend.at[k], recv_sem=srecv.at[k],
            device_id=small_steps[k], device_id_type=MESH)

    @pl.loop(0, chunks)
    def _(c):
        loads(c, True)

    small_copy(0).start()

    @pl.loop(0, chunks + steps)
    def _(tick):
        for s in range(steps + 1):
            c = tick - s

            @pl.when((c >= 0) & (c < chunks))
            def _(s=s, c=c):
                if s == 0:
                    loads(c, False)
                else:
                    copies[s - 1](c).wait_recv()
                    if adds[s - 1] is not None:
                        adds[s - 1](c)
                if s < steps:
                    copies[s](c).start()
                else:
                    out_copy(c).start()

        for k in range(len(small_steps)):
            @pl.when(tick == k + 1)
            def _(k=k):
                small_copy(k).wait()
                small[section] = small[section] + small_in[k]
                if k + 1 < len(small_steps):
                    small_copy(k + 1).start()

    small_out[...] = small[section]

    @pl.loop(0, chunks)
    def _(c):
        for s in range(steps):
            copies[s](c).wait_send()
        out_copy(c).wait()


def sum_everywhere(groups, small, devices):
    kinds, ins = [], []
    for first, second in groups:
        kinds += [first.shape[0]] * 2
        ins += [first, second]
    chunks = sum(kinds[::2])
    halved, rest = halvings(devices, CHUNK)
    landing = [pltpu.VMEM((chunks, 2, CHUNK // 2, 512), BF), pltpu.VMEM((chunks, CHUNK // 2, 512), BF)]
    for bit in (halved + rest)[1:]:
        landing.append(pltpu.VMEM((chunks, CHUNK >> min(bit + 1, len(halved)), 512), BF))
    steps = 1 + len(halved + rest) + len(halved)
    n_small = 1 + len(halved + rest)
    vm = pl.BlockSpec(memory_space=pltpu.VMEM)
    return pl.pallas_call(
        functools.partial(sum_kernel, devices, kinds),
        out_shape=[jax.ShapeDtypeStruct((chunks, CHUNK, 512), BF), jax.ShapeDtypeStruct((16, 512), F32)],
        in_specs=[ANY] * len(ins) + [vm],
        out_specs=[ANY, vm],
        scratch_shapes=[
            pltpu.VMEM((chunks, 2, CHUNK, 512), BF),
            pltpu.VMEM((chunks, CHUNK, 512), BF),
            pltpu.SemaphoreType.DMA((chunks, 2)),
            pltpu.SemaphoreType.DMA((chunks,)),
            pltpu.SemaphoreType.DMA((steps, chunks)),
            pltpu.SemaphoreType.DMA((steps, chunks)),
            pltpu.VMEM((2, 16, 512), F32),
            pltpu.VMEM((n_small, 16, 512), F32),
            pltpu.SemaphoreType.DMA((n_small,)),
            pltpu.SemaphoreType.DMA((n_small,)),
        ] + landing,
        compiler_params=pltpu.CompilerParams(collective_id=1, has_side_effects=True, vmem_limit_bytes=VMEM_LIMIT),
        name="sum_gradients",
    )(*ins, small)


def unpack_kernel(kinds, g_ref, mem_ref, out_ref, low_far_ref, dx_ref, dy_ref, grad_far_ref, *refs):
    n = len(kinds)
    low_out, grad_out = refs[:2]
    outs = refs[2 : n + 2]
    stage, sem, low_buf, grad_buf, far_buf, row_in, row_out = refs[n + 2 :]
    step = pl.program_id(0)
    slot = step % 2
    section = lax.axis_index("section")
    fetch = [
        pltpu.make_async_copy(mem_ref, low_buf.at[0], row_in.at[0]),
        pltpu.make_async_copy(low_far_ref, low_buf.at[1], row_in.at[1]),
        pltpu.make_async_copy(dx_ref, grad_buf.at[0], row_in.at[2]),
        pltpu.make_async_copy(grad_far_ref, far_buf, row_in.at[3]),
    ]
    send = [
        pltpu.make_async_copy(low_buf.at[0], low_out.at[section], row_out.at[0]),
        pltpu.make_async_copy(low_buf.at[1], low_out.at[1 - section], row_out.at[1]),
        pltpu.make_async_copy(grad_buf.at[0], grad_out.at[section], row_out.at[2]),
        pltpu.make_async_copy(grad_buf.at[1], grad_out.at[1 - section], row_out.at[3]),
    ]

    @pl.when(step == 0)
    def _():
        fetch[1].start()
        fetch[3].start()

        @pl.when(section == 0)
        def _():
            fetch[0].start()
            fetch[2].start()

        @pl.when(section != 0)
        def _():
            pltpu.make_async_copy(out_ref, low_buf.at[0], row_in.at[0]).start()
            pltpu.make_async_copy(dy_ref, grad_buf.at[0], row_in.at[2]).start()

    for k in range(4):
        @pl.when(step == k + 2)
        def _(k=k):
            fetch[k].wait()
            if k == 3:
                grad_buf[1] = far_buf[...].astype(F32)
            send[k].start()

    def copy(kind, dest, k, c_slot):
        flipped, axis = kinds[kind][1:]
        at = pl.ds(pl.multiple_of(k * 512, 512), 512)
        dst = dest.at[:, at] if axis else dest.at[at, :]
        return pltpu.make_async_copy(stage.at[c_slot], dst, sem.at[c_slot])

    @pl.when(step >= 2)
    def _():
        copy(0, outs[0], 0, slot).wait()

    at = 0
    for kind, (count, flipped, axis) in enumerate(kinds):
        @pl.when((step >= at) & (step < at + count))
        def _(kind=kind, at=at, flipped=flipped):
            value = g_ref[0].astype(F32)
            stage[slot] = value.T if flipped else value
            copy(kind, outs[kind], step - at, slot).start()
        at += count

    @pl.when(step == pl.num_programs(0) - 1)
    def _():
        copy(0, outs[0], 0, 1 - slot).wait()
        copy(0, outs[0], 0, slot).wait()
        for one in send:
            one.wait()


def unpack(g, low, low_far, grad, grad_far, kinds, shapes):
    n, w = low_far.shape
    return pl.pallas_call(
        functools.partial(unpack_kernel, kinds),
        grid=(g.shape[0],),
        out_shape=[jax.ShapeDtypeStruct((2, n, w), BF), jax.ShapeDtypeStruct((2, n, w), F32)]
        + [jax.ShapeDtypeStruct(s, F32) for s in shapes],
        in_specs=[pl.BlockSpec((1, 512, 512), lambda i: (i, 0, 0))] + [ANY] * 6,
        out_specs=[ANY] * (len(shapes) + 2),
        scratch_shapes=[
            pltpu.VMEM((2, 512, 512), F32), pltpu.SemaphoreType.DMA((2,)),
            pltpu.VMEM((2, n, w), BF), pltpu.VMEM((2, n, w), F32), pltpu.VMEM((n, w), BF),
            pltpu.SemaphoreType.DMA((4,)), pltpu.SemaphoreType.DMA((4,)),
        ],
        compiler_params=pltpu.CompilerParams(vmem_limit_bytes=VMEM_LIMIT),
        name="unpack_results",
    )(g, *low, low_far, *grad, grad_far)


def spread_kernel(devices, *refs):
    tokens, small = refs[0], refs[1]
    weights = refs[2:7]
    tokens_out, small_out = refs[7], refs[8]
    outs = refs[9:14]
    tok_send, tok_recv, send_sem, recv_sem = refs[14:18]
    index = lax.axis_index("dp")
    section = lax.axis_index("section")
    bits = halvings(devices, 512)[0]
    across = (1 - section, index)
    mates = [(section, partner_of(index, bit)) for bit in bits]
    chunks = []
    for w in range(5):
        rows, cols = weights[w].shape
        chunks += [(w, r, c) for r in range(0, rows, 512) for c in range(0, cols, 512)]
    steps = len(bits) + 1
    land, flush_sem = refs[18:]
    greet([across] + mates)

    def window(k, at, size, ref_of):
        w, r, c = chunks[k]
        return ref_of(w).at[pl.ds(pl.multiple_of(r + at, 16), size), c : c + 512]

    def landing(k, at, size):
        return land.at[k, pl.ds(pl.multiple_of(at, 16), size)]

    def copy(k, step):
        if step == 0:
            at, size = place(index, len(bits), 512)
            src, device = window(k, at, size, lambda w: weights[w]), across
        else:
            bit = bits[len(bits) - step]
            at, size = place(index, bit + 1, 512)
            src, device = landing(k, at, size), mates[bit]
        return pltpu.make_async_remote_copy(
            src_ref=src, dst_ref=landing(k, at, size), send_sem=send_sem.at[step, k], recv_sem=recv_sem.at[step, k],
            device_id=device, device_id_type=MESH)

    swaps = [
        pltpu.make_async_remote_copy(
            src_ref=src, dst_ref=dst, send_sem=tok_send.at[i], recv_sem=tok_recv.at[i],
            device_id=across, device_id_type=MESH)
        for i, (src, dst) in enumerate([(small, small_out), (tokens.at[1 - section], tokens_out)])
    ]
    count = len(chunks)

    def flush(k):
        w, r, c = chunks[k]
        return pltpu.make_async_copy(land.at[k], outs[w].at[r : r + 512, c : c + 512], flush_sem.at[k])

    for k in range(count):
        copy(k, 0).start()
    for one in swaps:
        one.start()
    for tick in range(count + steps):
        for step in range(1, steps + 1):
            k = tick - step + 1
            if 0 <= k < count:
                copy(k, step - 1).wait_recv()
                if step < steps:
                    copy(k, step).start()
                else:
                    flush(k).start()
    for k in range(count):
        for step in range(steps):
            copy(k, step).wait_send()
        flush(k).wait()
    for one in swaps:
        one.wait()


def spread(tokens, small, weights, devices):
    steps = len(halvings(devices, 512)[0]) + 1
    count = sum(w.size for w in weights) // 512**2
    return pl.pallas_call(
        functools.partial(spread_kernel, devices),
        out_shape=[jax.ShapeDtypeStruct(tokens.shape[1:], BF), jax.ShapeDtypeStruct(small.shape, F32)]
        + [jax.ShapeDtypeStruct(w.shape, BF) for w in weights],
        in_specs=[ANY] * 7,
        out_specs=[ANY] * 7,
        scratch_shapes=[
            pltpu.SemaphoreType.DMA((2,)),
            pltpu.SemaphoreType.DMA((2,)),
            pltpu.SemaphoreType.DMA((steps, count)),
            pltpu.SemaphoreType.DMA((steps, count)),
            pltpu.VMEM((count, 512, 512), BF),
            pltpu.SemaphoreType.DMA((count,)),
        ],
        compiler_params=pltpu.CompilerParams(collective_id=0, has_side_effects=True, vmem_limit_bytes=VMEM_LIMIT),
        name="spread_weights",
    )(tokens, small, *weights)


def shards(layer_input, cotangent, src_segments, tgt_segments, attn_qkv, attn_out, cross_proj,
           ffn_in, ffn_in_bias, ffn_out, ffn_out_bias, norm_gain, norm_bias):
    devices = lax.axis_size("dp")
    sec = lax.axis_index("section")
    first = sec == 0
    swap = lambda a: lax.ppermute(a, "section", [(0, 1), (1, 0)])
    width = attn_out.shape[-1]
    vectors = jnp.concatenate(
        [ffn_in_bias.reshape(-1, width), ffn_out_bias, norm_gain[0], norm_bias[0], jnp.zeros((5, width), F32)])
    tokens = layer_input[0, :, 0]
    near = (attn_qkv[0], attn_out[0], cross_proj[0], ffn_in[0], ffn_out[0])
    far_tokens, far_vectors, *far = spread(tokens, vectors, near, devices)
    mem, out, dx, dy, groups, dsmall = row_step(
        tokens, far_tokens, cotangent[:, 0], src_segments, tgt_segments, near, far, vectors, far_vectors)
    low_far = swap(jnp.where(first, out, mem))
    grad_far = swap(jnp.where(first, dy, dx).astype(BF))
    sums, s = sum_everywhere(groups, dsmall, devices)
    kinds = ((4, False, 1), (4, True, 0), (2, True, 1), (3, True, 1), (1, False, 0))
    layer_output, input_grad, win, wout, cross, qkv, wo = unpack(
        sums, (mem, out), low_far, (dx, dy), grad_far, kinds,
        [ffn_in.shape[1:], ffn_out.shape[1:], cross_proj.shape[1:], attn_qkv.shape[1:], attn_out.shape[1:]])
    return (layer_output[None, :, None], input_grad[None, :, None], qkv[None], wo[None], cross[None], win[None],
            s[0:4].reshape(1, -1), wout[None], s[4:5], s[5:8][None], s[8:11][None])


def solution(mesh):
    return jax.shard_map(
        shards,
        mesh=mesh,
        in_specs=(
            P("section", None, "dp", None, None),
            P(None, "dp", None, None),
            P(None, "dp", None),
            P(None, "dp", None),
            P("section", None, None),
            P("section", None, None),
            P("section", None, None),
            P("section", None, None),
            P("section", None),
            P("section", None, None),
            P("section", None),
            P("section", None, None),
            P("section", None, None),
        ),
        out_specs=(
            P("section", None, "dp", None, None),
            P("section", None, "dp", None, None),
            P("section", None, None),
            P("section", None, None),
            P("section", None, None),
            P("section", None, None),
            P("section", None),
            P("section", None, None),
            P("section", None),
            P("section", None, None),
            P("section", None, None),
        ),
        check_vma=False,
    )
```

```python
import functools
import math

import jax
import jax.numpy as jnp
from jax import lax
from jax.experimental import pallas as pl
from jax.experimental.pallas import tpu as pltpu
from jax.sharding import PartitionSpec as P

HEADS = 8
EPSILON = 1e-05
NEGATIVE = -1000000000.0
BF = jnp.bfloat16
F32 = jnp.float32
LOG2E = 1.4426950408889634
QB = 256
UNIT = 128
WIDE = 256
TB = 256
VMEM_LIMIT = 60 * 1024 * 1024


def dot(left, right, lc=1, rc=0):
    return lax.dot_general(
        left, right, (((lc,), (rc,)), ((), ())), preferred_element_type=F32
    )


def norm_stats(value):
    centered = value - jnp.mean(value, axis=-1, keepdims=True)
    spread = jnp.mean(centered * centered, axis=-1, keepdims=True)
    scale = lax.rsqrt(spread + EPSILON)
    return centered * scale, scale


def norm_back(out_grad, unit, scale, gain):
    gain_grad = jnp.sum(out_grad * unit, axis=0, keepdims=True)
    shift_grad = jnp.sum(out_grad, axis=0, keepdims=True)
    inner = out_grad * gain
    mean_one = jnp.mean(inner, axis=-1, keepdims=True)
    mean_two = jnp.mean(inner * unit, axis=-1, keepdims=True)
    return scale * (inner - mean_one - unit * mean_two), gain_grad, shift_grad


def gelu_pair(u):
    phi = 0.5 + 0.5 * lax.erf(u * (1.0 / math.sqrt(2.0)))
    bell = jnp.exp(-0.5 * u * u) * (1.0 / math.sqrt(2.0 * math.pi))
    return u * phi, phi + u * bell


def gain_of(small, norm):
    return small[5 + norm : 6 + norm, :]


def shift_of(small, norm):
    return small[8 + norm : 9 + norm, :]


def key_codes(ids_row, length):
    column = jnp.broadcast_to(ids_row.astype(F32), (128, length)).T
    lane = lax.broadcasted_iota(jnp.int32, (length, 128), 1)
    spot = jnp.where(lane < 64, lane, lane - 64)
    codes = jnp.where(
        spot < 4,
        jnp.where(column == spot.astype(F32), 0.0, NEGATIVE),
        jnp.where(spot < 7, -1.0, 0.0),
    )
    return codes, lane < 64


def fill_keys(dst, keys_ref, codes, low_half):
    for pair in range(HEADS // 2):
        slab = keys_ref[:, pair * 128 : pair * 128 + 128].astype(F32)
        dst[2 * pair] = jnp.where(low_half, slab, codes).astype(BF)
        dst[2 * pair + 1] = jnp.where(low_half, codes, slab).astype(BF)


def query_rows(head):
    return (0, 64) if head % 2 == 0 else (64, 0)


def key_range(query_ids, key_ids, qb):
    ids = query_ids[:, pl.ds(pl.multiple_of(qb * QB, QB), QB)].astype(F32)
    keys = key_ids[...].astype(F32)
    start = jnp.sum((keys < jnp.min(ids)).astype(F32)).astype(jnp.int32)
    stop = jnp.sum((keys <= jnp.max(ids)).astype(F32)).astype(jnp.int32)
    return start // UNIT, (stop + UNIT - 1) // UNIT


def visit_keys(query_ids, key_ids, qb, causal, step):
    lo, hi = key_range(query_ids, key_ids, qb)
    if causal is not None:
        diagonal = qb * (QB // UNIT)
        hi = jnp.where(causal, diagonal, hi)
    count = hi - lo

    @pl.loop(0, count // 2)
    def _(i):
        step(lo + 2 * i, WIDE, False)

    @pl.when(count % 2 == 1)
    def _():
        step(hi - 1, UNIT, False)

    if causal is not None:
        @pl.when(causal)
        def _():
            step(diagonal, WIDE, True)


def below_diagonal():
    return lax.broadcasted_iota(jnp.int32, (WIDE, QB), 0) <= lax.broadcasted_iota(jnp.int32, (WIDE, QB), 1)


def staged(first, lag_one, second, lag_two, third):
    for i in range(HEADS + lag_one + lag_two):
        if i < HEADS:
            first(i)
        if 0 <= i - lag_one < HEADS:
            second(i - lag_one)
        if 0 <= i - lag_one - lag_two < HEADS:
            third(i - lag_one - lag_two)


def attend_loop(query_ids, key_ids, causal, qaug, kaug, vt, attT_ref, lse_ref, oacc, mrow, lrow, sbuf, pbuf, length):
    @pl.loop(0, length // QB)
    def _(qb):
        q = pl.ds(pl.multiple_of(qb * QB, QB), QB)
        oacc[...] = jnp.zeros_like(oacc)
        mrow[...] = jnp.full_like(mrow, -3e38)
        lrow[...] = jnp.zeros_like(lrow)

        def step(unit, size, masked):
            ks = pl.ds(pl.multiple_of(unit * UNIT, UNIT), size)
            scale = {}

            def scores(h):
                s = dot(kaug[h, ks, :], qaug[h, :, q])
                sbuf[h, :size] = jnp.where(below_diagonal(), s, NEGATIVE) if masked else s

            def softmax(h):
                s = sbuf[h, :size]
                m_old = mrow[h : h + 1, :]
                m_new = jnp.maximum(m_old, jnp.max(s, axis=0, keepdims=True))
                scale[h] = jnp.exp2(m_old - m_new)
                p = jnp.exp2(s - m_new)
                lrow[h : h + 1, :] = lrow[h : h + 1, :] * scale[h] + jnp.sum(p, axis=0, keepdims=True)
                mrow[h : h + 1, :] = m_new
                pbuf[h, :size] = p.astype(BF)

            def mix(h):
                hs = slice(h * 64, h * 64 + 64)
                oacc[hs, :] = oacc[hs, :] * scale[h] + dot(vt[hs, ks], pbuf[h, :size])

            staged(scores, 7, softmax, 1, mix)

        visit_keys(query_ids, key_ids, qb, causal, step)
        for h in range(HEADS):
            hs = slice(h * 64, h * 64 + 64)
            attT_ref[hs, q] = (oacc[hs, :] * (1.0 / lrow[h : h + 1, :])).astype(BF)
        lse_ref[:, q] = mrow[...] + jnp.log2(lrow[...])


def query_codes(ids_row, length):
    row = lax.broadcasted_iota(jnp.int32, (16, length), 0)
    return jnp.where(row == jnp.broadcast_to(ids_row, (16, length)), 1.0, 0.0), row


def fill_queries(qaug, qT_ref, codes, row, lse_ref, length):
    for h in range(HEADS):
        a, b = query_rows(h)
        qaug[h, a : a + 64, :] = qT_ref[h * 64 : h * 64 + 64, :]
        extra = codes
        if lse_ref is not None:
            lse = lse_ref[h : h + 1, :]
            hi = lse.astype(BF).astype(F32)
            mid = (lse - hi).astype(BF).astype(F32)
            low = lse - hi - mid
            extra = jnp.where(row == 4, hi, jnp.where(row == 5, mid, jnp.where(row == 6, low, codes)))
        qaug[h, b : b + 16, :] = extra.astype(BF)
        qaug[h, b + 16 : b + 64, :] = jnp.zeros((48, length), BF)


def project_queries(src_ref, w_ref, qT_ref, length, width):
    @pl.loop(0, length // TB)
    def _(t):
        rows = pl.ds(pl.multiple_of(t * TB, TB), TB)
        q = dot(src_ref[rows, :], w_ref[:, :width]) * (0.125 * LOG2E)
        qT_ref[:, rows] = q.T.astype(BF)


def out_and_norm(attT_ref, w_ref, resid_ref, sm_ref, norm, res_ref, hid_ref, length):
    @pl.loop(0, length // TB)
    def _(t):
        rows = pl.ds(pl.multiple_of(t * TB, TB), TB)
        a = dot(attT_ref[:, rows], w_ref[...], 0, 0)
        r = resid_ref[rows, :].astype(F32) + a
        res_ref[rows, :] = r.astype(BF)
        unit, _ = norm_stats(r)
        hid_ref[rows, :] = (unit * gain_of(sm_ref, norm) + shift_of(sm_ref, norm)).astype(BF)


def self_fwd_kernel(own, x_ref, ids_ref, w_ref, wout_ref, ln_ref,
                    qT_ref, k_ref, v_ref, attT_ref, lse_ref, res_ref, hid_ref,
                    kaug, qaug, vt, oacc, mrow, lrow, sbuf, pbuf):
    x_ref, w_ref = ready(x_ref, w_ref)
    length, width = x_ref.shape
    project_queries(x_ref, w_ref, qT_ref, length, width)

    @pl.loop(0, length // TB)
    def _(t):
        rows = pl.ds(pl.multiple_of(t * TB, TB), TB)
        k_ref[rows, :] = dot(x_ref[rows, :], w_ref[:, width : 2 * width]).astype(BF)
        v = dot(x_ref[rows, :], w_ref[:, 2 * width :])
        v_ref[rows, :] = v.astype(BF)
        vt[:, rows] = v.T.astype(BF)

    for result in (qT_ref, k_ref, v_ref):
        result.flush()
    (ids_ref,) = ready(ids_ref)
    codes, low_half = key_codes(ids_ref[...], length)
    fill_keys(kaug, k_ref, codes, low_half)
    qcodes, row = query_codes(ids_ref[...], length)
    fill_queries(qaug, qT_ref, qcodes, row, None, length)
    causal = lax.axis_index("section") == (1 if own else 0)
    attend_loop(ids_ref, ids_ref, causal, qaug, kaug, vt, attT_ref, lse_ref, oacc, mrow, lrow, sbuf, pbuf, length)
    attT_ref.flush()
    lse_ref.flush()
    wout_ref, ln_ref = ready(wout_ref, ln_ref)
    out_and_norm(attT_ref, wout_ref, x_ref, ln_ref, 0, res_ref, hid_ref, length)


def cross_fwd_kernel(h_ref, kv_ref, qids_ref, kids_ref, w_ref, ln_ref,
                     qT_ref, attT_ref, lse_ref, res_ref, hid_ref,
                     kaug, qaug, vt, oacc, mrow, lrow, sbuf, pbuf):
    h_ref, w_ref = ready(h_ref, w_ref)
    length, width = h_ref.shape
    project_queries(h_ref, w_ref, qT_ref, length, width)
    qT_ref.flush()
    kv_ref, qids_ref, kids_ref = ready(kv_ref, qids_ref, kids_ref)

    @pl.loop(0, length // TB)
    def _(t):
        rows = pl.ds(pl.multiple_of(t * TB, TB), TB)
        vt[:, rows] = kv_ref[rows, width:].astype(F32).T.astype(BF)

    codes, low_half = key_codes(kids_ref[...], length)
    fill_keys(kaug, kv_ref, codes, low_half)
    qcodes, row = query_codes(qids_ref[...], length)
    fill_queries(qaug, qT_ref, qcodes, row, None, length)
    attend_loop(qids_ref, kids_ref, None, qaug, kaug, vt, attT_ref, lse_ref, oacc, mrow, lrow, sbuf, pbuf, length)
    attT_ref.flush()
    lse_ref.flush()
    (ln_ref,) = ready(ln_ref)
    out_and_norm(attT_ref, w_ref.at[:, width:], h_ref, ln_ref, 1, res_ref, hid_ref, length)


def attend_back_loop(query_ids, key_ids, causal, qaug, kaug, kt, vaug, doaug, jgT, dqacc, sbuf, dbuf, pbuf, gbuf, length):
    width = HEADS * 64

    @pl.loop(0, length // QB)
    def _(qb):
        q = pl.ds(pl.multiple_of(qb * QB, QB), QB)
        dqacc[...] = jnp.zeros_like(dqacc)

        def step(unit, size, masked):
            ks = pl.ds(pl.multiple_of(unit * UNIT, UNIT), size)

            def products(h):
                s = dot(kaug[h, ks, :], qaug[h, :, q])
                sbuf[h, :size] = jnp.where(below_diagonal(), s, NEGATIVE) if masked else s
                dbuf[h, :size] = dot(vaug[h, ks, :], doaug[h, :, q])

            def grads(h):
                p = jnp.exp2(sbuf[h, :size])
                pbuf[h, :size] = p.astype(BF)
                gbuf[h, :size] = (p * dbuf[h, :size]).astype(BF)

            def add(h):
                a, _ = query_rows(h)
                at = h * 64
                hs = slice(at, at + 64)
                dqacc[hs, :] += dot(kt[hs, ks], gbuf[h, :size])
                jgT[2 * width + at : 2 * width + at + 64, ks] += dot(doaug[h, a : a + 64, q], pbuf[h, :size], 1, 1)
                jgT[width + at : width + at + 64, ks] += dot(qaug[h, a : a + 64, q], gbuf[h, :size], 1, 1)

            lag = 1 if size == WIDE else 2
            staged(products, lag, grads, lag, add)

        visit_keys(query_ids, key_ids, qb, causal, step)
        jgT[:width, q] = dqacc[...] * 0.125


def prepare_back(dr_ref, w_out, attT_ref, doT, doaug, length):
    @pl.loop(0, length // TB)
    def _(t):
        rows = pl.ds(pl.multiple_of(t * TB, TB), TB)
        doT[:, rows] = dot(w_out, dr_ref[rows, :], 1, 1).astype(BF)

    row = lax.broadcasted_iota(jnp.int32, (16, length), 0)
    for h in range(HEADS):
        a, b = query_rows(h)
        hs = slice(h * 64, h * 64 + 64)
        doh = doT[hs, :]
        doaug[h, a : a + 64, :] = doh
        delta = jnp.sum(doh.astype(F32) * attT_ref[hs, :].astype(F32), axis=0, keepdims=True)
        hi = delta.astype(BF).astype(F32)
        mid = (delta - hi).astype(BF).astype(F32)
        low = delta - hi - mid
        extra = jnp.where(row == 4, hi, jnp.where(row == 5, mid, jnp.where(row == 6, low, 0.0)))
        doaug[h, b : b + 16, :] = extra.astype(BF)
        doaug[h, b + 16 : b + 64, :] = jnp.zeros((48, length), BF)


def prepare_keys(keys_ref, values_ref, codes, low_half, kaug, kt, vaug, length):
    fill_keys(kaug, keys_ref, codes, low_half)
    fill_keys(vaug, values_ref, jnp.where(codes == NEGATIVE, 0.0, codes), low_half)

    @pl.loop(0, length // TB)
    def _(t):
        rows = pl.ds(pl.multiple_of(t * TB, TB), TB)
        kt[:, rows] = keys_ref[rows, :].astype(F32).T.astype(BF)


def finish_grads(jgT, jg, koff, length):
    rows_total = jgT.shape[0]
    for r in range(0, rows_total, 512):
        f = math.log(2.0) if r == koff else 1.0
        jg[r : r + 512, :] = (jgT[r : r + 512, :] * f).astype(BF)


def self_bwd_kernel(own, dh_ref, res_ref, x_ref, ids_ref, qT_ref, k_ref, v_ref, attT_ref,
                    lse_ref, w_ref, wout_ref, ln_ref,
                    dx_ref, dw_ref, dln_ref,
                    kaug, kt, vaug, qaug, doaug, doT, dqacc, jgT, jg, sbuf, dbuf, pbuf, gbuf, dr):
    dh_ref, res_ref, ln_ref = ready(dh_ref, res_ref, ln_ref)
    length, width = res_ref.shape
    dln_ref[...] = jnp.zeros(dln_ref.shape, F32)

    @pl.loop(0, length // TB)
    def _(t):
        rows = pl.ds(pl.multiple_of(t * TB, TB), TB)
        unit, scale = norm_stats(res_ref[rows, :].astype(F32))
        d, gg, sg = norm_back(dh_ref[rows, :].astype(F32), unit, scale, gain_of(ln_ref, 0))
        dln_ref[5:6, :] += gg
        dln_ref[8:9, :] += sg
        dr[rows, :] = d.astype(BF)

    attT_ref, wout_ref, ids_ref = ready(attT_ref, wout_ref, ids_ref)
    dw_ref[3] = dot(attT_ref[...], dr[...]).astype(BF)
    prepare_back(dr, wout_ref[...], attT_ref, doT, doaug, length)
    codes, low_half = key_codes(ids_ref[...], length)
    k_ref, v_ref, qT_ref, lse_ref = ready(k_ref, v_ref, qT_ref, lse_ref)
    prepare_keys(k_ref, v_ref, codes, low_half, kaug, kt, vaug, length)
    qcodes, row = query_codes(ids_ref[...], length)
    fill_queries(qaug, qT_ref, qcodes, row, lse_ref, length)
    jgT[width:, :] = jnp.zeros((2 * width, length), F32)
    causal = lax.axis_index("section") == (1 if own else 0)
    attend_back_loop(ids_ref, ids_ref, causal, qaug, kaug, kt, vaug, doaug, jgT, dqacc, sbuf, dbuf, pbuf, gbuf, length)
    finish_grads(jgT, jg, width, length)
    x_ref, w_ref = ready(x_ref, w_ref)

    @pl.loop(0, 3)
    def _(t):
        rows = pl.ds(pl.multiple_of(t * 512, 512), 512)
        dw_ref[t] = dot(jg[rows, :], x_ref[...]).astype(BF)

    dw_ref.flush()

    @pl.loop(0, length // TB)
    def _(t):
        rows = pl.ds(pl.multiple_of(t * TB, TB), TB)
        d = dot(jg[:, rows], w_ref[...], 0, 1)
        dx_ref[rows, :] = (dr[rows, :].astype(F32) + d).astype(dx_ref.dtype)


def cross_bwd_kernel(dr_ref, h_ref, mem_ref, qids_ref, kids_ref, qT_ref, kv_ref, attT_ref,
                     lse_ref, w_ref, wkv_ref,
                     dh_ref, dmem_ref, dwd_ref, dwe_ref,
                     kaug, kt, vaug, qaug, doaug, doT, dqacc, jgT, jg, sbuf, dbuf, pbuf, gbuf):
    dr_ref, attT_ref, w_ref, qids_ref, kids_ref = ready(dr_ref, attT_ref, w_ref, qids_ref, kids_ref)
    length, width = dr_ref.shape
    dwd_ref[1] = dot(dr_ref[...], attT_ref[...], 0, 1).astype(BF)
    prepare_back(dr_ref, w_ref[:, width:], attT_ref, doT, doaug, length)
    codes, low_half = key_codes(kids_ref[...], length)
    kv_ref, qT_ref, lse_ref = ready(kv_ref, qT_ref, lse_ref)
    prepare_keys(kv_ref.at[:, :width], kv_ref.at[:, width:], codes, low_half, kaug, kt, vaug, length)
    qcodes, row = query_codes(qids_ref[...], length)
    fill_queries(qaug, qT_ref, qcodes, row, lse_ref, length)
    jgT[width:, :] = jnp.zeros((2 * width, length), F32)
    attend_back_loop(qids_ref, kids_ref, None, qaug, kaug, kt, vaug, doaug, jgT, dqacc, sbuf, dbuf, pbuf, gbuf, length)
    finish_grads(jgT, jg, width, length)
    h_ref, mem_ref, wkv_ref = ready(h_ref, mem_ref, wkv_ref)
    dwd_ref[0] = dot(jg[:width, :], h_ref[...]).astype(BF)
    for half in range(2):
        dwe_ref[half] = dot(jg[(half + 1) * width : (half + 2) * width, :], mem_ref[...]).astype(BF)
    dwd_ref.flush()
    dwe_ref.flush()

    @pl.loop(0, length // TB)
    def _(t):
        rows = pl.ds(pl.multiple_of(t * TB, TB), TB)
        d = dot(jg[:width, rows], w_ref[:, :width], 0, 1)
        dh_ref[rows, :] = (dr_ref[rows, :].astype(F32) + d).astype(BF)
        dmem_ref[rows, :] = dot(jg[width:, rows], wkv_ref[...], 0, 1).astype(BF)


def enc_ffn_fwd_kernel(e1_ref, win_ref, wout_ref, ln_ref, wkv_ref,
                       g_ref, gp_ref, r_ref, mem_ref, kv_ref):
    e1_ref, win_ref, wout_ref, ln_ref, wkv_ref = ready(e1_ref, win_ref, wout_ref, ln_ref, wkv_ref)
    length, width = e1_ref.shape
    ff = win_ref.shape[1]

    @pl.loop(0, length // TB)
    def _(t):
        rows = pl.ds(pl.multiple_of(t * TB, TB), TB)
        e1 = e1_ref[rows, :]
        total = e1.astype(F32) + ln_ref[4:5, :]
        for j in range(0, ff, 512):
            u = dot(e1, win_ref[:, j : j + 512]) + ln_ref[j // 512 : j // 512 + 1, :]
            g, gp = gelu_pair(u)
            gb = g.astype(BF)
            g_ref[rows, j : j + 512] = gb
            gp_ref[rows, j : j + 512] = gp.astype(BF)
            total += dot(gb, wout_ref[j : j + 512, :])
        r_ref[rows, :] = total.astype(BF)
        unit, _ = norm_stats(total)
        e2 = unit * gain_of(ln_ref, 1) + shift_of(ln_ref, 1)
        unit, _ = norm_stats(e2)
        mem = (unit * gain_of(ln_ref, 2) + shift_of(ln_ref, 2)).astype(BF)
        mem_ref[rows, :] = mem
        kv_ref[rows, :] = dot(mem, wkv_ref[...]).astype(BF)


def weight_grads(act_ref, du_ref, df_ref, g_ref, dw_ref):
    slabs = du_ref.shape[1] // 512

    @pl.loop(0, slabs)
    def _(t):
        cols = pl.ds(pl.multiple_of(t * 512, 512), 512)
        dw_ref[t] = dot(act_ref[...], du_ref[:, cols], 0, 0).astype(BF)
        dw_ref[slabs + t] = dot(df_ref[...], g_ref[:, cols], 0, 0).astype(BF)


def enc_ffn_bwd_kernel(dmem_ref, r_ref, g_ref, gp_ref, e1_ref, win_ref, wout_ref, ln_ref,
                       de1_ref, dw_ref, dln_ref,
                       du_ref, df_ref):
    dmem_ref, r_ref, ln_ref, wout_ref, gp_ref, win_ref = ready(dmem_ref, r_ref, ln_ref, wout_ref, gp_ref, win_ref)
    length, width = r_ref.shape
    ff = win_ref.shape[1]
    dln_ref[...] = jnp.zeros(dln_ref.shape, F32)

    @pl.loop(0, length // TB)
    def _(t):
        rows = pl.ds(pl.multiple_of(t * TB, TB), TB)
        unit2, scale2 = norm_stats(r_ref[rows, :].astype(F32))
        e2 = unit2 * gain_of(ln_ref, 1) + shift_of(ln_ref, 1)
        unit3, scale3 = norm_stats(e2)
        de2, gg, sg = norm_back(dmem_ref[rows, :].astype(F32), unit3, scale3, gain_of(ln_ref, 2))
        dln_ref[7:8, :] += gg
        dln_ref[10:11, :] += sg
        dr, gg, sg = norm_back(de2, unit2, scale2, gain_of(ln_ref, 1))
        dln_ref[6:7, :] += gg
        dln_ref[9:10, :] += sg
        df = dr.astype(BF)
        df_ref[rows, :] = df
        dln_ref[4:5, :] += jnp.sum(df.astype(F32), axis=0, keepdims=True)
        total = dr
        for j in range(0, ff, 512):
            dg = dot(df, wout_ref[j : j + 512, :], 1, 1)
            du = dg * gp_ref[rows, j : j + 512].astype(F32)
            dub = du.astype(BF)
            du_ref[rows, j : j + 512] = dub
            dln_ref[j // 512 : j // 512 + 1, :] += jnp.sum(du, axis=0, keepdims=True)
            total += dot(dub, win_ref[:, j : j + 512], 1, 1)
        de1_ref[rows, :] = total.astype(BF)

    de1_ref.flush()
    e1_ref, g_ref = ready(e1_ref, g_ref)
    weight_grads(e1_ref, du_ref, df_ref, g_ref, dw_ref)


def dec_ffn_kernel(h_ref, res_ref, cot_ref, win_ref, wout_ref, ln_ref,
                   out_ref, dres_ref, dw_ref, dln_ref,
                   g_ref, gp_ref, du_ref, df_ref):
    h_ref, win_ref, ln_ref, wout_ref, cot_ref, res_ref = ready(h_ref, win_ref, ln_ref, wout_ref, cot_ref, res_ref)
    length, width = h_ref.shape
    ff = win_ref.shape[1]
    dln_ref[...] = jnp.zeros(dln_ref.shape, F32)

    @pl.loop(0, length // TB)
    def _(t):
        rows = pl.ds(pl.multiple_of(t * TB, TB), TB)
        h = h_ref[rows, :]
        total = h.astype(F32) + ln_ref[4:5, :]
        for j in range(0, ff, 512):
            u = dot(h, win_ref[:, j : j + 512]) + ln_ref[j // 512 : j // 512 + 1, :]
            g, gp = gelu_pair(u)
            gb = g.astype(BF)
            g_ref[rows, j : j + 512] = gb
            gp_ref[:, j : j + 512] = gp.astype(BF)
            total += dot(gb, wout_ref[j : j + 512, :])
        unit3, scale3 = norm_stats(total)
        out_ref[rows, :] = (unit3 * gain_of(ln_ref, 2) + shift_of(ln_ref, 2)).astype(BF)
        dr, gg, sg = norm_back(cot_ref[rows, :].astype(F32), unit3, scale3, gain_of(ln_ref, 2))
        dln_ref[7:8, :] += gg
        dln_ref[10:11, :] += sg
        df = dr.astype(BF)
        df_ref[rows, :] = df
        dln_ref[4:5, :] += jnp.sum(df.astype(F32), axis=0, keepdims=True)
        total = dr
        for j in range(0, ff, 512):
            dg = dot(df, wout_ref[j : j + 512, :], 1, 1)
            du = dg * gp_ref[:, j : j + 512].astype(F32)
            dub = du.astype(BF)
            du_ref[rows, j : j + 512] = dub
            dln_ref[j // 512 : j // 512 + 1, :] += jnp.sum(du, axis=0, keepdims=True)
            total += dot(dub, win_ref[:, j : j + 512], 1, 1)
        unit2, scale2 = norm_stats(res_ref[rows, :].astype(F32))
        d, gg, sg = norm_back(total, unit2, scale2, gain_of(ln_ref, 1))
        dln_ref[6:7, :] += gg
        dln_ref[9:10, :] += sg
        dres_ref[rows, :] = d.astype(BF)

    out_ref.flush()
    dres_ref.flush()
    weight_grads(h_ref, du_ref, df_ref, g_ref, dw_ref)


class Operand:
    def __init__(self, copy, ref):
        self.copy, self.ref = copy, ref


def ready(*operands):
    refs = []
    for operand in operands:
        if operand.copy is not None:
            operand.copy.wait()
            operand.copy = None
        refs.append(operand.ref)
    return refs


class Result:
    def __init__(self, copy, ref):
        self.copy, self.ref, self.started = copy, ref, False

    def __getitem__(self, at):
        return self.ref[at]

    def __setitem__(self, at, value):
        self.ref[at] = value

    def __getattr__(self, name):
        return getattr(self.ref, name)

    def flush(self):
        if not self.started:
            self.copy.start()
            self.started = True


class Row:
    def __init__(self, array):
        self.array, self.shape, self.dtype = array, array.shape[1:], array.dtype


class Pick:
    def __init__(self, zero, one=None):
        self.parts = [zero] if one is None else [zero, one]
        self.arrays = [p.array if isinstance(p, Row) else p for p in self.parts]
        self.shape, self.dtype = zero.shape, zero.dtype

    def copy(self, refs, dst, sem, section):
        sources = [ref.at[section] if isinstance(p, Row) else ref for p, ref in zip(self.parts, refs)]
        if len(sources) == 1:
            copy = pltpu.make_async_copy(sources[0], dst, sem)
            copy.start()
            return copy
        for k, source in enumerate(sources):
            @pl.when(section == k)
            def _(source=source):
                pltpu.make_async_copy(source, dst, sem).start()
        return pltpu.make_async_copy(sources[1], dst, sem)


def run_kernel(kernel, plan, n_out, *refs):
    n_in = sum(len(p.arrays) for p in plan)
    ins, outs = list(refs[:n_in]), refs[n_in : n_in + n_out]
    rest = refs[n_in + n_out :]
    in_bufs, out_bufs = rest[: len(plan)], rest[len(plan) : len(plan) + n_out]
    in_sem, out_sem = rest[len(plan) + n_out : len(plan) + n_out + 2]
    scratch = rest[len(plan) + n_out + 2 :]
    section = lax.axis_index("section")
    operands = []
    for k, entry in enumerate(plan):
        given = [ins.pop(0) for _ in entry.arrays]
        operands.append(Operand(entry.copy(given, in_bufs[k], in_sem.at[k], section), in_bufs[k]))
    results = [
        Result(pltpu.make_async_copy(out_bufs[k], outs[k], out_sem.at[k]), out_bufs[k]) for k in range(n_out)
    ]
    kernel(*operands, *results, *scratch)
    ready(*operands)
    for result in results:
        result.flush()
    for result in results:
        result.copy.wait()


def call(kernel, name, outs, scratch, flops, *args):
    any_space = pl.BlockSpec(memory_space=pl.ANY)
    plan = [a if isinstance(a, Pick) else Pick(a) for a in args]
    given = [array for entry in plan for array in entry.arrays]
    return pl.pallas_call(
        functools.partial(run_kernel, kernel, plan, len(outs)),
        out_shape=[jax.ShapeDtypeStruct(s, d) for s, d in outs],
        in_specs=[any_space] * len(given),
        out_specs=[any_space] * len(outs),
        scratch_shapes=[pltpu.VMEM(entry.shape, entry.dtype) for entry in plan]
        + [pltpu.VMEM(s, d) for s, d in outs]
        + [pltpu.SemaphoreType.DMA((len(plan),)), pltpu.SemaphoreType.DMA((len(outs),))]
        + scratch,
        compiler_params=pltpu.CompilerParams(vmem_limit_bytes=VMEM_LIMIT),
        cost_estimate=pl.CostEstimate(flops=flops, bytes_accessed=8 << 20, transcendentals=0),
        name=name,
    )(*given)


def fwd_scratch(n, w):
    return [
        pltpu.VMEM((HEADS, n, 128), BF),
        pltpu.VMEM((HEADS, 128, n), BF),
        pltpu.VMEM((w, n), BF),
        pltpu.VMEM((w, QB), F32),
        pltpu.VMEM((HEADS, QB), F32),
        pltpu.VMEM((HEADS, QB), F32),
        pltpu.VMEM((HEADS, WIDE, QB), F32),
        pltpu.VMEM((HEADS, WIDE, QB), BF),
    ]


def self_fwd(own, x, ids, w, wout, small):
    n, w_ = x.shape
    return call(functools.partial(self_fwd_kernel, own), "self_forward",
                [((w_, n), BF), ((n, w_), BF), ((n, w_), BF), ((w_, n), BF), ((HEADS, n), F32), ((n, w_), BF), ((n, w_), BF)],
                fwd_scratch(n, w_), 10 << 30, x, ids, w, wout, small)


def cross_fwd(h, kv, qids, kids, w, small):
    n, w_ = h.shape
    return call(cross_fwd_kernel, "cross_forward",
                [((w_, n), BF), ((w_, n), BF), ((HEADS, n), F32), ((n, w_), BF), ((n, w_), BF)],
                fwd_scratch(n, w_), 10 << 30, h, kv, qids, kids, w, small)


def bwd_scratch(n, w):
    return [
        pltpu.VMEM((HEADS, n, 128), BF),
        pltpu.VMEM((w, n), BF),
        pltpu.VMEM((HEADS, n, 128), BF),
        pltpu.VMEM((HEADS, 128, n), BF),
        pltpu.VMEM((HEADS, 128, n), BF),
        pltpu.VMEM((w, n), BF),
        pltpu.VMEM((w, QB), F32),
        pltpu.VMEM((3 * w, n), F32),
        pltpu.VMEM((3 * w, n), BF),
        pltpu.VMEM((HEADS, WIDE, QB), F32),
        pltpu.VMEM((HEADS, WIDE, QB), F32),
        pltpu.VMEM((HEADS, WIDE, QB), BF),
        pltpu.VMEM((HEADS, WIDE, QB), BF),
    ]


def self_bwd(own, dh, res, x, ids, qT, k, v, attT, lse, w, wout, small):
    n, w_ = res.shape
    return call(functools.partial(self_bwd_kernel, own), "self_backward",
                [((n, w_), F32 if own else BF), ((4, w_, w_), BF), ((16, w_), F32)],
                bwd_scratch(n, w_) + [pltpu.VMEM((n, w_), BF)], 25 << 30,
                dh, res, x, ids, qT, k, v, attT, lse, w, wout, small)


def cross_bwd(dr, h, mem, qids, kids, qT, kv, attT, lse, w, wkv):
    n, w_ = h.shape
    return call(cross_bwd_kernel, "cross_backward",
                [((n, w_), BF), ((n, w_), BF), ((2, w_, w_), BF), ((2, w_, w_), BF)],
                bwd_scratch(n, w_), 25 << 30,
                dr, h, mem, qids, kids, qT, kv, attT, lse, w, wkv)


def enc_ffn_fwd(e1, win, wout, small, wkv):
    n, w_ = e1.shape
    ff = win.shape[-1]
    return call(enc_ffn_fwd_kernel, "encoder_ffn_forward",
                [((n, ff), BF), ((n, ff), BF), ((n, w_), BF), ((n, w_), BF), ((n, 2 * w_), BF)],
                [], 6 << 30, e1, win, wout, small, wkv)


def enc_ffn_bwd(dmem, r, g, gp, e1, win, wout, small):
    n, w_ = e1.shape
    ff = win.shape[-1]
    return call(enc_ffn_bwd_kernel, "encoder_ffn_backward",
                [((n, w_), BF), ((2 * ff // w_, w_, w_), BF), ((16, w_), F32)],
                [pltpu.VMEM((n, ff), BF), pltpu.VMEM((n, w_), BF)], 9 << 30,
                dmem, r, g, gp, e1, win, wout, small)


def dec_ffn(h, res, cot, win, wout, small):
    n, w_ = h.shape
    ff = win.shape[-1]
    return call(dec_ffn_kernel, "decoder_ffn",
                [((n, w_), BF), ((n, w_), BF), ((2 * ff // w_, w_, w_), BF), ((16, w_), F32)],
                [pltpu.VMEM((n, ff), BF), pltpu.VMEM((TB, ff), BF), pltpu.VMEM((n, ff), BF), pltpu.VMEM((n, w_), BF)], 13 << 30,
                h, res, cot, win, wout, small)


CHUNK = 512
MESH = pl.DeviceIdType.MESH
ANY = pl.BlockSpec(memory_space=pl.ANY)


def bit_of(index, bit):
    return (index // 2**bit) % 2


def partner_of(index, bit):
    return index + 2**bit - 2 * 2**bit * bit_of(index, bit)


def greet(partners):
    barrier = pltpu.get_barrier_semaphore()
    for device in partners:
        pl.semaphore_signal(barrier, inc=1, device_id=device, device_id_type=MESH)
    pl.semaphore_wait(barrier, len(partners))


def halvings(devices, rows):
    bits = devices.bit_length() - 1
    halved = 0
    while halved < bits and (rows >> (halved + 1)) >= 16 and (rows >> (halved + 1)) % 16 == 0:
        halved += 1
    return list(range(halved)), list(range(halved, bits))


def place(index, count, rows):
    at, size = 0, rows
    for bit in range(count):
        size //= 2
        at = at + bit_of(index, bit) * size
    return at, size


def sum_kernel(devices, kinds, *refs):
    n_in = len(kinds)
    ins, small_ref = refs[:n_in], refs[n_in]
    out_ref, small_out = refs[n_in + 1 : n_in + 3]
    scratch = refs[n_in + 3 :]
    held, gathered, load_sem, out_sem, send_sem, recv_sem = scratch[:6]
    small, small_in, ssend, srecv = scratch[6:10]
    landing = scratch[10:]
    chunks = held.shape[0]
    index = lax.axis_index("dp")
    section = lax.axis_index("section")
    halved, rest = halvings(devices, CHUNK)
    all_bits = halved + rest
    across = (1 - section, index)
    mates = [(section, partner_of(index, bit)) for bit in all_bits]
    greet([across] + mates)

    def loads(c, go):
        at = 0
        for pair, count in zip(range(0, n_in, 2), [k for k in kinds[::2]]):
            @pl.when((c >= at) & (c < at + count))
            def _(pair=pair, at=at):
                for k in range(2):
                    layer = k if pair + 2 < n_in else section * k + (1 - section) * (1 - k)
                    copy = pltpu.make_async_copy(ins[pair + k].at[c - at], held.at[c, layer], load_sem.at[c, k])
                    copy.start() if go else copy.wait()
            at += count

    def remote(src, dst, slot, c, device):
        return pltpu.make_async_remote_copy(
            src_ref=src, dst_ref=dst, send_sem=send_sem.at[slot, c], recv_sem=recv_sem.at[slot, c],
            device_id=device, device_id_type=MESH)

    def copy_core(c):
        _, size = place(index, 1, CHUNK)
        other = (1 - bit_of(index, 0)) * size
        return remote(held.at[c, :, pl.ds(pl.multiple_of(other, 16), size)], landing[0].at[c], 0, c, mates[0])

    def copy_section(c):
        at, size = place(index, 1, CHUNK)
        return remote(held.at[c, 1 - section, pl.ds(pl.multiple_of(at, 16), size)], landing[1].at[c], 1, c, across)

    def copy_bit(bit):
        def make(c):
            if bit in halved:
                at, size = place(index, bit, CHUNK)
                size //= 2
                at = at + (1 - bit_of(index, bit)) * size
            else:
                at, size = place(index, len(halved), CHUNK)
            return remote(held.at[c, section, pl.ds(pl.multiple_of(at, 16), size)], landing[bit + 1].at[c], bit + 1, c, mates[bit])
        return make

    def copy_gather(bit, slot):
        def make(c):
            at, size = place(index, bit + 1, CHUNK)
            rows = pl.ds(pl.multiple_of(at, 16), size)
            return remote(gathered.at[c, rows], gathered.at[c, rows], slot, c, mates[bit])
        return make

    def add_core(c):
        at, size = place(index, 1, CHUNK)
        rows = pl.ds(pl.multiple_of(at, 16), size)
        for layer in range(2):
            held[c, layer, rows, :] = (held[c, layer, rows, :].astype(F32) + landing[0][c, layer].astype(F32)).astype(BF)

    def add_to(step, count, last):
        def add(c):
            at, size = place(index, count, CHUNK)
            rows = pl.ds(pl.multiple_of(at, 16), size)
            total = (held[c, section, rows, :].astype(F32) + landing[step][c].astype(F32)).astype(BF)
            if last:
                gathered[c, rows, :] = total
            else:
                held[c, section, rows, :] = total
        return add

    copies = [copy_core, copy_section] + [copy_bit(bit) for bit in all_bits[1:]]
    n_reduce = len(copies)
    adds = [add_core, add_to(1, 1, n_reduce == 2)]
    for bit in all_bits[1:]:
        adds.append(add_to(bit + 1, min(bit + 1, len(halved)), bit == all_bits[-1]))
    for bit in reversed(halved):
        copies.append(copy_gather(bit, len(copies)))
        adds.append(None)
    steps = len(copies)

    def out_copy(c):
        return pltpu.make_async_copy(gathered.at[c], out_ref.at[c], out_sem.at[c])

    small[...] = small_ref[...]
    small_steps = [across] + mates

    def small_copy(k):
        src = small.at[1 - section] if k == 0 else small.at[section]
        return pltpu.make_async_remote_copy(
            src_ref=src, dst_ref=small_in.at[k], send_sem=ssend.at[k], recv_sem=srecv.at[k],
            device_id=small_steps[k], device_id_type=MESH)

    @pl.loop(0, chunks)
    def _(c):
        loads(c, True)

    small_copy(0).start()

    @pl.loop(0, chunks + steps)
    def _(tick):
        for s in range(steps + 1):
            c = tick - s

            @pl.when((c >= 0) & (c < chunks))
            def _(s=s, c=c):
                if s == 0:
                    loads(c, False)
                else:
                    copies[s - 1](c).wait_recv()
                    if adds[s - 1] is not None:
                        adds[s - 1](c)
                if s < steps:
                    copies[s](c).start()
                else:
                    out_copy(c).start()

        for k in range(len(small_steps)):
            @pl.when(tick == k + 1)
            def _(k=k):
                small_copy(k).wait()
                small[section] = small[section] + small_in[k]
                if k + 1 < len(small_steps):
                    small_copy(k + 1).start()

    small_out[...] = small[section]

    @pl.loop(0, chunks)
    def _(c):
        for s in range(steps):
            copies[s](c).wait_send()
        out_copy(c).wait()


def sum_everywhere(groups, small, devices):
    kinds, ins = [], []
    for first, second in groups:
        kinds += [first.shape[0]] * 2
        ins += [first, second]
    chunks = sum(kinds[::2])
    halved, rest = halvings(devices, CHUNK)
    landing = [pltpu.VMEM((chunks, 2, CHUNK // 2, 512), BF), pltpu.VMEM((chunks, CHUNK // 2, 512), BF)]
    for bit in (halved + rest)[1:]:
        landing.append(pltpu.VMEM((chunks, CHUNK >> min(bit + 1, len(halved)), 512), BF))
    steps = 1 + len(halved + rest) + len(halved)
    n_small = 1 + len(halved + rest)
    vm = pl.BlockSpec(memory_space=pltpu.VMEM)
    return pl.pallas_call(
        functools.partial(sum_kernel, devices, kinds),
        out_shape=[jax.ShapeDtypeStruct((chunks, CHUNK, 512), BF), jax.ShapeDtypeStruct((16, 512), F32)],
        in_specs=[ANY] * len(ins) + [vm],
        out_specs=[ANY, vm],
        scratch_shapes=[
            pltpu.VMEM((chunks, 2, CHUNK, 512), BF),
            pltpu.VMEM((chunks, CHUNK, 512), BF),
            pltpu.SemaphoreType.DMA((chunks, 2)),
            pltpu.SemaphoreType.DMA((chunks,)),
            pltpu.SemaphoreType.DMA((steps, chunks)),
            pltpu.SemaphoreType.DMA((steps, chunks)),
            pltpu.VMEM((2, 16, 512), F32),
            pltpu.VMEM((n_small, 16, 512), F32),
            pltpu.SemaphoreType.DMA((n_small,)),
            pltpu.SemaphoreType.DMA((n_small,)),
        ] + landing,
        compiler_params=pltpu.CompilerParams(collective_id=1, has_side_effects=True, vmem_limit_bytes=VMEM_LIMIT),
        name="sum_gradients",
    )(*ins, small)


def unpack_kernel(kinds, g_ref, mem_ref, out_ref, low_far_ref, grad_ref, grad_far_ref, *refs):
    n = len(kinds)
    low_out, grad_out = refs[:2]
    outs = refs[2 : n + 2]
    stage, sem, low_buf, grad_buf, far_buf, row_in, row_out = refs[n + 2 :]
    step = pl.program_id(0)
    slot = step % 2
    section = lax.axis_index("section")
    fetch = [
        pltpu.make_async_copy(mem_ref, low_buf.at[0], row_in.at[0]),
        pltpu.make_async_copy(low_far_ref, low_buf.at[1], row_in.at[1]),
        pltpu.make_async_copy(grad_ref, grad_buf.at[0], row_in.at[2]),
        pltpu.make_async_copy(grad_far_ref, far_buf, row_in.at[3]),
    ]
    send = [
        pltpu.make_async_copy(low_buf.at[0], low_out.at[section], row_out.at[0]),
        pltpu.make_async_copy(low_buf.at[1], low_out.at[1 - section], row_out.at[1]),
        pltpu.make_async_copy(grad_buf.at[0], grad_out.at[section], row_out.at[2]),
        pltpu.make_async_copy(grad_buf.at[1], grad_out.at[1 - section], row_out.at[3]),
    ]

    @pl.when(step == 0)
    def _():
        for one in fetch[1:]:
            one.start()

        @pl.when(section == 0)
        def _():
            fetch[0].start()

        @pl.when(section != 0)
        def _():
            pltpu.make_async_copy(out_ref, low_buf.at[0], row_in.at[0]).start()

    for k in range(4):
        @pl.when(step == k + 2)
        def _(k=k):
            fetch[k].wait()
            if k == 3:
                grad_buf[1] = far_buf[...].astype(F32)
            send[k].start()

    def copy(kind, dest, k, c_slot):
        flipped, axis = kinds[kind][1:]
        at = pl.ds(pl.multiple_of(k * 512, 512), 512)
        dst = dest.at[:, at] if axis else dest.at[at, :]
        return pltpu.make_async_copy(stage.at[c_slot], dst, sem.at[c_slot])

    @pl.when(step >= 2)
    def _():
        copy(0, outs[0], 0, slot).wait()

    at = 0
    for kind, (count, flipped, axis) in enumerate(kinds):
        @pl.when((step >= at) & (step < at + count))
        def _(kind=kind, at=at, flipped=flipped):
            value = g_ref[0].astype(F32)
            stage[slot] = value.T if flipped else value
            copy(kind, outs[kind], step - at, slot).start()
        at += count

    @pl.when(step == pl.num_programs(0) - 1)
    def _():
        copy(0, outs[0], 0, 1 - slot).wait()
        copy(0, outs[0], 0, slot).wait()
        for one in send:
            one.wait()


def unpack(g, low, low_far, grad, grad_far, kinds, shapes):
    n, w = low_far.shape
    return pl.pallas_call(
        functools.partial(unpack_kernel, kinds),
        grid=(g.shape[0],),
        out_shape=[jax.ShapeDtypeStruct((2, n, w), BF), jax.ShapeDtypeStruct((2, n, w), F32)]
        + [jax.ShapeDtypeStruct(s, F32) for s in shapes],
        in_specs=[pl.BlockSpec((1, 512, 512), lambda i: (i, 0, 0))] + [ANY] * 5,
        out_specs=[ANY] * (len(shapes) + 2),
        scratch_shapes=[
            pltpu.VMEM((2, 512, 512), F32), pltpu.SemaphoreType.DMA((2,)),
            pltpu.VMEM((2, n, w), BF), pltpu.VMEM((2, n, w), F32), pltpu.VMEM((n, w), BF),
            pltpu.SemaphoreType.DMA((4,)), pltpu.SemaphoreType.DMA((4,)),
        ],
        compiler_params=pltpu.CompilerParams(vmem_limit_bytes=VMEM_LIMIT),
        name="unpack_results",
    )(g, *low, low_far, grad, grad_far)


def spread_kernel(devices, *refs):
    tokens, small = refs[0], refs[1]
    weights = refs[2:7]
    tokens_out, small_out = refs[7], refs[8]
    outs = refs[9:14]
    tok_send, tok_recv, send_sem, recv_sem = refs[14:18]
    index = lax.axis_index("dp")
    section = lax.axis_index("section")
    bits = halvings(devices, 512)[0]
    across = (1 - section, index)
    mates = [(section, partner_of(index, bit)) for bit in bits]
    chunks = []
    for w in range(5):
        rows, cols = weights[w].shape
        chunks += [(w, r, c) for r in range(0, rows, 512) for c in range(0, cols, 512)]
    steps = len(bits) + 1
    land, flush_sem = refs[18:]
    greet([across] + mates)

    def window(k, at, size, ref_of):
        w, r, c = chunks[k]
        return ref_of(w).at[pl.ds(pl.multiple_of(r + at, 16), size), c : c + 512]

    def landing(k, at, size):
        return land.at[k, pl.ds(pl.multiple_of(at, 16), size)]

    def copy(k, step):
        if step == 0:
            at, size = place(index, len(bits), 512)
            src, device = window(k, at, size, lambda w: weights[w]), across
        else:
            bit = bits[len(bits) - step]
            at, size = place(index, bit + 1, 512)
            src, device = landing(k, at, size), mates[bit]
        return pltpu.make_async_remote_copy(
            src_ref=src, dst_ref=landing(k, at, size), send_sem=send_sem.at[step, k], recv_sem=recv_sem.at[step, k],
            device_id=device, device_id_type=MESH)

    swaps = [
        pltpu.make_async_remote_copy(
            src_ref=src, dst_ref=dst, send_sem=tok_send.at[i], recv_sem=tok_recv.at[i],
            device_id=across, device_id_type=MESH)
        for i, (src, dst) in enumerate([(small, small_out), (tokens.at[1 - section], tokens_out)])
    ]
    count = len(chunks)

    def flush(k):
        w, r, c = chunks[k]
        return pltpu.make_async_copy(land.at[k], outs[w].at[r : r + 512, c : c + 512], flush_sem.at[k])

    for k in range(count):
        copy(k, 0).start()
    for one in swaps:
        one.start()
    for tick in range(count + steps):
        for step in range(1, steps + 1):
            k = tick - step + 1
            if 0 <= k < count:
                copy(k, step - 1).wait_recv()
                if step < steps:
                    copy(k, step).start()
                else:
                    flush(k).start()
    for k in range(count):
        for step in range(steps):
            copy(k, step).wait_send()
        flush(k).wait()
    for one in swaps:
        one.wait()


def spread(tokens, small, weights, devices):
    steps = len(halvings(devices, 512)[0]) + 1
    count = sum(w.size for w in weights) // 512**2
    return pl.pallas_call(
        functools.partial(spread_kernel, devices),
        out_shape=[jax.ShapeDtypeStruct(tokens.shape[1:], BF), jax.ShapeDtypeStruct(small.shape, F32)]
        + [jax.ShapeDtypeStruct(w.shape, BF) for w in weights],
        in_specs=[ANY] * 7,
        out_specs=[ANY] * 7,
        scratch_shapes=[
            pltpu.SemaphoreType.DMA((2,)),
            pltpu.SemaphoreType.DMA((2,)),
            pltpu.SemaphoreType.DMA((steps, count)),
            pltpu.SemaphoreType.DMA((steps, count)),
            pltpu.VMEM((count, 512, 512), BF),
            pltpu.SemaphoreType.DMA((count,)),
        ],
        compiler_params=pltpu.CompilerParams(collective_id=0, has_side_effects=True, vmem_limit_bytes=VMEM_LIMIT),
        name="spread_weights",
    )(tokens, small, *weights)


def shards(layer_input, cotangent, src_segments, tgt_segments, attn_qkv, attn_out, cross_proj,
           ffn_in, ffn_in_bias, ffn_out, ffn_out_bias, norm_gain, norm_bias):
    devices = lax.axis_size("dp")
    sec = lax.axis_index("section")
    first = sec == 0
    swap = lambda a: lax.ppermute(a, "section", [(0, 1), (1, 0)])
    width = attn_out.shape[-1]
    vectors = jnp.concatenate(
        [ffn_in_bias.reshape(-1, width), ffn_out_bias, norm_gain[0], norm_bias[0], jnp.zeros((5, width), F32)])
    tokens = layer_input[0, :, 0]
    near = (attn_qkv[0], attn_out[0], cross_proj[0], ffn_in[0], ffn_out[0])
    far_tokens, far_vectors, *far = spread(tokens, vectors, near, devices)
    enc = [Pick(a, b) for a, b in zip(near, far)]
    dec = [Pick(b, a) for a, b in zip(near, far)]
    enc_small, dec_small = Pick(vectors, far_vectors), Pick(far_vectors, vectors)
    src, tgt, cot = Row(src_segments), Row(tgt_segments), Row(cotangent[:, 0])
    own_ids, far_ids, src, tgt, cot = Pick(src, tgt), Pick(tgt, src), Pick(src), Pick(tgt), Pick(cot)
    own_tokens = Pick(Row(tokens))

    *own_saved, own_hid = self_fwd(True, own_tokens, own_ids, near[0], near[1], vectors)
    *far_saved, far_hid = self_fwd(False, far_tokens, far_ids, far[0], far[1], far_vectors)
    e1, d1 = Pick(own_hid, far_hid), Pick(far_hid, own_hid)
    g, gp, r2, mem, kv = enc_ffn_fwd(e1, enc[3], enc[4], enc_small, enc[2])
    cq, catt, clse, cr, d2 = cross_fwd(d1, kv, tgt, src, dec[2], dec_small)
    out, dres, dw_dffn, s_dffn = dec_ffn(d2, cr, cot, dec[3], dec[4], dec_small)
    low_far = swap(jnp.where(first, out, mem))
    dh1, dmem, dw_dcross, dw_ecross = cross_bwd(dres, d1, mem, tgt, src, cq, kv, catt, clse, dec[2], enc[2])
    de1, dw_effn, s_effn = enc_ffn_bwd(dmem, r2, g, gp, e1, enc[3], enc[4], enc_small)
    de1, low_far = lax.optimization_barrier((de1, low_far))

    def backward(own, dh, saved, tokens, ids, weights, small):
        qT, k, v, att, lse, res = saved
        return self_bwd(own, dh, res, tokens, ids, qT, k, v, att, lse, weights[0], weights[1], small)

    far_grad, dw_far, s_far = backward(False, Pick(dh1, de1), far_saved, far_tokens, far_ids, far, far_vectors)
    far_grad = swap(far_grad)
    own_grad, dw_own, s_own = backward(True, Pick(de1, dh1), own_saved, own_tokens, own_ids, near, vectors)
    groups = [(dw_effn, dw_dffn), (dw_ecross, dw_dcross), (dw_far, dw_own)]
    dsmall = jnp.stack([s_effn + jnp.where(first, s_own, s_far), s_dffn + jnp.where(first, s_far, s_own)])
    sums, s = sum_everywhere(groups, dsmall, devices)
    kinds = ((4, False, 1), (4, True, 0), (2, True, 1), (3, True, 1), (1, False, 0))
    layer_output, input_grad, win, wout, cross, qkv, wo = unpack(
        sums, (mem, out), low_far, own_grad, far_grad, kinds,
        [ffn_in.shape[1:], ffn_out.shape[1:], cross_proj.shape[1:], attn_qkv.shape[1:], attn_out.shape[1:]])
    return (layer_output[None, :, None], input_grad[None, :, None], qkv[None], wo[None], cross[None], win[None],
            s[0:4].reshape(1, -1), wout[None], s[4:5], s[5:8][None], s[8:11][None])


def solution(mesh):
    return jax.shard_map(
        shards,
        mesh=mesh,
        in_specs=(
            P("section", None, "dp", None, None),
            P(None, "dp", None, None),
            P(None, "dp", None),
            P(None, "dp", None),
            P("section", None, None),
            P("section", None, None),
            P("section", None, None),
            P("section", None, None),
            P("section", None),
            P("section", None, None),
            P("section", None),
            P("section", None, None),
            P("section", None, None),
        ),
        out_specs=(
            P("section", None, "dp", None, None),
            P("section", None, "dp", None, None),
            P("section", None, None),
            P("section", None, None),
            P("section", None, None),
            P("section", None, None),
            P("section", None),
            P("section", None, None),
            P("section", None),
            P("section", None, None),
            P("section", None, None),
        ),
        check_vma=False,
    )
```

```python
import functools
import math

import jax
import jax.numpy as jnp
from jax import lax
from jax.experimental import pallas as pl
from jax.experimental.pallas import tpu as pltpu
from jax.sharding import PartitionSpec as P

HEADS = 8
EPSILON = 1e-05
NEGATIVE = -1000000000.0
BF = jnp.bfloat16
F32 = jnp.float32
LOG2E = 1.4426950408889634
QB = 256
UNIT = 128
WIDE = 256
TB = 256
VMEM_LIMIT = 60 * 1024 * 1024


def dot(left, right, lc=1, rc=0):
    return lax.dot_general(
        left, right, (((lc,), (rc,)), ((), ())), preferred_element_type=F32
    )


def norm_stats(value):
    centered = value - jnp.mean(value, axis=-1, keepdims=True)
    spread = jnp.mean(centered * centered, axis=-1, keepdims=True)
    scale = lax.rsqrt(spread + EPSILON)
    return centered * scale, scale


def norm_back(out_grad, unit, scale, gain):
    gain_grad = jnp.sum(out_grad * unit, axis=0, keepdims=True)
    shift_grad = jnp.sum(out_grad, axis=0, keepdims=True)
    inner = out_grad * gain
    mean_one = jnp.mean(inner, axis=-1, keepdims=True)
    mean_two = jnp.mean(inner * unit, axis=-1, keepdims=True)
    return scale * (inner - mean_one - unit * mean_two), gain_grad, shift_grad


def gelu_pair(u):
    phi = 0.5 + 0.5 * lax.erf(u * (1.0 / math.sqrt(2.0)))
    bell = jnp.exp(-0.5 * u * u) * (1.0 / math.sqrt(2.0 * math.pi))
    return u * phi, phi + u * bell


def gain_of(small, norm):
    return small[5 + norm : 6 + norm, :]


def shift_of(small, norm):
    return small[8 + norm : 9 + norm, :]


def key_codes(ids_row, length):
    column = jnp.broadcast_to(ids_row.astype(F32), (128, length)).T
    lane = lax.broadcasted_iota(jnp.int32, (length, 128), 1)
    spot = jnp.where(lane < 64, lane, lane - 64)
    codes = jnp.where(
        spot < 4,
        jnp.where(column == spot.astype(F32), 0.0, NEGATIVE),
        jnp.where(spot < 7, -1.0, 0.0),
    )
    return codes, lane < 64


def fill_keys(dst, keys_ref, codes, low_half):
    for pair in range(HEADS // 2):
        slab = keys_ref[:, pair * 128 : pair * 128 + 128].astype(F32)
        dst[2 * pair] = jnp.where(low_half, slab, codes).astype(BF)
        dst[2 * pair + 1] = jnp.where(low_half, codes, slab).astype(BF)


def query_rows(head):
    return (0, 64) if head % 2 == 0 else (64, 0)


def key_range(query_ids, key_ids, qb):
    ids = query_ids[:, pl.ds(pl.multiple_of(qb * QB, QB), QB)].astype(F32)
    keys = key_ids[...].astype(F32)
    start = jnp.sum((keys < jnp.min(ids)).astype(F32)).astype(jnp.int32)
    stop = jnp.sum((keys <= jnp.max(ids)).astype(F32)).astype(jnp.int32)
    return start // UNIT, (stop + UNIT - 1) // UNIT


def visit_keys(query_ids, key_ids, qb, step):
    lo, hi = key_range(query_ids, key_ids, qb)
    count = hi - lo

    @pl.loop(0, count // 2)
    def _(i):
        step(lo + 2 * i, WIDE, False)

    @pl.when(count % 2 == 1)
    def _():
        step(hi - 1, UNIT, False)


def below_diagonal():
    return lax.broadcasted_iota(jnp.int32, (WIDE, QB), 0) <= lax.broadcasted_iota(jnp.int32, (WIDE, QB), 1)


def staged(first, lag_one, second, lag_two, third):
    for i in range(HEADS + lag_one + lag_two):
        if i < HEADS:
            first(i)
        if 0 <= i - lag_one < HEADS:
            second(i - lag_one)
        if 0 <= i - lag_one - lag_two < HEADS:
            third(i - lag_one - lag_two)


def attend_loop(visit, after, qaug, kaug, vt, attT_ref, lse_ref, oacc, mrow, lrow, sbuf, pbuf, length):
    @pl.loop(0, length // QB)
    def _(qb):
        q = pl.ds(pl.multiple_of(qb * QB, QB), QB)
        oacc[...] = jnp.zeros_like(oacc)
        mrow[...] = jnp.full_like(mrow, -3e38)
        lrow[...] = jnp.zeros_like(lrow)

        def step(unit, size, masked):
            ks = pl.ds(pl.multiple_of(unit * UNIT, UNIT), size)
            scale = {}

            def scores(h):
                s = dot(kaug[h, ks, :], qaug[h, :, q])
                sbuf[h, :size] = jnp.where(below_diagonal(), s, NEGATIVE) if masked else s

            def softmax(h):
                s = sbuf[h, :size]
                m_old = mrow[h : h + 1, :]
                m_new = jnp.maximum(m_old, jnp.max(s, axis=0, keepdims=True))
                scale[h] = jnp.exp2(m_old - m_new)
                p = jnp.exp2(s - m_new)
                lrow[h : h + 1, :] = lrow[h : h + 1, :] * scale[h] + jnp.sum(p, axis=0, keepdims=True)
                mrow[h : h + 1, :] = m_new
                pbuf[h, :size] = p.astype(BF)

            def mix(h):
                hs = slice(h * 64, h * 64 + 64)
                oacc[hs, :] = oacc[hs, :] * scale[h] + dot(vt[hs, ks], pbuf[h, :size])

            staged(scores, 7, softmax, 1, mix)

        visit(qb, step)
        for h in range(HEADS):
            hs = slice(h * 64, h * 64 + 64)
            attT_ref[hs, q] = (oacc[hs, :] * (1.0 / lrow[h : h + 1, :])).astype(BF)
        lse_ref[:, q] = mrow[...] + jnp.log2(lrow[...])
        after(qb)


def query_codes(ids_row, length):
    row = lax.broadcasted_iota(jnp.int32, (16, length), 0)
    return jnp.where(row == jnp.broadcast_to(ids_row, (16, length)), 1.0, 0.0), row


def fill_queries(qaug, qT_ref, codes, row, lse_ref, length):
    for h in range(HEADS):
        a, b = query_rows(h)
        qaug[h, a : a + 64, :] = qT_ref[h * 64 : h * 64 + 64, :]
        extra = codes
        if lse_ref is not None:
            lse = lse_ref[h : h + 1, :]
            hi = lse.astype(BF).astype(F32)
            mid = (lse - hi).astype(BF).astype(F32)
            low = lse - hi - mid
            extra = jnp.where(row == 4, hi, jnp.where(row == 5, mid, jnp.where(row == 6, low, codes)))
        qaug[h, b : b + 16, :] = extra.astype(BF)
        qaug[h, b + 16 : b + 64, :] = jnp.zeros((48, length), BF)


def project_queries(src_ref, w_ref, qT_ref, length, width):
    @pl.loop(0, length // TB)
    def _(t):
        rows = pl.ds(pl.multiple_of(t * TB, TB), TB)
        q = dot(src_ref[rows, :], w_ref[:, :width]) * (0.125 * LOG2E)
        qT_ref[:, rows] = q.T.astype(BF)


def out_and_norm(attT_ref, w_ref, resid_ref, sm_ref, norm, res_ref, hid_ref, length):
    @pl.loop(0, length // TB)
    def _(t):
        rows = pl.ds(pl.multiple_of(t * TB, TB), TB)
        a = dot(attT_ref[:, rows], w_ref[...], 0, 0)
        r = resid_ref[rows, :].astype(F32) + a
        res_ref[rows, :] = r.astype(BF)
        unit, _ = norm_stats(r)
        hid_ref[rows, :] = (unit * gain_of(sm_ref, norm) + shift_of(sm_ref, norm)).astype(BF)


def self_forward(causal, x_ref, ids_ref, weights, small_ref, results, tick,
                 kaug, qaug, vt, oacc, mrow, lrow, sbuf, pbuf):
    wq, wk, wv, wout = weights
    qT_ref, k_ref, v_ref, attT_ref, lse_ref, res_ref, hid_ref = results
    length, width = x_ref.shape
    tick(0)

    @pl.loop(0, length // TB)
    def _(t):
        rows = pl.ds(pl.multiple_of(t * TB, TB), TB)
        x = x_ref[rows, :]
        q = dot(x, wq[...]) * (0.125 * LOG2E)
        k = dot(x, wk[...])
        v = dot(x, wv[...])
        qT_ref[:, rows] = q.T.astype(BF)
        k_ref[rows, :] = k.astype(BF)
        v_ref[rows, :] = v.astype(BF)
        vt[:, rows] = v.T.astype(BF)

    for result in (qT_ref, k_ref, v_ref):
        result.flush()
    tick(1)
    codes, low_half = key_codes(ids_ref[...], length)
    fill_keys(kaug, k_ref, codes, low_half)
    qcodes, row = query_codes(ids_ref[...], length)
    fill_queries(qaug, qT_ref, qcodes, row, None, length)
    tick(2)
    attend_loop(functools.partial(visit_all, causal), lambda qb: tick(3 + qb), qaug, kaug, vt, attT_ref, lse_ref,
                oacc, mrow, lrow, sbuf, pbuf, length)
    attT_ref.flush()
    lse_ref.flush()
    tick(7)
    out_and_norm(attT_ref, wout, x_ref, small_ref, 0, res_ref, hid_ref, length)
    res_ref.flush()
    hid_ref.flush()


def cross_fwd_kernel(h_ref, kv_ref, qids_ref, kids_ref, w_ref, ln_ref,
                     qT_ref, attT_ref, lse_ref, res_ref, hid_ref,
                     kaug, qaug, vt, oacc, mrow, lrow, sbuf, pbuf):
    h_ref, w_ref = ready(h_ref, w_ref)
    length, width = h_ref.shape
    project_queries(h_ref, w_ref, qT_ref, length, width)
    qT_ref.flush()
    kv_ref, qids_ref, kids_ref = ready(kv_ref, qids_ref, kids_ref)

    @pl.loop(0, length // TB)
    def _(t):
        rows = pl.ds(pl.multiple_of(t * TB, TB), TB)
        vt[:, rows] = kv_ref[rows, width:].astype(F32).T.astype(BF)

    codes, low_half = key_codes(kids_ref[...], length)
    fill_keys(kaug, kv_ref, codes, low_half)
    qcodes, row = query_codes(qids_ref[...], length)
    fill_queries(qaug, qT_ref, qcodes, row, None, length)
    attend_loop(functools.partial(visit_keys, qids_ref, kids_ref), lambda qb: None, qaug, kaug, vt, attT_ref, lse_ref,
                oacc, mrow, lrow, sbuf, pbuf, length)
    attT_ref.flush()
    lse_ref.flush()
    (ln_ref,) = ready(ln_ref)
    out_and_norm(attT_ref, w_ref.at[:, width:], h_ref, ln_ref, 1, res_ref, hid_ref, length)


def visit_all(causal, qb, step):
    blocks = 1024 // WIDE
    lo = jnp.where(qb == blocks - 1, 1, 0)
    hi = jnp.where(qb == 0, blocks - 1, blocks)
    if causal is not False:
        lo, hi = jnp.where(causal, 0, lo), jnp.where(causal, qb, hi)

    @pl.loop(lo, hi)
    def _(i):
        step(i * (WIDE // UNIT), WIDE, False)

    if causal is not False:
        @pl.when(causal)
        def _():
            step(qb * (QB // UNIT), WIDE, True)


def attend_back_loop(visit, after, qaug, kaug, kt, vaug, doaug, jgT, jg, dqacc, sbuf, dbuf, pbuf, gbuf, length):
    width = HEADS * 64
    jgT[...] = jnp.zeros_like(jgT)

    @pl.loop(0, length // QB)
    def _(qb):
        q = pl.ds(pl.multiple_of(qb * QB, QB), QB)
        dqacc[...] = jnp.zeros_like(dqacc)

        def step(unit, size, masked):
            ks = pl.ds(pl.multiple_of(unit * UNIT, UNIT), size)

            def products(h):
                s = dot(kaug[h, ks, :], qaug[h, :, q])
                sbuf[h % 4, :size] = jnp.where(below_diagonal(), s, NEGATIVE) if masked else s
                dbuf[h % 4, :size] = dot(vaug[h, ks, :], doaug[h, :, q])

            def grads(h):
                p = jnp.exp2(sbuf[h % 4, :size])
                pbuf[h % 4, :size] = p.astype(BF)
                gbuf[h % 4, :size] = (p * dbuf[h % 4, :size]).astype(BF)

            def add(h):
                a, _ = query_rows(h)
                at = h * 64
                hs = slice(at, at + 64)
                dqacc[hs, :] += dot(kt[hs, ks], gbuf[h % 4, :size])
                jgT[width + at : width + at + 64, ks] += dot(doaug[h, a : a + 64, q], pbuf[h % 4, :size], 1, 1)
                jgT[at : at + 64, ks] += dot(qaug[h, a : a + 64, q], gbuf[h % 4, :size], 1, 1)

            lag = 1 if size == WIDE else 2
            staged(products, lag, grads, lag, add)

        visit(qb, step)
        jg[:width, q] = (dqacc[...] * 0.125).astype(BF)
        after(qb)

    jg[width : 2 * width, :] = (jgT[:width, :] * math.log(2.0)).astype(BF)
    jg[2 * width :, :] = jgT[width:, :].astype(BF)


def prepare_back(dr_ref, w_ref, attT_ref, doaug, length):
    @pl.loop(0, length // TB)
    def _(t):
        rows = pl.ds(pl.multiple_of(t * TB, TB), TB)
        row = lax.broadcasted_iota(jnp.int32, (16, TB), 0)
        d = dot(w_ref[...], dr_ref[rows, :], 1, 1).astype(BF)
        for h in range(HEADS):
            a, b = query_rows(h)
            hs = slice(h * 64, h * 64 + 64)
            doh = d[hs, :]
            doaug[h, a : a + 64, rows] = doh
            delta = jnp.sum(doh.astype(F32) * attT_ref[hs, rows].astype(F32), axis=0, keepdims=True)
            hi = delta.astype(BF).astype(F32)
            mid = (delta - hi).astype(BF).astype(F32)
            low = delta - hi - mid
            extra = jnp.where(row == 4, hi, jnp.where(row == 5, mid, jnp.where(row == 6, low, 0.0)))
            doaug[h, b : b + 16, rows] = extra.astype(BF)
            doaug[h, b + 16 : b + 64, rows] = jnp.zeros((48, TB), BF)


def prepare_keys(keys_ref, values_ref, codes, low_half, kaug, kt, vaug, length):
    fill_keys(kaug, keys_ref, codes, low_half)
    fill_keys(vaug, values_ref, jnp.where(codes == NEGATIVE, 0.0, codes), low_half)

    @pl.loop(0, length // TB)
    def _(t):
        rows = pl.ds(pl.multiple_of(t * TB, TB), TB)
        kt[:, rows] = keys_ref[rows, :].astype(F32).T.astype(BF)


def self_backward(causal, operands, tick, middle, reuse, put_dx, dw_ref, dln_ref,
                  kaug, kt, vaug, qaug, doaug, dqacc, jgT, jg, sbuf, dbuf, pbuf, gbuf):
    dh, res, x, ids, qT, keys, values, attT, lse, w, wout, small = operands
    tick(0)
    dh_ref, res_ref, ln_ref = ready(dh, res, small)
    length, width = res_ref.shape
    dln_ref[...] = jnp.zeros(dln_ref.shape, F32)
    dr = res_ref

    @pl.loop(0, length // TB)
    def _(t):
        rows = pl.ds(pl.multiple_of(t * TB, TB), TB)
        unit, scale = norm_stats(res_ref[rows, :].astype(F32))
        d, gg, sg = norm_back(dh_ref[rows, :].astype(F32), unit, scale, gain_of(ln_ref, 0))
        dln_ref[5:6, :] += gg
        dln_ref[8:9, :] += sg
        dr[rows, :] = d.astype(BF)

    attT_ref, wout_ref, ids_ref = ready(attT, wout, ids)
    dw_ref[3] = dot(attT_ref[...], dr[...]).astype(BF)
    prepare_back(dr, wout_ref, attT_ref, doaug, length)
    tick(1)
    codes, low_half = key_codes(ids_ref[...], length)
    k_ref, v_ref, qT_ref, lse_ref = ready(keys, values, qT, lse)
    prepare_keys(k_ref, v_ref, codes, low_half, kaug, kt, vaug, length)
    qcodes, row = query_codes(ids_ref[...], length)
    fill_queries(qaug, qT_ref, qcodes, row, lse_ref, length)
    tick(2)

    def after(qb):
        for k, block in ((3, middle), (4, length // QB - 1)):
            @pl.when(qb == block)
            def _(k=k):
                tick(k)

    attend_back_loop(functools.partial(visit_all, causal), after, qaug, kaug, kt, vaug, doaug,
                     jgT, jg, dqacc, sbuf, dbuf, pbuf, gbuf, length)
    reuse(dh, ids, qT, keys, values, attT, lse, wout, small)
    x_ref, w_ref = ready(x, w)

    @pl.loop(0, 3)
    def _(t):
        rows = pl.ds(pl.multiple_of(t * 512, 512), 512)
        dw_ref[t] = dot(jg[rows, :], x_ref[...]).astype(BF)

    tick(5)

    @pl.loop(0, length // TB)
    def _(t):
        rows = pl.ds(pl.multiple_of(t * TB, TB), TB)
        put_dx(rows, dr[rows, :].astype(F32) + dot(jg[:, rows], w_ref[...], 0, 1))

    reuse(res, x, w)


def cross_bwd_kernel(dr_ref, h_ref, mem_ref, qids_ref, kids_ref, qT_ref, kv_ref, attT_ref,
                     lse_ref, w_ref, wkv_ref,
                     dh_ref, dmem_ref, dwd_ref, dwe_ref,
                     kaug, kt, vaug, qaug, doaug, dqacc, jgT, jg, sbuf, dbuf, pbuf, gbuf):
    dr_ref, attT_ref, w_ref, qids_ref, kids_ref = ready(dr_ref, attT_ref, w_ref, qids_ref, kids_ref)
    length, width = dr_ref.shape
    dwd_ref[1] = dot(dr_ref[...], attT_ref[...], 0, 1).astype(BF)
    prepare_back(dr_ref, w_ref.at[:, width:], attT_ref, doaug, length)
    codes, low_half = key_codes(kids_ref[...], length)
    kv_ref, qT_ref, lse_ref = ready(kv_ref, qT_ref, lse_ref)
    prepare_keys(kv_ref.at[:, :width], kv_ref.at[:, width:], codes, low_half, kaug, kt, vaug, length)
    qcodes, row = query_codes(qids_ref[...], length)
    fill_queries(qaug, qT_ref, qcodes, row, lse_ref, length)
    attend_back_loop(functools.partial(visit_keys, qids_ref, kids_ref), lambda qb: None, qaug, kaug, kt, vaug,
                     doaug, jgT, jg, dqacc, sbuf, dbuf, pbuf, gbuf, length)
    h_ref, mem_ref, wkv_ref = ready(h_ref, mem_ref, wkv_ref)
    dwd_ref[0] = dot(jg[:width, :], h_ref[...]).astype(BF)
    for half in range(2):
        dwe_ref[half] = dot(jg[(half + 1) * width : (half + 2) * width, :], mem_ref[...]).astype(BF)
    dwd_ref.flush()
    dwe_ref.flush()

    @pl.loop(0, length // TB)
    def _(t):
        rows = pl.ds(pl.multiple_of(t * TB, TB), TB)
        d = dot(jg[:width, rows], w_ref[:, :width], 0, 1)
        dh_ref[rows, :] = (dr_ref[rows, :].astype(F32) + d).astype(BF)
        dmem_ref[rows, :] = dot(jg[width:, rows], wkv_ref[...], 0, 1).astype(BF)


def enc_ffn_fwd_kernel(e1_ref, win_ref, wout_ref, ln_ref, wkv_ref,
                       g_ref, gp_ref, r_ref, mem_ref, kv_ref):
    e1_ref, win_ref, wout_ref, ln_ref, wkv_ref = ready(e1_ref, win_ref, wout_ref, ln_ref, wkv_ref)
    length, width = e1_ref.shape
    ff = win_ref.shape[1]

    @pl.loop(0, length // TB)
    def _(t):
        rows = pl.ds(pl.multiple_of(t * TB, TB), TB)
        e1 = e1_ref[rows, :]
        total = e1.astype(F32) + ln_ref[4:5, :]
        for j in range(0, ff, 512):
            u = dot(e1, win_ref[:, j : j + 512]) + ln_ref[j // 512 : j // 512 + 1, :]
            g, gp = gelu_pair(u)
            gb = g.astype(BF)
            g_ref[rows, j : j + 512] = gb
            gp_ref[rows, j : j + 512] = gp.astype(BF)
            total += dot(gb, wout_ref[j : j + 512, :])
        r_ref[rows, :] = total.astype(BF)
        unit, _ = norm_stats(total)
        e2 = unit * gain_of(ln_ref, 1) + shift_of(ln_ref, 1)
        unit, _ = norm_stats(e2)
        mem = (unit * gain_of(ln_ref, 2) + shift_of(ln_ref, 2)).astype(BF)
        mem_ref[rows, :] = mem
        kv_ref[rows, :] = dot(mem, wkv_ref[...]).astype(BF)


def weight_grads(act_ref, du_ref, df_ref, g_ref, dw_ref):
    slabs = du_ref.shape[1] // 512

    @pl.loop(0, slabs)
    def _(t):
        cols = pl.ds(pl.multiple_of(t * 512, 512), 512)
        dw_ref[t] = dot(act_ref[...], du_ref[:, cols], 0, 0).astype(BF)
        dw_ref[slabs + t] = dot(df_ref[...], g_ref[:, cols], 0, 0).astype(BF)


def enc_ffn_bwd_kernel(dmem_ref, r_ref, g_ref, gp_ref, e1_ref, win_ref, wout_ref, ln_ref,
                       de1_ref, dw_ref, dln_ref,
                       du_ref, df_ref):
    dmem_ref, r_ref, ln_ref, wout_ref, gp_ref, win_ref = ready(dmem_ref, r_ref, ln_ref, wout_ref, gp_ref, win_ref)
    length, width = r_ref.shape
    ff = win_ref.shape[1]
    dln_ref[...] = jnp.zeros(dln_ref.shape, F32)

    @pl.loop(0, length // TB)
    def _(t):
        rows = pl.ds(pl.multiple_of(t * TB, TB), TB)
        unit2, scale2 = norm_stats(r_ref[rows, :].astype(F32))
        e2 = unit2 * gain_of(ln_ref, 1) + shift_of(ln_ref, 1)
        unit3, scale3 = norm_stats(e2)
        de2, gg, sg = norm_back(dmem_ref[rows, :].astype(F32), unit3, scale3, gain_of(ln_ref, 2))
        dln_ref[7:8, :] += gg
        dln_ref[10:11, :] += sg
        dr, gg, sg = norm_back(de2, unit2, scale2, gain_of(ln_ref, 1))
        dln_ref[6:7, :] += gg
        dln_ref[9:10, :] += sg
        df = dr.astype(BF)
        df_ref[rows, :] = df
        dln_ref[4:5, :] += jnp.sum(df.astype(F32), axis=0, keepdims=True)
        total = dr
        for j in range(0, ff, 512):
            dg = dot(df, wout_ref[j : j + 512, :], 1, 1)
            du = dg * gp_ref[rows, j : j + 512].astype(F32)
            dub = du.astype(BF)
            du_ref[rows, j : j + 512] = dub
            dln_ref[j // 512 : j // 512 + 1, :] += jnp.sum(du, axis=0, keepdims=True)
            total += dot(dub, win_ref[:, j : j + 512], 1, 1)
        de1_ref[rows, :] = total.astype(BF)

    de1_ref.flush()
    e1_ref, g_ref = ready(e1_ref, g_ref)
    weight_grads(e1_ref, du_ref, df_ref, g_ref, dw_ref)


def dec_ffn_kernel(h_ref, res_ref, cot_ref, win_ref, wout_ref, ln_ref,
                   out_ref, dres_ref, dw_ref, dln_ref,
                   g_ref, gp_ref, du_ref, df_ref):
    h_ref, win_ref, ln_ref, wout_ref, cot_ref, res_ref = ready(h_ref, win_ref, ln_ref, wout_ref, cot_ref, res_ref)
    length, width = h_ref.shape
    ff = win_ref.shape[1]
    dln_ref[...] = jnp.zeros(dln_ref.shape, F32)

    @pl.loop(0, length // TB)
    def _(t):
        rows = pl.ds(pl.multiple_of(t * TB, TB), TB)
        h = h_ref[rows, :]
        total = h.astype(F32) + ln_ref[4:5, :]
        for j in range(0, ff, 512):
            u = dot(h, win_ref[:, j : j + 512]) + ln_ref[j // 512 : j // 512 + 1, :]
            g, gp = gelu_pair(u)
            gb = g.astype(BF)
            g_ref[rows, j : j + 512] = gb
            gp_ref[:, j : j + 512] = gp.astype(BF)
            total += dot(gb, wout_ref[j : j + 512, :])
        unit3, scale3 = norm_stats(total)
        out_ref[rows, :] = (unit3 * gain_of(ln_ref, 2) + shift_of(ln_ref, 2)).astype(BF)
        dr, gg, sg = norm_back(cot_ref[rows, :].astype(F32), unit3, scale3, gain_of(ln_ref, 2))
        dln_ref[7:8, :] += gg
        dln_ref[10:11, :] += sg
        df = dr.astype(BF)
        df_ref[rows, :] = df
        dln_ref[4:5, :] += jnp.sum(df.astype(F32), axis=0, keepdims=True)
        total = dr
        for j in range(0, ff, 512):
            dg = dot(df, wout_ref[j : j + 512, :], 1, 1)
            du = dg * gp_ref[:, j : j + 512].astype(F32)
            dub = du.astype(BF)
            du_ref[rows, j : j + 512] = dub
            dln_ref[j // 512 : j // 512 + 1, :] += jnp.sum(du, axis=0, keepdims=True)
            total += dot(dub, win_ref[:, j : j + 512], 1, 1)
        unit2, scale2 = norm_stats(res_ref[rows, :].astype(F32))
        d, gg, sg = norm_back(total, unit2, scale2, gain_of(ln_ref, 1))
        dln_ref[6:7, :] += gg
        dln_ref[9:10, :] += sg
        dres_ref[rows, :] = d.astype(BF)

    out_ref.flush()
    dres_ref.flush()
    weight_grads(h_ref, du_ref, df_ref, g_ref, dw_ref)


class Operand:
    def __init__(self, copy, ref):
        self.copy, self.ref = copy, ref


def ready(*operands):
    refs = []
    for operand in operands:
        if operand.copy is not None:
            operand.copy.wait()
            operand.copy = None
        refs.append(operand.ref)
    return refs


class Result:
    def __init__(self, copy, ref):
        self.copy, self.ref, self.started = copy, ref, False

    def __getitem__(self, at):
        return self.ref[at]

    def __setitem__(self, at, value):
        self.ref[at] = value

    def __getattr__(self, name):
        return getattr(self.ref, name)

    def flush(self):
        if not self.started:
            self.copy.start()
            self.started = True


class Row:
    def __init__(self, array):
        self.array, self.shape, self.dtype = array, array.shape[1:], array.dtype


class Pick:
    def __init__(self, zero, one=None):
        self.parts = [zero] if one is None else [zero, one]
        self.arrays = [p.array if isinstance(p, Row) else p for p in self.parts]
        self.shape, self.dtype = zero.shape, zero.dtype

    def copy(self, refs, dst, sem, section):
        sources = [ref.at[section] if isinstance(p, Row) else ref for p, ref in zip(self.parts, refs)]
        if len(sources) == 1:
            copy = pltpu.make_async_copy(sources[0], dst, sem)
            copy.start()
            return copy
        for k, source in enumerate(sources):
            @pl.when(section == k)
            def _(source=source):
                pltpu.make_async_copy(source, dst, sem).start()
        return pltpu.make_async_copy(sources[1], dst, sem)


def run_kernel(kernel, plan, n_out, *refs):
    n_in = sum(len(p.arrays) for p in plan)
    ins, outs = list(refs[:n_in]), refs[n_in : n_in + n_out]
    rest = refs[n_in + n_out :]
    in_bufs, out_bufs = rest[: len(plan)], rest[len(plan) : len(plan) + n_out]
    in_sem, out_sem = rest[len(plan) + n_out : len(plan) + n_out + 2]
    scratch = rest[len(plan) + n_out + 2 :]
    section = lax.axis_index("section")
    operands = []
    for k, entry in enumerate(plan):
        given = [ins.pop(0) for _ in entry.arrays]
        operands.append(Operand(entry.copy(given, in_bufs[k], in_sem.at[k], section), in_bufs[k]))
    results = [
        Result(pltpu.make_async_copy(out_bufs[k], outs[k], out_sem.at[k]), out_bufs[k]) for k in range(n_out)
    ]
    kernel(*operands, *results, *scratch)
    ready(*operands)
    for result in results:
        result.flush()
    for result in results:
        result.copy.wait()


def call(kernel, name, outs, scratch, flops, *args):
    any_space = pl.BlockSpec(memory_space=pl.ANY)
    plan = [a if isinstance(a, Pick) else Pick(a) for a in args]
    given = [array for entry in plan for array in entry.arrays]
    return pl.pallas_call(
        functools.partial(run_kernel, kernel, plan, len(outs)),
        out_shape=[jax.ShapeDtypeStruct(s, d) for s, d in outs],
        in_specs=[any_space] * len(given),
        out_specs=[any_space] * len(outs),
        scratch_shapes=[pltpu.VMEM(entry.shape, entry.dtype) for entry in plan]
        + [pltpu.VMEM(s, d) for s, d in outs]
        + [pltpu.SemaphoreType.DMA((len(plan),)), pltpu.SemaphoreType.DMA((len(outs),))]
        + scratch,
        compiler_params=pltpu.CompilerParams(vmem_limit_bytes=VMEM_LIMIT),
        cost_estimate=pl.CostEstimate(flops=flops, bytes_accessed=8 << 20, transcendentals=0),
        name=name,
    )(*given)


def fwd_scratch(n, w):
    return [
        pltpu.VMEM((HEADS, n, 128), BF),
        pltpu.VMEM((HEADS, 128, n), BF),
        pltpu.VMEM((w, n), BF),
        pltpu.VMEM((w, QB), F32),
        pltpu.VMEM((HEADS, QB), F32),
        pltpu.VMEM((HEADS, QB), F32),
        pltpu.VMEM((HEADS, WIDE, QB), F32),
        pltpu.VMEM((HEADS, WIDE, QB), BF),
    ]


def cross_fwd(h, kv, qids, kids, w, small):
    n, w_ = h.shape
    return call(cross_fwd_kernel, "cross_forward",
                [((w_, n), BF), ((w_, n), BF), ((HEADS, n), F32), ((n, w_), BF), ((n, w_), BF)],
                fwd_scratch(n, w_), 10 << 30, h, kv, qids, kids, w, small)


def bwd_scratch(n, w):
    return [
        pltpu.VMEM((HEADS, n, 128), BF),
        pltpu.VMEM((w, n), BF),
        pltpu.VMEM((HEADS, n, 128), BF),
        pltpu.VMEM((HEADS, 128, n), BF),
        pltpu.VMEM((HEADS, 128, n), BF),
        pltpu.VMEM((w, QB), F32),
        pltpu.VMEM((2 * w, n), F32),
        pltpu.VMEM((3 * w, n), BF),
        pltpu.VMEM((4, WIDE, QB), F32),
        pltpu.VMEM((4, WIDE, QB), F32),
        pltpu.VMEM((4, WIDE, QB), BF),
        pltpu.VMEM((4, WIDE, QB), BF),
    ]


def cross_bwd(dr, h, mem, qids, kids, qT, kv, attT, lse, w, wkv):
    n, w_ = h.shape
    return call(cross_bwd_kernel, "cross_backward",
                [((n, w_), BF), ((n, w_), BF), ((2, w_, w_), BF), ((2, w_, w_), BF)],
                bwd_scratch(n, w_), 25 << 30,
                dr, h, mem, qids, kids, qT, kv, attT, lse, w, wkv)


def enc_ffn_fwd(e1, win, wout, small, wkv):
    n, w_ = e1.shape
    ff = win.shape[-1]
    return call(enc_ffn_fwd_kernel, "encoder_ffn_forward",
                [((n, ff), BF), ((n, ff), BF), ((n, w_), BF), ((n, w_), BF), ((n, 2 * w_), BF)],
                [], 6 << 30, e1, win, wout, small, wkv)


def enc_ffn_bwd(dmem, r, g, gp, e1, win, wout, small):
    n, w_ = e1.shape
    ff = win.shape[-1]
    return call(enc_ffn_bwd_kernel, "encoder_ffn_backward",
                [((n, w_), BF), ((2 * ff // w_, w_, w_), BF), ((16, w_), F32)],
                [pltpu.VMEM((n, ff), BF), pltpu.VMEM((n, w_), BF)], 9 << 30,
                dmem, r, g, gp, e1, win, wout, small)


def dec_ffn(h, res, cot, win, wout, small):
    n, w_ = h.shape
    ff = win.shape[-1]
    return call(dec_ffn_kernel, "decoder_ffn",
                [((n, w_), BF), ((n, w_), BF), ((2 * ff // w_, w_, w_), BF), ((16, w_), F32)],
                [pltpu.VMEM((n, ff), BF), pltpu.VMEM((TB, ff), BF), pltpu.VMEM((n, ff), BF), pltpu.VMEM((n, w_), BF)], 13 << 30,
                h, res, cot, win, wout, small)


CHUNK = 512
SLOTS = 4
MESH = pl.DeviceIdType.MESH
ANY = pl.BlockSpec(memory_space=pl.ANY)


def bit_of(index, bit):
    return (index // 2**bit) % 2


def partner_of(index, bit):
    return index + 2**bit - 2 * 2**bit * bit_of(index, bit)


def greet(partners):
    barrier = pltpu.get_barrier_semaphore()
    for device in partners:
        pl.semaphore_signal(barrier, inc=1, device_id=device, device_id_type=MESH)
    pl.semaphore_wait(barrier, len(partners))


def halvings(devices, rows):
    bits = devices.bit_length() - 1
    halved = 0
    while halved < bits and (rows >> (halved + 1)) >= 16 and (rows >> (halved + 1)) % 16 == 0:
        halved += 1
    return list(range(halved)), list(range(halved, bits))


def place(index, count, rows):
    at, size = 0, rows
    for bit in range(count):
        size //= 2
        at = at + bit_of(index, bit) * size
    return at, size


class Sums:
    def __init__(self, devices, groups, early, gap, out_ref, scratch):
        self.groups, self.early, self.gap, self.out = groups, early, gap, out_ref
        self.held, self.shard, self.load_sem, self.store_sem, self.core_sem, self.send_sem, self.recv_sem = scratch[:7]
        self.landing = scratch[7:]
        self.index, self.section = lax.axis_index("dp"), lax.axis_index("section")
        self.halved, self.rest = halvings(devices, CHUNK)
        self.bits = self.halved + self.rest
        self.across = (1 - self.section, self.index)
        self.mates = [(self.section, partner_of(self.index, bit)) for bit in self.bits]
        self.chunks = sum(group[0] for group in groups)
        self.steps = 1 + len(self.bits) + len(self.halved)
        self.ticks = self.chunks + gap + self.steps

    def rows(self, count, other=False):
        at, size = 0, CHUNK
        for bit in range(count):
            size //= 2
            side = bit_of(self.index, bit)
            at = at + (1 - side if other and bit == count - 1 else side) * size
        return at, size

    def window(self, count, other=False):
        at, size = self.rows(count, other)
        return pl.ds(pl.multiple_of(at - self.rows(1)[0], 16), size)

    def remote(self, src, dst, step, c, device):
        return pltpu.make_async_remote_copy(
            src_ref=src, dst_ref=dst, send_sem=self.send_sem.at[step, c], recv_sem=self.recv_sem.at[step, c],
            device_id=device, device_id_type=MESH)

    def begin(self, c):
        at, size = self.rows(1)
        far, _ = self.rows(1, True)
        first = 0
        for count, *pair in self.groups:
            @pl.when((c >= first) & (c < first + count))
            def _(first=first, pair=pair):
                for k, (ref, layer) in enumerate(pair):
                    near = ref.at[c - first, pl.ds(pl.multiple_of(at, 16), size)]
                    away = ref.at[c - first, pl.ds(pl.multiple_of(far, 16), size)]
                    pltpu.make_async_copy(near, self.held.at[c, layer], self.load_sem.at[k, c]).start()
                    self.core_copy(k, c, away, layer).start()
            first += count

    def core_copy(self, k, c, src, layer):
        return pltpu.make_async_remote_copy(
            src_ref=src, dst_ref=self.landing[0].at[c % SLOTS, layer], send_sem=self.core_sem.at[0, k, c],
            recv_sem=self.core_sem.at[1, k, c], device_id=self.mates[0], device_id_type=MESH)

    def copy(self, step, c):
        reduce_steps = 1 + len(self.bits)
        if step == 1:
            return self.remote(self.held.at[c, 1 - self.section], self.landing[1].at[c % SLOTS], 1, c, self.across)
        if step < reduce_steps:
            bit = step - 1
            window = self.window(bit + 1, True) if bit in self.halved else self.window(len(self.halved))
            return self.remote(self.held.at[c, self.section, window], self.landing[step].at[c % SLOTS], step, c, self.mates[bit])
        bit = self.halved[-1 - (step - reduce_steps)]
        at, size = self.rows(bit + 1)
        rows = self.out.at[c, pl.ds(pl.multiple_of(at, 16), size)]
        return self.remote(self.shard.at[c] if step == reduce_steps else rows, rows, step, c, self.mates[bit])

    def store(self, c):
        at, size = self.rows(len(self.halved))
        return pltpu.make_async_copy(self.shard.at[c], self.out.at[c, pl.ds(pl.multiple_of(at, 16), size)], self.store_sem.at[c])

    def arrive(self, step, c):
        reduce_steps = 1 + len(self.bits)
        if step == 0:
            for k in range(2):
                pltpu.make_async_copy(self.landing[0].at[c % SLOTS, k], self.held.at[c, k], self.load_sem.at[k, c]).wait()
                self.core_copy(k, c, self.held.at[c, k], k).wait_recv()
            for k in range(2):
                self.held[c, k] = (self.held[c, k].astype(F32) + self.landing[0][c % SLOTS, k].astype(F32)).astype(BF)
            return
        copy = self.copy(step, c)
        copy.wait_recv()
        if step < reduce_steps:
            bit = step - 1
            if bit in self.rest:
                copy.wait_send()
            window = self.window(1) if step == 1 else self.window(min(bit + 1, len(self.halved)))
            total = (self.held[c, self.section, window, :].astype(F32) + self.landing[step][c % SLOTS].astype(F32)).astype(BF)
            if step == reduce_steps - 1:
                self.shard[c] = total
                self.store(c).start()
            else:
                self.held[c, self.section, window, :] = total
        elif step == reduce_steps:
            self.store(c).wait()

    def tick(self, t):
        for step in range(self.steps + 1):
            at = t - step
            late = at >= self.early + self.gap
            c = jnp.where(late, at - self.gap, at)

            @pl.when(((at >= 0) & (at < self.early)) | (late & (c < self.chunks)))
            def _(step=step, c=c):
                if step == 0:
                    self.begin(c)
                else:
                    self.arrive(step - 1, c)
                    if step < self.steps:
                        self.copy(step, c).start()

    def finish(self):
        @pl.loop(0, self.chunks)
        def _(c):
            for k in range(2):
                self.core_copy(k, c, self.held.at[c, k], k).wait_send()
            for step in range(1, self.steps):
                if step - 1 not in self.rest or step - 1 >= len(self.bits):
                    self.copy(step, c).wait_send()

    @staticmethod
    def scratch(devices, chunks):
        halved, rest = halvings(devices, CHUNK)
        steps = 1 + len(halved + rest) + len(halved)
        sizes = [CHUNK >> min(bit + 1, len(halved)) for bit in halved + rest]
        return [
            pltpu.VMEM((chunks, 2, CHUNK // 2, 512), BF),
            pltpu.VMEM((chunks, CHUNK >> len(halved), 512), BF),
            pltpu.SemaphoreType.DMA((2, chunks)),
            pltpu.SemaphoreType.DMA((chunks,)),
            pltpu.SemaphoreType.DMA((2, 2, chunks)),
            pltpu.SemaphoreType.DMA((steps, chunks)),
            pltpu.SemaphoreType.DMA((steps, chunks)),
            pltpu.VMEM((SLOTS, 2, CHUNK // 2, 512), BF),
            pltpu.VMEM((SLOTS, CHUNK // 2, 512), BF),
        ] + [pltpu.VMEM((SLOTS, size, 512), BF) for size in sizes[1:]]


class Vectors:
    def __init__(self, sums, scratch):
        self.small, self.arrived, self.send_sem, self.recv_sem = scratch
        self.section = sums.section
        self.partners = [sums.across] + sums.mates

    def copy(self, k):
        return pltpu.make_async_remote_copy(
            src_ref=self.small.at[1 - self.section if k == 0 else self.section], dst_ref=self.arrived.at[k],
            send_sem=self.send_sem.at[k], recv_sem=self.recv_sem.at[k],
            device_id=self.partners[k], device_id_type=MESH)

    def tick(self, t):
        for k in range(len(self.partners) + 1):
            @pl.when(t == k)
            def _(k=k):
                if k > 0:
                    self.copy(k - 1).wait()
                    self.small[self.section] = self.small[self.section] + self.arrived[k - 1]
                if k < len(self.partners):
                    self.copy(k).start()

    @staticmethod
    def scratch(devices):
        n = 1 + len(sum(halvings(devices, CHUNK), []))
        return [pltpu.VMEM((2, 16, 512), F32), pltpu.VMEM((n, 16, 512), F32),
                pltpu.SemaphoreType.DMA((n,)), pltpu.SemaphoreType.DMA((n,))]


def tail_kernel(devices, plans, n_sums, *refs):
    section = lax.axis_index("section")
    refs = list(refs)
    take = lambda n: [refs.pop(0) for _ in range(n)]
    given = [[take(len(entry.arrays)) for entry in plan] for plan in plans]
    ffn_enc, ffn_dec, cross_enc, cross_dec, vec_enc, vec_dec = take(6)
    far_arrived, own_grad, sums_out, small_out = take(4)
    buffers = take(len(plans[0]))
    in_sem, out_sem, dx_send, dx_recv, far_dx, own_dx = take(6)
    dw, dln = take(2)
    vectors_scratch = take(4)
    sums_scratch = take(n_sums)

    groups = [
        (ffn_enc.shape[0], (ffn_enc, 0), (ffn_dec, 1)),
        (cross_enc.shape[0], (cross_enc, 0), (cross_dec, 1)),
        (4, (dw.at[0], 0), (dw.at[1], 1)),
    ]
    early = groups[0][0] + groups[1][0]
    sums = Sums(devices, groups, early, 0, sums_out, sums_scratch)
    vectors = Vectors(sums, vectors_scratch)
    greet([sums.across] + sums.mates)

    def fetch(layer, k):
        return Operand(plans[layer][k].copy(given[layer][k], buffers[k], in_sem.at[layer, k], section), buffers[k])

    second = [fetch(1, k) for k in range(len(buffers))]
    first = [None] * len(buffers)

    def reuse(*operands):
        for operand in operands:
            k = second.index(operand)
            first[k] = fetch(0, k)

    def put_dx(layer):
        def put(rows, value):
            @pl.when(section == layer)
            def _():
                own_dx[rows, :] = value

            @pl.when(section != layer)
            def _():
                far_dx[rows, :] = value.astype(BF)
        return put

    def ticks(base, without):
        return lambda k: None if k in without else sums.tick(base + k)

    self_backward(True, second, ticks(0, (5,)), 2, reuse, put_dx(1), dw.at[1], dln.at[1], *refs)
    self_backward(False, first, ticks(5, ()), 1, lambda *operands: None, put_dx(0), dw.at[0], dln.at[0], *refs)
    result = pltpu.make_async_copy(own_dx, own_grad, out_sem)
    result.start()
    vectors.small[0] = vec_enc[...] + dln[0]
    vectors.small[1] = vec_dec[...] + dln[1]
    far_copy = pltpu.make_async_remote_copy(
        src_ref=far_dx, dst_ref=far_arrived, send_sem=dx_send, recv_sem=dx_recv,
        device_id=sums.across, device_id_type=MESH)
    base = early + 1

    @pl.loop(base, sums.ticks)
    def _(t):
        sums.tick(t)
        vectors.tick(t - base)

        @pl.when(t == sums.chunks)
        def _():
            far_copy.start()

    small_out[...] = vectors.small[section]
    sums.finish()
    far_copy.wait()
    result.wait()


def backward_and_sums(first, second, groups, vectors, devices):
    plans = [[a if isinstance(a, Pick) else Pick(a) for a in operands] for operands in (first, second)]
    n, w = plans[0][1].shape
    chunks = sum(pair[0].shape[0] for pair in groups) + 4
    given = [array for plan in plans for entry in plan for array in entry.arrays]
    vm = pl.BlockSpec(memory_space=pltpu.VMEM)
    sums_scratch = Sums.scratch(devices, chunks)
    return pl.pallas_call(
        functools.partial(tail_kernel, devices, plans, len(sums_scratch)),
        out_shape=[
            jax.ShapeDtypeStruct((n, w), BF), jax.ShapeDtypeStruct((n, w), F32),
            jax.ShapeDtypeStruct((chunks, CHUNK, 512), BF), jax.ShapeDtypeStruct((16, 512), F32)],
        in_specs=[ANY] * (len(given) + 4) + [vm, vm],
        out_specs=[ANY] * 3 + [vm],
        scratch_shapes=[pltpu.VMEM(entry.shape, entry.dtype) for entry in plans[0]]
        + [pltpu.SemaphoreType.DMA((2, len(plans[0]))), pltpu.SemaphoreType.DMA, pltpu.SemaphoreType.DMA,
           pltpu.SemaphoreType.DMA, pltpu.VMEM((n, w), BF), pltpu.VMEM((n, w), F32)]
        + [pltpu.VMEM((2, 4, w, w), BF), pltpu.VMEM((2, 16, w), F32)]
        + Vectors.scratch(devices) + sums_scratch + bwd_scratch(n, w),
        compiler_params=pltpu.CompilerParams(collective_id=1, has_side_effects=True, vmem_limit_bytes=VMEM_LIMIT),
        name="backward_and_sums",
    )(*given, *[array for pair in groups for array in pair], *vectors)


def unpack_kernel(kinds, g_ref, mem_ref, out_ref, low_far_ref, grad_ref, grad_far_ref, *refs):
    n = len(kinds)
    low_out, grad_out = refs[:2]
    outs = refs[2 : n + 2]
    stage, sem, low_buf, grad_buf, far_buf, row_in, row_out = refs[n + 2 :]
    step = pl.program_id(0)
    slot = step % 2
    section = lax.axis_index("section")
    fetch = [
        pltpu.make_async_copy(mem_ref, low_buf.at[0], row_in.at[0]),
        pltpu.make_async_copy(low_far_ref, low_buf.at[1], row_in.at[1]),
        pltpu.make_async_copy(grad_ref, grad_buf.at[0], row_in.at[2]),
        pltpu.make_async_copy(grad_far_ref, far_buf, row_in.at[3]),
    ]
    send = [
        pltpu.make_async_copy(low_buf.at[0], low_out.at[section], row_out.at[0]),
        pltpu.make_async_copy(low_buf.at[1], low_out.at[1 - section], row_out.at[1]),
        pltpu.make_async_copy(grad_buf.at[0], grad_out.at[section], row_out.at[2]),
        pltpu.make_async_copy(grad_buf.at[1], grad_out.at[1 - section], row_out.at[3]),
    ]

    @pl.when(step == 0)
    def _():
        for one in fetch[1:]:
            one.start()

        @pl.when(section == 0)
        def _():
            fetch[0].start()

        @pl.when(section != 0)
        def _():
            pltpu.make_async_copy(out_ref, low_buf.at[0], row_in.at[0]).start()

    for k in range(4):
        @pl.when(step == k + 2)
        def _(k=k):
            fetch[k].wait()
            if k == 3:
                grad_buf[1] = far_buf[...].astype(F32)
            send[k].start()

    def copy(kind, dest, k, c_slot):
        flipped, axis = kinds[kind][1:]
        at = pl.ds(pl.multiple_of(k * 512, 512), 512)
        dst = dest.at[:, at] if axis else dest.at[at, :]
        return pltpu.make_async_copy(stage.at[c_slot], dst, sem.at[c_slot])

    @pl.when(step >= 2)
    def _():
        copy(0, outs[0], 0, slot).wait()

    at = 0
    for kind, (count, flipped, axis) in enumerate(kinds):
        @pl.when((step >= at) & (step < at + count))
        def _(kind=kind, at=at, flipped=flipped):
            value = g_ref[0].astype(F32)
            stage[slot] = value.T if flipped else value
            copy(kind, outs[kind], step - at, slot).start()
        at += count

    @pl.when(step == pl.num_programs(0) - 1)
    def _():
        copy(0, outs[0], 0, 1 - slot).wait()
        copy(0, outs[0], 0, slot).wait()
        for one in send:
            one.wait()


def unpack(g, low, low_far, grad, grad_far, kinds, shapes):
    n, w = low_far.shape
    return pl.pallas_call(
        functools.partial(unpack_kernel, kinds),
        grid=(g.shape[0],),
        out_shape=[jax.ShapeDtypeStruct((2, n, w), BF), jax.ShapeDtypeStruct((2, n, w), F32)]
        + [jax.ShapeDtypeStruct(s, F32) for s in shapes],
        in_specs=[pl.BlockSpec((1, 512, 512), lambda i: (i, 0, 0))] + [ANY] * 5,
        out_specs=[ANY] * (len(shapes) + 2),
        scratch_shapes=[
            pltpu.VMEM((2, 512, 512), F32), pltpu.SemaphoreType.DMA((2,)),
            pltpu.VMEM((2, n, w), BF), pltpu.VMEM((2, n, w), F32), pltpu.VMEM((n, w), BF),
            pltpu.SemaphoreType.DMA((4,)), pltpu.SemaphoreType.DMA((4,)),
        ],
        compiler_params=pltpu.CompilerParams(vmem_limit_bytes=VMEM_LIMIT),
        name="unpack_results",
    )(g, *low, low_far, grad, grad_far)


class Spread:
    def __init__(self, devices, weights, land, send_sem, recv_sem):
        self.weights, self.land, self.send_sem, self.recv_sem = weights, land, send_sem, recv_sem
        self.index, self.section = lax.axis_index("dp"), lax.axis_index("section")
        self.bits = halvings(devices, 512)[0]
        self.across = (1 - self.section, self.index)
        self.mates = [(self.section, partner_of(self.index, bit)) for bit in self.bits]
        self.chunks = []
        for w, ref in enumerate(weights):
            rows, cols = ref.shape
            self.chunks += [(w, r, c) for r in range(0, rows, 512) for c in range(0, cols, 512)]
        self.steps = len(self.bits) + 1
        self.ticks = len(self.chunks) + self.steps - 1

    def copy(self, c, step, src=None):
        if step == 0:
            count, device = len(self.bits), self.across
        else:
            bit = self.bits[len(self.bits) - step]
            count, device = bit + 1, self.mates[bit]
        at, size = place(self.index, count, 512)
        part = self.land.at[c, pl.ds(pl.multiple_of(at, 16), size)]
        return pltpu.make_async_remote_copy(
            src_ref=part if src is None else src, dst_ref=part, send_sem=self.send_sem.at[step, c],
            recv_sem=self.recv_sem.at[step, c], device_id=device, device_id_type=MESH)

    def begin(self, c):
        w, r, col = self.chunks[c]
        at, size = place(self.index, len(self.bits), 512)
        self.copy(c, 0, self.weights[w].at[pl.ds(pl.multiple_of(r + at, 16), size), col : col + 512]).start()

    def tick(self, t):
        for step in range(1, self.steps + 1):
            c = t - step + 1

            @pl.when((c >= 0) & (c < len(self.chunks)))
            def _(step=step, c=c):
                self.copy(c, step - 1).wait_recv()
                if step < self.steps:
                    self.copy(c, step).start()

    def finish(self):
        @pl.loop(0, len(self.chunks))
        def _(c):
            for step in range(self.steps):
                self.copy(c, step).wait_send()


def head_kernel(devices, plan, shapes, *refs):
    refs = list(refs)
    take = lambda n: [refs.pop(0) for _ in range(n)]
    given = [take(len(entry.arrays)) for entry in plan]
    tokens, vectors, *weights = take(7)
    outs = take(2 * len(shapes))
    far_tokens, far_vectors, *far = take(7)
    buffers = take(len(plan))
    results = [Result(None, ref) for ref in take(2 * len(shapes))]
    in_sem, out_sem, far_x, far_small, swap_send, swap_recv, keep_sem = take(7)
    land, send_sem, recv_sem, flush_sem = take(4)
    section = lax.axis_index("section")
    spread = Spread(devices, weights, land, send_sem, recv_sem)
    own = [Operand(entry.copy(ref, buffers[k], in_sem.at[k], section), buffers[k])
           for k, (entry, ref) in enumerate(zip(plan, given))]
    for k, result in enumerate(results):
        result.copy = pltpu.make_async_copy(result.ref, outs[k], out_sem.at[k])
    greet([spread.across] + spread.mates)
    for c in range(len(spread.chunks)):
        spread.begin(c)
    swaps = [
        pltpu.make_async_remote_copy(
            src_ref=src, dst_ref=dst, send_sem=swap_send.at[k], recv_sem=swap_recv.at[k],
            device_id=spread.across, device_id_type=MESH)
        for k, (src, dst) in enumerate([(vectors, far_small), (tokens.at[1 - section], far_x)])
    ]
    for one in swaps:
        one.start()

    def flush(c):
        w, r, col = spread.chunks[c]
        return pltpu.make_async_copy(land.at[c], far[w].at[r : r + 512, col : col + 512], flush_sem.at[c])

    x_ref, w_ref, wout_ref, small_ref, ids_ref, far_ids = ready(*own)
    width = x_ref.shape[1]
    n = len(shapes)
    self_forward(section == 1, x_ref, ids_ref,
                 [w_ref.at[:, k * width : (k + 1) * width] for k in range(3)] + [wout_ref],
                 small_ref, results[:n], spread.tick, *refs)
    for one in swaps:
        one.wait()
    keep = [pltpu.make_async_copy(far_x, far_tokens, keep_sem.at[0]), pltpu.make_async_copy(far_small, far_vectors, keep_sem.at[1])]
    for one in keep:
        one.start()
    self_forward(section == 0, far_x, far_ids, [land.at[k] for k in range(4)], far_small, results[n:],
                 lambda k: spread.tick(8 + k), *refs)
    done = 15 - spread.steps + 1
    for c in range(done + 1):
        flush(c).start()
    for t in range(16, spread.ticks):
        spread.tick(t)
        flush(t - spread.steps + 1).start()
    spread.finish()
    for c in range(len(spread.chunks)):
        flush(c).wait()
    for one in keep:
        one.wait()
    for result in results:
        result.copy.wait()


def forward_and_weights(own, tokens, vectors, weights, devices):
    plan = [a if isinstance(a, Pick) else Pick(a) for a in own]
    n, w = plan[0].shape
    shapes = [((w, n), BF), ((n, w), BF), ((n, w), BF), ((w, n), BF), ((HEADS, n), F32), ((n, w), BF), ((n, w), BF)]
    given = [array for entry in plan for array in entry.arrays] + [tokens, vectors, *weights]
    steps = len(halvings(devices, 512)[0]) + 1
    count = sum(a.size for a in weights) // 512**2
    dma = pltpu.SemaphoreType.DMA
    outs = pl.pallas_call(
        functools.partial(head_kernel, devices, plan, shapes),
        out_shape=[jax.ShapeDtypeStruct(s, d) for s, d in shapes * 2]
        + [jax.ShapeDtypeStruct((n, w), BF), jax.ShapeDtypeStruct(vectors.shape, F32)]
        + [jax.ShapeDtypeStruct(a.shape, BF) for a in weights],
        in_specs=[ANY] * len(given),
        out_specs=[ANY] * (2 * len(shapes) + 7),
        scratch_shapes=[pltpu.VMEM(entry.shape, entry.dtype) for entry in plan]
        + [pltpu.VMEM(s, d) for s, d in shapes * 2]
        + [dma((len(plan),)), dma((2 * len(shapes),)), pltpu.VMEM((n, w), BF), pltpu.VMEM(vectors.shape, F32),
           dma((2,)), dma((2,)), dma((2,))]
        + [pltpu.VMEM((count, 512, 512), BF), dma((steps, count)), dma((steps, count)), dma((count,))]
        + fwd_scratch(n, w),
        compiler_params=pltpu.CompilerParams(collective_id=0, has_side_effects=True, vmem_limit_bytes=VMEM_LIMIT),
        name="forward_and_weights",
    )(*given)
    k = len(shapes)
    return outs[:k], outs[k : 2 * k], outs[2 * k], outs[2 * k + 1], outs[2 * k + 2 :]


def shards(layer_input, cotangent, src_segments, tgt_segments, attn_qkv, attn_out, cross_proj,
           ffn_in, ffn_in_bias, ffn_out, ffn_out_bias, norm_gain, norm_bias):
    devices = lax.axis_size("dp")
    sec = lax.axis_index("section")
    first = sec == 0
    swap = lambda a: lax.ppermute(a, "section", [(0, 1), (1, 0)])
    width = attn_out.shape[-1]
    vectors = jnp.concatenate(
        [ffn_in_bias.reshape(-1, width), ffn_out_bias, norm_gain[0], norm_bias[0], jnp.zeros((5, width), F32)])
    tokens = layer_input[0, :, 0]
    near = (attn_qkv[0], attn_out[0], cross_proj[0], ffn_in[0], ffn_out[0])
    src, tgt, cot = Row(src_segments), Row(tgt_segments), Row(cotangent[:, 0])
    (*own_saved, own_hid), (*far_saved, far_hid), far_tokens, far_vectors, far = forward_and_weights(
        [Row(tokens), near[0], near[1], vectors, Pick(src, tgt), Pick(tgt, src)], tokens, vectors, near, devices)
    enc = [Pick(a, b) for a, b in zip(near, far)]
    dec = [Pick(b, a) for a, b in zip(near, far)]
    enc_small, dec_small = Pick(vectors, far_vectors), Pick(far_vectors, vectors)
    src, tgt, cot = Pick(src), Pick(tgt), Pick(cot)
    e1, d1 = Pick(own_hid, far_hid), Pick(far_hid, own_hid)
    g, gp, r2, mem, kv = enc_ffn_fwd(e1, enc[3], enc[4], enc_small, enc[2])
    cq, catt, clse, cr, d2 = cross_fwd(d1, kv, tgt, src, dec[2], dec_small)
    out, dres, dw_dffn, s_dffn = dec_ffn(d2, cr, cot, dec[3], dec[4], dec_small)
    low_far = swap(jnp.where(first, out, mem))
    dh1, dmem, dw_dcross, dw_ecross = cross_bwd(dres, d1, mem, tgt, src, cq, kv, catt, clse, dec[2], enc[2])
    de1, dw_effn, s_effn = enc_ffn_bwd(dmem, r2, g, gp, e1, enc[3], enc[4], enc_small)
    de1, low_far = lax.optimization_barrier((de1, low_far))

    def operands(dh, saved, tokens, ids, weights, small):
        qT, k, v, att, lse, res = saved
        return [dh, res, tokens, ids, qT, k, v, att, lse, weights[0], weights[1], small]

    far_grad, own_grad, sums, s = backward_and_sums(
        operands(de1, [Pick(a, b) for a, b in zip(own_saved, far_saved)], Pick(Row(tokens), far_tokens), src, enc, enc_small),
        operands(dh1, [Pick(b, a) for a, b in zip(own_saved, far_saved)], Pick(far_tokens, Row(tokens)), tgt, dec, dec_small),
        [(dw_effn, dw_dffn), (dw_ecross, dw_dcross)], (s_effn, s_dffn), devices)
    kinds = ((4, False, 1), (4, True, 0), (2, True, 1), (3, True, 1), (1, False, 0))
    layer_output, input_grad, win, wout, cross, qkv, wo = unpack(
        sums, (mem, out), low_far, own_grad, far_grad, kinds,
        [ffn_in.shape[1:], ffn_out.shape[1:], cross_proj.shape[1:], attn_qkv.shape[1:], attn_out.shape[1:]])
    return (layer_output[None, :, None], input_grad[None, :, None], qkv[None], wo[None], cross[None], win[None],
            s[0:4].reshape(1, -1), wout[None], s[4:5], s[5:8][None], s[8:11][None])


def solution(mesh):
    return jax.shard_map(
        shards,
        mesh=mesh,
        in_specs=(
            P("section", None, "dp", None, None),
            P(None, "dp", None, None),
            P(None, "dp", None),
            P(None, "dp", None),
            P("section", None, None),
            P("section", None, None),
            P("section", None, None),
            P("section", None, None),
            P("section", None),
            P("section", None, None),
            P("section", None),
            P("section", None, None),
            P("section", None, None),
        ),
        out_specs=(
            P("section", None, "dp", None, None),
            P("section", None, "dp", None, None),
            P("section", None, None),
            P("section", None, None),
            P("section", None, None),
            P("section", None, None),
            P("section", None),
            P("section", None, None),
            P("section", None),
            P("section", None, None),
            P("section", None, None),
        ),
        check_vma=False,
    )
```

```python
import functools
import math

import jax
import jax.numpy as jnp
from jax import lax
from jax.experimental import pallas as pl
from jax.experimental.pallas import tpu as pltpu
from jax.sharding import PartitionSpec as P

HEADS = 8
EPSILON = 1e-05
NEGATIVE = -1000000000.0
BF = jnp.bfloat16
F32 = jnp.float32
LOG2E = 1.4426950408889634
QB = 256
UNIT = 128
WIDE = 256
TB = 256
FB = 256
VMEM_LIMIT = 60 * 1024 * 1024


def dot(left, right, lc=1, rc=0):
    return lax.dot_general(
        left, right, (((lc,), (rc,)), ((), ())), preferred_element_type=F32
    )


def norm_stats(value):
    centered = value - jnp.mean(value, axis=-1, keepdims=True)
    spread = jnp.mean(centered * centered, axis=-1, keepdims=True)
    scale = lax.rsqrt(spread + EPSILON)
    return centered * scale, scale


def norm_back(out_grad, unit, scale, gain):
    gain_grad = jnp.sum(out_grad * unit, axis=0, keepdims=True)
    shift_grad = jnp.sum(out_grad, axis=0, keepdims=True)
    inner = out_grad * gain
    mean_one = jnp.mean(inner, axis=-1, keepdims=True)
    mean_two = jnp.mean(inner * unit, axis=-1, keepdims=True)
    return scale * (inner - mean_one - unit * mean_two), gain_grad, shift_grad


def gelu_pair(u):
    phi = 0.5 + 0.5 * lax.erf(u * (1.0 / math.sqrt(2.0)))
    bell = jnp.exp(-0.5 * u * u) * (1.0 / math.sqrt(2.0 * math.pi))
    return u * phi, phi + u * bell


def gain_of(small, norm):
    return small[5 + norm : 6 + norm, :]


def shift_of(small, norm):
    return small[8 + norm : 9 + norm, :]


def key_codes(ids_row, length):
    column = jnp.broadcast_to(ids_row.astype(F32), (128, length)).T
    lane = lax.broadcasted_iota(jnp.int32, (length, 128), 1)
    spot = jnp.where(lane < 64, lane, lane - 64)
    codes = jnp.where(
        spot < 4,
        jnp.where(column == spot.astype(F32), 0.0, NEGATIVE),
        jnp.where(spot < 7, -1.0, 0.0),
    )
    return codes, lane < 64


def fill_keys(dst, keys_ref, codes, low_half):
    for pair in range(HEADS // 2):
        slab = keys_ref[:, pair * 128 : pair * 128 + 128].astype(F32)
        dst[2 * pair] = jnp.where(low_half, slab, codes).astype(BF)
        dst[2 * pair + 1] = jnp.where(low_half, codes, slab).astype(BF)


def query_rows(head):
    return (0, 64) if head % 2 == 0 else (64, 0)


def key_range(query_ids, key_ids, qb):
    ids = query_ids[:, pl.ds(pl.multiple_of(qb * QB, QB), QB)].astype(F32)
    keys = key_ids[...].astype(F32)
    start = jnp.sum((keys < jnp.min(ids)).astype(F32)).astype(jnp.int32)
    stop = jnp.sum((keys <= jnp.max(ids)).astype(F32)).astype(jnp.int32)
    return start // UNIT, (stop + UNIT - 1) // UNIT


def visit_keys(query_ids, key_ids, qb, step):
    lo, hi = key_range(query_ids, key_ids, qb)
    count = hi - lo

    @pl.loop(0, count // 2)
    def _(i):
        step(lo + 2 * i, WIDE, False)

    @pl.when(count % 2 == 1)
    def _():
        step(hi - 1, UNIT, False)


def below_diagonal():
    return lax.broadcasted_iota(jnp.int32, (WIDE, QB), 0) <= lax.broadcasted_iota(jnp.int32, (WIDE, QB), 1)


def staged(first, lag_one, second, lag_two, third):
    for i in range(HEADS + lag_one + lag_two):
        if i < HEADS:
            first(i)
        if 0 <= i - lag_one < HEADS:
            second(i - lag_one)
        if 0 <= i - lag_one - lag_two < HEADS:
            third(i - lag_one - lag_two)


def attend_loop(visit, after, qaug, kaug, vt, attT_ref, lse_ref, oacc, mrow, lrow, sbuf, pbuf, length):
    @pl.loop(0, length // QB)
    def _(qb):
        q = pl.ds(pl.multiple_of(qb * QB, QB), QB)
        oacc[...] = jnp.zeros_like(oacc)
        mrow[...] = jnp.full_like(mrow, -3e38)
        lrow[...] = jnp.zeros_like(lrow)

        def step(unit, size, masked):
            ks = pl.ds(pl.multiple_of(unit * UNIT, UNIT), size)
            scale = {}

            def scores(h):
                s = dot(kaug[h, ks, :], qaug[h, :, q])
                sbuf[h, :size] = jnp.where(below_diagonal(), s, NEGATIVE) if masked else s

            def softmax(h):
                s = sbuf[h, :size]
                m_old = mrow[h : h + 1, :]
                m_new = jnp.maximum(m_old, jnp.max(s, axis=0, keepdims=True))
                scale[h] = jnp.exp2(m_old - m_new)
                p = jnp.exp2(s - m_new)
                lrow[h : h + 1, :] = lrow[h : h + 1, :] * scale[h] + jnp.sum(p, axis=0, keepdims=True)
                mrow[h : h + 1, :] = m_new
                pbuf[h, :size] = p.astype(BF)

            def mix(h):
                hs = slice(h * 64, h * 64 + 64)
                oacc[hs, :] = oacc[hs, :] * scale[h] + dot(vt[hs, ks], pbuf[h, :size])

            staged(scores, 7, softmax, 1, mix)

        visit(qb, step)
        for h in range(HEADS):
            hs = slice(h * 64, h * 64 + 64)
            attT_ref[hs, q] = (oacc[hs, :] * (1.0 / lrow[h : h + 1, :])).astype(BF)
        lse_ref[:, q] = mrow[...] + jnp.log2(lrow[...])
        after(qb)


def query_codes(ids_row, length):
    row = lax.broadcasted_iota(jnp.int32, (16, length), 0)
    return jnp.where(row == jnp.broadcast_to(ids_row, (16, length)), 1.0, 0.0), row


def fill_queries(qaug, qT_ref, codes, row, lse_ref, length):
    for h in range(HEADS):
        a, b = query_rows(h)
        qaug[h, a : a + 64, :] = qT_ref[h * 64 : h * 64 + 64, :]
        extra = codes
        if lse_ref is not None:
            lse = lse_ref[h : h + 1, :]
            hi = lse.astype(BF).astype(F32)
            mid = (lse - hi).astype(BF).astype(F32)
            low = lse - hi - mid
            extra = jnp.where(row == 4, hi, jnp.where(row == 5, mid, jnp.where(row == 6, low, codes)))
        qaug[h, b : b + 16, :] = extra.astype(BF)
        qaug[h, b + 16 : b + 64, :] = jnp.zeros((48, length), BF)


def project_queries(src_ref, w_ref, qT_ref, length, width):
    @pl.loop(0, length // TB)
    def _(t):
        rows = pl.ds(pl.multiple_of(t * TB, TB), TB)
        q = dot(src_ref[rows, :], w_ref[:, :width]) * (0.125 * LOG2E)
        qT_ref[:, rows] = q.T.astype(BF)


def out_and_norm(attT_ref, w_ref, resid_ref, sm_ref, norm, res_ref, hid_ref, length):
    @pl.loop(0, length // TB)
    def _(t):
        rows = pl.ds(pl.multiple_of(t * TB, TB), TB)
        a = dot(attT_ref[:, rows], w_ref[...], 0, 0)
        r = resid_ref[rows, :].astype(F32) + a
        res_ref[rows, :] = r.astype(BF)
        unit, _ = norm_stats(r)
        hid_ref[rows, :] = (unit * gain_of(sm_ref, norm) + shift_of(sm_ref, norm)).astype(BF)


def self_forward(causal, x_ref, ids_ref, weights, small_ref, results, tick,
                 kaug, qaug, vt, oacc, mrow, lrow, sbuf, pbuf):
    wq, wk, wv, wout = weights
    qT_ref, k_ref, v_ref, attT_ref, lse_ref, res_ref, hid_ref = results
    length, width = x_ref.shape
    tick(0)

    @pl.loop(0, length // TB)
    def _(t):
        rows = pl.ds(pl.multiple_of(t * TB, TB), TB)
        x = x_ref[rows, :]
        q = dot(x, wq[...]) * (0.125 * LOG2E)
        k = dot(x, wk[...])
        v = dot(x, wv[...])
        qT_ref[:, rows] = q.T.astype(BF)
        k_ref[rows, :] = k.astype(BF)
        v_ref[rows, :] = v.astype(BF)
        vt[:, rows] = v.T.astype(BF)

    for result in (qT_ref, k_ref, v_ref):
        result.flush()
    tick(1)
    codes, low_half = key_codes(ids_ref[...], length)
    fill_keys(kaug, k_ref, codes, low_half)
    qcodes, row = query_codes(ids_ref[...], length)
    fill_queries(qaug, qT_ref, qcodes, row, None, length)
    tick(2)
    attend_loop(functools.partial(visit_all, causal), lambda qb: tick(3 + qb), qaug, kaug, vt, attT_ref, lse_ref,
                oacc, mrow, lrow, sbuf, pbuf, length)
    attT_ref.flush()
    lse_ref.flush()
    tick(7)
    out_and_norm(attT_ref, wout, x_ref, small_ref, 0, res_ref, hid_ref, length)
    res_ref.flush()
    hid_ref.flush()


def cross_fwd_kernel(h_ref, kv_ref, qids_ref, kids_ref, w_ref, ln_ref,
                     qT_ref, attT_ref, lse_ref, res_ref, hid_ref,
                     kaug, qaug, vt, oacc, mrow, lrow, sbuf, pbuf):
    h_ref, w_ref = ready(h_ref, w_ref)
    length, width = h_ref.shape
    project_queries(h_ref, w_ref, qT_ref, length, width)
    qT_ref.flush()
    kv_ref, qids_ref, kids_ref = ready(kv_ref, qids_ref, kids_ref)

    @pl.loop(0, length // TB)
    def _(t):
        rows = pl.ds(pl.multiple_of(t * TB, TB), TB)
        vt[:, rows] = kv_ref[rows, width:].astype(F32).T.astype(BF)

    codes, low_half = key_codes(kids_ref[...], length)
    fill_keys(kaug, kv_ref, codes, low_half)
    qcodes, row = query_codes(qids_ref[...], length)
    fill_queries(qaug, qT_ref, qcodes, row, None, length)
    attend_loop(functools.partial(visit_keys, qids_ref, kids_ref), lambda qb: None, qaug, kaug, vt, attT_ref, lse_ref,
                oacc, mrow, lrow, sbuf, pbuf, length)
    attT_ref.flush()
    lse_ref.flush()
    (ln_ref,) = ready(ln_ref)
    out_and_norm(attT_ref, w_ref.at[:, width:], h_ref, ln_ref, 1, res_ref, hid_ref, length)


def visit_all(causal, qb, step):
    blocks = 1024 // WIDE
    lo = jnp.where(qb == blocks - 1, 1, 0)
    hi = jnp.where(qb == 0, blocks - 1, blocks)
    if causal is not False:
        lo, hi = jnp.where(causal, 0, lo), jnp.where(causal, qb, hi)

    @pl.loop(lo, hi)
    def _(i):
        step(i * (WIDE // UNIT), WIDE, False)

    if causal is not False:
        @pl.when(causal)
        def _():
            step(qb * (QB // UNIT), WIDE, True)


def attend_back_loop(visit, after, qaug, kaug, kt, vaug, doaug, jgT, jg, dqacc, sbuf, dbuf, pbuf, gbuf, length):
    width = HEADS * 64
    jgT[...] = jnp.zeros_like(jgT)

    @pl.loop(0, length // QB)
    def _(qb):
        q = pl.ds(pl.multiple_of(qb * QB, QB), QB)
        dqacc[...] = jnp.zeros_like(dqacc)

        def step(unit, size, masked):
            ks = pl.ds(pl.multiple_of(unit * UNIT, UNIT), size)

            def products(h):
                s = dot(kaug[h, ks, :], qaug[h, :, q])
                sbuf[h % 4, :size] = jnp.where(below_diagonal(), s, NEGATIVE) if masked else s
                dbuf[h % 4, :size] = dot(vaug[h, ks, :], doaug[h, :, q])

            def grads(h):
                p = jnp.exp2(sbuf[h % 4, :size])
                pbuf[h % 4, :size] = p.astype(BF)
                gbuf[h % 4, :size] = (p * dbuf[h % 4, :size]).astype(BF)

            def add(h):
                a, _ = query_rows(h)
                at = h * 64
                hs = slice(at, at + 64)
                dqacc[hs, :] += dot(kt[hs, ks], gbuf[h % 4, :size])
                jgT[width + at : width + at + 64, ks] += dot(doaug[h, a : a + 64, q], pbuf[h % 4, :size], 1, 1)
                jgT[at : at + 64, ks] += dot(qaug[h, a : a + 64, q], gbuf[h % 4, :size], 1, 1)

            lag = 1 if size == WIDE else 2
            staged(products, lag, grads, lag, add)

        visit(qb, step)
        jg[:width, q] = (dqacc[...] * 0.125).astype(BF)
        after(qb)

    jg[width : 2 * width, :] = (jgT[:width, :] * math.log(2.0)).astype(BF)
    jg[2 * width :, :] = jgT[width:, :].astype(BF)


def prepare_back(dr_ref, w_ref, attT_ref, doaug, length):
    @pl.loop(0, length // TB)
    def _(t):
        rows = pl.ds(pl.multiple_of(t * TB, TB), TB)
        row = lax.broadcasted_iota(jnp.int32, (16, TB), 0)
        d = dot(w_ref[...], dr_ref[rows, :], 1, 1).astype(BF)
        for h in range(HEADS):
            a, b = query_rows(h)
            hs = slice(h * 64, h * 64 + 64)
            doh = d[hs, :]
            doaug[h, a : a + 64, rows] = doh
            delta = jnp.sum(doh.astype(F32) * attT_ref[hs, rows].astype(F32), axis=0, keepdims=True)
            hi = delta.astype(BF).astype(F32)
            mid = (delta - hi).astype(BF).astype(F32)
            low = delta - hi - mid
            extra = jnp.where(row == 4, hi, jnp.where(row == 5, mid, jnp.where(row == 6, low, 0.0)))
            doaug[h, b : b + 16, rows] = extra.astype(BF)
            doaug[h, b + 16 : b + 64, rows] = jnp.zeros((48, TB), BF)


def prepare_keys(keys_ref, values_ref, codes, low_half, kaug, kt, vaug, length):
    fill_keys(kaug, keys_ref, codes, low_half)
    fill_keys(vaug, values_ref, jnp.where(codes == NEGATIVE, 0.0, codes), low_half)

    @pl.loop(0, length // TB)
    def _(t):
        rows = pl.ds(pl.multiple_of(t * TB, TB), TB)
        kt[:, rows] = keys_ref[rows, :].astype(F32).T.astype(BF)


def self_backward(causal, operands, tick, middle, reuse, put_dx, dw_ref, dln_ref,
                  kaug, kt, vaug, qaug, doaug, dqacc, jgT, jg, sbuf, dbuf, pbuf, gbuf):
    dh, res, x, ids, qT, keys, values, attT, lse, w, wout, small = operands
    tick(0)
    dh_ref, res_ref, ln_ref = ready(dh, res, small)
    length, width = res_ref.shape
    dln_ref[...] = jnp.zeros(dln_ref.shape, F32)
    dr = res_ref

    @pl.loop(0, length // TB)
    def _(t):
        rows = pl.ds(pl.multiple_of(t * TB, TB), TB)
        unit, scale = norm_stats(res_ref[rows, :].astype(F32))
        d, gg, sg = norm_back(dh_ref[rows, :].astype(F32), unit, scale, gain_of(ln_ref, 0))
        dln_ref[5:6, :] += gg
        dln_ref[8:9, :] += sg
        dr[rows, :] = d.astype(BF)

    attT_ref, wout_ref, ids_ref = ready(attT, wout, ids)
    dw_ref[3] = dot(attT_ref[...], dr[...]).astype(BF)
    prepare_back(dr, wout_ref, attT_ref, doaug, length)
    tick(1)
    codes, low_half = key_codes(ids_ref[...], length)
    k_ref, v_ref, qT_ref, lse_ref = ready(keys, values, qT, lse)
    prepare_keys(k_ref, v_ref, codes, low_half, kaug, kt, vaug, length)
    qcodes, row = query_codes(ids_ref[...], length)
    fill_queries(qaug, qT_ref, qcodes, row, lse_ref, length)
    tick(2)

    def after(qb):
        for k, block in ((3, middle), (4, length // QB - 1)):
            @pl.when(qb == block)
            def _(k=k):
                tick(k)

    attend_back_loop(functools.partial(visit_all, causal), after, qaug, kaug, kt, vaug, doaug,
                     jgT, jg, dqacc, sbuf, dbuf, pbuf, gbuf, length)
    reuse(dh, ids, qT, keys, values, attT, lse, wout, small)
    x_ref, w_ref = ready(x, w)

    @pl.loop(0, 3)
    def _(t):
        rows = pl.ds(pl.multiple_of(t * 512, 512), 512)
        dw_ref[t] = dot(jg[rows, :], x_ref[...]).astype(BF)

    tick(5)

    @pl.loop(0, length // TB)
    def _(t):
        rows = pl.ds(pl.multiple_of(t * TB, TB), TB)
        put_dx(rows, dr[rows, :].astype(F32) + dot(jg[:, rows], w_ref[...], 0, 1))

    reuse(res, x, w)


def cross_bwd_kernel(dr_ref, h_ref, mem_ref, qids_ref, kids_ref, qT_ref, kv_ref, attT_ref,
                     lse_ref, w_ref, wkv_ref,
                     dh_ref, dmem_ref, dwd_ref, dwe_ref,
                     kaug, kt, vaug, qaug, doaug, dqacc, jgT, jg, sbuf, dbuf, pbuf, gbuf):
    dr_ref, attT_ref, w_ref, qids_ref, kids_ref = ready(dr_ref, attT_ref, w_ref, qids_ref, kids_ref)
    length, width = dr_ref.shape
    dwd_ref[1] = dot(dr_ref[...], attT_ref[...], 0, 1).astype(BF)
    prepare_back(dr_ref, w_ref.at[:, width:], attT_ref, doaug, length)
    codes, low_half = key_codes(kids_ref[...], length)
    kv_ref, qT_ref, lse_ref = ready(kv_ref, qT_ref, lse_ref)
    prepare_keys(kv_ref.at[:, :width], kv_ref.at[:, width:], codes, low_half, kaug, kt, vaug, length)
    qcodes, row = query_codes(qids_ref[...], length)
    fill_queries(qaug, qT_ref, qcodes, row, lse_ref, length)
    attend_back_loop(functools.partial(visit_keys, qids_ref, kids_ref), lambda qb: None, qaug, kaug, kt, vaug,
                     doaug, jgT, jg, dqacc, sbuf, dbuf, pbuf, gbuf, length)
    h_ref, mem_ref, wkv_ref = ready(h_ref, mem_ref, wkv_ref)
    dwd_ref[0] = dot(jg[:width, :], h_ref[...]).astype(BF)
    for half in range(2):
        dwe_ref[half] = dot(jg[(half + 1) * width : (half + 2) * width, :], mem_ref[...]).astype(BF)
    dwd_ref.flush()
    dwe_ref.flush()

    @pl.loop(0, length // TB)
    def _(t):
        rows = pl.ds(pl.multiple_of(t * TB, TB), TB)
        d = dot(jg[:width, rows], w_ref[:, :width], 0, 1)
        dh_ref[rows, :] = (dr_ref[rows, :].astype(F32) + d).astype(BF)
        dmem_ref[rows, :] = dot(jg[width:, rows], wkv_ref[...], 0, 1).astype(BF)


def enc_ffn_fwd_kernel(e1_ref, win_ref, ln_ref, wout_ref, wkv_ref,
                       g_ref, gp_ref, r_ref, mem_ref, kv_ref, ubuf):
    e1_ref, win_ref, ln_ref = ready(e1_ref, win_ref, ln_ref)
    length, width = e1_ref.shape
    ff = win_ref.shape[1]
    slabs = ff // 512
    late = []
    later = (wout_ref, wkv_ref)

    def at(i):
        b, j = divmod(i, slabs)
        return slice(b * FB, b * FB + FB), slice(j * 512, j * 512 + 512), j

    def up(i):
        rows, cols, j = at(i)
        ubuf[i % 4] = dot(e1_ref[rows, :], win_ref[:, cols])

    def act(i):
        rows, cols, j = at(i)
        g, gp = gelu_pair(ubuf[i % 4] + ln_ref[j : j + 1, :])
        g_ref[rows, cols] = g.astype(BF)
        gp_ref[rows, cols] = gp.astype(BF)

    def down(b):
        rows = slice(b * FB, b * FB + FB)
        if not late:
            late.extend(ready(*later))
        total = dot(g_ref[rows, :], late[0][...]) + e1_ref[rows, :].astype(F32) + ln_ref[4:5, :]
        r_ref[rows, :] = total.astype(BF)
        unit, _ = norm_stats(total)
        e2 = unit * gain_of(ln_ref, 1) + shift_of(ln_ref, 1)
        unit, _ = norm_stats(e2)
        mem_ref[rows, :] = (unit * gain_of(ln_ref, 2) + shift_of(ln_ref, 2)).astype(BF)

    def project(b):
        rows = slice(b * FB, b * FB + FB)
        kv_ref[rows, :] = dot(mem_ref[rows, :], late[1][...]).astype(BF)
        for result in (g_ref, gp_ref, r_ref, mem_ref, kv_ref):
            result.flush_rows(b, FB)

    units = length // FB * slabs
    for tick in range(units + 4):
        if tick < units:
            up(tick)
        i = tick - 2
        if 0 <= i < units:
            act(i)
            if i % slabs == slabs - 1:
                down(i // slabs)
        i = tick - 4
        if 0 <= i < units and i % slabs == slabs - 1:
            project(i // slabs)
    for result in (g_ref, gp_ref, r_ref, mem_ref, kv_ref):
        result.started = True


def weight_grads(act_ref, du_ref, df_ref, g_ref, dw_ref):
    slabs = du_ref.shape[1] // 512

    @pl.loop(0, slabs)
    def _(t):
        cols = pl.ds(pl.multiple_of(t * 512, 512), 512)
        dw_ref[t] = dot(act_ref[...], du_ref[:, cols], 0, 0).astype(BF)
        dw_ref.flush_part(t)
        dw_ref[slabs + t] = dot(df_ref[...], g_ref[:, cols], 0, 0).astype(BF)
        dw_ref.flush_part(slabs + t)

    dw_ref.started = True


def enc_ffn_bwd_kernel(dmem_ref, r_ref, ln_ref, wout_ref, gp_ref, win_ref, e1_ref, g_ref,
                       de1_ref, dw_ref, dln_ref,
                       du_ref, df_ref, dgbuf, drbuf):
    dmem_ref, r_ref, ln_ref = ready(dmem_ref, r_ref, ln_ref)
    length, width = r_ref.shape
    ff = du_ref.shape[1]
    slabs = ff // 512
    dln_ref[...] = jnp.zeros(dln_ref.shape, F32)

    def at(i):
        b, j = divmod(i, slabs)
        return slice(b * FB, b * FB + FB), slice(j * 512, j * 512 + 512), j

    def norms(b):
        rows = slice(b * FB, b * FB + FB)
        unit2, scale2 = norm_stats(r_ref[rows, :].astype(F32))
        e2 = unit2 * gain_of(ln_ref, 1) + shift_of(ln_ref, 1)
        unit3, scale3 = norm_stats(e2)
        de2, gg, sg = norm_back(dmem_ref[rows, :].astype(F32), unit3, scale3, gain_of(ln_ref, 2))
        dln_ref[7:8, :] += gg
        dln_ref[10:11, :] += sg
        dr, gg, sg = norm_back(de2, unit2, scale2, gain_of(ln_ref, 1))
        dln_ref[6:7, :] += gg
        dln_ref[9:10, :] += sg
        df = dr.astype(BF)
        df_ref[rows, :] = df
        drbuf[b] = dr
        dln_ref[4:5, :] += jnp.sum(df.astype(F32), axis=0, keepdims=True)

    def up_back(i):
        rows, cols, j = at(i)
        dgbuf[i % 4] = dot(df_ref[rows, :], wout_ref[cols, :], 1, 1)

    def act_back(i):
        rows, cols, j = at(i)
        du = dgbuf[i % 4] * gp_ref[rows, cols].astype(F32)
        du_ref[rows, cols] = du.astype(BF)
        dln_ref[j : j + 1, :] += jnp.sum(du, axis=0, keepdims=True)

    def down_back(b):
        rows = slice(b * FB, b * FB + FB)
        de1_ref[rows, :] = (drbuf[b] + dot(du_ref[rows, :], win_ref[...], 1, 1)).astype(BF)

    norms(0)
    wout_ref, gp_ref, win_ref = ready(wout_ref, gp_ref, win_ref)
    units = length // FB * slabs
    for tick in range(units + 2):
        if tick < units:
            up_back(tick)
            if tick % slabs == 1 and tick // slabs + 1 < length // FB:
                norms(tick // slabs + 1)
        i = tick - 2
        if 0 <= i < units:
            act_back(i)
            if i % slabs == slabs - 1:
                down_back(i // slabs)
    de1_ref.flush()
    e1_ref, g_ref = ready(e1_ref, g_ref)
    weight_grads(e1_ref, du_ref, df_ref, g_ref, dw_ref)


def dec_ffn_kernel(h_ref, win_ref, ln_ref, wout_ref, cot_ref, res_ref, mem_ref,
                   out_ref, away_ref, dres_ref, dw_ref, dln_ref,
                   g_ref, du_ref, df_ref, ubuf, gpbuf, dgbuf, drbuf):
    h_ref, win_ref, ln_ref = ready(h_ref, win_ref, ln_ref)
    length, width = h_ref.shape
    ff = win_ref.shape[1]
    dln_ref[...] = jnp.zeros(dln_ref.shape, F32)
    slabs = ff // 512
    late = []

    def at(i):
        b, j = divmod(i, slabs)
        return slice(b * FB, b * FB + FB), slice(j * 512, j * 512 + 512), j

    def up(i):
        rows, cols, j = at(i)
        ubuf[i % 4] = dot(h_ref[rows, :], win_ref[:, cols])

    def act(i):
        rows, cols, j = at(i)
        g, gp = gelu_pair(ubuf[i % 4] + ln_ref[j : j + 1, :])
        g_ref[rows, cols] = g.astype(BF)
        gpbuf[i % 8] = gp.astype(BF)

    def down(b):
        rows = slice(b * FB, b * FB + FB)
        if not late:
            late.extend(ready(wout_op, cot_op, res_op))
        wout, cot, _ = late
        total = dot(g_ref[rows, :], wout[...]) + h_ref[rows, :].astype(F32) + ln_ref[4:5, :]
        unit3, scale3 = norm_stats(total)
        out_ref[rows, :] = (unit3 * gain_of(ln_ref, 2) + shift_of(ln_ref, 2)).astype(BF)
        dr, gg, sg = norm_back(cot[rows, :].astype(F32), unit3, scale3, gain_of(ln_ref, 2))
        dln_ref[7:8, :] += gg
        dln_ref[10:11, :] += sg
        df = dr.astype(BF)
        df_ref[rows, :] = df
        drbuf[b % 2] = dr
        dln_ref[4:5, :] += jnp.sum(df.astype(F32), axis=0, keepdims=True)

    def up_back(i):
        rows, cols, j = at(i)
        dgbuf[i % 4] = dot(df_ref[rows, :], late[0][cols, :], 1, 1)

    def act_back(i):
        rows, cols, j = at(i)
        du = dgbuf[i % 4] * gpbuf[i % 8].astype(F32)
        du_ref[rows, cols] = du.astype(BF)
        dln_ref[j : j + 1, :] += jnp.sum(du, axis=0, keepdims=True)

    def down_back(b):
        rows = slice(b * FB, b * FB + FB)
        total = drbuf[b % 2] + dot(du_ref[rows, :], win_ref[...], 1, 1)
        unit2, scale2 = norm_stats(late[2][rows, :].astype(F32))
        d, gg, sg = norm_back(total, unit2, scale2, gain_of(ln_ref, 1))
        dln_ref[6:7, :] += gg
        dln_ref[9:10, :] += sg
        dres_ref[rows, :] = d.astype(BF)

    wout_op, cot_op, res_op = wout_ref, cot_ref, res_ref
    units = length // FB * slabs
    for tick in range(units + 6 + 1):
        if tick < units:
            up(tick)
        i = tick - 2
        if 0 <= i < units:
            act(i)
            if i % slabs == slabs - 1:
                down(i // slabs)
        i = tick - 6
        if 0 <= i < units:
            up_back(i)
        i -= 1
        if 0 <= i < units:
            act_back(i)
            if i % slabs == slabs - 1:
                down_back(i // slabs)
    out_ref.flush()
    dres_ref.flush()
    (mem_ref,) = ready(mem_ref)
    section = lax.axis_index("section")

    @pl.when(section == 0)
    def _():
        pltpu.make_async_copy(out_ref.ref, away_ref.copy.dst_ref, away_ref.copy.dst_sem).start()

    @pl.when(section != 0)
    def _():
        pltpu.make_async_copy(mem_ref, away_ref.copy.dst_ref, away_ref.copy.dst_sem).start()

    away_ref.started = True
    weight_grads(h_ref, du_ref, df_ref, g_ref, dw_ref)


class Operand:
    def __init__(self, copy, ref):
        self.copy, self.ref = copy, ref


def ready(*operands):
    refs = []
    for operand in operands:
        if operand.copy is not None:
            operand.copy.wait()
            operand.copy = None
        refs.append(operand.ref)
    return refs


class Result:
    def __init__(self, copy, ref):
        self.copy, self.ref, self.started = copy, ref, False

    def __getitem__(self, at):
        return self.ref[at]

    def __setitem__(self, at, value):
        self.ref[at] = value

    def __getattr__(self, name):
        return getattr(self.ref, name)

    def flush_part(self, k):
        copy = self.copy
        pltpu.make_async_copy(self.ref.at[k], copy.dst_ref.at[k], copy.dst_sem).start()

    def flush_rows(self, k, size):
        rows = pl.ds(k * size, size)
        copy = self.copy
        pltpu.make_async_copy(self.ref.at[rows], copy.dst_ref.at[rows], copy.dst_sem).start()

    def flush(self):
        if not self.started:
            self.copy.start()
            self.started = True


class Row:
    def __init__(self, array):
        self.array, self.shape, self.dtype = array, array.shape[1:], array.dtype


class Pick:
    def __init__(self, zero, one=None):
        self.parts = [zero] if one is None else [zero, one]
        self.arrays = [p.array if isinstance(p, Row) else p for p in self.parts]
        self.shape, self.dtype = zero.shape, zero.dtype

    def copy(self, refs, dst, sem, section):
        sources = [ref.at[section] if isinstance(p, Row) else ref for p, ref in zip(self.parts, refs)]
        if len(sources) == 1:
            copy = pltpu.make_async_copy(sources[0], dst, sem)
            copy.start()
            return copy
        for k, source in enumerate(sources):
            @pl.when(section == k)
            def _(source=source):
                pltpu.make_async_copy(source, dst, sem).start()
        return pltpu.make_async_copy(sources[1], dst, sem)


def run_kernel(kernel, plan, n_out, *refs):
    n_in = sum(len(p.arrays) for p in plan)
    ins, outs = list(refs[:n_in]), refs[n_in : n_in + n_out]
    rest = refs[n_in + n_out :]
    in_bufs, out_bufs = rest[: len(plan)], rest[len(plan) : len(plan) + n_out]
    in_sem, out_sem = rest[len(plan) + n_out : len(plan) + n_out + 2]
    scratch = rest[len(plan) + n_out + 2 :]
    section = lax.axis_index("section")
    operands = []
    for k, entry in enumerate(plan):
        given = [ins.pop(0) for _ in entry.arrays]
        operands.append(Operand(entry.copy(given, in_bufs[k], in_sem.at[k], section), in_bufs[k]))
    results = [
        Result(pltpu.make_async_copy(out_bufs[k], outs[k], out_sem.at[k]), out_bufs[k]) for k in range(n_out)
    ]
    kernel(*operands, *results, *scratch)
    ready(*operands)
    for result in results:
        result.flush()
    for result in results:
        result.copy.wait()


def call(kernel, name, outs, scratch, flops, *args):
    any_space = pl.BlockSpec(memory_space=pl.ANY)
    plan = [a if isinstance(a, Pick) else Pick(a) for a in args]
    given = [array for entry in plan for array in entry.arrays]
    return pl.pallas_call(
        functools.partial(run_kernel, kernel, plan, len(outs)),
        out_shape=[jax.ShapeDtypeStruct(s, d) for s, d in outs],
        in_specs=[any_space] * len(given),
        out_specs=[any_space] * len(outs),
        scratch_shapes=[pltpu.VMEM(entry.shape, entry.dtype) for entry in plan]
        + [pltpu.VMEM(s, d) for s, d in outs]
        + [pltpu.SemaphoreType.DMA((len(plan),)), pltpu.SemaphoreType.DMA((len(outs),))]
        + scratch,
        compiler_params=pltpu.CompilerParams(vmem_limit_bytes=VMEM_LIMIT),
        cost_estimate=pl.CostEstimate(flops=flops, bytes_accessed=8 << 20, transcendentals=0),
        name=name,
    )(*given)


def fwd_scratch(n, w):
    return [
        pltpu.VMEM((HEADS, n, 128), BF),
        pltpu.VMEM((HEADS, 128, n), BF),
        pltpu.VMEM((w, n), BF),
        pltpu.VMEM((w, QB), F32),
        pltpu.VMEM((HEADS, QB), F32),
        pltpu.VMEM((HEADS, QB), F32),
        pltpu.VMEM((HEADS, WIDE, QB), F32),
        pltpu.VMEM((HEADS, WIDE, QB), BF),
    ]


def cross_fwd(h, kv, qids, kids, w, small):
    n, w_ = h.shape
    return call(cross_fwd_kernel, "cross_forward",
                [((w_, n), BF), ((w_, n), BF), ((HEADS, n), F32), ((n, w_), BF), ((n, w_), BF)],
                fwd_scratch(n, w_), 10 << 30, h, kv, qids, kids, w, small)


def bwd_scratch(n, w):
    return [
        pltpu.VMEM((HEADS, n, 128), BF),
        pltpu.VMEM((w, n), BF),
        pltpu.VMEM((HEADS, n, 128), BF),
        pltpu.VMEM((HEADS, 128, n), BF),
        pltpu.VMEM((HEADS, 128, n), BF),
        pltpu.VMEM((w, QB), F32),
        pltpu.VMEM((2 * w, n), F32),
        pltpu.VMEM((3 * w, n), BF),
        pltpu.VMEM((4, WIDE, QB), F32),
        pltpu.VMEM((4, WIDE, QB), F32),
        pltpu.VMEM((4, WIDE, QB), BF),
        pltpu.VMEM((4, WIDE, QB), BF),
    ]


def cross_bwd(dr, h, mem, qids, kids, qT, kv, attT, lse, w, wkv):
    n, w_ = h.shape
    return call(cross_bwd_kernel, "cross_backward",
                [((n, w_), BF), ((n, w_), BF), ((2, w_, w_), BF), ((2, w_, w_), BF)],
                bwd_scratch(n, w_), 25 << 30,
                dr, h, mem, qids, kids, qT, kv, attT, lse, w, wkv)


def enc_ffn_fwd(e1, win, wout, small, wkv):
    n, w_ = e1.shape
    ff = win.shape[-1]
    return call(enc_ffn_fwd_kernel, "encoder_ffn_forward",
                [((n, ff), BF), ((n, ff), BF), ((n, w_), BF), ((n, w_), BF), ((n, 2 * w_), BF)],
                [pltpu.VMEM((4, FB, 512), F32)], 6 << 30, e1, win, small, wout, wkv)


def enc_ffn_bwd(dmem, r, g, gp, e1, win, wout, small):
    n, w_ = e1.shape
    ff = win.shape[-1]
    return call(enc_ffn_bwd_kernel, "encoder_ffn_backward",
                [((n, w_), BF), ((2 * ff // w_, w_, w_), BF), ((16, w_), F32)],
                [pltpu.VMEM((n, ff), BF), pltpu.VMEM((n, w_), BF), pltpu.VMEM((4, FB, 512), F32), pltpu.VMEM((n // FB, FB, w_), F32)],
                9 << 30, dmem, r, small, wout, gp, win, e1, g)


def dec_ffn(h, res, cot, win, wout, small, mem):
    n, w_ = h.shape
    ff = win.shape[-1]
    return call(dec_ffn_kernel, "decoder_ffn",
                [((n, w_), BF), ((n, w_), BF), ((n, w_), BF), ((2 * ff // w_, w_, w_), BF), ((16, w_), F32)],
                [pltpu.VMEM((n, ff), BF), pltpu.VMEM((n, ff), BF), pltpu.VMEM((n, w_), BF), pltpu.VMEM((4, FB, 512), F32),
                 pltpu.VMEM((8, FB, 512), BF), pltpu.VMEM((4, FB, 512), F32), pltpu.VMEM((2, FB, w_), F32)], 13 << 30,
                h, win, small, wout, cot, res, mem)


CHUNK = 512
SLOTS = 4
MESH = pl.DeviceIdType.MESH
ANY = pl.BlockSpec(memory_space=pl.ANY)


def bit_of(index, bit):
    return (index // 2**bit) % 2


def partner_of(index, bit):
    return index + 2**bit - 2 * 2**bit * bit_of(index, bit)


def greet(partners):
    barrier = pltpu.get_barrier_semaphore()
    for device in partners:
        pl.semaphore_signal(barrier, inc=1, device_id=device, device_id_type=MESH)
    pl.semaphore_wait(barrier, len(partners))


def halvings(devices, rows):
    bits = devices.bit_length() - 1
    halved = 0
    while halved < bits and (rows >> (halved + 1)) >= 16 and (rows >> (halved + 1)) % 16 == 0:
        halved += 1
    return list(range(halved)), list(range(halved, bits))


def place(index, count, rows):
    at, size = 0, rows
    for bit in range(count):
        size //= 2
        at = at + bit_of(index, bit) * size
    return at, size


class Sums:
    def __init__(self, devices, groups, early, gap, out_ref, scratch):
        self.groups, self.early, self.gap, self.out = groups, early, gap, out_ref
        self.held, self.shard, self.load_sem, self.store_sem, self.core_sem, self.send_sem, self.recv_sem = scratch[:7]
        self.landing = scratch[7:]
        self.index, self.section = lax.axis_index("dp"), lax.axis_index("section")
        self.halved, self.rest = halvings(devices, CHUNK)
        self.bits = self.halved + self.rest
        self.across = (1 - self.section, self.index)
        self.mates = [(self.section, partner_of(self.index, bit)) for bit in self.bits]
        self.chunks = sum(group[0] for group in groups)
        self.steps = 1 + len(self.bits) + len(self.halved)
        self.ticks = self.chunks + gap + self.steps

    def rows(self, count, other=False):
        at, size = 0, CHUNK
        for bit in range(count):
            size //= 2
            side = bit_of(self.index, bit)
            at = at + (1 - side if other and bit == count - 1 else side) * size
        return at, size

    def window(self, count, other=False):
        at, size = self.rows(count, other)
        return pl.ds(pl.multiple_of(at - self.rows(1)[0], 16), size)

    def remote(self, src, dst, step, c, device):
        return pltpu.make_async_remote_copy(
            src_ref=src, dst_ref=dst, send_sem=self.send_sem.at[step, c], recv_sem=self.recv_sem.at[step, c],
            device_id=device, device_id_type=MESH)

    def begin(self, c):
        at, size = self.rows(1)
        far, _ = self.rows(1, True)
        first = 0
        for count, *pair in self.groups:
            @pl.when((c >= first) & (c < first + count))
            def _(first=first, pair=pair):
                for k, (ref, layer) in enumerate(pair):
                    near = ref.at[c - first, pl.ds(pl.multiple_of(at, 16), size)]
                    away = ref.at[c - first, pl.ds(pl.multiple_of(far, 16), size)]
                    pltpu.make_async_copy(near, self.held.at[c, layer], self.load_sem.at[k, c]).start()
                    self.core_copy(k, c, away, layer).start()
            first += count

    def core_copy(self, k, c, src, layer):
        return pltpu.make_async_remote_copy(
            src_ref=src, dst_ref=self.landing[0].at[c % SLOTS, layer], send_sem=self.core_sem.at[0, k, c],
            recv_sem=self.core_sem.at[1, k, c], device_id=self.mates[0], device_id_type=MESH)

    def copy(self, step, c):
        reduce_steps = 1 + len(self.bits)
        if step == 1:
            return self.remote(self.held.at[c, 1 - self.section], self.landing[1].at[c % SLOTS], 1, c, self.across)
        if step < reduce_steps:
            bit = step - 1
            window = self.window(bit + 1, True) if bit in self.halved else self.window(len(self.halved))
            return self.remote(self.held.at[c, self.section, window], self.landing[step].at[c % SLOTS], step, c, self.mates[bit])
        bit = self.halved[-1 - (step - reduce_steps)]
        at, size = self.rows(bit + 1)
        rows = self.out.at[c, pl.ds(pl.multiple_of(at, 16), size)]
        return self.remote(self.shard.at[c] if step == reduce_steps else rows, rows, step, c, self.mates[bit])

    def store(self, c):
        at, size = self.rows(len(self.halved))
        return pltpu.make_async_copy(self.shard.at[c], self.out.at[c, pl.ds(pl.multiple_of(at, 16), size)], self.store_sem.at[c])

    def arrive(self, step, c):
        reduce_steps = 1 + len(self.bits)
        if step == 0:
            for k in range(2):
                pltpu.make_async_copy(self.landing[0].at[c % SLOTS, k], self.held.at[c, k], self.load_sem.at[k, c]).wait()
                self.core_copy(k, c, self.held.at[c, k], k).wait_recv()
            for k in range(2):
                self.held[c, k] = (self.held[c, k].astype(F32) + self.landing[0][c % SLOTS, k].astype(F32)).astype(BF)
            return
        copy = self.copy(step, c)
        copy.wait_recv()
        if step < reduce_steps:
            bit = step - 1
            if bit in self.rest:
                copy.wait_send()
            window = self.window(1) if step == 1 else self.window(min(bit + 1, len(self.halved)))
            total = (self.held[c, self.section, window, :].astype(F32) + self.landing[step][c % SLOTS].astype(F32)).astype(BF)
            if step == reduce_steps - 1:
                self.shard[c] = total
                self.store(c).start()
            else:
                self.held[c, self.section, window, :] = total
        elif step == reduce_steps:
            self.store(c).wait()

    def tick(self, t):
        for step in range(self.steps + 1):
            at = t - step
            late = at >= self.early + self.gap
            c = jnp.where(late, at - self.gap, at)

            @pl.when(((at >= 0) & (at < self.early)) | (late & (c < self.chunks)))
            def _(step=step, c=c):
                if step == 0:
                    self.begin(c)
                else:
                    self.arrive(step - 1, c)
                    if step < self.steps:
                        self.copy(step, c).start()

    def finish(self):
        @pl.loop(0, self.chunks)
        def _(c):
            for k in range(2):
                self.core_copy(k, c, self.held.at[c, k], k).wait_send()
            for step in range(1, self.steps):
                if step - 1 not in self.rest or step - 1 >= len(self.bits):
                    self.copy(step, c).wait_send()

    @staticmethod
    def scratch(devices, chunks):
        halved, rest = halvings(devices, CHUNK)
        steps = 1 + len(halved + rest) + len(halved)
        sizes = [CHUNK >> min(bit + 1, len(halved)) for bit in halved + rest]
        return [
            pltpu.VMEM((chunks, 2, CHUNK // 2, 512), BF),
            pltpu.VMEM((chunks, CHUNK >> len(halved), 512), BF),
            pltpu.SemaphoreType.DMA((2, chunks)),
            pltpu.SemaphoreType.DMA((chunks,)),
            pltpu.SemaphoreType.DMA((2, 2, chunks)),
            pltpu.SemaphoreType.DMA((steps, chunks)),
            pltpu.SemaphoreType.DMA((steps, chunks)),
            pltpu.VMEM((SLOTS, 2, CHUNK // 2, 512), BF),
            pltpu.VMEM((SLOTS, CHUNK // 2, 512), BF),
        ] + [pltpu.VMEM((SLOTS, size, 512), BF) for size in sizes[1:]]


class Vectors:
    def __init__(self, sums, scratch):
        self.small, self.arrived, self.send_sem, self.recv_sem = scratch
        self.section = sums.section
        self.partners = [sums.across] + sums.mates

    def copy(self, k):
        return pltpu.make_async_remote_copy(
            src_ref=self.small.at[1 - self.section if k == 0 else self.section], dst_ref=self.arrived.at[k],
            send_sem=self.send_sem.at[k], recv_sem=self.recv_sem.at[k],
            device_id=self.partners[k], device_id_type=MESH)

    def tick(self, t):
        for k in range(len(self.partners) + 1):
            @pl.when(t == k)
            def _(k=k):
                if k > 0:
                    self.copy(k - 1).wait()
                    self.small[self.section] = self.small[self.section] + self.arrived[k - 1]
                if k < len(self.partners):
                    self.copy(k).start()

    @staticmethod
    def scratch(devices):
        n = 1 + len(sum(halvings(devices, CHUNK), []))
        return [pltpu.VMEM((2, 16, 512), F32), pltpu.VMEM((n, 16, 512), F32),
                pltpu.SemaphoreType.DMA((n,)), pltpu.SemaphoreType.DMA((n,))]


def tail_kernel(devices, plans, n_sums, *refs):
    section = lax.axis_index("section")
    refs = list(refs)
    take = lambda n: [refs.pop(0) for _ in range(n)]
    given = [[take(len(entry.arrays)) for entry in plan] for plan in plans]
    ffn_enc, ffn_dec, cross_enc, cross_dec, vec_enc, vec_dec = take(6)
    far_arrived, own_grad, sums_out, small_out = take(4)
    buffers = take(len(plans[0]))
    in_sem, out_sem, dx_send, dx_recv, far_dx, own_dx = take(6)
    dw, dln = take(2)
    vectors_scratch = take(4)
    sums_scratch = take(n_sums)

    groups = [
        (ffn_enc.shape[0], (ffn_enc, 0), (ffn_dec, 1)),
        (cross_enc.shape[0], (cross_enc, 0), (cross_dec, 1)),
        (4, (dw.at[0], 0), (dw.at[1], 1)),
    ]
    early = groups[0][0] + groups[1][0]
    sums = Sums(devices, groups, early, 0, sums_out, sums_scratch)
    vectors = Vectors(sums, vectors_scratch)
    greet([sums.across] + sums.mates)

    def fetch(layer, k):
        return Operand(plans[layer][k].copy(given[layer][k], buffers[k], in_sem.at[layer, k], section), buffers[k])

    second = [fetch(1, k) for k in range(len(buffers))]
    first = [None] * len(buffers)

    def reuse(*operands):
        for operand in operands:
            k = second.index(operand)
            first[k] = fetch(0, k)

    def put_dx(layer):
        def put(rows, value):
            @pl.when(section == layer)
            def _():
                own_dx[rows, :] = value

            @pl.when(section != layer)
            def _():
                far_dx[rows, :] = value.astype(BF)
        return put

    def ticks(base, without):
        return lambda k: None if k in without else sums.tick(base + k)

    self_backward(True, second, ticks(0, (5,)), 2, reuse, put_dx(1), dw.at[1], dln.at[1], *refs)
    self_backward(False, first, ticks(5, ()), 1, lambda *operands: None, put_dx(0), dw.at[0], dln.at[0], *refs)
    result = pltpu.make_async_copy(own_dx, own_grad, out_sem)
    result.start()
    vectors.small[0] = vec_enc[...] + dln[0]
    vectors.small[1] = vec_dec[...] + dln[1]
    far_copy = pltpu.make_async_remote_copy(
        src_ref=far_dx, dst_ref=far_arrived, send_sem=dx_send, recv_sem=dx_recv,
        device_id=sums.across, device_id_type=MESH)
    base = early + 1

    @pl.loop(base, sums.ticks)
    def _(t):
        sums.tick(t)
        vectors.tick(t - base)

        @pl.when(t == sums.chunks)
        def _():
            far_copy.start()

    small_out[...] = vectors.small[section]
    sums.finish()
    far_copy.wait()
    result.wait()


def backward_and_sums(first, second, groups, vectors, devices):
    plans = [[a if isinstance(a, Pick) else Pick(a) for a in operands] for operands in (first, second)]
    n, w = plans[0][1].shape
    chunks = sum(pair[0].shape[0] for pair in groups) + 4
    given = [array for plan in plans for entry in plan for array in entry.arrays]
    vm = pl.BlockSpec(memory_space=pltpu.VMEM)
    sums_scratch = Sums.scratch(devices, chunks)
    return pl.pallas_call(
        functools.partial(tail_kernel, devices, plans, len(sums_scratch)),
        out_shape=[
            jax.ShapeDtypeStruct((n, w), BF), jax.ShapeDtypeStruct((n, w), F32),
            jax.ShapeDtypeStruct((chunks, CHUNK, 512), BF), jax.ShapeDtypeStruct((16, 512), F32)],
        in_specs=[ANY] * (len(given) + 4) + [vm, vm],
        out_specs=[ANY] * 3 + [vm],
        scratch_shapes=[pltpu.VMEM(entry.shape, entry.dtype) for entry in plans[0]]
        + [pltpu.SemaphoreType.DMA((2, len(plans[0]))), pltpu.SemaphoreType.DMA, pltpu.SemaphoreType.DMA,
           pltpu.SemaphoreType.DMA, pltpu.VMEM((n, w), BF), pltpu.VMEM((n, w), F32)]
        + [pltpu.VMEM((2, 4, w, w), BF), pltpu.VMEM((2, 16, w), F32)]
        + Vectors.scratch(devices) + sums_scratch + bwd_scratch(n, w),
        compiler_params=pltpu.CompilerParams(collective_id=1, has_side_effects=True, vmem_limit_bytes=VMEM_LIMIT),
        name="backward_and_sums",
    )(*given, *[array for pair in groups for array in pair], *vectors)


def unpack_kernel(kinds, g_ref, mem_ref, out_ref, low_far_ref, grad_ref, grad_far_ref, s_ref, *refs):
    n = len(kinds)
    low_out, grad_out = refs[:2]
    outs = refs[2 : n + 2]
    b_in, b_out, gains, shifts = refs[n + 2 : n + 6]
    chunk, stage, in_sem, sem, low_buf, grad_buf, far_buf, row_in, row_out = refs[n + 6 :]
    section = lax.axis_index("section")
    chunks = chunk.shape[0]
    loads = [pltpu.make_async_copy(g_ref.at[c], chunk.at[c], in_sem.at[c]) for c in range(chunks)]
    fetch = [
        pltpu.make_async_copy(mem_ref, low_buf.at[0], row_in.at[0]),
        pltpu.make_async_copy(low_far_ref, low_buf.at[1], row_in.at[1]),
        pltpu.make_async_copy(grad_ref, grad_buf.at[0], row_in.at[2]),
        pltpu.make_async_copy(grad_far_ref, far_buf, row_in.at[3]),
    ]
    send = [
        pltpu.make_async_copy(low_buf.at[0], low_out.at[section], row_out.at[0]),
        pltpu.make_async_copy(low_buf.at[1], low_out.at[1 - section], row_out.at[1]),
        pltpu.make_async_copy(grad_buf.at[0], grad_out.at[section], row_out.at[2]),
        pltpu.make_async_copy(grad_buf.at[1], grad_out.at[1 - section], row_out.at[3]),
    ]
    for c in range(4):
        loads[c].start()
    for one in fetch[1:]:
        one.start()

    @pl.when(section == 0)
    def _():
        fetch[0].start()

    @pl.when(section != 0)
    def _():
        pltpu.make_async_copy(out_ref, low_buf.at[0], row_in.at[0]).start()

    for c in range(4, chunks):
        loads[c].start()
    for k in range(4):
        b_in[:, k * 512 : (k + 1) * 512] = s_ref[k : k + 1, :]
    b_out[...] = s_ref[4:5, :]
    for k in range(3):
        gains[k] = s_ref[5 + k : 6 + k, :]
        shifts[k] = s_ref[8 + k : 9 + k, :]

    slots = stage.shape[0]
    copies, c = [], 0
    for kind, (count, flipped, axis) in enumerate(kinds):
        for k in range(count):
            at = slice(k * 512, k * 512 + 512)
            dst = outs[kind].at[:, at] if axis else outs[kind].at[at, :]
            copies.append(pltpu.make_async_copy(stage.at[c % slots], dst, sem.at[c % slots]))
            loads[c].wait()
            if c >= slots:
                copies[c - slots].wait()
            value = chunk[c].astype(F32)
            stage[c % slots] = value.T if flipped else value
            copies[c].start()
            if c < 4:
                fetch[c].wait()
                if c == 3:
                    grad_buf[1] = far_buf[...].astype(F32)
                send[c].start()
            c += 1
    for copy in copies[-slots:] + send:
        copy.wait()


def unpack(g, low, low_far, grad, grad_far, vectors, kinds, shapes):
    n, w = low_far.shape
    vm = pl.BlockSpec(memory_space=pltpu.VMEM)
    vector_shapes = [(1, 4 * w), (1, w), (3, 1, w), (3, 1, w)]
    return pl.pallas_call(
        functools.partial(unpack_kernel, kinds),
        out_shape=[jax.ShapeDtypeStruct((2, n, w), BF), jax.ShapeDtypeStruct((2, n, w), F32)]
        + [jax.ShapeDtypeStruct(s, F32) for s in shapes + vector_shapes],
        in_specs=[ANY] * 6 + [vm],
        out_specs=[ANY] * (len(shapes) + 2) + [vm] * 4,
        scratch_shapes=[
            pltpu.VMEM(g.shape, BF), pltpu.VMEM((6, 512, 512), F32),
            pltpu.SemaphoreType.DMA((g.shape[0],)), pltpu.SemaphoreType.DMA((6,)),
            pltpu.VMEM((2, n, w), BF), pltpu.VMEM((2, n, w), F32), pltpu.VMEM((n, w), BF),
            pltpu.SemaphoreType.DMA((4,)), pltpu.SemaphoreType.DMA((4,)),
        ],
        compiler_params=pltpu.CompilerParams(vmem_limit_bytes=VMEM_LIMIT),
        name="unpack_results",
    )(g, *low, low_far, grad, grad_far, vectors)


class Spread:
    def __init__(self, devices, weights, land, send_sem, recv_sem):
        self.weights, self.land, self.send_sem, self.recv_sem = weights, land, send_sem, recv_sem
        self.index, self.section = lax.axis_index("dp"), lax.axis_index("section")
        self.bits = halvings(devices, 512)[0]
        self.across = (1 - self.section, self.index)
        self.mates = [(self.section, partner_of(self.index, bit)) for bit in self.bits]
        self.chunks = []
        for w, ref in enumerate(weights):
            rows, cols = ref.shape
            self.chunks += [(w, r, c) for r in range(0, rows, 512) for c in range(0, cols, 512)]
        self.steps = len(self.bits) + 1
        self.ticks = len(self.chunks) + self.steps - 1

    def copy(self, c, step, src=None):
        if step == 0:
            count, device = len(self.bits), self.across
        else:
            bit = self.bits[len(self.bits) - step]
            count, device = bit + 1, self.mates[bit]
        at, size = place(self.index, count, 512)
        part = self.land.at[c, pl.ds(pl.multiple_of(at, 16), size)]
        return pltpu.make_async_remote_copy(
            src_ref=part if src is None else src, dst_ref=part, send_sem=self.send_sem.at[step, c],
            recv_sem=self.recv_sem.at[step, c], device_id=device, device_id_type=MESH)

    def begin(self, c):
        w, r, col = self.chunks[c]
        at, size = place(self.index, len(self.bits), 512)
        self.copy(c, 0, self.weights[w].at[pl.ds(pl.multiple_of(r + at, 16), size), col : col + 512]).start()

    def tick(self, t):
        for step in range(1, self.steps + 1):
            c = t - step + 1

            @pl.when((c >= 0) & (c < len(self.chunks)))
            def _(step=step, c=c):
                self.copy(c, step - 1).wait_recv()
                if step < self.steps:
                    self.copy(c, step).start()

    def finish(self):
        @pl.loop(0, len(self.chunks))
        def _(c):
            for step in range(self.steps):
                self.copy(c, step).wait_send()


def head_kernel(devices, plan, shapes, *refs):
    refs = list(refs)
    take = lambda n: [refs.pop(0) for _ in range(n)]
    given = [take(len(entry.arrays)) for entry in plan]
    tokens, *weights = take(6)
    b_in, b_out, gains, shifts = take(4)
    outs = take(2 * len(shapes))
    far_tokens, own_vectors, far_vectors, *far = take(8)
    buffers = take(len(plan))
    results = [Result(None, ref) for ref in take(2 * len(shapes))]
    in_sem, out_sem, far_x, small_ref, far_small, swap_send, swap_recv, keep_sem = take(8)
    land, send_sem, recv_sem, flush_sem = take(4)
    section = lax.axis_index("section")
    spread = Spread(devices, weights, land, send_sem, recv_sem)
    own = [Operand(entry.copy(ref, buffers[k], in_sem.at[k], section), buffers[k])
           for k, (entry, ref) in enumerate(zip(plan, given))]
    for k, result in enumerate(results):
        result.copy = pltpu.make_async_copy(result.ref, outs[k], out_sem.at[k])
    small_ref[...] = jnp.zeros(small_ref.shape, F32)
    for k in range(4):
        small_ref[k : k + 1, :] = b_in[:, k * 512 : (k + 1) * 512]
    small_ref[4:5, :] = b_out[...]
    for k in range(3):
        small_ref[5 + k : 6 + k, :] = gains[k]
        small_ref[8 + k : 9 + k, :] = shifts[k]
    greet([spread.across] + spread.mates)
    for c in range(len(spread.chunks)):
        spread.begin(c)
    swaps = [
        pltpu.make_async_remote_copy(
            src_ref=src, dst_ref=dst, send_sem=swap_send.at[k], recv_sem=swap_recv.at[k],
            device_id=spread.across, device_id_type=MESH)
        for k, (src, dst) in enumerate([(small_ref, far_small), (tokens.at[1 - section], far_x)])
    ]
    for one in swaps:
        one.start()

    def flush(c):
        w, r, col = spread.chunks[c]
        return pltpu.make_async_copy(land.at[c], far[w].at[r : r + 512, col : col + 512], flush_sem.at[c])

    x_ref, w_ref, wout_ref, ids_ref, far_ids = ready(*own)
    width = x_ref.shape[1]
    n = len(shapes)
    self_forward(section == 1, x_ref, ids_ref,
                 [w_ref.at[:, k * width : (k + 1) * width] for k in range(3)] + [wout_ref],
                 small_ref, results[:n], spread.tick, *refs)
    for one in swaps:
        one.wait()
    keep = [
        pltpu.make_async_copy(src, dst, keep_sem.at[k])
        for k, (src, dst) in enumerate([(far_x, far_tokens), (small_ref, own_vectors), (far_small, far_vectors)])
    ]
    for one in keep:
        one.start()
    self_forward(section == 0, far_x, far_ids, [land.at[k] for k in range(4)], far_small, results[n:],
                 lambda k: spread.tick(8 + k), *refs)
    done = 15 - spread.steps + 1
    for c in range(done + 1):
        flush(c).start()
    for t in range(16, spread.ticks):
        spread.tick(t)
        flush(t - spread.steps + 1).start()
    spread.finish()
    for c in range(len(spread.chunks)):
        flush(c).wait()
    for one in keep:
        one.wait()
    for result in results:
        result.copy.wait()


def forward_and_weights(own, tokens, vectors, weights, devices):
    plan = [a if isinstance(a, Pick) else Pick(a) for a in own]
    n, w = plan[0].shape
    shapes = [((w, n), BF), ((n, w), BF), ((n, w), BF), ((w, n), BF), ((HEADS, n), F32), ((n, w), BF), ((n, w), BF)]
    given = [array for entry in plan for array in entry.arrays] + [tokens, *weights]
    steps = len(halvings(devices, 512)[0]) + 1
    count = sum(a.size for a in weights) // 512**2
    dma = pltpu.SemaphoreType.DMA
    outs = pl.pallas_call(
        functools.partial(head_kernel, devices, plan, shapes),
        out_shape=[jax.ShapeDtypeStruct(s, d) for s, d in shapes * 2]
        + [jax.ShapeDtypeStruct((n, w), BF)] + [jax.ShapeDtypeStruct((16, w), F32)] * 2
        + [jax.ShapeDtypeStruct(a.shape, BF) for a in weights],
        in_specs=[ANY] * len(given) + [pl.BlockSpec(memory_space=pltpu.VMEM)] * 4,
        out_specs=[ANY] * (2 * len(shapes) + 8),
        scratch_shapes=[pltpu.VMEM(entry.shape, entry.dtype) for entry in plan]
        + [pltpu.VMEM(s, d) for s, d in shapes * 2]
        + [dma((len(plan),)), dma((2 * len(shapes),)), pltpu.VMEM((n, w), BF),
           pltpu.VMEM((16, w), F32), pltpu.VMEM((16, w), F32), dma((2,)), dma((2,)), dma((3,))]
        + [pltpu.VMEM((count, 512, 512), BF), dma((steps, count)), dma((steps, count)), dma((count,))]
        + fwd_scratch(n, w),
        compiler_params=pltpu.CompilerParams(collective_id=0, has_side_effects=True, vmem_limit_bytes=VMEM_LIMIT),
        name="forward_and_weights",
    )(*given, *vectors)
    k = len(shapes)
    return outs[:k], outs[k : 2 * k], outs[2 * k], outs[2 * k + 1], outs[2 * k + 2], outs[2 * k + 3 :]


def shards(layer_input, cotangent, src_segments, tgt_segments, attn_qkv, attn_out, cross_proj,
           ffn_in, ffn_in_bias, ffn_out, ffn_out_bias, norm_gain, norm_bias):
    devices = lax.axis_size("dp")
    swap = lambda a: lax.ppermute(a, "section", [(0, 1), (1, 0)])
    vectors = [ffn_in_bias, ffn_out_bias, norm_gain.transpose(1, 0, 2), norm_bias.transpose(1, 0, 2)]
    tokens = layer_input[0, :, 0]
    near = (attn_qkv[0], attn_out[0], cross_proj[0], ffn_in[0], ffn_out[0])
    src, tgt, cot = Row(src_segments), Row(tgt_segments), Row(cotangent[:, 0])
    (*own_saved, own_hid), (*far_saved, far_hid), far_tokens, vectors, far_vectors, far = forward_and_weights(
        [Row(tokens), near[0], near[1], Pick(src, tgt), Pick(tgt, src)], tokens, vectors, near, devices)
    enc = [Pick(a, b) for a, b in zip(near, far)]
    dec = [Pick(b, a) for a, b in zip(near, far)]
    enc_small, dec_small = Pick(vectors, far_vectors), Pick(far_vectors, vectors)
    src, tgt, cot = Pick(src), Pick(tgt), Pick(cot)
    e1, d1 = Pick(own_hid, far_hid), Pick(far_hid, own_hid)
    g, gp, r2, mem, kv = enc_ffn_fwd(e1, enc[3], enc[4], enc_small, enc[2])
    cq, catt, clse, cr, d2 = cross_fwd(d1, kv, tgt, src, dec[2], dec_small)
    out, away, dres, dw_dffn, s_dffn = dec_ffn(d2, cr, cot, dec[3], dec[4], dec_small, mem)
    low_far = swap(away)
    dh1, dmem, dw_dcross, dw_ecross = cross_bwd(dres, d1, mem, tgt, src, cq, kv, catt, clse, dec[2], enc[2])
    de1, dw_effn, s_effn = enc_ffn_bwd(dmem, r2, g, gp, e1, enc[3], enc[4], enc_small)
    de1, low_far = lax.optimization_barrier((de1, low_far))

    def operands(dh, saved, tokens, ids, weights, small):
        qT, k, v, att, lse, res = saved
        return [dh, res, tokens, ids, qT, k, v, att, lse, weights[0], weights[1], small]

    far_grad, own_grad, sums, s = backward_and_sums(
        operands(de1, [Pick(a, b) for a, b in zip(own_saved, far_saved)], Pick(Row(tokens), far_tokens), src, enc, enc_small),
        operands(dh1, [Pick(b, a) for a, b in zip(own_saved, far_saved)], Pick(far_tokens, Row(tokens)), tgt, dec, dec_small),
        [(dw_effn, dw_dffn), (dw_ecross, dw_dcross)], (s_effn, s_dffn), devices)
    kinds = ((4, False, 1), (4, True, 0), (2, True, 1), (3, True, 1), (1, False, 0))
    layer_output, input_grad, win, wout, cross, qkv, wo, b_in, b_out, gains, shifts = unpack(
        sums, (mem, out), low_far, own_grad, far_grad, s, kinds,
        [ffn_in.shape[1:], ffn_out.shape[1:], cross_proj.shape[1:], attn_qkv.shape[1:], attn_out.shape[1:]])
    return (layer_output[None, :, None], input_grad[None, :, None], qkv[None], wo[None], cross[None], win[None],
            b_in, wout[None], b_out, gains.transpose(1, 0, 2), shifts.transpose(1, 0, 2))


def solution(mesh):
    return jax.shard_map(
        shards,
        mesh=mesh,
        in_specs=(
            P("section", None, "dp", None, None),
            P(None, "dp", None, None),
            P(None, "dp", None),
            P(None, "dp", None),
            P("section", None, None),
            P("section", None, None),
            P("section", None, None),
            P("section", None, None),
            P("section", None),
            P("section", None, None),
            P("section", None),
            P("section", None, None),
            P("section", None, None),
        ),
        out_specs=(
            P("section", None, "dp", None, None),
            P("section", None, "dp", None, None),
            P("section", None, None),
            P("section", None, None),
            P("section", None, None),
            P("section", None, None),
            P("section", None),
            P("section", None, None),
            P("section", None),
            P("section", None, None),
            P("section", None, None),
        ),
        check_vma=False,
    )
```

```python
import functools
import math

import jax
import jax.numpy as jnp
from jax import lax
from jax.experimental import pallas as pl
from jax.experimental.pallas import tpu as pltpu
from jax.sharding import PartitionSpec as P

HEADS = 8
EPSILON = 1e-05
NEGATIVE = -1000000000.0
BF = jnp.bfloat16
F32 = jnp.float32
LOG2E = 1.4426950408889634
QB = 256
UNIT = 128
WIDE = 256
TB = 256
FB = 256
VMEM_LIMIT = 60 * 1024 * 1024


def dot(left, right, lc=1, rc=0):
    return lax.dot_general(
        left, right, (((lc,), (rc,)), ((), ())), preferred_element_type=F32
    )


def norm_stats(value):
    centered = value - jnp.mean(value, axis=-1, keepdims=True)
    spread = jnp.mean(centered * centered, axis=-1, keepdims=True)
    scale = lax.rsqrt(spread + EPSILON)
    return centered * scale, scale


def norm_back(out_grad, unit, scale, gain):
    gain_grad = jnp.sum(out_grad * unit, axis=0, keepdims=True)
    shift_grad = jnp.sum(out_grad, axis=0, keepdims=True)
    inner = out_grad * gain
    mean_one = jnp.mean(inner, axis=-1, keepdims=True)
    mean_two = jnp.mean(inner * unit, axis=-1, keepdims=True)
    return scale * (inner - mean_one - unit * mean_two), gain_grad, shift_grad


def gelu_pair(u):
    phi = 0.5 + 0.5 * lax.erf(u * (1.0 / math.sqrt(2.0)))
    bell = jnp.exp(-0.5 * u * u) * (1.0 / math.sqrt(2.0 * math.pi))
    return u * phi, phi + u * bell


def gain_of(small, norm):
    return small[5 + norm : 6 + norm, :]


def shift_of(small, norm):
    return small[8 + norm : 9 + norm, :]


def key_codes(ids_row, length):
    column = jnp.broadcast_to(ids_row.astype(F32), (128, length)).T
    lane = lax.broadcasted_iota(jnp.int32, (length, 128), 1)
    spot = jnp.where(lane < 64, lane, lane - 64)
    codes = jnp.where(
        spot < 4,
        jnp.where(column == spot.astype(F32), 0.0, NEGATIVE),
        jnp.where(spot < 7, -1.0, 0.0),
    )
    return codes, lane < 64


def fill_keys(dst, keys_ref, codes, low_half):
    for pair in range(HEADS // 2):
        slab = keys_ref[:, pair * 128 : pair * 128 + 128].astype(F32)
        dst[2 * pair] = jnp.where(low_half, slab, codes).astype(BF)
        dst[2 * pair + 1] = jnp.where(low_half, codes, slab).astype(BF)


def query_rows(head):
    return (0, 64) if head % 2 == 0 else (64, 0)


def key_range(query_ids, key_ids, qb):
    ids = query_ids[:, pl.ds(pl.multiple_of(qb * QB, QB), QB)].astype(F32)
    keys = key_ids[...].astype(F32)
    start = jnp.sum((keys < jnp.min(ids)).astype(F32)).astype(jnp.int32)
    stop = jnp.sum((keys <= jnp.max(ids)).astype(F32)).astype(jnp.int32)
    return start // UNIT, (stop + UNIT - 1) // UNIT


def visit_keys(query_ids, key_ids, qb, step):
    lo, hi = key_range(query_ids, key_ids, qb)
    count = hi - lo

    @pl.loop(0, count // 2)
    def _(i):
        step(lo + 2 * i, WIDE, False)

    @pl.when(count % 2 == 1)
    def _():
        step(hi - 1, UNIT, False)


def below_diagonal():
    return lax.broadcasted_iota(jnp.int32, (WIDE, QB), 0) <= lax.broadcasted_iota(jnp.int32, (WIDE, QB), 1)


def staged(first, lag_one, second, lag_two, third):
    for i in range(HEADS + lag_one + lag_two):
        if i < HEADS:
            first(i)
        if 0 <= i - lag_one < HEADS:
            second(i - lag_one)
        if 0 <= i - lag_one - lag_two < HEADS:
            third(i - lag_one - lag_two)


def attend_loop(visit, after, qaug, kaug, vt, attT_ref, lse_ref, oacc, mrow, lrow, sbuf, pbuf, length):
    @pl.loop(0, length // QB)
    def _(qb):
        q = pl.ds(pl.multiple_of(qb * QB, QB), QB)
        oacc[...] = jnp.zeros_like(oacc)
        mrow[...] = jnp.full_like(mrow, -3e38)
        lrow[...] = jnp.zeros_like(lrow)

        def step(unit, size, masked):
            ks = pl.ds(pl.multiple_of(unit * UNIT, UNIT), size)
            scale = {}

            def scores(h):
                s = dot(kaug[h, ks, :], qaug[h, :, q])
                sbuf[h, :size] = jnp.where(below_diagonal(), s, NEGATIVE) if masked else s

            def softmax(h):
                s = sbuf[h, :size]
                m_old = mrow[h : h + 1, :]
                m_new = jnp.maximum(m_old, jnp.max(s, axis=0, keepdims=True))
                scale[h] = jnp.exp2(m_old - m_new)
                p = jnp.exp2(s - m_new)
                lrow[h : h + 1, :] = lrow[h : h + 1, :] * scale[h] + jnp.sum(p, axis=0, keepdims=True)
                mrow[h : h + 1, :] = m_new
                pbuf[h, :size] = p.astype(BF)

            def mix(h):
                hs = slice(h * 64, h * 64 + 64)
                oacc[hs, :] = oacc[hs, :] * scale[h] + dot(vt[hs, ks], pbuf[h, :size])

            staged(scores, 7, softmax, 1, mix)

        visit(qb, step)
        for h in range(HEADS):
            hs = slice(h * 64, h * 64 + 64)
            attT_ref[hs, q] = (oacc[hs, :] * (1.0 / lrow[h : h + 1, :])).astype(BF)
        lse_ref[:, q] = mrow[...] + jnp.log2(lrow[...])
        after(qb)


def query_codes(ids_row, length):
    row = lax.broadcasted_iota(jnp.int32, (16, length), 0)
    return jnp.where(row == jnp.broadcast_to(ids_row, (16, length)), 1.0, 0.0), row


def fill_queries(qaug, qT_ref, codes, row, lse_ref, length):
    for h in range(HEADS):
        a, b = query_rows(h)
        qaug[h, a : a + 64, :] = qT_ref[h * 64 : h * 64 + 64, :]
        extra = codes
        if lse_ref is not None:
            lse = lse_ref[h : h + 1, :]
            hi = lse.astype(BF).astype(F32)
            mid = (lse - hi).astype(BF).astype(F32)
            low = lse - hi - mid
            extra = jnp.where(row == 4, hi, jnp.where(row == 5, mid, jnp.where(row == 6, low, codes)))
        qaug[h, b : b + 16, :] = extra.astype(BF)
        qaug[h, b + 16 : b + 64, :] = jnp.zeros((48, length), BF)


def project_queries(src_ref, w_ref, qT_ref, length, width):
    @pl.loop(0, length // TB)
    def _(t):
        rows = pl.ds(pl.multiple_of(t * TB, TB), TB)
        q = dot(src_ref[rows, :], w_ref[:, :width]) * (0.125 * LOG2E)
        qT_ref[:, rows] = q.T.astype(BF)


def out_and_norm(attT_ref, w_ref, resid_ref, sm_ref, norm, res_ref, hid_ref, length):
    @pl.loop(0, length // TB)
    def _(t):
        rows = pl.ds(pl.multiple_of(t * TB, TB), TB)
        a = dot(attT_ref[:, rows], w_ref[...], 0, 0)
        r = resid_ref[rows, :].astype(F32) + a
        res_ref[rows, :] = r.astype(BF)
        unit, _ = norm_stats(r)
        hid_ref[rows, :] = (unit * gain_of(sm_ref, norm) + shift_of(sm_ref, norm)).astype(BF)


def self_forward(causal, x_ref, ids_ref, weights, small_ref, results, tick,
                 kaug, qaug, vt, oacc, mrow, lrow, sbuf, pbuf):
    wq, wk, wv, wout = weights
    qT_ref, k_ref, v_ref, attT_ref, lse_ref, res_ref, hid_ref = results
    length, width = x_ref.shape
    tick(0)

    @pl.loop(0, length // TB)
    def _(t):
        rows = pl.ds(pl.multiple_of(t * TB, TB), TB)
        x = x_ref[rows, :]
        q = dot(x, wq[...]) * (0.125 * LOG2E)
        k = dot(x, wk[...])
        v = dot(x, wv[...])
        qT_ref[:, rows] = q.T.astype(BF)
        k_ref[rows, :] = k.astype(BF)
        v_ref[rows, :] = v.astype(BF)
        vt[:, rows] = v.T.astype(BF)

    for result in (qT_ref, k_ref, v_ref):
        result.flush()
    tick(1)
    codes, low_half = key_codes(ids_ref[...], length)
    fill_keys(kaug, k_ref, codes, low_half)
    qcodes, row = query_codes(ids_ref[...], length)
    fill_queries(qaug, qT_ref, qcodes, row, None, length)
    tick(2)
    attend_loop(functools.partial(visit_all, causal), lambda qb: tick(3 + qb), qaug, kaug, vt, attT_ref, lse_ref,
                oacc, mrow, lrow, sbuf, pbuf, length)
    attT_ref.flush()
    lse_ref.flush()
    tick(7)
    out_and_norm(attT_ref, wout, x_ref, small_ref, 0, res_ref, hid_ref, length)
    res_ref.flush()
    hid_ref.flush()


def cross_fwd_kernel(h_ref, kv_ref, qids_ref, kids_ref, w_ref, ln_ref,
                     qT_ref, attT_ref, lse_ref, res_ref, hid_ref,
                     kaug, qaug, vt, oacc, mrow, lrow, sbuf, pbuf):
    h_ref, w_ref = ready(h_ref, w_ref)
    length, width = h_ref.shape
    project_queries(h_ref, w_ref, qT_ref, length, width)
    qT_ref.flush()
    kv_ref, qids_ref, kids_ref = ready(kv_ref, qids_ref, kids_ref)

    @pl.loop(0, length // TB)
    def _(t):
        rows = pl.ds(pl.multiple_of(t * TB, TB), TB)
        vt[:, rows] = kv_ref[rows, width:].astype(F32).T.astype(BF)

    codes, low_half = key_codes(kids_ref[...], length)
    fill_keys(kaug, kv_ref, codes, low_half)
    qcodes, row = query_codes(qids_ref[...], length)
    fill_queries(qaug, qT_ref, qcodes, row, None, length)
    attend_loop(functools.partial(visit_keys, qids_ref, kids_ref), lambda qb: None, qaug, kaug, vt, attT_ref, lse_ref,
                oacc, mrow, lrow, sbuf, pbuf, length)
    attT_ref.flush()
    lse_ref.flush()
    (ln_ref,) = ready(ln_ref)
    out_and_norm(attT_ref, w_ref.at[:, width:], h_ref, ln_ref, 1, res_ref, hid_ref, length)


def visit_all(causal, qb, step):
    blocks = 1024 // WIDE
    lo = jnp.where(qb == blocks - 1, 1, 0)
    hi = jnp.where(qb == 0, blocks - 1, blocks)
    if causal is not False:
        lo, hi = jnp.where(causal, 0, lo), jnp.where(causal, qb, hi)

    @pl.loop(lo, hi)
    def _(i):
        step(i * (WIDE // UNIT), WIDE, False)

    if causal is not False:
        @pl.when(causal)
        def _():
            step(qb * (QB // UNIT), WIDE, True)


def attend_back_block(visit, qb, qaug, kaug, kt, vaug, doaug, jgT, jg, dqacc, sbuf, dbuf, pbuf, gbuf):
    width = HEADS * 64
    q = pl.ds(pl.multiple_of(qb * QB, QB), QB)
    dqacc[...] = jnp.zeros_like(dqacc)

    def step(unit, size, masked):
        ks = pl.ds(pl.multiple_of(unit * UNIT, UNIT), size)

        def products(h):
            s = dot(kaug[h, ks, :], qaug[h, :, q])
            sbuf[h % 4, :size] = jnp.where(below_diagonal(), s, NEGATIVE) if masked else s
            dbuf[h % 4, :size] = dot(vaug[h, ks, :], doaug[h, :, q])

        def grads(h):
            p = jnp.exp2(sbuf[h % 4, :size])
            pbuf[h % 4, :size] = p.astype(BF)
            gbuf[h % 4, :size] = (p * dbuf[h % 4, :size]).astype(BF)

        def add(h):
            a, _ = query_rows(h)
            at = h * 64
            hs = slice(at, at + 64)
            dqacc[hs, :] += dot(kt[hs, ks], gbuf[h % 4, :size])
            jgT[width + at : width + at + 64, ks] += dot(doaug[h, a : a + 64, q], pbuf[h % 4, :size], 1, 1)
            jgT[at : at + 64, ks] += dot(qaug[h, a : a + 64, q], gbuf[h % 4, :size], 1, 1)

        lag = 1 if size == WIDE else 2
        staged(products, lag, grads, lag, add)

    visit(qb, step)
    jg[:width, q] = (dqacc[...] * 0.125).astype(BF)


def attend_back_finish(jgT, jg):
    width = HEADS * 64
    jg[width : 2 * width, :] = (jgT[:width, :] * math.log(2.0)).astype(BF)
    jg[2 * width :, :] = jgT[width:, :].astype(BF)


def prepare_back(dr_ref, w_ref, attT_ref, doaug, length):
    @pl.loop(0, length // TB)
    def _(t):
        rows = pl.ds(pl.multiple_of(t * TB, TB), TB)
        row = lax.broadcasted_iota(jnp.int32, (16, TB), 0)
        d = dot(w_ref[...], dr_ref[rows, :], 1, 1).astype(BF)
        for h in range(HEADS):
            a, b = query_rows(h)
            hs = slice(h * 64, h * 64 + 64)
            doh = d[hs, :]
            doaug[h, a : a + 64, rows] = doh
            delta = jnp.sum(doh.astype(F32) * attT_ref[hs, rows].astype(F32), axis=0, keepdims=True)
            hi = delta.astype(BF).astype(F32)
            mid = (delta - hi).astype(BF).astype(F32)
            low = delta - hi - mid
            extra = jnp.where(row == 4, hi, jnp.where(row == 5, mid, jnp.where(row == 6, low, 0.0)))
            doaug[h, b : b + 16, rows] = extra.astype(BF)
            doaug[h, b + 16 : b + 64, rows] = jnp.zeros((48, TB), BF)


def prepare_keys(keys_ref, values_ref, codes, low_half, kaug, kt, vaug, length):
    fill_keys(kaug, keys_ref, codes, low_half)
    fill_keys(vaug, values_ref, jnp.where(codes == NEGATIVE, 0.0, codes), low_half)

    @pl.loop(0, length // TB)
    def _(t):
        rows = pl.ds(pl.multiple_of(t * TB, TB), TB)
        kt[:, rows] = keys_ref[rows, :].astype(F32).T.astype(BF)


def self_backward_phases(causal, operands, arrived, reuse, put_dx, dw_ref, dln_ref,
                         kaug, kt, vaug, qaug, doaug, dqacc, jgT, jg, sbuf, dbuf, pbuf, gbuf):
    dh_ref, res_ref, x_ref, ids_ref, qT_ref, k_ref, v_ref, attT_ref, lse_ref, w_ref, wout_ref, ln_ref = operands
    dh, res, x, ids, qT, keys, values, attT, lse, w, wout, small = range(len(operands))
    length, width = res_ref.shape
    dr = res_ref

    def before():
        arrived(dh, res, small)
        dln_ref[...] = jnp.zeros(dln_ref.shape, F32)

        @pl.loop(0, length // TB)
        def _(t):
            rows = pl.ds(pl.multiple_of(t * TB, TB), TB)
            unit, scale = norm_stats(res_ref[rows, :].astype(F32))
            d, gg, sg = norm_back(dh_ref[rows, :].astype(F32), unit, scale, gain_of(ln_ref, 0))
            dln_ref[5:6, :] += gg
            dln_ref[8:9, :] += sg
            dr[rows, :] = d.astype(BF)

        arrived(attT, wout, ids)
        dw_ref[3] = dot(attT_ref[...], dr[...]).astype(BF)
        prepare_back(dr, wout_ref, attT_ref, doaug, length)

    def block(qb):
        attend_back_block(functools.partial(visit_all, causal), qb, qaug, kaug, kt, vaug, doaug,
                          jgT, jg, dqacc, sbuf, dbuf, pbuf, gbuf)

    def fill():
        codes, low_half = key_codes(ids_ref[...], length)
        arrived(keys, values, qT, lse)
        prepare_keys(k_ref, v_ref, codes, low_half, kaug, kt, vaug, length)
        qcodes, row = query_codes(ids_ref[...], length)
        fill_queries(qaug, qT_ref, qcodes, row, lse_ref, length)
        jgT[...] = jnp.zeros_like(jgT)

    def after():
        reuse(dh, ids, qT, keys, values, attT, lse, wout, small)
        attend_back_finish(jgT, jg)
        arrived(x, w)

        @pl.loop(0, 3)
        def _(t):
            rows = pl.ds(pl.multiple_of(t * 512, 512), 512)
            dw_ref[t] = dot(jg[rows, :], x_ref[...]).astype(BF)

        @pl.loop(0, length // TB)
        def _(t):
            rows = pl.ds(pl.multiple_of(t * TB, TB), TB)
            put_dx(rows, dr[rows, :].astype(F32) + dot(jg[:, rows], w_ref[...], 0, 1))

        reuse(res, x, w)

    return before, fill, block, after


def cross_bwd_kernel(dr_ref, h_ref, mem_ref, qids_ref, kids_ref, qT_ref, kv_ref, attT_ref,
                     lse_ref, w_ref, wkv_ref,
                     dh_ref, dmem_ref, dwd_ref, dwe_ref,
                     kaug, kt, vaug, qaug, doaug, dqacc, jgT, jg, sbuf, dbuf, pbuf, gbuf):
    dr_ref, attT_ref, w_ref, qids_ref, kids_ref = ready(dr_ref, attT_ref, w_ref, qids_ref, kids_ref)
    length, width = dr_ref.shape
    dwd_ref[1] = dot(dr_ref[...], attT_ref[...], 0, 1).astype(BF)
    prepare_back(dr_ref, w_ref.at[:, width:], attT_ref, doaug, length)
    codes, low_half = key_codes(kids_ref[...], length)
    kv_ref, qT_ref, lse_ref = ready(kv_ref, qT_ref, lse_ref)
    prepare_keys(kv_ref.at[:, :width], kv_ref.at[:, width:], codes, low_half, kaug, kt, vaug, length)
    qcodes, row = query_codes(qids_ref[...], length)
    fill_queries(qaug, qT_ref, qcodes, row, lse_ref, length)
    jgT[...] = jnp.zeros_like(jgT)

    @pl.loop(0, length // QB)
    def _(qb):
        attend_back_block(functools.partial(visit_keys, qids_ref, kids_ref), qb, qaug, kaug, kt, vaug,
                          doaug, jgT, jg, dqacc, sbuf, dbuf, pbuf, gbuf)

    attend_back_finish(jgT, jg)
    h_ref, mem_ref, wkv_ref = ready(h_ref, mem_ref, wkv_ref)
    dwd_ref[0] = dot(jg[:width, :], h_ref[...]).astype(BF)
    for half in range(2):
        dwe_ref[half] = dot(jg[(half + 1) * width : (half + 2) * width, :], mem_ref[...]).astype(BF)
    dwd_ref.flush()
    dwe_ref.flush()

    @pl.loop(0, length // TB)
    def _(t):
        rows = pl.ds(pl.multiple_of(t * TB, TB), TB)
        d = dot(jg[:width, rows], w_ref[:, :width], 0, 1)
        dh_ref[rows, :] = (dr_ref[rows, :].astype(F32) + d).astype(BF)
        dmem_ref[rows, :] = dot(jg[width:, rows], wkv_ref[...], 0, 1).astype(BF)


def enc_ffn_fwd_kernel(e1_ref, win_ref, ln_ref, wout_ref, wkv_ref,
                       g_ref, gp_ref, r_ref, mem_ref, kv_ref, ubuf):
    e1_ref, win_ref, ln_ref = ready(e1_ref, win_ref, ln_ref)
    length, width = e1_ref.shape
    ff = win_ref.shape[1]
    slabs = ff // 512
    late = []
    later = (wout_ref, wkv_ref)

    def at(i):
        b, j = divmod(i, slabs)
        return slice(b * FB, b * FB + FB), slice(j * 512, j * 512 + 512), j

    def up(i):
        rows, cols, j = at(i)
        ubuf[i % 4] = dot(e1_ref[rows, :], win_ref[:, cols])

    def act(i):
        rows, cols, j = at(i)
        g, gp = gelu_pair(ubuf[i % 4] + ln_ref[j : j + 1, :])
        g_ref[rows, cols] = g.astype(BF)
        gp_ref[rows, cols] = gp.astype(BF)

    def down(b):
        rows = slice(b * FB, b * FB + FB)
        if not late:
            late.extend(ready(*later))
        total = dot(g_ref[rows, :], late[0][...]) + e1_ref[rows, :].astype(F32) + ln_ref[4:5, :]
        r_ref[rows, :] = total.astype(BF)
        unit, _ = norm_stats(total)
        e2 = unit * gain_of(ln_ref, 1) + shift_of(ln_ref, 1)
        unit, _ = norm_stats(e2)
        mem_ref[rows, :] = (unit * gain_of(ln_ref, 2) + shift_of(ln_ref, 2)).astype(BF)

    def project(b):
        rows = slice(b * FB, b * FB + FB)
        kv_ref[rows, :] = dot(mem_ref[rows, :], late[1][...]).astype(BF)
        for result in (g_ref, gp_ref, r_ref, mem_ref, kv_ref):
            result.flush_rows(b, FB)

    units = length // FB * slabs
    for tick in range(units + 4):
        if tick < units:
            up(tick)
        i = tick - 2
        if 0 <= i < units:
            act(i)
            if i % slabs == slabs - 1:
                down(i // slabs)
        i = tick - 4
        if 0 <= i < units and i % slabs == slabs - 1:
            project(i // slabs)
    for result in (g_ref, gp_ref, r_ref, mem_ref, kv_ref):
        result.started = True


def weight_grads(act_ref, du_ref, df_ref, g_ref, dw_ref):
    slabs = du_ref.shape[1] // 512

    @pl.loop(0, slabs)
    def _(t):
        cols = pl.ds(pl.multiple_of(t * 512, 512), 512)
        dw_ref[t] = dot(act_ref[...], du_ref[:, cols], 0, 0).astype(BF)
        dw_ref.flush_part(t)
        dw_ref[slabs + t] = dot(df_ref[...], g_ref[:, cols], 0, 0).astype(BF)
        dw_ref.flush_part(slabs + t)

    dw_ref.started = True


def enc_ffn_bwd_kernel(dmem_ref, r_ref, ln_ref, wout_ref, gp_ref, win_ref, e1_ref, g_ref,
                       de1_ref, dw_ref, dln_ref,
                       df_ref, dgbuf, drbuf):
    dmem_ref, r_ref, ln_ref = ready(dmem_ref, r_ref, ln_ref)
    length, width = r_ref.shape
    ff = gp_ref.ref.shape[1]
    slabs = ff // 512
    dln_ref[...] = jnp.zeros(dln_ref.shape, F32)

    def at(i):
        b, j = divmod(i, slabs)
        return slice(b * FB, b * FB + FB), slice(j * 512, j * 512 + 512), j

    def norms(b):
        rows = slice(b * FB, b * FB + FB)
        unit2, scale2 = norm_stats(r_ref[rows, :].astype(F32))
        e2 = unit2 * gain_of(ln_ref, 1) + shift_of(ln_ref, 1)
        unit3, scale3 = norm_stats(e2)
        de2, gg, sg = norm_back(dmem_ref[rows, :].astype(F32), unit3, scale3, gain_of(ln_ref, 2))
        dln_ref[7:8, :] += gg
        dln_ref[10:11, :] += sg
        dr, gg, sg = norm_back(de2, unit2, scale2, gain_of(ln_ref, 1))
        dln_ref[6:7, :] += gg
        dln_ref[9:10, :] += sg
        df = dr.astype(BF)
        df_ref[rows, :] = df
        drbuf[b] = dr
        dln_ref[4:5, :] += jnp.sum(df.astype(F32), axis=0, keepdims=True)

    def up_back(i):
        rows, cols, j = at(i)
        dgbuf[i % 4] = dot(df_ref[rows, :], wout_ref[cols, :], 1, 1)

    def act_back(i):
        rows, cols, j = at(i)
        du = dgbuf[i % 4] * gp_ref[rows, cols].astype(F32)
        gp_ref[rows, cols] = du.astype(BF)
        dln_ref[j : j + 1, :] += jnp.sum(du, axis=0, keepdims=True)

    def down_back(b):
        rows = slice(b * FB, b * FB + FB)
        de1_ref[rows, :] = (drbuf[b] + dot(gp_ref[rows, :], win_ref[...], 1, 1)).astype(BF)

    norms(0)
    wout_ref, gp_ref, win_ref = ready(wout_ref, gp_ref, win_ref)
    units = length // FB * slabs
    for tick in range(units + 2):
        if tick < units:
            up_back(tick)
            if tick % slabs == 1 and tick // slabs + 1 < length // FB:
                norms(tick // slabs + 1)
        i = tick - 2
        if 0 <= i < units:
            act_back(i)
            if i % slabs == slabs - 1:
                down_back(i // slabs)
    de1_ref.flush()
    e1_ref, g_ref = ready(e1_ref, g_ref)
    weight_grads(e1_ref, gp_ref, df_ref, g_ref, dw_ref)


def dec_ffn_kernel(h_ref, win_ref, ln_ref, wout_ref, cot_ref, res_ref, mem_ref,
                   out_ref, away_ref, dres_ref, dw_ref, dln_ref,
                   g_ref, du_ref, df_ref, ubuf, gpbuf, dgbuf, drbuf):
    h_ref, win_ref, ln_ref = ready(h_ref, win_ref, ln_ref)
    length, width = h_ref.shape
    ff = win_ref.shape[1]
    dln_ref[...] = jnp.zeros(dln_ref.shape, F32)
    slabs = ff // 512
    late = []

    def at(i):
        b, j = divmod(i, slabs)
        return slice(b * FB, b * FB + FB), slice(j * 512, j * 512 + 512), j

    def up(i):
        rows, cols, j = at(i)
        ubuf[i % 4] = dot(h_ref[rows, :], win_ref[:, cols])

    def act(i):
        rows, cols, j = at(i)
        g, gp = gelu_pair(ubuf[i % 4] + ln_ref[j : j + 1, :])
        g_ref[rows, cols] = g.astype(BF)
        gpbuf[i % 8] = gp.astype(BF)

    def down(b):
        rows = slice(b * FB, b * FB + FB)
        if not late:
            late.extend(ready(wout_op, cot_op, res_op))
        wout, cot, _ = late
        total = dot(g_ref[rows, :], wout[...]) + h_ref[rows, :].astype(F32) + ln_ref[4:5, :]
        unit3, scale3 = norm_stats(total)
        out_ref[rows, :] = (unit3 * gain_of(ln_ref, 2) + shift_of(ln_ref, 2)).astype(BF)
        dr, gg, sg = norm_back(cot[rows, :].astype(F32), unit3, scale3, gain_of(ln_ref, 2))
        dln_ref[7:8, :] += gg
        dln_ref[10:11, :] += sg
        df = dr.astype(BF)
        df_ref[rows, :] = df
        drbuf[b % 2] = dr
        dln_ref[4:5, :] += jnp.sum(df.astype(F32), axis=0, keepdims=True)

    def up_back(i):
        rows, cols, j = at(i)
        dgbuf[i % 4] = dot(df_ref[rows, :], late[0][cols, :], 1, 1)

    def act_back(i):
        rows, cols, j = at(i)
        du = dgbuf[i % 4] * gpbuf[i % 8].astype(F32)
        du_ref[rows, cols] = du.astype(BF)
        dln_ref[j : j + 1, :] += jnp.sum(du, axis=0, keepdims=True)

    def down_back(b):
        rows = slice(b * FB, b * FB + FB)
        total = drbuf[b % 2] + dot(du_ref[rows, :], win_ref[...], 1, 1)
        unit2, scale2 = norm_stats(late[2][rows, :].astype(F32))
        d, gg, sg = norm_back(total, unit2, scale2, gain_of(ln_ref, 1))
        dln_ref[6:7, :] += gg
        dln_ref[9:10, :] += sg
        dres_ref[rows, :] = d.astype(BF)

    wout_op, cot_op, res_op = wout_ref, cot_ref, res_ref
    units = length // FB * slabs
    for tick in range(units + 6 + 1):
        if tick < units:
            up(tick)
        i = tick - 2
        if 0 <= i < units:
            act(i)
            if i % slabs == slabs - 1:
                down(i // slabs)
        i = tick - 6
        if 0 <= i < units:
            up_back(i)
        i -= 1
        if 0 <= i < units:
            act_back(i)
            if i % slabs == slabs - 1:
                down_back(i // slabs)
    out_ref.flush()
    dres_ref.flush()
    (mem_ref,) = ready(mem_ref)
    section = lax.axis_index("section")

    @pl.when(section == 0)
    def _():
        pltpu.make_async_copy(out_ref.ref, away_ref.copy.dst_ref, away_ref.copy.dst_sem).start()

    @pl.when(section != 0)
    def _():
        pltpu.make_async_copy(mem_ref, away_ref.copy.dst_ref, away_ref.copy.dst_sem).start()

    away_ref.started = True
    weight_grads(h_ref, du_ref, df_ref, g_ref, dw_ref)


class Operand:
    def __init__(self, copy, ref):
        self.copy, self.ref = copy, ref


def ready(*operands):
    refs = []
    for operand in operands:
        if operand.copy is not None:
            operand.copy.wait()
            operand.copy = None
        refs.append(operand.ref)
    return refs


class Result:
    def __init__(self, copy, ref):
        self.copy, self.ref, self.started, self.waited = copy, ref, False, False

    def __getitem__(self, at):
        return self.ref[at]

    def __setitem__(self, at, value):
        self.ref[at] = value

    def __getattr__(self, name):
        return getattr(self.ref, name)

    def wait(self):
        if not self.waited:
            self.copy.wait()
            self.waited = True

    def flush_part(self, k):
        copy = self.copy
        pltpu.make_async_copy(self.ref.at[k], copy.dst_ref.at[k], copy.dst_sem).start()

    def flush_rows(self, k, size):
        rows = pl.ds(k * size, size)
        copy = self.copy
        pltpu.make_async_copy(self.ref.at[rows], copy.dst_ref.at[rows], copy.dst_sem).start()

    def flush(self):
        if not self.started:
            self.copy.start()
            self.started = True


class Row:
    def __init__(self, array):
        self.array, self.shape, self.dtype = array, array.shape[1:], array.dtype


class Pick:
    def __init__(self, zero, one=None):
        self.parts = [zero] if one is None else [zero, one]
        self.arrays = [p.array if isinstance(p, Row) else p for p in self.parts]
        self.shape, self.dtype = zero.shape, zero.dtype

    def start(self, refs, dst, sem, section):
        sources = [ref.at[section] if isinstance(p, Row) else ref for p, ref in zip(self.parts, refs)]
        if len(sources) == 1:
            pltpu.make_async_copy(sources[0], dst, sem).start()
            return
        for k, source in enumerate(sources):
            @pl.when(section == k)
            def _(source=source):
                pltpu.make_async_copy(source, dst, sem).start()

    def copy(self, refs, dst, sem, section):
        self.start(refs, dst, sem, section)
        return pltpu.make_async_copy(dst, dst, sem)


def run_kernel(kernel, plan, n_out, *refs):
    n_in = sum(len(p.arrays) for p in plan)
    ins, outs = list(refs[:n_in]), refs[n_in : n_in + n_out]
    rest = refs[n_in + n_out :]
    in_bufs, out_bufs = rest[: len(plan)], rest[len(plan) : len(plan) + n_out]
    in_sem, out_sem = rest[len(plan) + n_out : len(plan) + n_out + 2]
    scratch = rest[len(plan) + n_out + 2 :]
    section = lax.axis_index("section")
    operands = []
    for k, entry in enumerate(plan):
        given = [ins.pop(0) for _ in entry.arrays]
        operands.append(Operand(entry.copy(given, in_bufs[k], in_sem.at[k], section), in_bufs[k]))
    results = [
        Result(pltpu.make_async_copy(out_bufs[k], outs[k], out_sem.at[k]), out_bufs[k]) for k in range(n_out)
    ]
    kernel(*operands, *results, *scratch)
    ready(*operands)
    for result in results:
        result.flush()
    for result in results:
        result.wait()


def call(kernel, name, outs, scratch, flops, *args):
    any_space = pl.BlockSpec(memory_space=pl.ANY)
    plan = [a if isinstance(a, Pick) else Pick(a) for a in args]
    given = [array for entry in plan for array in entry.arrays]
    return pl.pallas_call(
        functools.partial(run_kernel, kernel, plan, len(outs)),
        out_shape=[jax.ShapeDtypeStruct(s, d) for s, d in outs],
        in_specs=[any_space] * len(given),
        out_specs=[any_space] * len(outs),
        scratch_shapes=[pltpu.VMEM(entry.shape, entry.dtype) for entry in plan]
        + [pltpu.VMEM(s, d) for s, d in outs]
        + [pltpu.SemaphoreType.DMA((len(plan),)), pltpu.SemaphoreType.DMA((len(outs),))]
        + scratch,
        compiler_params=pltpu.CompilerParams(vmem_limit_bytes=VMEM_LIMIT),
        cost_estimate=pl.CostEstimate(flops=flops, bytes_accessed=8 << 20, transcendentals=0),
        name=name,
    )(*given)


def fwd_scratch(n, w):
    return [
        pltpu.VMEM((HEADS, n, 128), BF),
        pltpu.VMEM((HEADS, 128, n), BF),
        pltpu.VMEM((w, n), BF),
        pltpu.VMEM((w, QB), F32),
        pltpu.VMEM((HEADS, QB), F32),
        pltpu.VMEM((HEADS, QB), F32),
        pltpu.VMEM((HEADS, WIDE, QB), F32),
        pltpu.VMEM((HEADS, WIDE, QB), BF),
    ]


def bwd_scratch(n, w):
    return [
        pltpu.VMEM((HEADS, n, 128), BF),
        pltpu.VMEM((w, n), BF),
        pltpu.VMEM((HEADS, n, 128), BF),
        pltpu.VMEM((HEADS, 128, n), BF),
        pltpu.VMEM((HEADS, 128, n), BF),
        pltpu.VMEM((w, QB), F32),
        pltpu.VMEM((2 * w, n), F32),
        pltpu.VMEM((3 * w, n), BF),
        pltpu.VMEM((4, WIDE, QB), F32),
        pltpu.VMEM((4, WIDE, QB), F32),
        pltpu.VMEM((4, WIDE, QB), BF),
        pltpu.VMEM((4, WIDE, QB), BF),
    ]


def middle_back_kernel(dr, h, mem, tgt, src, qT, kv, att, lse, cross, wkv, r, small, wout, gp, win, e1, g,
                       dh, dwd, dwe, de1, dw, dln, dmem, df, dgbuf, drbuf, *bwd):
    cross_bwd_kernel(dr, h, mem, tgt, src, qT, kv, att, lse, cross, wkv, dh, dmem, dwd, dwe, *bwd)
    dh.flush()
    enc_ffn_bwd_kernel(Operand(None, dmem), r, small, wout, gp, win, e1, g, de1, dw, dln, df, dgbuf, drbuf)


def middle_back(dr, h, mem, tgt, src, qT, kv, att, lse, cross, wkv, r, small, wout, gp, win, e1, g):
    n, w = r.shape
    ff = win.shape[-1]
    row, pair = ((n, w), BF), ((2, w, w), BF)
    return call(middle_back_kernel, "cross_and_ffn_backward",
                [row, pair, pair, row, ((2 * ff // w, w, w), BF), ((16, w), F32)],
                [pltpu.VMEM((n, w), BF), pltpu.VMEM((n, w), BF), pltpu.VMEM((4, FB, 512), F32),
                 pltpu.VMEM((n // FB, FB, w), F32)] + bwd_scratch(n, w), 30 << 30,
                dr, h, mem, tgt, src, qT, kv, att, lse, cross, wkv, r, small, wout, gp, win, e1, g)


def middle_kernel(e1, win, small, wout, wkv, d1, tgt, src, cross, small2, win2, wout2, cot,
                  g, gp, r2, mem, kv, qT, att, lse, out, away, dres, dw, dln,
                  cr, d2, ubuf, df, gpbuf, dgbuf, drbuf, *fwd):
    enc_ffn_fwd_kernel(e1, win, small, wout, wkv, g, gp, r2, mem, kv, ubuf)
    cross_fwd_kernel(d1, Operand(None, kv.ref), tgt, src, cross, small2, qT, att, lse, cr, d2, *fwd)
    g.wait()
    gp.wait()
    dec_ffn_kernel(Operand(None, d2), win2, small2, wout2, cot, Operand(None, cr), Operand(None, mem.ref),
                   out, away, dres, dw, dln, g.ref, gp.ref, df, ubuf, gpbuf, dgbuf, drbuf)


def middle(e1, win, small, wout, wkv, d1, tgt, src, cross, small2, win2, wout2, cot):
    n, w = e1.shape
    ff = win.shape[-1]
    row = ((n, w), BF)
    return call(middle_kernel, "feed_forward_and_cross",
                [((n, ff), BF), ((n, ff), BF), row, row, ((n, 2 * w), BF), ((w, n), BF), ((w, n), BF), ((HEADS, n), F32),
                 row, row, row, ((2 * ff // w, w, w), BF), ((16, w), F32)],
                [pltpu.VMEM((n, w), BF), pltpu.VMEM((n, w), BF), pltpu.VMEM((4, FB, 512), F32), pltpu.VMEM((n, w), BF),
                 pltpu.VMEM((8, FB, 512), BF), pltpu.VMEM((4, FB, 512), F32), pltpu.VMEM((2, FB, w), F32)] + fwd_scratch(n, w),
                30 << 30, e1, win, small, wout, wkv, d1, tgt, src, cross, small2, win2, wout2, cot)


CHUNK = 512
SLOTS = 4
PARTS = 5
MESH = pl.DeviceIdType.MESH
ANY = pl.BlockSpec(memory_space=pl.ANY)


def bit_of(index, bit):
    return (index // 2**bit) % 2


def partner_of(index, bit):
    return index + 2**bit - 2 * 2**bit * bit_of(index, bit)


def greet(partners):
    barrier = pltpu.get_barrier_semaphore()
    for device in partners:
        pl.semaphore_signal(barrier, inc=1, device_id=device, device_id_type=MESH)
    pl.semaphore_wait(barrier, len(partners))


def halvings(devices, rows):
    bits = devices.bit_length() - 1
    halved = 0
    while halved < bits and (rows >> (halved + 1)) >= 16 and (rows >> (halved + 1)) % 16 == 0:
        halved += 1
    return list(range(halved)), list(range(halved, bits))


def place(index, count, rows):
    at, size = 0, rows
    for bit in range(count):
        size //= 2
        at = at + bit_of(index, bit) * size
    return at, size


class Sums:
    def __init__(self, devices, groups, early, gap, out_ref, scratch):
        self.groups, self.early, self.gap, self.out = groups, early, gap, out_ref
        self.held, self.shard, self.load_sem, self.store_sem, self.core_sem, self.send_sem, self.recv_sem = scratch[:7]
        self.landing = scratch[7:]
        self.index, self.section = lax.axis_index("dp"), lax.axis_index("section")
        self.halved, self.rest = halvings(devices, CHUNK)
        self.bits = self.halved + self.rest
        self.across = (1 - self.section, self.index)
        self.mates = [(self.section, partner_of(self.index, bit)) for bit in self.bits]
        self.chunks = sum(group[0] for group in groups)
        self.steps = 1 + len(self.bits) + len(self.halved)
        self.ticks = self.chunks + gap + self.steps

    def rows(self, count, other=False):
        at, size = 0, CHUNK
        for bit in range(count):
            size //= 2
            side = bit_of(self.index, bit)
            at = at + (1 - side if other and bit == count - 1 else side) * size
        return at, size

    def window(self, count, other=False):
        at, size = self.rows(count, other)
        return pl.ds(pl.multiple_of(at - self.rows(1)[0], 16), size)

    def remote(self, src, dst, step, c, device):
        return pltpu.make_async_remote_copy(
            src_ref=src, dst_ref=dst, send_sem=self.send_sem.at[step, c], recv_sem=self.recv_sem.at[step, c],
            device_id=device, device_id_type=MESH)

    def begin(self, c):
        at, size = self.rows(1)
        far, _ = self.rows(1, True)
        first = 0
        for count, *pair in self.groups:
            @pl.when((c >= first) & (c < first + count))
            def _(first=first, pair=pair):
                for k, (ref, layer) in enumerate(pair):
                    near = ref.at[c - first, pl.ds(pl.multiple_of(at, 16), size)]
                    away = ref.at[c - first, pl.ds(pl.multiple_of(far, 16), size)]
                    pltpu.make_async_copy(near, self.held.at[c, layer], self.load_sem.at[k, c]).start()
                    self.core_copy(k, c, away, layer).start()
            first += count

    def core_copy(self, k, c, src, layer):
        return pltpu.make_async_remote_copy(
            src_ref=src, dst_ref=self.landing[0].at[c % SLOTS, layer], send_sem=self.core_sem.at[0, k, c],
            recv_sem=self.core_sem.at[1, k, c], device_id=self.mates[0], device_id_type=MESH)

    def copy(self, step, c):
        reduce_steps = 1 + len(self.bits)
        if step == 1:
            return self.remote(self.held.at[c, 1 - self.section], self.landing[1].at[c % SLOTS], 1, c, self.across)
        if step < reduce_steps:
            bit = step - 1
            window = self.window(bit + 1, True) if bit in self.halved else self.window(len(self.halved))
            return self.remote(self.held.at[c, self.section, window], self.landing[step].at[c % SLOTS], step, c, self.mates[bit])
        bit = self.halved[-1 - (step - reduce_steps)]
        at, size = self.rows(bit + 1)
        rows = self.out.at[c, pl.ds(pl.multiple_of(at, 16), size)]
        return self.remote(self.shard.at[c] if step == reduce_steps else rows, rows, step, c, self.mates[bit])

    def store(self, c):
        at, size = self.rows(len(self.halved))
        return pltpu.make_async_copy(self.shard.at[c], self.out.at[c, pl.ds(pl.multiple_of(at, 16), size)], self.store_sem.at[c])

    def arrive(self, step, c):
        reduce_steps = 1 + len(self.bits)
        if step == 0:
            for k in range(2):
                pltpu.make_async_copy(self.landing[0].at[c % SLOTS, k], self.held.at[c, k], self.load_sem.at[k, c]).wait()
                self.core_copy(k, c, self.held.at[c, k], k).wait()
            for k in range(2):
                self.held[c, k] = (self.held[c, k].astype(F32) + self.landing[0][c % SLOTS, k].astype(F32)).astype(BF)
            return
        self.copy(step, c).wait()
        if step < reduce_steps:
            bit = step - 1
            window = self.window(1) if step == 1 else self.window(min(bit + 1, len(self.halved)))
            total = (self.held[c, self.section, window, :].astype(F32) + self.landing[step][c % SLOTS].astype(F32)).astype(BF)
            if step == reduce_steps - 1:
                self.shard[c] = total
                self.store(c).start()
            else:
                self.held[c, self.section, window, :] = total
        elif step == reduce_steps:
            self.store(c).wait()

    def tick(self, t):
        for step in range(self.steps + 1):
            at = t - step
            late = at >= self.early + self.gap
            c = jnp.where(late, at - self.gap, at)

            @pl.when(((at >= 0) & (at < self.early)) | (late & (c < self.chunks)))
            def _(step=step, c=c):
                if step == 0:
                    self.begin(c)
                else:
                    self.arrive(step - 1, c)
                    if step < self.steps:
                        self.copy(step, c).start()

    @staticmethod
    def scratch(devices, chunks):
        halved, rest = halvings(devices, CHUNK)
        steps = 1 + len(halved + rest) + len(halved)
        sizes = [CHUNK >> min(bit + 1, len(halved)) for bit in halved + rest]
        return [
            pltpu.VMEM((chunks, 2, CHUNK // 2, 512), BF),
            pltpu.VMEM((chunks, CHUNK >> len(halved), 512), BF),
            pltpu.SemaphoreType.DMA((2, chunks)),
            pltpu.SemaphoreType.DMA((chunks,)),
            pltpu.SemaphoreType.DMA((2, 2, chunks)),
            pltpu.SemaphoreType.DMA((steps, chunks)),
            pltpu.SemaphoreType.DMA((steps, chunks)),
            pltpu.VMEM((SLOTS, 2, CHUNK // 2, 512), BF),
            pltpu.VMEM((SLOTS, CHUNK // 2, 512), BF),
        ] + [pltpu.VMEM((SLOTS, size, 512), BF) for size in sizes[1:]]


class Vectors:
    def __init__(self, sums, scratch):
        self.small, self.arrived, self.send_sem, self.recv_sem = scratch
        self.section = sums.section
        self.partners = [sums.across] + sums.mates

    def copy(self, k):
        return pltpu.make_async_remote_copy(
            src_ref=self.small.at[1 - self.section if k == 0 else self.section], dst_ref=self.arrived.at[k],
            send_sem=self.send_sem.at[k], recv_sem=self.recv_sem.at[k],
            device_id=self.partners[k], device_id_type=MESH)

    def tick(self, t):
        for k in range(len(self.partners) + 1):
            @pl.when(t == k)
            def _(k=k):
                if k > 0:
                    self.copy(k - 1).wait()
                    self.small[self.section] = self.small[self.section] + self.arrived[k - 1]
                if k < len(self.partners):
                    self.copy(k).start()

    @staticmethod
    def scratch(devices):
        n = 1 + len(sum(halvings(devices, CHUNK), []))
        return [pltpu.VMEM((2, 16, 512), F32), pltpu.VMEM((n, 16, 512), F32),
                pltpu.SemaphoreType.DMA((n,)), pltpu.SemaphoreType.DMA((n,))]


def tail_kernel(devices, plans, n_sums, *refs):
    section = lax.axis_index("section")
    refs = list(refs)
    take = lambda n: [refs.pop(0) for _ in range(n)]
    given = [[take(len(entry.arrays)) for entry in plan] for plan in plans]
    ffn_enc, ffn_dec, cross_enc, cross_dec, vec_enc, vec_dec = take(6)
    far_arrived, own_grad, sums_out, small_out = take(4)
    buffers = take(len(plans[0]))
    in_sem, out_sem, dx_send, dx_recv, far_dx, own_dx = take(6)
    dw, dln = take(2)
    vectors_scratch = take(4)
    sums_scratch = take(n_sums)

    groups = [
        (ffn_enc.shape[0], (ffn_enc, 0), (ffn_dec, 1)),
        (cross_enc.shape[0], (cross_enc, 0), (cross_dec, 1)),
        (4, (dw.at[0], 0), (dw.at[1], 1)),
    ]
    early = groups[0][0] + groups[1][0]
    sums = Sums(devices, groups, early, 0, sums_out, sums_scratch)
    vectors = Vectors(sums, vectors_scratch)
    greet([sums.across] + sums.mates)

    def fetch(layer, k):
        plans[layer][k].start(given[layer][k], buffers[k], in_sem.at[layer, k], section)

    for k in range(len(buffers)):
        fetch(1, k)
    result = pltpu.make_async_copy(own_dx, own_grad, out_sem)
    far_copy = pltpu.make_async_remote_copy(
        src_ref=far_dx, dst_ref=far_arrived, send_sem=dx_send, recv_sem=dx_recv,
        device_id=sums.across, device_id_type=MESH)

    @pl.loop(0, sums.ticks)
    def _(t):
        sums.tick(t)
        vectors.tick(t - early)
        part, layer = t % PARTS, 1 - t // PARTS

        def arrived(*numbers):
            for k in numbers:
                pltpu.make_async_copy(buffers[k], buffers[k], in_sem.at[layer, k]).wait()

        def reuse(*numbers):
            @pl.when(layer == 1)
            def _():
                for k in numbers:
                    fetch(0, k)

        def put_dx(rows, value):
            @pl.when(section == layer)
            def _():
                own_dx[rows, :] = value

            @pl.when(section != layer)
            def _():
                far_dx[rows, :] = value.astype(BF)

        before, fill, block, after = self_backward_phases(
            layer == 1, buffers, arrived, reuse, put_dx, dw.at[layer], dln.at[layer], *refs)
        working = t < 2 * PARTS
        pl.when(working & (part == 0))(before)
        pl.when(working & (part == 1))(fill)

        @pl.when(working & (part >= 1) & (part <= 3))
        def _():
            first = jnp.where(part == 1, 0, jnp.where(part == 2, 1, 3))
            last = jnp.where(part == 1, 1, jnp.where(part == 2, 3, 4))

            @pl.loop(first, last)
            def _(qb):
                block(qb)

        pl.when(working & (part == 4))(after)

        @pl.when(t == 2 * PARTS - 1)
        def _():
            result.start()
            vectors.small[0] = vec_enc[...] + dln[0]
            vectors.small[1] = vec_dec[...] + dln[1]

        @pl.when(t == sums.chunks)
        def _():
            far_copy.start()

    small_out[...] = vectors.small[section]
    far_copy.wait()
    result.wait()


def backward_and_sums(first, second, groups, vectors, devices):
    plans = [[a if isinstance(a, Pick) else Pick(a) for a in operands] for operands in (first, second)]
    n, w = plans[0][1].shape
    chunks = sum(pair[0].shape[0] for pair in groups) + 4
    given = [array for plan in plans for entry in plan for array in entry.arrays]
    vm = pl.BlockSpec(memory_space=pltpu.VMEM)
    sums_scratch = Sums.scratch(devices, chunks)
    return pl.pallas_call(
        functools.partial(tail_kernel, devices, plans, len(sums_scratch)),
        out_shape=[
            jax.ShapeDtypeStruct((n, w), BF), jax.ShapeDtypeStruct((n, w), F32),
            jax.ShapeDtypeStruct((chunks, CHUNK, 512), BF), jax.ShapeDtypeStruct((16, 512), F32)],
        in_specs=[ANY] * (len(given) + 4) + [vm, vm],
        out_specs=[ANY] * 3 + [vm],
        scratch_shapes=[pltpu.VMEM(entry.shape, entry.dtype) for entry in plans[0]]
        + [pltpu.SemaphoreType.DMA((2, len(plans[0]))), pltpu.SemaphoreType.DMA, pltpu.SemaphoreType.DMA,
           pltpu.SemaphoreType.DMA, pltpu.VMEM((n, w), BF), pltpu.VMEM((n, w), F32)]
        + [pltpu.VMEM((2, 4, w, w), BF), pltpu.VMEM((2, 16, w), F32)]
        + Vectors.scratch(devices) + sums_scratch + bwd_scratch(n, w),
        compiler_params=pltpu.CompilerParams(collective_id=1, has_side_effects=True, vmem_limit_bytes=VMEM_LIMIT),
        name="backward_and_sums",
    )(*given, *[array for pair in groups for array in pair], *vectors)


def unpack_kernel(kinds, g_ref, mem_ref, out_ref, low_far_ref, grad_ref, grad_far_ref, s_ref, *refs):
    n = len(kinds)
    low_out, grad_out = refs[:2]
    outs = refs[2 : n + 2]
    b_in, b_out, gains, shifts = refs[n + 2 : n + 6]
    chunk, stage, in_sem, sem, low_buf, grad_buf, far_buf, row_in, row_out = refs[n + 6 :]
    section = lax.axis_index("section")
    chunks = chunk.shape[0]
    loads = [pltpu.make_async_copy(g_ref.at[c], chunk.at[c], in_sem.at[c]) for c in range(chunks)]
    fetch = [
        pltpu.make_async_copy(mem_ref, low_buf.at[0], row_in.at[0]),
        pltpu.make_async_copy(low_far_ref, low_buf.at[1], row_in.at[1]),
        pltpu.make_async_copy(grad_ref, grad_buf.at[0], row_in.at[2]),
        pltpu.make_async_copy(grad_far_ref, far_buf, row_in.at[3]),
    ]
    send = [
        pltpu.make_async_copy(low_buf.at[0], low_out.at[section], row_out.at[0]),
        pltpu.make_async_copy(low_buf.at[1], low_out.at[1 - section], row_out.at[1]),
        pltpu.make_async_copy(grad_buf.at[0], grad_out.at[section], row_out.at[2]),
        pltpu.make_async_copy(grad_buf.at[1], grad_out.at[1 - section], row_out.at[3]),
    ]
    for c in range(4):
        loads[c].start()
    for one in fetch[1:]:
        one.start()

    @pl.when(section == 0)
    def _():
        fetch[0].start()

    @pl.when(section != 0)
    def _():
        pltpu.make_async_copy(out_ref, low_buf.at[0], row_in.at[0]).start()

    for c in range(4, chunks):
        loads[c].start()
    for k in range(4):
        b_in[:, k * 512 : (k + 1) * 512] = s_ref[k : k + 1, :]
    b_out[...] = s_ref[4:5, :]
    for k in range(3):
        gains[k] = s_ref[5 + k : 6 + k, :]
        shifts[k] = s_ref[8 + k : 9 + k, :]

    slots = stage.shape[0]
    copies, c = [], 0
    for kind, (count, flipped, axis) in enumerate(kinds):
        for k in range(count):
            at = slice(k * 512, k * 512 + 512)
            dst = outs[kind].at[:, at] if axis else outs[kind].at[at, :]
            copies.append(pltpu.make_async_copy(stage.at[c % slots], dst, sem.at[c % slots]))
            loads[c].wait()
            if c >= slots:
                copies[c - slots].wait()
            value = chunk[c].astype(F32)
            stage[c % slots] = value.T if flipped else value
            copies[c].start()
            if c < 4:
                fetch[c].wait()
                if c == 3:
                    grad_buf[1] = far_buf[...].astype(F32)
                send[c].start()
            c += 1
    for copy in copies[-slots:] + send:
        copy.wait()


def unpack(g, low, low_far, grad, grad_far, vectors, kinds, shapes):
    n, w = low_far.shape
    vm = pl.BlockSpec(memory_space=pltpu.VMEM)
    vector_shapes = [(1, 4 * w), (1, w), (3, 1, w), (3, 1, w)]
    return pl.pallas_call(
        functools.partial(unpack_kernel, kinds),
        out_shape=[jax.ShapeDtypeStruct((2, n, w), BF), jax.ShapeDtypeStruct((2, n, w), F32)]
        + [jax.ShapeDtypeStruct(s, F32) for s in shapes + vector_shapes],
        in_specs=[ANY] * 6 + [vm],
        out_specs=[ANY] * (len(shapes) + 2) + [vm] * 4,
        scratch_shapes=[
            pltpu.VMEM(g.shape, BF), pltpu.VMEM((6, 512, 512), F32),
            pltpu.SemaphoreType.DMA((g.shape[0],)), pltpu.SemaphoreType.DMA((6,)),
            pltpu.VMEM((2, n, w), BF), pltpu.VMEM((2, n, w), F32), pltpu.VMEM((n, w), BF),
            pltpu.SemaphoreType.DMA((4,)), pltpu.SemaphoreType.DMA((4,)),
        ],
        compiler_params=pltpu.CompilerParams(vmem_limit_bytes=VMEM_LIMIT),
        name="unpack_results",
    )(g, *low, low_far, grad, grad_far, vectors)


class Spread:
    def __init__(self, devices, weights, land, send_sem, recv_sem):
        self.weights, self.land, self.send_sem, self.recv_sem = weights, land, send_sem, recv_sem
        self.index, self.section = lax.axis_index("dp"), lax.axis_index("section")
        self.bits = halvings(devices, 512)[0]
        self.across = (1 - self.section, self.index)
        self.mates = [(self.section, partner_of(self.index, bit)) for bit in self.bits]
        self.chunks = []
        for w, ref in enumerate(weights):
            rows, cols = ref.shape
            self.chunks += [(w, r, c) for r in range(0, rows, 512) for c in range(0, cols, 512)]
        self.steps = len(self.bits) + 1
        self.lags = list(range(self.steps))
        if self.steps <= 5:
            self.lags[-2:] = [lag + 1 for lag in self.lags[-2:]]
        self.ticks = len(self.chunks) + self.lags[-1]

    def copy(self, c, step, src=None):
        if step == 0:
            count, device = len(self.bits), self.across
        else:
            bit = self.bits[len(self.bits) - step]
            count, device = bit + 1, self.mates[bit]
        at, size = place(self.index, count, 512)
        part = self.land.at[c, pl.ds(pl.multiple_of(at, 16), size)]
        return pltpu.make_async_remote_copy(
            src_ref=part if src is None else src, dst_ref=part, send_sem=self.send_sem.at[step, c],
            recv_sem=self.recv_sem.at[step, c], device_id=device, device_id_type=MESH)

    def begin(self, c):
        w, r, col = self.chunks[c]
        at, size = place(self.index, len(self.bits), 512)
        self.copy(c, 0, self.weights[w].at[pl.ds(pl.multiple_of(r + at, 16), size), col : col + 512]).start()

    def tick(self, t):
        for step in range(1, self.steps + 1):
            c = t - self.lags[step - 1]

            @pl.when((c >= 0) & (c < len(self.chunks)))
            def _(step=step, c=c):
                self.copy(c, step - 1).wait()
                if step < self.steps:
                    self.copy(c, step).start()


def head_kernel(devices, plan, shapes, *refs):
    refs = list(refs)
    take = lambda n: [refs.pop(0) for _ in range(n)]
    given = [take(len(entry.arrays)) for entry in plan]
    tokens, *weights = take(6)
    b_in, b_out, gains, shifts = take(4)
    outs = take(2 * len(shapes))
    far_tokens, own_vectors, far_vectors, *far = take(8)
    buffers = take(len(plan))
    results = [Result(None, ref) for ref in take(2 * len(shapes))]
    in_sem, out_sem, far_x, small_ref, far_small, swap_send, swap_recv, keep_sem = take(8)
    land, send_sem, recv_sem, flush_sem = take(4)
    section = lax.axis_index("section")
    spread = Spread(devices, weights, land, send_sem, recv_sem)
    own = [Operand(entry.copy(ref, buffers[k], in_sem.at[k], section), buffers[k])
           for k, (entry, ref) in enumerate(zip(plan, given))]
    for k, result in enumerate(results):
        result.copy = pltpu.make_async_copy(result.ref, outs[k], out_sem.at[k])
    small_ref[...] = jnp.zeros(small_ref.shape, F32)
    for k in range(4):
        small_ref[k : k + 1, :] = b_in[:, k * 512 : (k + 1) * 512]
    small_ref[4:5, :] = b_out[...]
    for k in range(3):
        small_ref[5 + k : 6 + k, :] = gains[k]
        small_ref[8 + k : 9 + k, :] = shifts[k]
    greet([spread.across] + spread.mates)
    for c in range(len(spread.chunks)):
        spread.begin(c)
    swaps = [
        pltpu.make_async_remote_copy(
            src_ref=src, dst_ref=dst, send_sem=swap_send.at[k], recv_sem=swap_recv.at[k],
            device_id=spread.across, device_id_type=MESH)
        for k, (src, dst) in enumerate([(small_ref, far_small), (tokens.at[1 - section], far_x)])
    ]
    swaps[0].start()

    def own_tick(k):
        spread.tick(k)
        if isinstance(k, int) and k == 1:
            swaps[1].start()

    def flush(c):
        w, r, col = spread.chunks[c]
        return pltpu.make_async_copy(land.at[c], far[w].at[r : r + 512, col : col + 512], flush_sem.at[c])

    x_ref, w_ref, wout_ref, ids_ref, far_ids = ready(*own)
    width = x_ref.shape[1]
    n = len(shapes)
    self_forward(section == 1, x_ref, ids_ref,
                 [w_ref.at[:, k * width : (k + 1) * width] for k in range(3)] + [wout_ref],
                 small_ref, results[:n], own_tick, *refs)
    for one in swaps:
        one.wait()
    keep = [
        pltpu.make_async_copy(src, dst, keep_sem.at[k])
        for k, (src, dst) in enumerate([(far_x, far_tokens), (small_ref, own_vectors), (far_small, far_vectors)])
    ]
    for one in keep:
        one.start()
    self_forward(section == 0, far_x, far_ids, [land.at[k] for k in range(4)], far_small, results[n:],
                 lambda k: spread.tick(8 + k), *refs)
    done = 15 - spread.lags[-1]
    for c in range(done + 1):
        flush(c).start()
    for t in range(16, spread.ticks):
        spread.tick(t)
        flush(t - spread.lags[-1]).start()
    for c in range(len(spread.chunks)):
        flush(c).wait()
    for one in keep:
        one.wait()
    for result in results:
        result.copy.wait()


def forward_and_weights(own, tokens, vectors, weights, devices):
    plan = [a if isinstance(a, Pick) else Pick(a) for a in own]
    n, w = plan[0].shape
    shapes = [((w, n), BF), ((n, w), BF), ((n, w), BF), ((w, n), BF), ((HEADS, n), F32), ((n, w), BF), ((n, w), BF)]
    given = [array for entry in plan for array in entry.arrays] + [tokens, *weights]
    steps = len(halvings(devices, 512)[0]) + 1
    count = sum(a.size for a in weights) // 512**2
    dma = pltpu.SemaphoreType.DMA
    outs = pl.pallas_call(
        functools.partial(head_kernel, devices, plan, shapes),
        out_shape=[jax.ShapeDtypeStruct(s, d) for s, d in shapes * 2]
        + [jax.ShapeDtypeStruct((n, w), BF)] + [jax.ShapeDtypeStruct((16, w), F32)] * 2
        + [jax.ShapeDtypeStruct(a.shape, BF) for a in weights],
        in_specs=[ANY] * len(given) + [pl.BlockSpec(memory_space=pltpu.VMEM)] * 4,
        out_specs=[ANY] * (2 * len(shapes) + 8),
        scratch_shapes=[pltpu.VMEM(entry.shape, entry.dtype) for entry in plan]
        + [pltpu.VMEM(s, d) for s, d in shapes * 2]
        + [dma((len(plan),)), dma((2 * len(shapes),)), pltpu.VMEM((n, w), BF),
           pltpu.VMEM((16, w), F32), pltpu.VMEM((16, w), F32), dma((2,)), dma((2,)), dma((3,))]
        + [pltpu.VMEM((count, 512, 512), BF), dma((steps, count)), dma((steps, count)), dma((count,))]
        + fwd_scratch(n, w),
        compiler_params=pltpu.CompilerParams(collective_id=0, has_side_effects=True, vmem_limit_bytes=VMEM_LIMIT),
        name="forward_and_weights",
    )(*given, *vectors)
    k = len(shapes)
    return outs[:k], outs[k : 2 * k], outs[2 * k], outs[2 * k + 1], outs[2 * k + 2], outs[2 * k + 3 :]


def shards(layer_input, cotangent, src_segments, tgt_segments, attn_qkv, attn_out, cross_proj,
           ffn_in, ffn_in_bias, ffn_out, ffn_out_bias, norm_gain, norm_bias):
    devices = lax.axis_size("dp")
    swap = lambda a: lax.ppermute(a, "section", [(0, 1), (1, 0)])
    vectors = [ffn_in_bias, ffn_out_bias, norm_gain.transpose(1, 0, 2), norm_bias.transpose(1, 0, 2)]
    tokens = layer_input[0, :, 0]
    near = (attn_qkv[0], attn_out[0], cross_proj[0], ffn_in[0], ffn_out[0])
    src, tgt, cot = Row(src_segments), Row(tgt_segments), Row(cotangent[:, 0])
    (*own_saved, own_hid), (*far_saved, far_hid), far_tokens, vectors, far_vectors, far = forward_and_weights(
        [Row(tokens), near[0], near[1], Pick(src, tgt), Pick(tgt, src)], tokens, vectors, near, devices)
    enc = [Pick(a, b) for a, b in zip(near, far)]
    dec = [Pick(b, a) for a, b in zip(near, far)]
    enc_small, dec_small = Pick(vectors, far_vectors), Pick(far_vectors, vectors)
    src, tgt, cot = Pick(src), Pick(tgt), Pick(cot)
    e1, d1 = Pick(own_hid, far_hid), Pick(far_hid, own_hid)
    g, gp, r2, mem, kv, cq, catt, clse, out, away, dres, dw_dffn, s_dffn = middle(
        e1, enc[3], enc_small, enc[4], enc[2], d1, tgt, src, dec[2], dec_small, dec[3], dec[4], cot)
    low_far = swap(away)
    dh1, dw_dcross, dw_ecross, de1, dw_effn, s_effn = middle_back(
        dres, d1, mem, tgt, src, cq, kv, catt, clse, dec[2], enc[2], r2, enc_small, enc[4], gp, enc[3], e1, g)
    de1, low_far = lax.optimization_barrier((de1, low_far))

    def operands(dh, saved, tokens, ids, weights, small):
        qT, k, v, att, lse, res = saved
        return [dh, res, tokens, ids, qT, k, v, att, lse, weights[0], weights[1], small]

    far_grad, own_grad, sums, s = backward_and_sums(
        operands(de1, [Pick(a, b) for a, b in zip(own_saved, far_saved)], Pick(Row(tokens), far_tokens), src, enc, enc_small),
        operands(dh1, [Pick(b, a) for a, b in zip(own_saved, far_saved)], Pick(far_tokens, Row(tokens)), tgt, dec, dec_small),
        [(dw_effn, dw_dffn), (dw_ecross, dw_dcross)], (s_effn, s_dffn), devices)
    kinds = ((4, False, 1), (4, True, 0), (2, True, 1), (3, True, 1), (1, False, 0))
    layer_output, input_grad, win, wout, cross, qkv, wo, b_in, b_out, gains, shifts = unpack(
        sums, (mem, out), low_far, own_grad, far_grad, s, kinds,
        [ffn_in.shape[1:], ffn_out.shape[1:], cross_proj.shape[1:], attn_qkv.shape[1:], attn_out.shape[1:]])
    return (layer_output[None, :, None], input_grad[None, :, None], qkv[None], wo[None], cross[None], win[None],
            b_in, wout[None], b_out, gains.transpose(1, 0, 2), shifts.transpose(1, 0, 2))


def solution(mesh):
    return jax.shard_map(
        shards,
        mesh=mesh,
        in_specs=(
            P("section", None, "dp", None, None),
            P(None, "dp", None, None),
            P(None, "dp", None),
            P(None, "dp", None),
            P("section", None, None),
            P("section", None, None),
            P("section", None, None),
            P("section", None, None),
            P("section", None),
            P("section", None, None),
            P("section", None),
            P("section", None, None),
            P("section", None, None),
        ),
        out_specs=(
            P("section", None, "dp", None, None),
            P("section", None, "dp", None, None),
            P("section", None, None),
            P("section", None, None),
            P("section", None, None),
            P("section", None, None),
            P("section", None),
            P("section", None, None),
            P("section", None),
            P("section", None, None),
            P("section", None, None),
        ),
        check_vma=False,
    )
```

```python
import functools
import math

import jax
import jax.numpy as jnp
from jax import lax
from jax.experimental import pallas as pl
from jax.experimental.pallas import tpu as pltpu
from jax.sharding import PartitionSpec as P

HEADS = 8
EPSILON = 1e-05
NEGATIVE = -1000000000.0
BF = jnp.bfloat16
F32 = jnp.float32
LOG2E = 1.4426950408889634
QB = 256
UNIT = 128
WIDE = 256
TB = 256
FB = 256
VMEM_LIMIT = 60 * 1024 * 1024


def dot(left, right, lc=1, rc=0):
    return lax.dot_general(
        left, right, (((lc,), (rc,)), ((), ())), preferred_element_type=F32
    )


def norm_stats(value):
    centered = value - jnp.mean(value, axis=-1, keepdims=True)
    spread = jnp.mean(centered * centered, axis=-1, keepdims=True)
    scale = lax.rsqrt(spread + EPSILON)
    return centered * scale, scale


def norm_back(out_grad, unit, scale, gain):
    gain_grad = jnp.sum(out_grad * unit, axis=0, keepdims=True)
    shift_grad = jnp.sum(out_grad, axis=0, keepdims=True)
    inner = out_grad * gain
    mean_one = jnp.mean(inner, axis=-1, keepdims=True)
    mean_two = jnp.mean(inner * unit, axis=-1, keepdims=True)
    return scale * (inner - mean_one - unit * mean_two), gain_grad, shift_grad


def gelu_pair(u):
    phi = 0.5 + 0.5 * lax.erf(u * (1.0 / math.sqrt(2.0)))
    bell = jnp.exp(-0.5 * u * u) * (1.0 / math.sqrt(2.0 * math.pi))
    return u * phi, phi + u * bell


def gain_of(small, norm):
    return small[5 + norm : 6 + norm, :]


def shift_of(small, norm):
    return small[8 + norm : 9 + norm, :]


def key_codes(ids_row, length):
    column = jnp.broadcast_to(ids_row.astype(F32), (128, length)).T
    lane = lax.broadcasted_iota(jnp.int32, (length, 128), 1)
    spot = jnp.where(lane < 64, lane, lane - 64)
    codes = jnp.where(
        spot < 4,
        jnp.where(column == spot.astype(F32), 0.0, NEGATIVE),
        jnp.where(spot < 7, -1.0, 0.0),
    )
    return codes, lane < 64


def fill_keys(dst, keys_ref, codes, low_half):
    for pair in range(HEADS // 2):
        slab = keys_ref[:, pair * 128 : pair * 128 + 128].astype(F32)
        dst[2 * pair] = jnp.where(low_half, slab, codes).astype(BF)
        dst[2 * pair + 1] = jnp.where(low_half, codes, slab).astype(BF)


def query_rows(head):
    return (0, 64) if head % 2 == 0 else (64, 0)


def key_range(query_ids, key_ids, qb):
    ids = query_ids[:, pl.ds(pl.multiple_of(qb * QB, QB), QB)].astype(F32)
    keys = key_ids[...].astype(F32)
    start = jnp.sum((keys < jnp.min(ids)).astype(F32)).astype(jnp.int32)
    stop = jnp.sum((keys <= jnp.max(ids)).astype(F32)).astype(jnp.int32)
    return start // UNIT, (stop + UNIT - 1) // UNIT


def visit_keys(query_ids, key_ids, qb, step):
    lo, hi = key_range(query_ids, key_ids, qb)
    count = hi - lo

    @pl.loop(0, count // 2)
    def _(i):
        step(lo + 2 * i, WIDE, False)

    @pl.when(count % 2 == 1)
    def _():
        step(hi - 1, UNIT, False)


def below_diagonal():
    return lax.broadcasted_iota(jnp.int32, (WIDE, QB), 0) <= lax.broadcasted_iota(jnp.int32, (WIDE, QB), 1)


def staged(first, lag_one, second, lag_two, third):
    for i in range(HEADS + lag_one + lag_two):
        if i < HEADS:
            first(i)
        if 0 <= i - lag_one < HEADS:
            second(i - lag_one)
        if 0 <= i - lag_one - lag_two < HEADS:
            third(i - lag_one - lag_two)


def attend_loop(visit, after, qaug, kaug, vt, attT_ref, lse_ref, oacc, mrow, lrow, sbuf, pbuf, length):
    @pl.loop(0, length // QB)
    def _(qb):
        q = pl.ds(pl.multiple_of(qb * QB, QB), QB)
        oacc[...] = jnp.zeros_like(oacc)
        mrow[...] = jnp.full_like(mrow, -3e38)
        lrow[...] = jnp.zeros_like(lrow)

        def step(unit, size, masked):
            ks = pl.ds(pl.multiple_of(unit * UNIT, UNIT), size)
            scale = {}

            def scores(h):
                s = dot(kaug[h, ks, :], qaug[h, :, q])
                sbuf[h, :size] = jnp.where(below_diagonal(), s, NEGATIVE) if masked else s

            def softmax(h):
                s = sbuf[h, :size]
                m_old = mrow[h : h + 1, :]
                m_new = jnp.maximum(m_old, jnp.max(s, axis=0, keepdims=True))
                scale[h] = jnp.exp2(m_old - m_new)
                p = jnp.exp2(s - m_new)
                lrow[h : h + 1, :] = lrow[h : h + 1, :] * scale[h] + jnp.sum(p, axis=0, keepdims=True)
                mrow[h : h + 1, :] = m_new
                pbuf[h, :size] = p.astype(BF)

            def mix(h):
                hs = slice(h * 64, h * 64 + 64)
                oacc[hs, :] = oacc[hs, :] * scale[h] + dot(vt[hs, ks], pbuf[h, :size])

            staged(scores, 7, softmax, 1, mix)

        visit(qb, step)
        for h in range(HEADS):
            hs = slice(h * 64, h * 64 + 64)
            attT_ref[hs, q] = (oacc[hs, :] * (1.0 / lrow[h : h + 1, :])).astype(BF)
        lse_ref[:, q] = mrow[...] + jnp.log2(lrow[...])
        after(qb)


def query_codes(ids_row, length):
    row = lax.broadcasted_iota(jnp.int32, (16, length), 0)
    return jnp.where(row == jnp.broadcast_to(ids_row, (16, length)), 1.0, 0.0), row


def fill_queries(qaug, qT_ref, codes, row, lse_ref, length):
    for h in range(HEADS):
        a, b = query_rows(h)
        qaug[h, a : a + 64, :] = qT_ref[h * 64 : h * 64 + 64, :]
        extra = codes
        if lse_ref is not None:
            lse = lse_ref[h : h + 1, :]
            hi = lse.astype(BF).astype(F32)
            mid = (lse - hi).astype(BF).astype(F32)
            low = lse - hi - mid
            extra = jnp.where(row == 4, hi, jnp.where(row == 5, mid, jnp.where(row == 6, low, codes)))
        qaug[h, b : b + 16, :] = extra.astype(BF)
        qaug[h, b + 16 : b + 64, :] = jnp.zeros((48, length), BF)


def project_queries(src_ref, w_ref, qT_ref, length, width):
    @pl.loop(0, length // TB)
    def _(t):
        rows = pl.ds(pl.multiple_of(t * TB, TB), TB)
        q = dot(src_ref[rows, :], w_ref[:, :width]) * (0.125 * LOG2E)
        qT_ref[:, rows] = q.T.astype(BF)


def out_and_norm(attT_ref, w_ref, resid_ref, sm_ref, norm, res_ref, hid_ref, length):
    @pl.loop(0, length // TB)
    def _(t):
        rows = pl.ds(pl.multiple_of(t * TB, TB), TB)
        a = dot(attT_ref[:, rows], w_ref[...], 0, 0)
        r = resid_ref[rows, :].astype(F32) + a
        res_ref[rows, :] = r.astype(BF)
        unit, _ = norm_stats(r)
        hid_ref[rows, :] = (unit * gain_of(sm_ref, norm) + shift_of(sm_ref, norm)).astype(BF)


def self_forward(causal, x_ref, ids_ref, weights, small_ref, results, tick,
                 kaug, qaug, vt, oacc, mrow, lrow, sbuf, pbuf):
    wq, wk, wv, wout = weights
    qT_ref, k_ref, v_ref, attT_ref, lse_ref, res_ref, hid_ref = results
    length, width = x_ref.shape
    tick(0)

    @pl.loop(0, length // TB)
    def _(t):
        rows = pl.ds(pl.multiple_of(t * TB, TB), TB)
        x = x_ref[rows, :]
        q = dot(x, wq[...]) * (0.125 * LOG2E)
        k = dot(x, wk[...])
        v = dot(x, wv[...])
        qT_ref[:, rows] = q.T.astype(BF)
        k_ref[rows, :] = k.astype(BF)
        v_ref[rows, :] = v.astype(BF)
        vt[:, rows] = v.T.astype(BF)

    for result in (qT_ref, k_ref, v_ref):
        result.flush()
    tick(1)
    codes, low_half = key_codes(ids_ref[...], length)
    fill_keys(kaug, k_ref, codes, low_half)
    qcodes, row = query_codes(ids_ref[...], length)
    fill_queries(qaug, qT_ref, qcodes, row, None, length)
    tick(2)
    attend_loop(functools.partial(visit_all, causal), lambda qb: tick(3 + qb), qaug, kaug, vt, attT_ref, lse_ref,
                oacc, mrow, lrow, sbuf, pbuf, length)
    attT_ref.flush()
    lse_ref.flush()
    tick(7)
    out_and_norm(attT_ref, wout, x_ref, small_ref, 0, res_ref, hid_ref, length)
    res_ref.flush()
    hid_ref.flush()


def cross_fwd_kernel(h_ref, kv_ref, qids_ref, kids_ref, w_ref, ln_ref,
                     qT_ref, attT_ref, lse_ref, res_ref, hid_ref,
                     kaug, qaug, vt, oacc, mrow, lrow, sbuf, pbuf):
    h_ref, w_ref = ready(h_ref, w_ref)
    length, width = h_ref.shape
    project_queries(h_ref, w_ref, qT_ref, length, width)
    qT_ref.flush()
    kv_ref, qids_ref, kids_ref = ready(kv_ref, qids_ref, kids_ref)

    @pl.loop(0, length // TB)
    def _(t):
        rows = pl.ds(pl.multiple_of(t * TB, TB), TB)
        vt[:, rows] = kv_ref[rows, width:].astype(F32).T.astype(BF)

    codes, low_half = key_codes(kids_ref[...], length)
    fill_keys(kaug, kv_ref, codes, low_half)
    qcodes, row = query_codes(qids_ref[...], length)
    fill_queries(qaug, qT_ref, qcodes, row, None, length)
    attend_loop(functools.partial(visit_keys, qids_ref, kids_ref), lambda qb: None, qaug, kaug, vt, attT_ref, lse_ref,
                oacc, mrow, lrow, sbuf, pbuf, length)
    attT_ref.flush()
    lse_ref.flush()
    (ln_ref,) = ready(ln_ref)
    out_and_norm(attT_ref, w_ref.at[:, width:], h_ref, ln_ref, 1, res_ref, hid_ref, length)


def visit_all(causal, qb, step):
    blocks = 1024 // WIDE
    lo = jnp.where(qb == blocks - 1, 1, 0)
    hi = jnp.where(qb == 0, blocks - 1, blocks)
    if causal is not False:
        lo, hi = jnp.where(causal, 0, lo), jnp.where(causal, qb, hi)

    @pl.loop(lo, hi)
    def _(i):
        step(i * (WIDE // UNIT), WIDE, False)

    if causal is not False:
        @pl.when(causal)
        def _():
            step(qb * (QB // UNIT), WIDE, True)


def attend_back_block(visit, qb, qaug, kaug, kt, vaug, doaug, jgT, jg, dqacc, sbuf, dbuf, pbuf, gbuf):
    width = HEADS * 64
    q = pl.ds(pl.multiple_of(qb * QB, QB), QB)
    dqacc[...] = jnp.zeros_like(dqacc)

    def step(unit, size, masked):
        ks = pl.ds(pl.multiple_of(unit * UNIT, UNIT), size)

        def products(h):
            s = dot(kaug[h, ks, :], qaug[h, :, q])
            sbuf[h % 4, :size] = jnp.where(below_diagonal(), s, NEGATIVE) if masked else s
            dbuf[h % 4, :size] = dot(vaug[h, ks, :], doaug[h, :, q])

        def grads(h):
            p = jnp.exp2(sbuf[h % 4, :size])
            pbuf[h % 4, :size] = p.astype(BF)
            gbuf[h % 4, :size] = (p * dbuf[h % 4, :size]).astype(BF)

        def add(h):
            a, _ = query_rows(h)
            at = h * 64
            hs = slice(at, at + 64)
            dqacc[hs, :] += dot(kt[hs, ks], gbuf[h % 4, :size])
            jgT[width + at : width + at + 64, ks] += dot(doaug[h, a : a + 64, q], pbuf[h % 4, :size], 1, 1)
            jgT[at : at + 64, ks] += dot(qaug[h, a : a + 64, q], gbuf[h % 4, :size], 1, 1)

        lag = 1 if size == WIDE else 2
        staged(products, lag, grads, lag, add)

    visit(qb, step)
    jg[:width, q] = (dqacc[...] * 0.125).astype(BF)


def attend_back_finish(jgT, jg):
    width = HEADS * 64
    jg[width : 2 * width, :] = (jgT[:width, :] * math.log(2.0)).astype(BF)
    jg[2 * width :, :] = jgT[width:, :].astype(BF)


def prepare_back(dr_ref, w_ref, attT_ref, doaug, length):
    @pl.loop(0, length // TB)
    def _(t):
        rows = pl.ds(pl.multiple_of(t * TB, TB), TB)
        row = lax.broadcasted_iota(jnp.int32, (16, TB), 0)
        d = dot(w_ref[...], dr_ref[rows, :], 1, 1).astype(BF)
        for h in range(HEADS):
            a, b = query_rows(h)
            hs = slice(h * 64, h * 64 + 64)
            doh = d[hs, :]
            doaug[h, a : a + 64, rows] = doh
            delta = jnp.sum(doh.astype(F32) * attT_ref[hs, rows].astype(F32), axis=0, keepdims=True)
            hi = delta.astype(BF).astype(F32)
            mid = (delta - hi).astype(BF).astype(F32)
            low = delta - hi - mid
            extra = jnp.where(row == 4, hi, jnp.where(row == 5, mid, jnp.where(row == 6, low, 0.0)))
            doaug[h, b : b + 16, rows] = extra.astype(BF)
            doaug[h, b + 16 : b + 64, rows] = jnp.zeros((48, TB), BF)


def prepare_keys(keys_ref, values_ref, codes, low_half, kaug, kt, vaug, length):
    fill_keys(kaug, keys_ref, codes, low_half)
    fill_keys(vaug, values_ref, jnp.where(codes == NEGATIVE, 0.0, codes), low_half)

    @pl.loop(0, length // TB)
    def _(t):
        rows = pl.ds(pl.multiple_of(t * TB, TB), TB)
        kt[:, rows] = keys_ref[rows, :].astype(F32).T.astype(BF)


def self_backward_phases(causal, operands, arrived, reuse, put_dx, dw_ref, dln_ref,
                         kaug, kt, vaug, qaug, doaug, dqacc, jgT, jg, sbuf, dbuf, pbuf, gbuf):
    dh_ref, res_ref, x_ref, ids_ref, qT_ref, k_ref, v_ref, attT_ref, lse_ref, w_ref, wout_ref, ln_ref = operands
    dh, res, x, ids, qT, keys, values, attT, lse, w, wout, small = range(len(operands))
    length, width = res_ref.shape
    dr = res_ref

    def before():
        arrived(dh, res, small)
        dln_ref[...] = jnp.zeros(dln_ref.shape, F32)

        @pl.loop(0, length // TB)
        def _(t):
            rows = pl.ds(pl.multiple_of(t * TB, TB), TB)
            unit, scale = norm_stats(res_ref[rows, :].astype(F32))
            d, gg, sg = norm_back(dh_ref[rows, :].astype(F32), unit, scale, gain_of(ln_ref, 0))
            dln_ref[5:6, :] += gg
            dln_ref[8:9, :] += sg
            dr[rows, :] = d.astype(BF)

        arrived(attT, wout, ids)
        dw_ref[3] = dot(attT_ref[...], dr[...]).astype(BF)
        prepare_back(dr, wout_ref, attT_ref, doaug, length)

    def block(qb):
        attend_back_block(functools.partial(visit_all, causal), qb, qaug, kaug, kt, vaug, doaug,
                          jgT, jg, dqacc, sbuf, dbuf, pbuf, gbuf)

    def fill():
        codes, low_half = key_codes(ids_ref[...], length)
        arrived(keys, values, qT, lse)
        prepare_keys(k_ref, v_ref, codes, low_half, kaug, kt, vaug, length)
        qcodes, row = query_codes(ids_ref[...], length)
        fill_queries(qaug, qT_ref, qcodes, row, lse_ref, length)
        jgT[...] = jnp.zeros_like(jgT)

    def after():
        reuse(dh, ids, qT, keys, values, attT, lse, wout, small)
        attend_back_finish(jgT, jg)
        arrived(x, w)

        @pl.loop(0, 3)
        def _(t):
            rows = pl.ds(pl.multiple_of(t * 512, 512), 512)
            dw_ref[t] = dot(jg[rows, :], x_ref[...]).astype(BF)

    def inputs():
        @pl.loop(0, length // TB)
        def _(t):
            rows = pl.ds(pl.multiple_of(t * TB, TB), TB)
            put_dx(rows, dr[rows, :].astype(F32) + dot(jg[:, rows], w_ref[...], 0, 1))

        reuse(res, x, w)

    return before, fill, block, after, inputs


def cross_bwd_kernel(dr_ref, h_ref, mem_ref, qids_ref, kids_ref, qT_ref, kv_ref, attT_ref,
                     lse_ref, w_ref, wkv_ref,
                     dh_ref, dmem_ref, dwd_ref, dwe_ref,
                     kaug, kt, vaug, qaug, doaug, dqacc, jgT, jg, sbuf, dbuf, pbuf, gbuf):
    dr_ref, attT_ref, w_ref, qids_ref, kids_ref = ready(dr_ref, attT_ref, w_ref, qids_ref, kids_ref)
    length, width = dr_ref.shape
    dwd_ref[1] = dot(dr_ref[...], attT_ref[...], 0, 1).astype(BF)
    prepare_back(dr_ref, w_ref.at[:, width:], attT_ref, doaug, length)
    codes, low_half = key_codes(kids_ref[...], length)
    kv_ref, qT_ref, lse_ref = ready(kv_ref, qT_ref, lse_ref)
    prepare_keys(kv_ref.at[:, :width], kv_ref.at[:, width:], codes, low_half, kaug, kt, vaug, length)
    qcodes, row = query_codes(qids_ref[...], length)
    fill_queries(qaug, qT_ref, qcodes, row, lse_ref, length)
    jgT[...] = jnp.zeros_like(jgT)

    @pl.loop(0, length // QB)
    def _(qb):
        attend_back_block(functools.partial(visit_keys, qids_ref, kids_ref), qb, qaug, kaug, kt, vaug,
                          doaug, jgT, jg, dqacc, sbuf, dbuf, pbuf, gbuf)

    attend_back_finish(jgT, jg)
    h_ref, mem_ref, wkv_ref = ready(h_ref, mem_ref, wkv_ref)
    dwd_ref[0] = dot(jg[:width, :], h_ref[...]).astype(BF)
    for half in range(2):
        dwe_ref[half] = dot(jg[(half + 1) * width : (half + 2) * width, :], mem_ref[...]).astype(BF)
    dwd_ref.flush()
    dwe_ref.flush()

    @pl.loop(0, length // TB)
    def _(t):
        rows = pl.ds(pl.multiple_of(t * TB, TB), TB)
        d = dot(jg[:width, rows], w_ref[:, :width], 0, 1)
        dh_ref[rows, :] = (dr_ref[rows, :].astype(F32) + d).astype(BF)
        dmem_ref[rows, :] = dot(jg[width:, rows], wkv_ref[...], 0, 1).astype(BF)


def enc_ffn_fwd_kernel(e1_ref, win_ref, ln_ref, wout_ref, wkv_ref,
                       g_ref, gp_ref, r_ref, mem_ref, kv_ref, ubuf):
    e1_ref, win_ref, ln_ref = ready(e1_ref, win_ref, ln_ref)
    length, width = e1_ref.shape
    ff = win_ref.shape[1]
    slabs = ff // 512
    late = []
    later = (wout_ref, wkv_ref)

    def at(i):
        b, j = divmod(i, slabs)
        return slice(b * FB, b * FB + FB), slice(j * 512, j * 512 + 512), j

    def up(i):
        rows, cols, j = at(i)
        ubuf[i % 4] = dot(e1_ref[rows, :], win_ref[:, cols])

    def act(i):
        rows, cols, j = at(i)
        g, gp = gelu_pair(ubuf[i % 4] + ln_ref[j : j + 1, :])
        g_ref[rows, cols] = g.astype(BF)
        gp_ref[rows, cols] = gp.astype(BF)

    def down(b):
        rows = slice(b * FB, b * FB + FB)
        if not late:
            late.extend(ready(*later))
        total = dot(g_ref[rows, :], late[0][...]) + e1_ref[rows, :].astype(F32) + ln_ref[4:5, :]
        r_ref[rows, :] = total.astype(BF)
        unit, _ = norm_stats(total)
        e2 = unit * gain_of(ln_ref, 1) + shift_of(ln_ref, 1)
        unit, _ = norm_stats(e2)
        mem_ref[rows, :] = (unit * gain_of(ln_ref, 2) + shift_of(ln_ref, 2)).astype(BF)

    def project(b):
        rows = slice(b * FB, b * FB + FB)
        kv_ref[rows, :] = dot(mem_ref[rows, :], late[1][...]).astype(BF)
        for result in (g_ref, gp_ref, r_ref, mem_ref, kv_ref):
            result.flush_rows(b, FB)

    units = length // FB * slabs
    for tick in range(units + 4):
        if tick < units:
            up(tick)
        i = tick - 2
        if 0 <= i < units:
            act(i)
            if i % slabs == slabs - 1:
                down(i // slabs)
        i = tick - 4
        if 0 <= i < units and i % slabs == slabs - 1:
            project(i // slabs)
    for result in (g_ref, gp_ref, r_ref, mem_ref, kv_ref):
        result.started = True


def weight_grads(act_ref, du_ref, df_ref, g_ref, dw_ref):
    slabs = du_ref.shape[1] // 512

    @pl.loop(0, slabs)
    def _(t):
        cols = pl.ds(pl.multiple_of(t * 512, 512), 512)
        dw_ref[t] = dot(act_ref[...], du_ref[:, cols], 0, 0).astype(BF)
        dw_ref.flush_part(t)
        dw_ref[slabs + t] = dot(df_ref[...], g_ref[:, cols], 0, 0).astype(BF)
        dw_ref.flush_part(slabs + t)

    dw_ref.started = True


def enc_ffn_bwd_kernel(dmem_ref, r_ref, ln_ref, wout_ref, gp_ref, win_ref, e1_ref, g_ref,
                       de1_ref, dw_ref, dln_ref,
                       df_ref, dgbuf, drbuf):
    dmem_ref, r_ref, ln_ref = ready(dmem_ref, r_ref, ln_ref)
    length, width = r_ref.shape
    ff = gp_ref.ref.shape[1]
    slabs = ff // 512
    dln_ref[...] = jnp.zeros(dln_ref.shape, F32)

    def at(i):
        b, j = divmod(i, slabs)
        return slice(b * FB, b * FB + FB), slice(j * 512, j * 512 + 512), j

    def norms(b):
        rows = slice(b * FB, b * FB + FB)
        unit2, scale2 = norm_stats(r_ref[rows, :].astype(F32))
        e2 = unit2 * gain_of(ln_ref, 1) + shift_of(ln_ref, 1)
        unit3, scale3 = norm_stats(e2)
        de2, gg, sg = norm_back(dmem_ref[rows, :].astype(F32), unit3, scale3, gain_of(ln_ref, 2))
        dln_ref[7:8, :] += gg
        dln_ref[10:11, :] += sg
        dr, gg, sg = norm_back(de2, unit2, scale2, gain_of(ln_ref, 1))
        dln_ref[6:7, :] += gg
        dln_ref[9:10, :] += sg
        df = dr.astype(BF)
        df_ref[rows, :] = df
        drbuf[b] = dr
        dln_ref[4:5, :] += jnp.sum(df.astype(F32), axis=0, keepdims=True)

    def up_back(i):
        rows, cols, j = at(i)
        dgbuf[i % 4] = dot(df_ref[rows, :], wout_ref[cols, :], 1, 1)

    def act_back(i):
        rows, cols, j = at(i)
        du = dgbuf[i % 4] * gp_ref[rows, cols].astype(F32)
        gp_ref[rows, cols] = du.astype(BF)
        dln_ref[j : j + 1, :] += jnp.sum(du, axis=0, keepdims=True)

    def down_back(b):
        rows = slice(b * FB, b * FB + FB)
        de1_ref[rows, :] = (drbuf[b] + dot(gp_ref[rows, :], win_ref[...], 1, 1)).astype(BF)

    norms(0)
    wout_ref, gp_ref, win_ref = ready(wout_ref, gp_ref, win_ref)
    units = length // FB * slabs
    for tick in range(units + 2):
        if tick < units:
            up_back(tick)
            if tick % slabs == 1 and tick // slabs + 1 < length // FB:
                norms(tick // slabs + 1)
        i = tick - 2
        if 0 <= i < units:
            act_back(i)
            if i % slabs == slabs - 1:
                down_back(i // slabs)
    de1_ref.flush()
    e1_ref, g_ref = ready(e1_ref, g_ref)
    weight_grads(e1_ref, gp_ref, df_ref, g_ref, dw_ref)


def dec_ffn_kernel(h_ref, win_ref, ln_ref, wout_ref, cot_ref, res_ref, mem_ref,
                   out_ref, away_ref, dres_ref, dw_ref, dln_ref,
                   g_ref, du_ref, df_ref, ubuf, gpbuf, dgbuf, drbuf):
    h_ref, win_ref, ln_ref = ready(h_ref, win_ref, ln_ref)
    length, width = h_ref.shape
    ff = win_ref.shape[1]
    dln_ref[...] = jnp.zeros(dln_ref.shape, F32)
    slabs = ff // 512
    late = []

    def at(i):
        b, j = divmod(i, slabs)
        return slice(b * FB, b * FB + FB), slice(j * 512, j * 512 + 512), j

    def up(i):
        rows, cols, j = at(i)
        ubuf[i % 4] = dot(h_ref[rows, :], win_ref[:, cols])

    def act(i):
        rows, cols, j = at(i)
        g, gp = gelu_pair(ubuf[i % 4] + ln_ref[j : j + 1, :])
        g_ref[rows, cols] = g.astype(BF)
        gpbuf[i % 8] = gp.astype(BF)

    def down(b):
        rows = slice(b * FB, b * FB + FB)
        if not late:
            late.extend(ready(wout_op, cot_op, res_op))
        wout, cot, _ = late
        total = dot(g_ref[rows, :], wout[...]) + h_ref[rows, :].astype(F32) + ln_ref[4:5, :]
        unit3, scale3 = norm_stats(total)
        out_ref[rows, :] = (unit3 * gain_of(ln_ref, 2) + shift_of(ln_ref, 2)).astype(BF)
        dr, gg, sg = norm_back(cot[rows, :].astype(F32), unit3, scale3, gain_of(ln_ref, 2))
        dln_ref[7:8, :] += gg
        dln_ref[10:11, :] += sg
        df = dr.astype(BF)
        df_ref[rows, :] = df
        drbuf[b % 2] = dr
        dln_ref[4:5, :] += jnp.sum(df.astype(F32), axis=0, keepdims=True)

    def up_back(i):
        rows, cols, j = at(i)
        dgbuf[i % 4] = dot(df_ref[rows, :], late[0][cols, :], 1, 1)

    def act_back(i):
        rows, cols, j = at(i)
        du = dgbuf[i % 4] * gpbuf[i % 8].astype(F32)
        du_ref[rows, cols] = du.astype(BF)
        dln_ref[j : j + 1, :] += jnp.sum(du, axis=0, keepdims=True)

    def down_back(b):
        rows = slice(b * FB, b * FB + FB)
        total = drbuf[b % 2] + dot(du_ref[rows, :], win_ref[...], 1, 1)
        unit2, scale2 = norm_stats(late[2][rows, :].astype(F32))
        d, gg, sg = norm_back(total, unit2, scale2, gain_of(ln_ref, 1))
        dln_ref[6:7, :] += gg
        dln_ref[9:10, :] += sg
        dres_ref[rows, :] = d.astype(BF)

    wout_op, cot_op, res_op = wout_ref, cot_ref, res_ref
    units = length // FB * slabs
    for tick in range(units + 6 + 1):
        if tick < units:
            up(tick)
        i = tick - 2
        if 0 <= i < units:
            act(i)
            if i % slabs == slabs - 1:
                down(i // slabs)
        i = tick - 6
        if 0 <= i < units:
            up_back(i)
        i -= 1
        if 0 <= i < units:
            act_back(i)
            if i % slabs == slabs - 1:
                down_back(i // slabs)
    out_ref.flush()
    dres_ref.flush()
    (mem_ref,) = ready(mem_ref)
    section = lax.axis_index("section")

    @pl.when(section == 0)
    def _():
        pltpu.make_async_copy(out_ref.ref, away_ref.copy.dst_ref, away_ref.copy.dst_sem).start()

    @pl.when(section != 0)
    def _():
        pltpu.make_async_copy(mem_ref, away_ref.copy.dst_ref, away_ref.copy.dst_sem).start()

    away_ref.started = True
    weight_grads(h_ref, du_ref, df_ref, g_ref, dw_ref)


class Operand:
    def __init__(self, copy, ref):
        self.copy, self.ref = copy, ref


def ready(*operands):
    refs = []
    for operand in operands:
        if operand.copy is not None:
            operand.copy.wait()
            operand.copy = None
        refs.append(operand.ref)
    return refs


class Result:
    def __init__(self, copy, ref):
        self.copy, self.ref, self.started, self.waited = copy, ref, False, False

    def __getitem__(self, at):
        return self.ref[at]

    def __setitem__(self, at, value):
        self.ref[at] = value

    def __getattr__(self, name):
        return getattr(self.ref, name)

    def wait(self):
        if not self.waited:
            self.copy.wait()
            self.waited = True

    def flush_part(self, k):
        copy = self.copy
        pltpu.make_async_copy(self.ref.at[k], copy.dst_ref.at[k], copy.dst_sem).start()

    def flush_rows(self, k, size):
        rows = pl.ds(k * size, size)
        copy = self.copy
        pltpu.make_async_copy(self.ref.at[rows], copy.dst_ref.at[rows], copy.dst_sem).start()

    def flush(self):
        if not self.started:
            self.copy.start()
            self.started = True


class Row:
    def __init__(self, array):
        self.array, self.shape, self.dtype = array, array.shape[1:], array.dtype


class Pick:
    def __init__(self, zero, one=None):
        self.parts = [zero] if one is None else [zero, one]
        self.arrays = [p.array if isinstance(p, Row) else p for p in self.parts]
        self.shape, self.dtype = zero.shape, zero.dtype

    def start(self, refs, dst, sem, section):
        sources = [ref.at[section] if isinstance(p, Row) else ref for p, ref in zip(self.parts, refs)]
        if len(sources) == 1:
            pltpu.make_async_copy(sources[0], dst, sem).start()
            return
        for k, source in enumerate(sources):
            @pl.when(section == k)
            def _(source=source):
                pltpu.make_async_copy(source, dst, sem).start()

    def copy(self, refs, dst, sem, section):
        self.start(refs, dst, sem, section)
        return pltpu.make_async_copy(dst, dst, sem)


def run_kernel(kernel, plan, n_out, *refs):
    n_in = sum(len(p.arrays) for p in plan)
    ins, outs = list(refs[:n_in]), refs[n_in : n_in + n_out]
    rest = refs[n_in + n_out :]
    in_bufs, out_bufs = rest[: len(plan)], rest[len(plan) : len(plan) + n_out]
    in_sem, out_sem = rest[len(plan) + n_out : len(plan) + n_out + 2]
    scratch = rest[len(plan) + n_out + 2 :]
    section = lax.axis_index("section")
    operands = []
    for k, entry in enumerate(plan):
        given = [ins.pop(0) for _ in entry.arrays]
        operands.append(Operand(entry.copy(given, in_bufs[k], in_sem.at[k], section), in_bufs[k]))
    results = [
        Result(pltpu.make_async_copy(out_bufs[k], outs[k], out_sem.at[k]), out_bufs[k]) for k in range(n_out)
    ]
    kernel(*operands, *results, *scratch)
    ready(*operands)
    for result in results:
        result.flush()
    for result in results:
        result.wait()


def call(kernel, name, outs, scratch, flops, *args):
    any_space = pl.BlockSpec(memory_space=pl.ANY)
    plan = [a if isinstance(a, Pick) else Pick(a) for a in args]
    given = [array for entry in plan for array in entry.arrays]
    return pl.pallas_call(
        functools.partial(run_kernel, kernel, plan, len(outs)),
        out_shape=[jax.ShapeDtypeStruct(s, d) for s, d in outs],
        in_specs=[any_space] * len(given),
        out_specs=[any_space] * len(outs),
        scratch_shapes=[pltpu.VMEM(entry.shape, entry.dtype) for entry in plan]
        + [pltpu.VMEM(s, d) for s, d in outs]
        + [pltpu.SemaphoreType.DMA((len(plan),)), pltpu.SemaphoreType.DMA((len(outs),))]
        + scratch,
        compiler_params=pltpu.CompilerParams(vmem_limit_bytes=VMEM_LIMIT),
        cost_estimate=pl.CostEstimate(flops=flops, bytes_accessed=8 << 20, transcendentals=0),
        name=name,
    )(*given)


def fwd_scratch(n, w):
    return [
        pltpu.VMEM((HEADS, n, 128), BF),
        pltpu.VMEM((HEADS, 128, n), BF),
        pltpu.VMEM((w, n), BF),
        pltpu.VMEM((w, QB), F32),
        pltpu.VMEM((HEADS, QB), F32),
        pltpu.VMEM((HEADS, QB), F32),
        pltpu.VMEM((HEADS, WIDE, QB), F32),
        pltpu.VMEM((HEADS, WIDE, QB), BF),
    ]


def bwd_scratch(n, w):
    return [
        pltpu.VMEM((HEADS, n, 128), BF),
        pltpu.VMEM((w, n), BF),
        pltpu.VMEM((HEADS, n, 128), BF),
        pltpu.VMEM((HEADS, 128, n), BF),
        pltpu.VMEM((HEADS, 128, n), BF),
        pltpu.VMEM((w, QB), F32),
        pltpu.VMEM((2 * w, n), F32),
        pltpu.VMEM((3 * w, n), BF),
        pltpu.VMEM((4, WIDE, QB), F32),
        pltpu.VMEM((4, WIDE, QB), F32),
        pltpu.VMEM((4, WIDE, QB), BF),
        pltpu.VMEM((4, WIDE, QB), BF),
    ]


def middle_back_kernel(dr, h, mem, tgt, src, qT, kv, att, lse, cross, wkv, r, small, wout, gp, win, e1, g,
                       dh, dwd, dwe, de1, dw, dln, dmem, df, dgbuf, drbuf, *bwd):
    cross_bwd_kernel(dr, h, mem, tgt, src, qT, kv, att, lse, cross, wkv, dh, dmem, dwd, dwe, *bwd)
    dh.flush()
    enc_ffn_bwd_kernel(Operand(None, dmem), r, small, wout, gp, win, e1, g, de1, dw, dln, df, dgbuf, drbuf)


def middle_back(dr, h, mem, tgt, src, qT, kv, att, lse, cross, wkv, r, small, wout, gp, win, e1, g):
    n, w = r.shape
    ff = win.shape[-1]
    row, pair = ((n, w), BF), ((2, w, w), BF)
    return call(middle_back_kernel, "cross_and_ffn_backward",
                [row, pair, pair, row, ((2 * ff // w, w, w), BF), ((16, w), F32)],
                [pltpu.VMEM((n, w), BF), pltpu.VMEM((n, w), BF), pltpu.VMEM((4, FB, 512), F32),
                 pltpu.VMEM((n // FB, FB, w), F32)] + bwd_scratch(n, w), 30 << 30,
                dr, h, mem, tgt, src, qT, kv, att, lse, cross, wkv, r, small, wout, gp, win, e1, g)


def middle_kernel(e1, win, small, wout, wkv, d1, tgt, src, cross, small2, win2, wout2, cot,
                  g, gp, r2, mem, kv, qT, att, lse, out, away, dres, dw, dln,
                  cr, d2, ubuf, df, gpbuf, dgbuf, drbuf, *fwd):
    enc_ffn_fwd_kernel(e1, win, small, wout, wkv, g, gp, r2, mem, kv, ubuf)
    cross_fwd_kernel(d1, Operand(None, kv.ref), tgt, src, cross, small2, qT, att, lse, cr, d2, *fwd)
    g.wait()
    gp.wait()
    dec_ffn_kernel(Operand(None, d2), win2, small2, wout2, cot, Operand(None, cr), Operand(None, mem.ref),
                   out, away, dres, dw, dln, g.ref, gp.ref, df, ubuf, gpbuf, dgbuf, drbuf)


def middle(e1, win, small, wout, wkv, d1, tgt, src, cross, small2, win2, wout2, cot):
    n, w = e1.shape
    ff = win.shape[-1]
    row = ((n, w), BF)
    return call(middle_kernel, "feed_forward_and_cross",
                [((n, ff), BF), ((n, ff), BF), row, row, ((n, 2 * w), BF), ((w, n), BF), ((w, n), BF), ((HEADS, n), F32),
                 row, row, row, ((2 * ff // w, w, w), BF), ((16, w), F32)],
                [pltpu.VMEM((n, w), BF), pltpu.VMEM((n, w), BF), pltpu.VMEM((4, FB, 512), F32), pltpu.VMEM((n, w), BF),
                 pltpu.VMEM((8, FB, 512), BF), pltpu.VMEM((4, FB, 512), F32), pltpu.VMEM((2, FB, w), F32)] + fwd_scratch(n, w),
                30 << 30, e1, win, small, wout, wkv, d1, tgt, src, cross, small2, win2, wout2, cot)


CHUNK = 512
SLOTS = 4
PARTS = 5
MESH = pl.DeviceIdType.MESH
ANY = pl.BlockSpec(memory_space=pl.ANY)


def bit_of(index, bit):
    return (index // 2**bit) % 2


def partner_of(index, bit):
    return index + 2**bit - 2 * 2**bit * bit_of(index, bit)


def greet(partners):
    barrier = pltpu.get_barrier_semaphore()
    for device in partners:
        pl.semaphore_signal(barrier, inc=1, device_id=device, device_id_type=MESH)
    pl.semaphore_wait(barrier, len(partners))


def halvings(devices, rows):
    bits = devices.bit_length() - 1
    halved = 0
    while halved < bits and (rows >> (halved + 1)) >= 16 and (rows >> (halved + 1)) % 16 == 0:
        halved += 1
    return list(range(halved)), list(range(halved, bits))


def place(index, count, rows):
    at, size = 0, rows
    for bit in range(count):
        size //= 2
        at = at + bit_of(index, bit) * size
    return at, size


class Sums:
    def __init__(self, devices, groups, early, gap, out_ref, scratch):
        self.groups, self.early, self.gap, self.out = groups, early, gap, out_ref
        self.held, self.shard, self.load_sem, self.store_sem, self.core_sem, self.send_sem, self.recv_sem = scratch[:7]
        self.landing = scratch[7:]
        self.index, self.section = lax.axis_index("dp"), lax.axis_index("section")
        self.halved, self.rest = halvings(devices, CHUNK)
        self.bits = self.halved + self.rest
        self.across = (1 - self.section, self.index)
        self.mates = [(self.section, partner_of(self.index, bit)) for bit in self.bits]
        self.chunks = sum(group[0] for group in groups)
        self.steps = 1 + len(self.bits) + len(self.halved)
        self.ticks = self.chunks + gap + self.steps

    def rows(self, count, other=False):
        at, size = 0, CHUNK
        for bit in range(count):
            size //= 2
            side = bit_of(self.index, bit)
            at = at + (1 - side if other and bit == count - 1 else side) * size
        return at, size

    def window(self, count, other=False):
        at, size = self.rows(count, other)
        return pl.ds(pl.multiple_of(at - self.rows(1)[0], 16), size)

    def remote(self, src, dst, step, c, device):
        return pltpu.make_async_remote_copy(
            src_ref=src, dst_ref=dst, send_sem=self.send_sem.at[step, c], recv_sem=self.recv_sem.at[step, c],
            device_id=device, device_id_type=MESH)

    def begin(self, c):
        at, size = self.rows(1)
        far, _ = self.rows(1, True)
        first = 0
        for count, *pair in self.groups:
            @pl.when((c >= first) & (c < first + count))
            def _(first=first, pair=pair):
                for k, (ref, layer) in enumerate(pair):
                    near = ref.at[c - first, pl.ds(pl.multiple_of(at, 16), size)]
                    away = ref.at[c - first, pl.ds(pl.multiple_of(far, 16), size)]
                    pltpu.make_async_copy(near, self.held.at[c, layer], self.load_sem.at[k, c]).start()
                    self.core_copy(k, c, away, layer).start()
            first += count

    def core_copy(self, k, c, src, layer):
        return pltpu.make_async_remote_copy(
            src_ref=src, dst_ref=self.landing[0].at[c % SLOTS, layer], send_sem=self.core_sem.at[0, k, c],
            recv_sem=self.core_sem.at[1, k, c], device_id=self.mates[0], device_id_type=MESH)

    def copy(self, step, c):
        reduce_steps = 1 + len(self.bits)
        if step == 1:
            return self.remote(self.held.at[c, 1 - self.section], self.landing[1].at[c % SLOTS], 1, c, self.across)
        if step < reduce_steps:
            bit = step - 1
            window = self.window(bit + 1, True) if bit in self.halved else self.window(len(self.halved))
            return self.remote(self.held.at[c, self.section, window], self.landing[step].at[c % SLOTS], step, c, self.mates[bit])
        bit = self.halved[-1 - (step - reduce_steps)]
        at, size = self.rows(bit + 1)
        rows = self.out.at[c, pl.ds(pl.multiple_of(at, 16), size)]
        return self.remote(self.shard.at[c] if step == reduce_steps else rows, rows, step, c, self.mates[bit])

    def store(self, c):
        at, size = self.rows(len(self.halved))
        return pltpu.make_async_copy(self.shard.at[c], self.out.at[c, pl.ds(pl.multiple_of(at, 16), size)], self.store_sem.at[c])

    def arrive(self, step, c):
        reduce_steps = 1 + len(self.bits)
        if step == 0:
            for k in range(2):
                pltpu.make_async_copy(self.landing[0].at[c % SLOTS, k], self.held.at[c, k], self.load_sem.at[k, c]).wait()
                self.core_copy(k, c, self.held.at[c, k], k).wait()
            for k in range(2):
                self.held[c, k] = (self.held[c, k].astype(F32) + self.landing[0][c % SLOTS, k].astype(F32)).astype(BF)
            return
        self.copy(step, c).wait()
        if step < reduce_steps:
            bit = step - 1
            window = self.window(1) if step == 1 else self.window(min(bit + 1, len(self.halved)))
            total = (self.held[c, self.section, window, :].astype(F32) + self.landing[step][c % SLOTS].astype(F32)).astype(BF)
            if step == reduce_steps - 1:
                self.shard[c] = total
                self.store(c).start()
            else:
                self.held[c, self.section, window, :] = total
        elif step == reduce_steps:
            self.store(c).wait()

    def tick(self, t):
        for step in range(self.steps + 1):
            at = t - step
            late = at >= self.early + self.gap
            c = jnp.where(late, at - self.gap, at)

            @pl.when(((at >= 0) & (at < self.early)) | (late & (c < self.chunks)))
            def _(step=step, c=c):
                if step == 0:
                    self.begin(c)
                else:
                    self.arrive(step - 1, c)
                    if step < self.steps:
                        self.copy(step, c).start()

    @staticmethod
    def scratch(devices, chunks):
        halved, rest = halvings(devices, CHUNK)
        steps = 1 + len(halved + rest) + len(halved)
        sizes = [CHUNK >> min(bit + 1, len(halved)) for bit in halved + rest]
        return [
            pltpu.VMEM((chunks, 2, CHUNK // 2, 512), BF),
            pltpu.VMEM((chunks, CHUNK >> len(halved), 512), BF),
            pltpu.SemaphoreType.DMA((2, chunks)),
            pltpu.SemaphoreType.DMA((chunks,)),
            pltpu.SemaphoreType.DMA((2, 2, chunks)),
            pltpu.SemaphoreType.DMA((steps, chunks)),
            pltpu.SemaphoreType.DMA((steps, chunks)),
            pltpu.VMEM((SLOTS, 2, CHUNK // 2, 512), BF),
            pltpu.VMEM((SLOTS, CHUNK // 2, 512), BF),
        ] + [pltpu.VMEM((SLOTS, size, 512), BF) for size in sizes[1:]]


class Vectors:
    def __init__(self, sums, scratch):
        self.small, self.arrived, self.send_sem, self.recv_sem = scratch
        self.section = sums.section
        self.partners = [sums.across] + sums.mates

    def copy(self, k):
        return pltpu.make_async_remote_copy(
            src_ref=self.small.at[1 - self.section if k == 0 else self.section], dst_ref=self.arrived.at[k],
            send_sem=self.send_sem.at[k], recv_sem=self.recv_sem.at[k],
            device_id=self.partners[k], device_id_type=MESH)

    def tick(self, t):
        for k in range(len(self.partners) + 1):
            @pl.when(t == k)
            def _(k=k):
                if k > 0:
                    self.copy(k - 1).wait()
                    self.small[self.section] = self.small[self.section] + self.arrived[k - 1]
                if k < len(self.partners):
                    self.copy(k).start()

    @staticmethod
    def scratch(devices):
        n = 1 + len(sum(halvings(devices, CHUNK), []))
        return [pltpu.VMEM((2, 16, 512), F32), pltpu.VMEM((n, 16, 512), F32),
                pltpu.SemaphoreType.DMA((n,)), pltpu.SemaphoreType.DMA((n,))]


def tail_kernel(devices, plans, n_sums, *refs):
    section = lax.axis_index("section")
    refs = list(refs)
    take = lambda n: [refs.pop(0) for _ in range(n)]
    given = [[take(len(entry.arrays)) for entry in plan] for plan in plans]
    ffn_enc, ffn_dec, cross_enc, cross_dec, vec_enc, vec_dec = take(6)
    far_arrived, own_grad, sums_out, small_out = take(4)
    buffers = take(len(plans[0]))
    in_sem, out_sem, dx_send, dx_recv, far_dx, own_dx = take(6)
    dw, dln = take(2)
    vectors_scratch = take(4)
    sums_scratch = take(n_sums)

    groups = [
        (ffn_enc.shape[0], (ffn_enc, 0), (ffn_dec, 1)),
        (cross_enc.shape[0], (cross_enc, 0), (cross_dec, 1)),
        (4, (dw.at[0], 0), (dw.at[1], 1)),
    ]
    early = groups[0][0] + groups[1][0]
    sums = Sums(devices, groups, early, 0, sums_out, sums_scratch)
    vectors = Vectors(sums, vectors_scratch)
    greet([sums.across] + sums.mates)

    def fetch(layer, k):
        plans[layer][k].start(given[layer][k], buffers[k], in_sem.at[layer, k], section)

    for k in range(len(buffers)):
        fetch(1, k)
    result = pltpu.make_async_copy(own_dx, own_grad, out_sem)
    far_copy = pltpu.make_async_remote_copy(
        src_ref=far_dx, dst_ref=far_arrived, send_sem=dx_send, recv_sem=dx_recv,
        device_id=sums.across, device_id_type=MESH)

    @pl.loop(0, sums.ticks)
    def _(t):
        sums.tick(t)
        vectors.tick(t - early)
        part, layer = t % PARTS, jnp.where(t < PARTS, 1, 0)

        def arrived(*numbers):
            for k in numbers:
                pltpu.make_async_copy(buffers[k], buffers[k], in_sem.at[layer, k]).wait()

        def reuse(*numbers):
            @pl.when(layer == 1)
            def _():
                for k in numbers:
                    fetch(0, k)

        def put_dx(rows, value):
            @pl.when(section == layer)
            def _():
                own_dx[rows, :] = value

            @pl.when(section != layer)
            def _():
                far_dx[rows, :] = value.astype(BF)

        before, fill, block, after, inputs = self_backward_phases(
            layer == 1, buffers, arrived, reuse, put_dx, dw.at[layer], dln.at[layer], *refs)
        working = t < 2 * PARTS
        pl.when(working & (part == 0))(before)
        pl.when(working & (part == 1))(fill)

        @pl.when(working & (part >= 1) & (part <= 3))
        def _():
            first = jnp.where(part == 1, 0, jnp.where(part == 2, 1, 3))
            last = jnp.where(part == 1, 1, jnp.where(part == 2, 3, 4))

            @pl.loop(first, last)
            def _(qb):
                block(qb)

        pl.when(working & (part == 4))(after)
        pl.when((t == PARTS - 1) | (t == 2 * PARTS))(inputs)

        @pl.when(t == 2 * PARTS)
        def _():
            result.start()

        @pl.when(t == 2 * PARTS - 1)
        def _():
            vectors.small[0] = vec_enc[...] + dln[0]
            vectors.small[1] = vec_dec[...] + dln[1]

        @pl.when(t == sums.chunks)
        def _():
            far_copy.start()

    small_out[...] = vectors.small[section]
    far_copy.wait()
    result.wait()


def backward_and_sums(first, second, groups, vectors, devices):
    plans = [[a if isinstance(a, Pick) else Pick(a) for a in operands] for operands in (first, second)]
    n, w = plans[0][1].shape
    chunks = sum(pair[0].shape[0] for pair in groups) + 4
    given = [array for plan in plans for entry in plan for array in entry.arrays]
    vm = pl.BlockSpec(memory_space=pltpu.VMEM)
    sums_scratch = Sums.scratch(devices, chunks)
    return pl.pallas_call(
        functools.partial(tail_kernel, devices, plans, len(sums_scratch)),
        out_shape=[
            jax.ShapeDtypeStruct((n, w), BF), jax.ShapeDtypeStruct((n, w), F32),
            jax.ShapeDtypeStruct((chunks, CHUNK, 512), BF), jax.ShapeDtypeStruct((16, 512), F32)],
        in_specs=[ANY] * (len(given) + 4) + [vm, vm],
        out_specs=[ANY] * 3 + [vm],
        scratch_shapes=[pltpu.VMEM(entry.shape, entry.dtype) for entry in plans[0]]
        + [pltpu.SemaphoreType.DMA((2, len(plans[0]))), pltpu.SemaphoreType.DMA, pltpu.SemaphoreType.DMA,
           pltpu.SemaphoreType.DMA, pltpu.VMEM((n, w), BF), pltpu.VMEM((n, w), F32)]
        + [pltpu.VMEM((2, 4, w, w), BF), pltpu.VMEM((2, 16, w), F32)]
        + Vectors.scratch(devices) + sums_scratch + bwd_scratch(n, w),
        compiler_params=pltpu.CompilerParams(collective_id=1, has_side_effects=True, vmem_limit_bytes=VMEM_LIMIT),
        name="backward_and_sums",
    )(*given, *[array for pair in groups for array in pair], *vectors)


def unpack_kernel(kinds, g_ref, mem_ref, out_ref, low_far_ref, grad_ref, grad_far_ref, s_ref, *refs):
    n = len(kinds)
    low_out, grad_out = refs[:2]
    outs = refs[2 : n + 2]
    b_in, b_out, gains, shifts = refs[n + 2 : n + 6]
    chunk, stage, in_sem, sem, low_buf, grad_buf, far_buf, row_in, row_out = refs[n + 6 :]
    section = lax.axis_index("section")
    chunks = chunk.shape[0]
    loads = [pltpu.make_async_copy(g_ref.at[c], chunk.at[c], in_sem.at[c]) for c in range(chunks)]
    fetch = [
        pltpu.make_async_copy(mem_ref, low_buf.at[0], row_in.at[0]),
        pltpu.make_async_copy(low_far_ref, low_buf.at[1], row_in.at[1]),
        pltpu.make_async_copy(grad_ref, grad_buf.at[0], row_in.at[2]),
        pltpu.make_async_copy(grad_far_ref, far_buf, row_in.at[3]),
    ]
    send = [
        pltpu.make_async_copy(low_buf.at[0], low_out.at[section], row_out.at[0]),
        pltpu.make_async_copy(low_buf.at[1], low_out.at[1 - section], row_out.at[1]),
        pltpu.make_async_copy(grad_buf.at[0], grad_out.at[section], row_out.at[2]),
        pltpu.make_async_copy(grad_buf.at[1], grad_out.at[1 - section], row_out.at[3]),
    ]
    for c in range(4):
        loads[c].start()
    for one in fetch[1:]:
        one.start()

    @pl.when(section == 0)
    def _():
        fetch[0].start()

    @pl.when(section != 0)
    def _():
        pltpu.make_async_copy(out_ref, low_buf.at[0], row_in.at[0]).start()

    for c in range(4, chunks):
        loads[c].start()
    for k in range(4):
        b_in[:, k * 512 : (k + 1) * 512] = s_ref[k : k + 1, :]
    b_out[...] = s_ref[4:5, :]
    for k in range(3):
        gains[k] = s_ref[5 + k : 6 + k, :]
        shifts[k] = s_ref[8 + k : 9 + k, :]

    slots = stage.shape[0]
    copies, c = [], 0
    for kind, (count, flipped, axis) in enumerate(kinds):
        for k in range(count):
            at = slice(k * 512, k * 512 + 512)
            dst = outs[kind].at[:, at] if axis else outs[kind].at[at, :]
            copies.append(pltpu.make_async_copy(stage.at[c % slots], dst, sem.at[c % slots]))
            loads[c].wait()
            if c >= slots:
                copies[c - slots].wait()
            value = chunk[c].astype(F32)
            stage[c % slots] = value.T if flipped else value
            copies[c].start()
            if c < 4:
                fetch[c].wait()
                if c == 3:
                    grad_buf[1] = far_buf[...].astype(F32)
                send[c].start()
            c += 1
    for copy in copies[-slots:] + send:
        copy.wait()


def unpack(g, low, low_far, grad, grad_far, vectors, kinds, shapes):
    n, w = low_far.shape
    vm = pl.BlockSpec(memory_space=pltpu.VMEM)
    vector_shapes = [(1, 4 * w), (1, w), (3, 1, w), (3, 1, w)]
    return pl.pallas_call(
        functools.partial(unpack_kernel, kinds),
        out_shape=[jax.ShapeDtypeStruct((2, n, w), BF), jax.ShapeDtypeStruct((2, n, w), F32)]
        + [jax.ShapeDtypeStruct(s, F32) for s in shapes + vector_shapes],
        in_specs=[ANY] * 6 + [vm],
        out_specs=[ANY] * (len(shapes) + 2) + [vm] * 4,
        scratch_shapes=[
            pltpu.VMEM(g.shape, BF), pltpu.VMEM((6, 512, 512), F32),
            pltpu.SemaphoreType.DMA((g.shape[0],)), pltpu.SemaphoreType.DMA((6,)),
            pltpu.VMEM((2, n, w), BF), pltpu.VMEM((2, n, w), F32), pltpu.VMEM((n, w), BF),
            pltpu.SemaphoreType.DMA((4,)), pltpu.SemaphoreType.DMA((4,)),
        ],
        compiler_params=pltpu.CompilerParams(vmem_limit_bytes=VMEM_LIMIT),
        name="unpack_results",
    )(g, *low, low_far, grad, grad_far, vectors)


class Spread:
    def __init__(self, devices, weights, land, send_sem, recv_sem):
        self.weights, self.land, self.send_sem, self.recv_sem = weights, land, send_sem, recv_sem
        self.index, self.section = lax.axis_index("dp"), lax.axis_index("section")
        self.bits = halvings(devices, 512)[0]
        self.across = (1 - self.section, self.index)
        self.mates = [(self.section, partner_of(self.index, bit)) for bit in self.bits]
        self.chunks = []
        for w, ref in enumerate(weights):
            rows, cols = ref.shape
            self.chunks += [(w, r, c) for r in range(0, rows, 512) for c in range(0, cols, 512)]
        self.steps = len(self.bits) + 1
        self.lags = list(range(self.steps))
        if self.steps <= 5:
            self.lags[-2:] = [lag + 1 for lag in self.lags[-2:]]
        self.ticks = len(self.chunks) + self.lags[-1]

    def copy(self, c, step, src=None):
        if step == 0:
            count, device = len(self.bits), self.across
        else:
            bit = self.bits[len(self.bits) - step]
            count, device = bit + 1, self.mates[bit]
        at, size = place(self.index, count, 512)
        part = self.land.at[c, pl.ds(pl.multiple_of(at, 16), size)]
        return pltpu.make_async_remote_copy(
            src_ref=part if src is None else src, dst_ref=part, send_sem=self.send_sem.at[step, c],
            recv_sem=self.recv_sem.at[step, c], device_id=device, device_id_type=MESH)

    def begin(self, c):
        w, r, col = self.chunks[c]
        at, size = place(self.index, len(self.bits), 512)
        self.copy(c, 0, self.weights[w].at[pl.ds(pl.multiple_of(r + at, 16), size), col : col + 512]).start()

    def tick(self, t):
        for step in range(1, self.steps + 1):
            c = t - self.lags[step - 1]

            @pl.when((c >= 0) & (c < len(self.chunks)))
            def _(step=step, c=c):
                self.copy(c, step - 1).wait()
                if step < self.steps:
                    self.copy(c, step).start()


def head_kernel(devices, plan, shapes, *refs):
    refs = list(refs)
    take = lambda n: [refs.pop(0) for _ in range(n)]
    given = [take(len(entry.arrays)) for entry in plan]
    tokens, *weights = take(6)
    b_in, b_out, gains, shifts = take(4)
    outs = take(2 * len(shapes))
    far_tokens, own_vectors, far_vectors, *far = take(8)
    buffers = take(len(plan))
    results = [Result(None, ref) for ref in take(2 * len(shapes))]
    in_sem, out_sem, far_x, small_ref, far_small, swap_send, swap_recv, keep_sem = take(8)
    land, send_sem, recv_sem, flush_sem = take(4)
    section = lax.axis_index("section")
    spread = Spread(devices, weights, land, send_sem, recv_sem)
    own = [Operand(entry.copy(ref, buffers[k], in_sem.at[k], section), buffers[k])
           for k, (entry, ref) in enumerate(zip(plan, given))]
    for k, result in enumerate(results):
        result.copy = pltpu.make_async_copy(result.ref, outs[k], out_sem.at[k])
    small_ref[...] = jnp.zeros(small_ref.shape, F32)
    for k in range(4):
        small_ref[k : k + 1, :] = b_in[:, k * 512 : (k + 1) * 512]
    small_ref[4:5, :] = b_out[...]
    for k in range(3):
        small_ref[5 + k : 6 + k, :] = gains[k]
        small_ref[8 + k : 9 + k, :] = shifts[k]
    greet([spread.across] + spread.mates)
    for c in range(len(spread.chunks)):
        spread.begin(c)
    swaps = [
        pltpu.make_async_remote_copy(
            src_ref=src, dst_ref=dst, send_sem=swap_send.at[k], recv_sem=swap_recv.at[k],
            device_id=spread.across, device_id_type=MESH)
        for k, (src, dst) in enumerate([(small_ref, far_small), (tokens.at[1 - section], far_x)])
    ]
    swaps[0].start()

    def own_tick(k):
        spread.tick(k)
        if isinstance(k, int) and k == 1:
            swaps[1].start()

    def flush(c):
        w, r, col = spread.chunks[c]
        return pltpu.make_async_copy(land.at[c], far[w].at[r : r + 512, col : col + 512], flush_sem.at[c])

    x_ref, w_ref, wout_ref, ids_ref, far_ids = ready(*own)
    width = x_ref.shape[1]
    n = len(shapes)
    self_forward(section == 1, x_ref, ids_ref,
                 [w_ref.at[:, k * width : (k + 1) * width] for k in range(3)] + [wout_ref],
                 small_ref, results[:n], own_tick, *refs)
    for one in swaps:
        one.wait()
    keep = [
        pltpu.make_async_copy(src, dst, keep_sem.at[k])
        for k, (src, dst) in enumerate([(far_x, far_tokens), (small_ref, own_vectors), (far_small, far_vectors)])
    ]
    for one in keep:
        one.start()
    self_forward(section == 0, far_x, far_ids, [land.at[k] for k in range(4)], far_small, results[n:],
                 lambda k: spread.tick(8 + k), *refs)
    done = 15 - spread.lags[-1]
    for c in range(done + 1):
        flush(c).start()
    for t in range(16, spread.ticks):
        spread.tick(t)
        flush(t - spread.lags[-1]).start()
    for c in range(len(spread.chunks)):
        flush(c).wait()
    for one in keep:
        one.wait()
    for result in results:
        result.copy.wait()


def forward_and_weights(own, tokens, vectors, weights, devices):
    plan = [a if isinstance(a, Pick) else Pick(a) for a in own]
    n, w = plan[0].shape
    shapes = [((w, n), BF), ((n, w), BF), ((n, w), BF), ((w, n), BF), ((HEADS, n), F32), ((n, w), BF), ((n, w), BF)]
    given = [array for entry in plan for array in entry.arrays] + [tokens, *weights]
    steps = len(halvings(devices, 512)[0]) + 1
    count = sum(a.size for a in weights) // 512**2
    dma = pltpu.SemaphoreType.DMA
    outs = pl.pallas_call(
        functools.partial(head_kernel, devices, plan, shapes),
        out_shape=[jax.ShapeDtypeStruct(s, d) for s, d in shapes * 2]
        + [jax.ShapeDtypeStruct((n, w), BF)] + [jax.ShapeDtypeStruct((16, w), F32)] * 2
        + [jax.ShapeDtypeStruct(a.shape, BF) for a in weights],
        in_specs=[ANY] * len(given) + [pl.BlockSpec(memory_space=pltpu.VMEM)] * 4,
        out_specs=[ANY] * (2 * len(shapes) + 8),
        scratch_shapes=[pltpu.VMEM(entry.shape, entry.dtype) for entry in plan]
        + [pltpu.VMEM(s, d) for s, d in shapes * 2]
        + [dma((len(plan),)), dma((2 * len(shapes),)), pltpu.VMEM((n, w), BF),
           pltpu.VMEM((16, w), F32), pltpu.VMEM((16, w), F32), dma((2,)), dma((2,)), dma((3,))]
        + [pltpu.VMEM((count, 512, 512), BF), dma((steps, count)), dma((steps, count)), dma((count,))]
        + fwd_scratch(n, w),
        compiler_params=pltpu.CompilerParams(collective_id=0, has_side_effects=True, vmem_limit_bytes=VMEM_LIMIT),
        name="forward_and_weights",
    )(*given, *vectors)
    k = len(shapes)
    return outs[:k], outs[k : 2 * k], outs[2 * k], outs[2 * k + 1], outs[2 * k + 2], outs[2 * k + 3 :]


def shards(layer_input, cotangent, src_segments, tgt_segments, attn_qkv, attn_out, cross_proj,
           ffn_in, ffn_in_bias, ffn_out, ffn_out_bias, norm_gain, norm_bias):
    devices = lax.axis_size("dp")
    swap = lambda a: lax.ppermute(a, "section", [(0, 1), (1, 0)])
    vectors = [ffn_in_bias, ffn_out_bias, norm_gain.transpose(1, 0, 2), norm_bias.transpose(1, 0, 2)]
    tokens = layer_input[0, :, 0]
    near = (attn_qkv[0], attn_out[0], cross_proj[0], ffn_in[0], ffn_out[0])
    src, tgt, cot = Row(src_segments), Row(tgt_segments), Row(cotangent[:, 0])
    (*own_saved, own_hid), (*far_saved, far_hid), far_tokens, vectors, far_vectors, far = forward_and_weights(
        [Row(tokens), near[0], near[1], Pick(src, tgt), Pick(tgt, src)], tokens, vectors, near, devices)
    enc = [Pick(a, b) for a, b in zip(near, far)]
    dec = [Pick(b, a) for a, b in zip(near, far)]
    enc_small, dec_small = Pick(vectors, far_vectors), Pick(far_vectors, vectors)
    src, tgt, cot = Pick(src), Pick(tgt), Pick(cot)
    e1, d1 = Pick(own_hid, far_hid), Pick(far_hid, own_hid)
    g, gp, r2, mem, kv, cq, catt, clse, out, away, dres, dw_dffn, s_dffn = middle(
        e1, enc[3], enc_small, enc[4], enc[2], d1, tgt, src, dec[2], dec_small, dec[3], dec[4], cot)
    low_far = swap(away)
    dh1, dw_dcross, dw_ecross, de1, dw_effn, s_effn = middle_back(
        dres, d1, mem, tgt, src, cq, kv, catt, clse, dec[2], enc[2], r2, enc_small, enc[4], gp, enc[3], e1, g)
    de1, low_far = lax.optimization_barrier((de1, low_far))

    def operands(dh, saved, tokens, ids, weights, small):
        qT, k, v, att, lse, res = saved
        return [dh, res, tokens, ids, qT, k, v, att, lse, weights[0], weights[1], small]

    far_grad, own_grad, sums, s = backward_and_sums(
        operands(de1, [Pick(a, b) for a, b in zip(own_saved, far_saved)], Pick(Row(tokens), far_tokens), src, enc, enc_small),
        operands(dh1, [Pick(b, a) for a, b in zip(own_saved, far_saved)], Pick(far_tokens, Row(tokens)), tgt, dec, dec_small),
        [(dw_effn, dw_dffn), (dw_ecross, dw_dcross)], (s_effn, s_dffn), devices)
    kinds = ((4, False, 1), (4, True, 0), (2, True, 1), (3, True, 1), (1, False, 0))
    layer_output, input_grad, win, wout, cross, qkv, wo, b_in, b_out, gains, shifts = unpack(
        sums, (mem, out), low_far, own_grad, far_grad, s, kinds,
        [ffn_in.shape[1:], ffn_out.shape[1:], cross_proj.shape[1:], attn_qkv.shape[1:], attn_out.shape[1:]])
    return (layer_output[None, :, None], input_grad[None, :, None], qkv[None], wo[None], cross[None], win[None],
            b_in, wout[None], b_out, gains.transpose(1, 0, 2), shifts.transpose(1, 0, 2))


def solution(mesh):
    return jax.shard_map(
        shards,
        mesh=mesh,
        in_specs=(
            P("section", None, "dp", None, None),
            P(None, "dp", None, None),
            P(None, "dp", None),
            P(None, "dp", None),
            P("section", None, None),
            P("section", None, None),
            P("section", None, None),
            P("section", None, None),
            P("section", None),
            P("section", None, None),
            P("section", None),
            P("section", None, None),
            P("section", None, None),
        ),
        out_specs=(
            P("section", None, "dp", None, None),
            P("section", None, "dp", None, None),
            P("section", None, None),
            P("section", None, None),
            P("section", None, None),
            P("section", None, None),
            P("section", None),
            P("section", None, None),
            P("section", None),
            P("section", None, None),
            P("section", None, None),
        ),
        check_vma=False,
    )
```
